128 devices in a mesh: gx: 32 (over y, x, core), gy: 4 (over z).
Axes of the slice: x: 4, y: 4, z: 4, core: 2. Of those that a mesh axis runs over, the one named last changes fastest.
Arguments:
- flux_x: float32 [5, 512, 128, 128], P(None, 'gx', 'gy'), may hold values from -6 to 6
- flux_y: float32 [5, 512, 128, 128], P(None, 'gx', 'gy'), may hold values from -6 to 6
- state: float32 [5, 512, 128, 128], P(None, 'gx', 'gy'), may hold values from -10 to 10
- metric_x: float32 [512, 128], P('gx', 'gy'), may hold values from 0.5 to 2
- metric_y: float32 [512, 128], P('gx', 'gy'), may hold values from 0.5 to 2
- filter_gap: float32 [512], P('gx'), may hold values from 7.8125e-05 to 0.0003125
Outputs:
- section_state: float32 [5, 512, 128, 128], P(None, 'gx', 'gy')
The draws below stay inside these ranges and needn't reach their ends.
All inputs are finite; a program needn't handle non-finite values.
Results may differ from the reference program's by a relative error of at most 0.0003.
Values sent between devices are 32-bit elements; how exact they have to be, the bound alone decides.
No kernel may reach another device: no remote copies, remote signals or barrier semaphores. Data moves between devices by JAX's collectives and lax.ppermute only.
A program may use at most 64 MiB of HBM per device.

```python
import math
import jax
import jax.numpy as jnp
from jax import lax

VARS = 5
NX = 512
NY = 128
NZ = 128


def draw_state(key, part):
    shape_all = (VARS, NX, NY, NZ)
    key_noise = jax.random.fold_in(key, 11)
    key_wave = jax.random.fold_in(key, 12)
    column = lax.broadcasted_iota(jnp.int32, shape_all, 1)
    parity = (1 - 2 * (column % 2)).astype(jnp.float32)
    wave_amp = jax.random.truncated_normal(key_wave, -4.0, 4.0, (VARS, 1, NY, NZ), jnp.float32)
    noise = jax.random.truncated_normal(key_noise, -4.0, 4.0, shape_all, jnp.float32)
    values = noise + 0.8 * parity * wave_amp
    return values


def shard_levels(key, extent, shards, least, high):
    def one(axis_at, parts):
        steps = jax.random.uniform(jax.random.fold_in(jax.random.fold_in(key, 6), axis_at), (parts,), jnp.float32, least / len(shards), high / len(shards))
        return jnp.repeat(jnp.exp(steps), extent[axis_at] // parts).reshape((-1,) + (1,) * (len(extent) - axis_at - 1))

    loudness = one(*shards[0])
    for cut in shards[1:]:
        loudness = loudness * one(*cut)
    return loudness


def centred(rng, dims, deviation, limit, split=(), kind=jnp.bfloat16):
    gain = shard_levels(rng, dims, split, -0.22, 0.18) if split else 1.0
    array = jax.random.normal(rng, dims, jnp.float32) * deviation * gain
    return jnp.minimum(jnp.maximum(array, -limit), limit).astype(kind)


def setup_inputs(seed: int = 0) -> dict:
    arg_keys = jax.random.split(jax.random.key(seed), 7)
    return {
        "flux_x": centred(arg_keys[0], (VARS, NX, NY, NZ), 1.0, 6.0, ((1, 32), (2, 4)), jnp.float32),
        "flux_y": centred(arg_keys[1], (VARS, NX, NY, NZ), 1.0, 6.0, ((1, 32), (2, 4)), jnp.float32),
        "state": draw_state(jax.random.fold_in(arg_keys[6], 71), 0),
        "metric_x": jnp.clip(jnp.exp(math.log(2.0) - 1.3862944 * jax.random.uniform(arg_keys[3], (NX, NY), jnp.float32) ** shard_levels(arg_keys[3], (NX, NY), ((0, 32), (1, 4)), -0.2, 0.2)), 0.5, 2.0),
        "metric_y": jnp.clip(jnp.exp(math.log(2.0) - 1.3862944 * jax.random.uniform(arg_keys[4], (NX, NY), jnp.float32) ** shard_levels(arg_keys[4], (NX, NY), ((0, 32), (1, 4)), -0.2, 0.2)), 0.5, 2.0),
        "filter_gap": jnp.clip(jnp.exp(math.log(0.0003125) - 1.3862944 * jax.random.uniform(arg_keys[5], (NX,), jnp.float32) ** shard_levels(arg_keys[5], (NX,), ((0, 32),), -0.2, 0.2)), 7.812499825377017e-05, 0.0003125),
    }


STEP_SIZE = 0.5
DERIV_ALPHA = 1.0 / 3.0
STENCIL_WEIGHTS = (4.0 / 5.0, -1.0 / 5.0, 4.0 / 105.0, -1.0 / 280.0)


def thomas_solve(under_coef, above_coef, right_side):
    zero_val = jnp.zeros(right_side.shape[1:], jnp.float32)
    zero_coef = jnp.zeros((), jnp.float32)

    def forward(carry, inputs):
        prev_coef, prev_val = carry
        under_row, above_row, value_row = inputs
        divisor = 1.0 - under_row * prev_coef
        next_coef = above_row / divisor
        next_val = (value_row - under_row * prev_val) / divisor
        return (next_coef, next_val), (next_coef, next_val)

    ignored, stored = lax.scan(forward, (zero_coef, zero_val), (under_coef, above_coef, right_side))

    def backward(carry, inputs):
        coef_row, val_row = inputs
        value_now = val_row - coef_row * carry
        return value_now, value_now

    ignored_too, solved = lax.scan(backward, zero_val, stored, reverse=True)
    return solved


def reference(flux_x, flux_y, state, metric_x, metric_y, filter_gap):
    cells_x = flux_x.shape[1]

    def offset(padded, shift_by):
        return lax.slice_in_dim(padded, 3 + shift_by, 3 + shift_by + cells_x, axis=1)

    widths = ((0, 0), (3, 3), (0, 0), (0, 0))
    flux_pad = jnp.pad(flux_x, widths)
    state_pad = jnp.pad(state, widths)
    rhs_deriv = (7.0 / 9.0) * (offset(flux_pad, 1) - offset(flux_pad, -1)) + (1.0 / 36.0) * (offset(flux_pad, 2) - offset(flux_pad, -2))
    filter_alpha = 0.5 - filter_gap
    weight = filter_alpha[None, :, None, None]
    rhs_filter = (11.0 / 16.0 + 5.0 * weight / 8.0) * state
    rhs_filter = rhs_filter + (15.0 / 32.0 + 17.0 * weight / 16.0) / 2.0 * (offset(state_pad, 1) + offset(state_pad, -1))
    rhs_filter = rhs_filter + (-3.0 / 16.0 + 3.0 * weight / 8.0) / 2.0 * (offset(state_pad, 2) + offset(state_pad, -2))
    rhs_filter = rhs_filter + (1.0 / 32.0 - weight / 16.0) / 2.0 * (offset(state_pad, 3) + offset(state_pad, -3))
    row_index = jnp.arange(cells_x)
    inner_low = row_index > 0
    inner_high = row_index < cells_x - 1
    third_coef = jnp.full((cells_x,), DERIV_ALPHA, jnp.float32)
    zero_row = jnp.zeros((cells_x,), jnp.float32)
    deriv_x = jnp.moveaxis(thomas_solve(jnp.where(inner_low, third_coef, zero_row), jnp.where(inner_high, third_coef, zero_row), jnp.moveaxis(rhs_deriv, 1, 0)), 0, 1)
    filtered = jnp.moveaxis(thomas_solve(jnp.where(inner_low, filter_alpha, zero_row), jnp.where(inner_high, filter_alpha, zero_row), jnp.moveaxis(rhs_filter, 1, 0)), 0, 1)
    deriv_y = jnp.zeros_like(flux_y)
    for distance, factor in enumerate(STENCIL_WEIGHTS, start=1):
        deriv_y = deriv_y + factor * (jnp.roll(flux_y, -distance, 2) - jnp.roll(flux_y, distance, 2))
    return filtered - STEP_SIZE * (metric_x[None, :, :, None] * deriv_x + metric_y[None, :, :, None] * deriv_y)
```

```python
import jax
import jax.numpy as jnp
import numpy as np
from jax import lax
from jax.experimental import pallas as pl
from jax.experimental.pallas import tpu as pltpu
from jax.sharding import PartitionSpec as P

NV, NI, NJ, NK = 5, 16, 32, 128
PIECES = 32
ROWS = 24
SUB = 8
F32 = jnp.float32
Y_WEIGHTS = (4.0 / 5.0, -1.0 / 5.0, 4.0 / 105.0, -1.0 / 280.0)
D6 = (1.0, -6.0, 15.0, -20.0, 15.0, -6.0, 1.0)

C_C, C_MG, C_LEFT, C_RIGHT, C_ENDS, C_HALO, C_COUNT = 0, 16, 32, 48, 64, 68, 80


def constant_system():
    a = 1.0 / 3.0
    t = np.eye(NI) + a * (np.eye(NI, k=1) + np.eye(NI, k=-1))
    inv = np.linalg.inv(t)
    m, c = [], []
    prev = 0.0
    for _ in range(NI):
        m.append(1.0 / (1.0 - a * prev))
        prev = a * m[-1]
        c.append(prev)
    left, right = -a * inv[:, 0], -a * inv[:, -1]
    hl, hr, tl, tr = left[0], right[0], left[-1], right[-1]
    e = [tr]
    for _ in range(PIECES - 1):
        e.append(tr + tl * hr * e[-1] / (1.0 - hl * e[-1]))
    return dict(m=m, c=c, inv=inv, left=left, right=right, hl=hl, hr=hr, tl=tl, tr=tr, e=e)


CS = constant_system()
RHO = 25.0 / 36.0


def flux_weight(row, j):
    w = CS["inv"][row]
    lo = w[j - 1] if 0 <= j - 1 < NI else 0.0
    hi = w[j + 1] if 0 <= j + 1 < NI else 0.0
    return float(RHO * (lo - hi))


def splat(x):
    return jnp.full((SUB, NK), x, F32)


def parity(name):
    return lax.rem(lax.axis_index(name), 2)


def pack_x_body(s_lo, s_hi, f_lo, f_hi, one, two):
    core = parity("gx")

    def put(right, left):
        right[:, 0:3] = s_hi[:, 1:4]
        right[:, 3:4] = f_hi[...]
        left[:, 0:3] = s_lo[:, 0:3]
        left[:, 3:4] = f_lo[...]

    @pl.when(core == 0)
    def _():
        put(one, two)

    @pl.when(core == 1)
    def _():
        put(two, one)


def pack_x(state, flux_x):
    out = jax.ShapeDtypeStruct((NV, 4, NJ, NK), F32)
    return pl.pallas_call(
        pack_x_body,
        grid=(1,),
        out_shape=(out, out),
        in_specs=[
            pl.BlockSpec((NV, 4, NJ, NK), lambda g: (0, 0, 0, 0)),
            pl.BlockSpec((NV, 4, NJ, NK), lambda g: (0, 3, 0, 0)),
            pl.BlockSpec((NV, 1, NJ, NK), lambda g: (0, 0, 0, 0)),
            pl.BlockSpec((NV, 1, NJ, NK), lambda g: (0, NI - 1, 0, 0)),
        ],
        out_specs=[pl.BlockSpec((NV, 4, NJ, NK), lambda g: (0, 0, 0, 0))] * 2,
        compiler_params=pltpu.CompilerParams(vmem_limit_bytes=8 << 20),
        cost_estimate=pl.CostEstimate(flops=0, bytes_accessed=1 << 20, transcendentals=0),
        name="pack_x",
    )(state, state, flux_x, flux_x)


def pack_y_body(lo, hi, one, two):
    odd = parity("gy")

    def put(top, bottom):
        for v in range(NV):
            for i in range(NI):
                rows = pl.ds(4 * (i % 2), 4)
                top[v, i // 2, rows, :] = hi[v, i, 4:8, :]
                bottom[v, i // 2, rows, :] = lo[v, i, 0:4, :]

    @pl.when(odd == 0)
    def _():
        put(one, two)

    @pl.when(odd == 1)
    def _():
        put(two, one)


def pack_y(flux_y):
    out = jax.ShapeDtypeStruct((NV, NI // 2, SUB, NK), F32)
    return pl.pallas_call(
        pack_y_body,
        grid=(1,),
        out_shape=(out, out),
        in_specs=[
            pl.BlockSpec((NV, NI, SUB, NK), lambda g: (0, 0, 0, 0)),
            pl.BlockSpec((NV, NI, SUB, NK), lambda g: (0, 0, NJ // SUB - 1, 0)),
        ],
        out_specs=[pl.BlockSpec((NV, NI // 2, SUB, NK), lambda g: (0, 0, 0, 0))] * 2,
        compiler_params=pltpu.CompilerParams(vmem_limit_bytes=8 << 20),
        cost_estimate=pl.CostEstimate(flops=0, bytes_accessed=1 << 20, transcendentals=0),
        name="pack_y",
    )(flux_y, flux_y)


def own_body(gap, s, f, coef, part):
    core = parity("gx")
    piece = lax.axis_index("gx")
    alpha = [0.5 - splat(gap[i]) for i in range(NI)]
    g32 = [(0.5 - a) * (1.0 / 32.0) for a in alpha]
    m, c = [None] * NI, [None] * NI
    n, b = [None] * NI, [None] * NI
    for k in range(NI):
        m[k] = 1.0 / (1.0 - alpha[k] * c[k - 1]) if k else jnp.ones((SUB, NK), F32)
        c[k] = alpha[k] * m[k]
        r = NI - 1 - k
        n[r] = 1.0 / (1.0 - alpha[r] * b[r + 1]) if k else jnp.ones((SUB, NK), F32)
        b[r] = alpha[r] * n[r]
    left, right = [None] * NI, [None] * NI
    wh, wt = [None] * NI, [None] * NI
    left[0], right[NI - 1] = -b[0], -c[NI - 1]
    qh, qt = None, None
    for k in range(NI):
        r = NI - 1 - k
        if k:
            left[k] = -b[k] * left[k - 1]
            right[r] = -c[r] * right[r + 1]
            qh = -b[k - 1] if qh is None else -b[k - 1] * qh
            qt = -c[r + 1] if qt is None else -c[r + 1] * qt
            wh[k] = qh * n[k]
            wt[r] = qt * m[r]
        else:
            wh[0], wt[NI - 1] = n[0], m[NI - 1]
    for k in range(NI):
        coef[C_C + k] = c[k]
        coef[C_MG + k] = m[k] * g32[k]
        coef[C_LEFT + k] = left[k]
        coef[C_RIGHT + k] = right[k]
    coef[C_ENDS + 0] = -alpha[0] * wh[0]
    coef[C_ENDS + 1] = -alpha[NI - 1] * wh[NI - 1]
    coef[C_ENDS + 2] = -alpha[0] * wt[0]
    coef[C_ENDS + 3] = -alpha[NI - 1] * wt[NI - 1]
    vh = [wh[k] * g32[k] for k in range(NI)]
    vt = [wt[k] * g32[k] for k in range(NI)]

    def spread(v, j):
        terms = [D6[q + 3] * v[j - q] for q in range(-3, 4) if 0 <= j - q < NI]
        total = terms[0]
        for t in terms[1:]:
            total = total + t
        return total

    for q in range(3):
        for e, v in enumerate((vh, vt)):
            low, high = spread(v, q - 3), spread(v, NI + q)
            coef[C_HALO + 3 * e + q] = jnp.where(core == 0, high, low)
            coef[C_HALO + 6 + 3 * e + q] = jnp.where(core == 0, low, high)
    sh = [spread(vh, j) for j in range(NI)]
    st = [spread(vt, j) for j in range(NI)]
    first = jnp.where(piece == 0, 1.0 / 36.0, 0.0).astype(F32)
    last = jnp.where(piece == PIECES - 1, -1.0 / 36.0, 0.0).astype(F32)
    inv = CS["inv"]
    fh = [flux_weight(0, j) for j in range(NI)]
    ft = [flux_weight(NI - 1, j) for j in range(NI)]
    fh[0] = fh[0] + float(inv[0, 0]) * first
    ft[0] = ft[0] + float(inv[NI - 1, 0]) * first
    fh[NI - 1] = fh[NI - 1] + float(inv[0, NI - 1]) * last
    ft[NI - 1] = ft[NI - 1] + float(inv[NI - 1, NI - 1]) * last

    for i in range(NI):
        coef[C_COUNT + i] = sh[i]
        coef[C_COUNT + NI + i] = st[i]

    @pl.loop(0, NV)
    def _(v):
        for q in range(NJ // SUB):
            rows = pl.ds(SUB * q, SUB)
            sums = [None] * 4
            for i in range(NI):
                a, z = s[v, i, rows, :], f[v, i, rows, :]
                terms = (
                    coef[C_COUNT + i] * a,
                    coef[C_COUNT + NI + i] * a,
                    fh[i] * z,
                    ft[i] * z,
                )
                sums = [t if o is None else o + t for o, t in zip(sums, terms)]
            for e in range(4):
                part[e, v, rows, :] = sums[e]


def own_share(gap, state, flux_x):
    return pl.pallas_call(
        own_body,
        out_shape=(
            jax.ShapeDtypeStruct((C_COUNT + 2 * NI, SUB, NK), F32),
            jax.ShapeDtypeStruct((4, NV, NJ, NK), F32),
        ),
        in_specs=[
            pl.BlockSpec(memory_space=pltpu.SMEM),
            pl.BlockSpec(memory_space=pltpu.VMEM),
            pl.BlockSpec(memory_space=pltpu.VMEM),
        ],
        out_specs=(pl.BlockSpec(memory_space=pltpu.VMEM),) * 2,
        compiler_params=pltpu.CompilerParams(vmem_limit_bytes=12 << 20),
        cost_estimate=pl.CostEstimate(flops=1 << 24, bytes_accessed=4 << 20, transcendentals=0),
        name="own_share",
    )(gap, state, flux_x)


def ends_body(coef, part, one, two, out):
    core = parity("gx")
    is0 = core == 0
    fw = []
    for row in (0, NI - 1):
        low, high = flux_weight(row, -1), flux_weight(row, NI)
        fw.append((jnp.where(is0, high, low).astype(F32), jnp.where(is0, low, high).astype(F32)))

    for v in range(NV):
        for q in range(NJ // SUB):
            rows = pl.ds(SUB * q, SUB)
            a = [one[v, k, rows, :] for k in range(4)]
            b = [two[v, k, rows, :] for k in range(4)]
            for e in range(2):
                total = part[e, v, rows, :]
                for k in range(3):
                    total = total + coef[C_HALO + 3 * e + k] * a[k]
                    total = total + coef[C_HALO + 6 + 3 * e + k] * b[k]
                out[pl.ds(ROWS * SUB * q + NV * e + v, SUB, stride=ROWS), :] = total
                total = part[2 + e, v, rows, :] + fw[e][0] * a[3] + fw[e][1] * b[3]
                out[pl.ds(ROWS * SUB * q + NV * (2 + e) + v, SUB, stride=ROWS), :] = total
    for k in range(4):
        for q in range(NJ // SUB):
            out[pl.ds(ROWS * SUB * q + 4 * NV + k, SUB, stride=ROWS), :] = coef[C_ENDS + k]


def end_values(coef, part, one, two):
    return pl.pallas_call(
        ends_body,
        out_shape=jax.ShapeDtypeStruct((PIECES * ROWS, NK), F32),
        in_specs=[pl.BlockSpec(memory_space=pltpu.VMEM)] * 4,
        out_specs=pl.BlockSpec(memory_space=pltpu.VMEM),
        compiler_params=pltpu.CompilerParams(vmem_limit_bytes=12 << 20),
        cost_estimate=pl.CostEstimate(flops=1 << 20, bytes_accessed=1 << 20, transcendentals=0),
        name="end_values",
    )(coef, part, one, two)


def join_body(x, out):
    def row(p, k):
        return jnp.broadcast_to(x[pl.ds(ROWS * p + 4 * NV + k, 1), :], (NV, NK))

    def value(p, k):
        return x[pl.ds(ROWS * p + NV * k, NV), :]

    scale = 8.0
    num, den = [None] * PIECES, [None] * PIECES
    hl, hr, tl, tr = ([row(p, k) for p in range(PIECES)] for k in range(4))
    num[0], den[0] = tr[0], jnp.ones((NV, NK), F32)
    for p in range(1, PIECES):
        cross = tl[p] * hr[p] - tr[p] * hl[p]
        num[p] = (scale * tr[p]) * den[p - 1] + (scale * cross) * num[p - 1]
        den[p] = scale * den[p - 1] - (scale * hl[p]) * num[p - 1]
    inv = [None] + [1.0 / den[p] for p in range(1, PIECES)]
    e = [num[0]] + [num[p] * inv[p] for p in range(1, PIECES)]
    keep = [None] + [(scale * den[p - 1]) * inv[p] for p in range(1, PIECES)]

    fwd_f, fwd_d = [value(0, 1)], [value(0, 3)]
    chl, chr_, ctl, ce = CS["hl"], CS["hr"], CS["tl"], CS["e"]
    for p in range(1, PIECES):
        a = tl[p] * keep[p]
        fwd_f.append((value(p, 1) + (a * e[p - 1]) * value(p, 0)) + a * fwd_f[-1])
        k = ctl / (1.0 - chl * ce[p - 1])
        fwd_d.append((value(p, 3) + float(k * ce[p - 1]) * value(p, 2)) + float(k) * fwd_d[-1])

    zero = jnp.zeros((NV, NK), F32)
    right_f, right_d = zero, zero
    for p in range(PIECES - 1, -1, -1):
        if p:
            h = keep[p]
            head_f = (value(p, 0) + hl[p] * fwd_f[p - 1]) * h + (hr[p] * h) * right_f
            left_f = fwd_f[p - 1] + e[p - 1] * head_f
            k = 1.0 / (1.0 - chl * ce[p - 1])
            head_d = (float(k) * value(p, 2) + float(k * chl) * fwd_d[p - 1]) + float(k * chr_) * right_d
            left_d = fwd_d[p - 1] + float(ce[p - 1]) * head_d
        else:
            head_f = head_d = left_f = left_d = zero
        for k, val in enumerate((left_f, right_f, left_d, right_d)):
            out[pl.ds(ROWS * p + NV * k, NV), :] = val
        right_f, right_d = head_f, head_d


def join(x):
    return pl.pallas_call(
        join_body,
        out_shape=jax.ShapeDtypeStruct((PIECES * ROWS, NK), F32),
        in_specs=[pl.BlockSpec(memory_space=pltpu.VMEM)],
        out_specs=pl.BlockSpec(memory_space=pltpu.VMEM),
        compiler_params=pltpu.CompilerParams(vmem_limit_bytes=12 << 20),
        cost_estimate=pl.CostEstimate(flops=1 << 20, bytes_accessed=1 << 20, transcendentals=0),
        name="join",
    )(x)


def block_body(coef, s, f, fy, one, two, yone, ytwo, mx, my, base, mxb, pad):
    piece = lax.axis_index("gx")
    is0 = parity("gx") == 0
    even = parity("gy") == 0
    first = jnp.where(piece == 0, 1.0 / 36.0, 0.0).astype(F32)
    last = jnp.where(piece == PIECES - 1, -1.0 / 36.0, 0.0).astype(F32)
    mxt = jnp.transpose(mx[...] * -0.5)
    myt = jnp.transpose(my[...] * -0.5)
    for i in range(NI):
        mxb[i] = jnp.broadcast_to(mxt[:, i : i + 1], (NJ, NK))
        pad[NI + i, 0:NJ, :] = jnp.broadcast_to(myt[:, i : i + 1], (NJ, NK))

    @pl.loop(0, NV)
    def _(v):
        for i in range(NI):
            for q in range(NJ // SUB):
                pad[i, pl.ds(SUB + SUB * q, SUB), :] = fy[v, i, pl.ds(SUB * q, SUB), :]
            part = pl.ds(4 * (i % 2), 4)
            a, b = yone[v, i // 2, part, :], ytwo[v, i // 2, part, :]
            pad[i, SUB - 4 : SUB, :] = jnp.where(even, b, a)
            pad[i, SUB + NJ : SUB + NJ + 4, :] = jnp.where(even, a, b)

        for q in range(NJ // SUB):
            rows = pl.ds(SUB * q, SUB)
            a = [one[v, k, rows, :] for k in range(4)]
            b = [two[v, k, rows, :] for k in range(4)]
            low = [jnp.where(is0, b[k], a[k]) for k in range(4)]
            high = [jnp.where(is0, a[k], b[k]) for k in range(4)]
            st = low[:3] + [s[v, i, rows, :] for i in range(NI)] + high[:3]
            fl = [low[3]] + [f[v, i, rows, :] for i in range(NI)] + [high[3]]
            ye, yd, us = [], [], []
            for i in range(NI):
                d6 = (
                    (st[i] + st[i + 6])
                    - 6.0 * (st[i + 1] + st[i + 5])
                    + 15.0 * (st[i + 2] + st[i + 4])
                    - 20.0 * st[i + 3]
                )
                y = coef[C_MG + i] * d6
                ye.append(y - coef[C_C + i] * ye[-1] if i else y)
                u = fl[i + 2] - fl[i]
                us.append(u)
                r = float(RHO * CS["m"][i]) * u
                if i == 0:
                    r = r + (first * float(CS["m"][i])) * fl[1]
                if i == NI - 1:
                    r = r + (last * float(CS["m"][i])) * fl[NI]
                yd.append(r - float(CS["c"][i]) * yd[-1] if i else r)
            xe = xd = None
            for i in range(NI - 1, -1, -1):
                xe = ye[i] if xe is None else ye[i] - coef[C_C + i] * xe
                xd = yd[i] if xd is None else yd[i] - float(CS["c"][i]) * xd
                at = SUB + SUB * q
                dy = None
                for k, w in enumerate(Y_WEIGHTS, start=1):
                    t = w * (pad[i, pl.ds(at + k, SUB), :] - pad[i, pl.ds(at - k, SUB), :])
                    dy = t if dy is None else dy + t
                d = us[i] * (1.0 / 12.0) + xd
                base[v, i, rows, :] = (st[i + 3] + xe) + (mxb[i, rows, :] * d + pad[NI + i, rows, :] * dy)


def block(coef, state, flux_x, flux_y, one, two, yone, ytwo, mx, my):
    return pl.pallas_call(
        block_body,
        out_shape=(
            jax.ShapeDtypeStruct((NV, NI, NJ, NK), F32),
            jax.ShapeDtypeStruct((NI, NJ, NK), F32),
        ),
        in_specs=[pl.BlockSpec(memory_space=pltpu.VMEM)] * 10,
        out_specs=(pl.BlockSpec(memory_space=pltpu.VMEM),) * 2,
        scratch_shapes=[pltpu.VMEM((2 * NI, SUB + NJ + SUB, NK), F32)],
        compiler_params=pltpu.CompilerParams(vmem_limit_bytes=16 << 20),
        cost_estimate=pl.CostEstimate(flops=1 << 25, bytes_accessed=8 << 20, transcendentals=0),
        name="block",
    )(coef, state, flux_x, flux_y, one, two, yone, ytwo, mx, my)


def finish_body(coef, base, mxb, z, out):
    @pl.loop(0, NV)
    def _(v):
        for q in range(NJ // SUB):
            rows = pl.ds(SUB * q, SUB)
            lf, rf, ld, rd = (
                z[pl.ds(ROWS * SUB * q + NV * k + v, SUB, stride=ROWS), :] for k in range(4)
            )
            for i in range(NI):
                d = float(CS["left"][i]) * ld + float(CS["right"][i]) * rd
                e = coef[C_LEFT + i] * lf + coef[C_RIGHT + i] * rf
                out[v, i, rows, :] = (base[v, i, rows, :] + e) + mxb[i, rows, :] * d


def finish(coef, base, mxb, z):
    return pl.pallas_call(
        finish_body,
        out_shape=jax.ShapeDtypeStruct((NV, NI, NJ, NK), F32),
        in_specs=[pl.BlockSpec(memory_space=pltpu.VMEM)] * 4,
        out_specs=pl.BlockSpec(memory_space=pltpu.VMEM),
        compiler_params=pltpu.CompilerParams(vmem_limit_bytes=12 << 20),
        cost_estimate=pl.CostEstimate(flops=1 << 22, bytes_accessed=3 << 20, transcendentals=0),
        name="finish",
    )(coef, base, mxb, z)


def exchange(x):
    y = lax.all_to_all(x.reshape(PIECES, ROWS, NK), "gx", 0, 0, tiled=True)
    return y.reshape(PIECES * ROWS, NK)


def per_device(flux_x, flux_y, state, metric_x, metric_y, filter_gap):
    count_y = lax.axis_size("gy")
    pair_in = [(i, i ^ 1) for i in range(PIECES)]
    pair_out = [(i, i + 1 if i % 2 else i - 1) for i in range(1, PIECES - 1)]
    y_in = [(i, i ^ 1) for i in range(count_y)]
    y_out = [(i, (i + 1 if i % 2 else i - 1) % count_y) for i in range(count_y)]

    send_one, send_two = pack_x(state, flux_x)
    one = lax.ppermute(send_one, "gx", pair_in)
    two = lax.ppermute(send_two, "gx", pair_out)
    ysend_one, ysend_two = pack_y(flux_y)
    yone = lax.ppermute(ysend_one, "gy", y_in)
    ytwo = lax.ppermute(ysend_two, "gy", y_out)
    coef, part = own_share(filter_gap, state, flux_x)
    ends = exchange(end_values(coef, part, one, two))
    base, mxb = block(coef, state, flux_x, flux_y, one, two, yone, ytwo, metric_x, metric_y)
    outside = exchange(join(ends))
    return finish(coef, base, mxb, outside)


def solution(mesh):
    return jax.shard_map(
        per_device,
        mesh=mesh,
        in_specs=(
            P(None, "gx", "gy", None),
            P(None, "gx", "gy", None),
            P(None, "gx", "gy", None),
            P("gx", "gy"),
            P("gx", "gy"),
            P("gx"),
        ),
        out_specs=P(None, "gx", "gy", None),
        check_vma=False,
    )
```

```python
import jax
import jax.numpy as jnp
import numpy as np
from jax import lax
from jax.experimental import pallas as pl
from jax.experimental.pallas import tpu as pltpu
from jax.sharding import PartitionSpec as P

NV, NI, NJ, NK = 5, 16, 32, 128
PIECES = 32
ROWS = 24
SUB = 8
F32 = jnp.float32
Y_WEIGHTS = (4.0 / 5.0, -1.0 / 5.0, 4.0 / 105.0, -1.0 / 280.0)
D6 = (1.0, -6.0, 15.0, -20.0, 15.0, -6.0, 1.0)

C_C, C_MG = 0, NI
C_LEFT, C_RIGHT = 0, NI
C_ENDS, C_HALO = 0, 4


def constant_system():
    a = 1.0 / 3.0
    t = np.eye(NI) + a * (np.eye(NI, k=1) + np.eye(NI, k=-1))
    inv = np.linalg.inv(t)
    m, c = [], []
    prev = 0.0
    for _ in range(NI):
        m.append(1.0 / (1.0 - a * prev))
        prev = a * m[-1]
        c.append(prev)
    left, right = -a * inv[:, 0], -a * inv[:, -1]
    hl, hr, tl, tr = left[0], right[0], left[-1], right[-1]
    e = [tr]
    for _ in range(PIECES - 1):
        e.append(tr + tl * hr * e[-1] / (1.0 - hl * e[-1]))
    return dict(m=m, c=c, inv=inv, left=left, right=right, hl=hl, hr=hr, tl=tl, tr=tr, e=e)


CS = constant_system()
RHO = 25.0 / 36.0


def flux_weight(row, j):
    w = CS["inv"][row]
    lo = w[j - 1] if 0 <= j - 1 < NI else 0.0
    hi = w[j + 1] if 0 <= j + 1 < NI else 0.0
    return float(RHO * (lo - hi))


def splat(x):
    return jnp.full((SUB, NK), x, F32)


def in_hbm(*arrays):
    return tuple(pltpu.with_memory_space_constraint(a, pltpu.HBM) for a in arrays)


def parity(name):
    return lax.rem(lax.axis_index(name), 2)


def pack_body(s, f, fy, one, two, yone, ytwo, lo, hi, sem):
    core, odd = parity("gx"), parity("gy")
    copies = [
        pltpu.make_async_copy(fy.at[:, :, 0:SUB, :], lo, sem.at[0]),
        pltpu.make_async_copy(fy.at[:, :, NJ - SUB : NJ, :], hi, sem.at[1]),
    ]
    for c in copies:
        c.start()

    def faces(right, left):
        moves = [
            pltpu.make_async_copy(s.at[:, NI - 3 : NI], right.at[:, 0:3], sem.at[2]),
            pltpu.make_async_copy(f.at[:, NI - 1 : NI], right.at[:, 3:4], sem.at[3]),
            pltpu.make_async_copy(s.at[:, 0:3], left.at[:, 0:3], sem.at[4]),
            pltpu.make_async_copy(f.at[:, 0:1], left.at[:, 3:4], sem.at[5]),
        ]
        for c in moves:
            c.start()
        for c in moves:
            c.wait()

    def rows(top, bottom):
        for v in range(NV):
            for i in range(NI):
                part = pl.ds(4 * (i % 2), 4)
                top[v, i // 2, part, :] = hi[v, i, 4:8, :]
                bottom[v, i // 2, part, :] = lo[v, i, 0:4, :]

    @pl.when(core == 0)
    def _():
        faces(one, two)

    @pl.when(core == 1)
    def _():
        faces(two, one)

    for c in copies:
        c.wait()

    @pl.when(odd == 0)
    def _():
        rows(yone, ytwo)

    @pl.when(odd == 1)
    def _():
        rows(ytwo, yone)


def pack(state, flux_x, flux_y):
    x_out = jax.ShapeDtypeStruct((NV, 4, NJ, NK), F32)
    y_out = jax.ShapeDtypeStruct((NV, NI // 2, SUB, NK), F32)
    return pl.pallas_call(
        pack_body,
        out_shape=(x_out, x_out, y_out, y_out),
        in_specs=[pl.BlockSpec(memory_space=pltpu.HBM)] * 3,
        out_specs=(pl.BlockSpec(memory_space=pltpu.VMEM),) * 4,
        scratch_shapes=[
            pltpu.VMEM((NV, NI, SUB, NK), F32),
            pltpu.VMEM((NV, NI, SUB, NK), F32),
            pltpu.SemaphoreType.DMA((6,)),
        ],
        compiler_params=pltpu.CompilerParams(vmem_limit_bytes=8 << 20),
        cost_estimate=pl.CostEstimate(flops=0, bytes_accessed=2 << 20, transcendentals=0),
        name="pack",
    )(*in_hbm(state, flux_x, flux_y))


def own_body(gap, s_hbm, f_hbm, inner, outer, edge, part, s, f, own, sem):
    loads = [
        (pltpu.make_async_copy(s_hbm.at[v], s.at[v], sem.at[0, v]), pltpu.make_async_copy(f_hbm.at[v], f.at[v], sem.at[1, v]))
        for v in range(NV)
    ]
    for pair in loads:
        for c in pair:
            c.start()
    core = parity("gx")
    piece = lax.axis_index("gx")
    alpha = [0.5 - splat(gap[i]) for i in range(NI)]
    g32 = [(0.5 - a) * (1.0 / 32.0) for a in alpha]
    m, c = [None] * NI, [None] * NI
    n, b = [None] * NI, [None] * NI
    for k in range(NI):
        m[k] = 1.0 / (1.0 - alpha[k] * c[k - 1]) if k else jnp.ones((SUB, NK), F32)
        c[k] = alpha[k] * m[k]
        r = NI - 1 - k
        n[r] = 1.0 / (1.0 - alpha[r] * b[r + 1]) if k else jnp.ones((SUB, NK), F32)
        b[r] = alpha[r] * n[r]
    left, right = [None] * NI, [None] * NI
    wh, wt = [None] * NI, [None] * NI
    left[0], right[NI - 1] = -b[0], -c[NI - 1]
    qh, qt = None, None
    for k in range(NI):
        r = NI - 1 - k
        if k:
            left[k] = -b[k] * left[k - 1]
            right[r] = -c[r] * right[r + 1]
            qh = -b[k - 1] if qh is None else -b[k - 1] * qh
            qt = -c[r + 1] if qt is None else -c[r + 1] * qt
            wh[k] = qh * n[k]
            wt[r] = qt * m[r]
        else:
            wh[0], wt[NI - 1] = n[0], m[NI - 1]
    for k in range(NI):
        inner[C_C + k] = c[k]
        inner[C_MG + k] = m[k] * g32[k]
        outer[C_LEFT + k] = left[k]
        outer[C_RIGHT + k] = right[k]
    edge[C_ENDS + 0] = -alpha[0] * wh[0]
    edge[C_ENDS + 1] = -alpha[NI - 1] * wh[NI - 1]
    edge[C_ENDS + 2] = -alpha[0] * wt[0]
    edge[C_ENDS + 3] = -alpha[NI - 1] * wt[NI - 1]
    vh = [wh[k] * g32[k] for k in range(NI)]
    vt = [wt[k] * g32[k] for k in range(NI)]

    def spread(v, j):
        terms = [D6[q + 3] * v[j - q] for q in range(-3, 4) if 0 <= j - q < NI]
        total = terms[0]
        for t in terms[1:]:
            total = total + t
        return total

    for q in range(3):
        for e, v in enumerate((vh, vt)):
            low, high = spread(v, q - 3), spread(v, NI + q)
            edge[C_HALO + 3 * e + q] = jnp.where(core == 0, high, low)
            edge[C_HALO + 6 + 3 * e + q] = jnp.where(core == 0, low, high)
    sh = [spread(vh, j) for j in range(NI)]
    st = [spread(vt, j) for j in range(NI)]
    first = jnp.where(piece == 0, 1.0 / 36.0, 0.0).astype(F32)
    last = jnp.where(piece == PIECES - 1, -1.0 / 36.0, 0.0).astype(F32)
    inv = CS["inv"]
    fh = [flux_weight(0, j) for j in range(NI)]
    ft = [flux_weight(NI - 1, j) for j in range(NI)]
    fh[0] = fh[0] + float(inv[0, 0]) * first
    ft[0] = ft[0] + float(inv[NI - 1, 0]) * first
    fh[NI - 1] = fh[NI - 1] + float(inv[0, NI - 1]) * last
    ft[NI - 1] = ft[NI - 1] + float(inv[NI - 1, NI - 1]) * last

    for i in range(NI):
        own[i] = sh[i]
        own[NI + i] = st[i]

    for v in range(NV):
        for c in loads[v]:
            c.wait()
        for q in range(NJ // SUB):
            rows = pl.ds(SUB * q, SUB)
            sums = [None] * 4
            for i in range(NI):
                a, z = s[v, i, rows, :], f[v, i, rows, :]
                terms = (
                    own[i] * a,
                    own[NI + i] * a,
                    fh[i] * z,
                    ft[i] * z,
                )
                sums = [t if o is None else o + t for o, t in zip(sums, terms)]
            for e in range(4):
                part[e, v, rows, :] = sums[e]


def own_share(gap, state, flux_x):
    return pl.pallas_call(
        own_body,
        out_shape=(
            jax.ShapeDtypeStruct((2 * NI, SUB, NK), F32),
            jax.ShapeDtypeStruct((2 * NI, SUB, NK), F32),
            jax.ShapeDtypeStruct((16, SUB, NK), F32),
            jax.ShapeDtypeStruct((4, NV, NJ, NK), F32),
        ),
        in_specs=[
            pl.BlockSpec(memory_space=pltpu.SMEM),
            pl.BlockSpec(memory_space=pltpu.HBM),
            pl.BlockSpec(memory_space=pltpu.HBM),
        ],
        out_specs=(pl.BlockSpec(memory_space=pltpu.VMEM),) * 4,
        scratch_shapes=[
            pltpu.VMEM((NV, NI, NJ, NK), F32),
            pltpu.VMEM((NV, NI, NJ, NK), F32),
            pltpu.VMEM((2 * NI, SUB, NK), F32),
            pltpu.SemaphoreType.DMA((2, NV)),
        ],
        compiler_params=pltpu.CompilerParams(vmem_limit_bytes=12 << 20),
        cost_estimate=pl.CostEstimate(flops=1 << 24, bytes_accessed=4 << 20, transcendentals=0),
        name="own_share",
    )(gap, *in_hbm(state, flux_x))


def ends_body(edge, part, one, two, out):
    core = parity("gx")
    is0 = core == 0
    fw = []
    for row in (0, NI - 1):
        low, high = flux_weight(row, -1), flux_weight(row, NI)
        fw.append((jnp.where(is0, high, low).astype(F32), jnp.where(is0, low, high).astype(F32)))

    for v in range(NV):
        for q in range(NJ // SUB):
            rows = pl.ds(SUB * q, SUB)
            a = [one[v, k, rows, :] for k in range(4)]
            b = [two[v, k, rows, :] for k in range(4)]
            for e in range(2):
                total = part[e, v, rows, :]
                for k in range(3):
                    total = total + edge[C_HALO + 3 * e + k] * a[k]
                    total = total + edge[C_HALO + 6 + 3 * e + k] * b[k]
                out[pl.ds(ROWS * SUB * q + NV * e + v, SUB, stride=ROWS), :] = total
                total = part[2 + e, v, rows, :] + fw[e][0] * a[3] + fw[e][1] * b[3]
                out[pl.ds(ROWS * SUB * q + NV * (2 + e) + v, SUB, stride=ROWS), :] = total
    for k in range(4):
        for q in range(NJ // SUB):
            out[pl.ds(ROWS * SUB * q + 4 * NV + k, SUB, stride=ROWS), :] = edge[C_ENDS + k]


def end_values(edge, part, one, two):
    return pl.pallas_call(
        ends_body,
        out_shape=jax.ShapeDtypeStruct((PIECES * ROWS, NK), F32),
        in_specs=[pl.BlockSpec(memory_space=pltpu.VMEM)] * 4,
        out_specs=pl.BlockSpec(memory_space=pltpu.VMEM),
        compiler_params=pltpu.CompilerParams(vmem_limit_bytes=12 << 20),
        cost_estimate=pl.CostEstimate(flops=1 << 20, bytes_accessed=1 << 20, transcendentals=0),
        name="end_values",
    )(edge, part, one, two)


def join_body(x, out):
    def row(p, k):
        return jnp.broadcast_to(x[pl.ds(ROWS * p + 4 * NV + k, 1), :], (NV, NK))

    def value(p, k):
        return x[pl.ds(ROWS * p + NV * k, NV), :]

    scale = 8.0
    num, den = [None] * PIECES, [None] * PIECES
    hl, hr, tl, tr = ([row(p, k) for p in range(PIECES)] for k in range(4))
    num[0], den[0] = tr[0], jnp.ones((NV, NK), F32)
    for p in range(1, PIECES):
        cross = tl[p] * hr[p] - tr[p] * hl[p]
        num[p] = (scale * tr[p]) * den[p - 1] + (scale * cross) * num[p - 1]
        den[p] = scale * den[p - 1] - (scale * hl[p]) * num[p - 1]
    inv = [None] + [1.0 / den[p] for p in range(1, PIECES)]
    e = [num[0]] + [num[p] * inv[p] for p in range(1, PIECES)]
    keep = [None] + [(scale * den[p - 1]) * inv[p] for p in range(1, PIECES)]

    fwd_f, fwd_d = [value(0, 1)], [value(0, 3)]
    chl, chr_, ctl, ce = CS["hl"], CS["hr"], CS["tl"], CS["e"]
    for p in range(1, PIECES):
        a = tl[p] * keep[p]
        fwd_f.append((value(p, 1) + (a * e[p - 1]) * value(p, 0)) + a * fwd_f[-1])
        k = ctl / (1.0 - chl * ce[p - 1])
        fwd_d.append((value(p, 3) + float(k * ce[p - 1]) * value(p, 2)) + float(k) * fwd_d[-1])

    zero = jnp.zeros((NV, NK), F32)
    right_f, right_d = zero, zero
    for p in range(PIECES - 1, -1, -1):
        if p:
            h = keep[p]
            head_f = (value(p, 0) + hl[p] * fwd_f[p - 1]) * h + (hr[p] * h) * right_f
            left_f = fwd_f[p - 1] + e[p - 1] * head_f
            k = 1.0 / (1.0 - chl * ce[p - 1])
            head_d = (float(k) * value(p, 2) + float(k * chl) * fwd_d[p - 1]) + float(k * chr_) * right_d
            left_d = fwd_d[p - 1] + float(ce[p - 1]) * head_d
        else:
            head_f = head_d = left_f = left_d = zero
        for k, val in enumerate((left_f, right_f, left_d, right_d)):
            out[pl.ds(ROWS * p + NV * k, NV), :] = val
        right_f, right_d = head_f, head_d


def join(x):
    return pl.pallas_call(
        join_body,
        out_shape=jax.ShapeDtypeStruct((PIECES * ROWS, NK), F32),
        in_specs=[pl.BlockSpec(memory_space=pltpu.VMEM)],
        out_specs=pl.BlockSpec(memory_space=pltpu.VMEM),
        compiler_params=pltpu.CompilerParams(vmem_limit_bytes=12 << 20),
        cost_estimate=pl.CostEstimate(flops=1 << 20, bytes_accessed=1 << 20, transcendentals=0),
        name="join",
    )(x)


def block_body(inner, s_hbm, f_hbm, fy_hbm, one, two, yone, ytwo, mx, my, base, mxb, s, f, fy, pad, sem):
    loads = [
        [pltpu.make_async_copy(h.at[v], t.at[v], sem.at[k, v]) for k, (h, t) in enumerate(((fy_hbm, fy), (s_hbm, s), (f_hbm, f)))]
        for v in range(NV)
    ]
    for group in loads:
        for c in group:
            c.start()
    piece = lax.axis_index("gx")
    is0 = parity("gx") == 0
    even = parity("gy") == 0
    first = jnp.where(piece == 0, 1.0 / 36.0, 0.0).astype(F32)
    last = jnp.where(piece == PIECES - 1, -1.0 / 36.0, 0.0).astype(F32)
    mxt = jnp.transpose(mx[...] * -0.5)
    myt = jnp.transpose(my[...] * -0.5)
    for i in range(NI):
        mxb[i] = jnp.broadcast_to(mxt[:, i : i + 1], (NJ, NK))
        pad[NI + i, 0:NJ, :] = jnp.broadcast_to(myt[:, i : i + 1], (NJ, NK))

    for v in range(NV):
        for c in loads[v]:
            c.wait()

    @pl.loop(0, NV)
    def _(v):
        for i in range(NI):
            for q in range(NJ // SUB):
                pad[i, pl.ds(SUB + SUB * q, SUB), :] = fy[v, i, pl.ds(SUB * q, SUB), :]
            part = pl.ds(4 * (i % 2), 4)
            a, b = yone[v, i // 2, part, :], ytwo[v, i // 2, part, :]
            pad[i, SUB - 4 : SUB, :] = jnp.where(even, b, a)
            pad[i, SUB + NJ : SUB + NJ + 4, :] = jnp.where(even, a, b)

        for q in range(NJ // SUB):
            rows = pl.ds(SUB * q, SUB)
            a = [one[v, k, rows, :] for k in range(4)]
            b = [two[v, k, rows, :] for k in range(4)]
            low = [jnp.where(is0, b[k], a[k]) for k in range(4)]
            high = [jnp.where(is0, a[k], b[k]) for k in range(4)]
            st = low[:3] + [s[v, i, rows, :] for i in range(NI)] + high[:3]
            fl = [low[3]] + [f[v, i, rows, :] for i in range(NI)] + [high[3]]
            ye, yd, us = [], [], []
            for i in range(NI):
                d6 = (
                    (st[i] + st[i + 6])
                    - 6.0 * (st[i + 1] + st[i + 5])
                    + 15.0 * (st[i + 2] + st[i + 4])
                    - 20.0 * st[i + 3]
                )
                y = inner[C_MG + i] * d6
                ye.append(y - inner[C_C + i] * ye[-1] if i else y)
                u = fl[i + 2] - fl[i]
                us.append(u)
                r = float(RHO * CS["m"][i]) * u
                if i == 0:
                    r = r + (first * float(CS["m"][i])) * fl[1]
                if i == NI - 1:
                    r = r + (last * float(CS["m"][i])) * fl[NI]
                yd.append(r - float(CS["c"][i]) * yd[-1] if i else r)
            xe = xd = None
            for i in range(NI - 1, -1, -1):
                xe = ye[i] if xe is None else ye[i] - inner[C_C + i] * xe
                xd = yd[i] if xd is None else yd[i] - float(CS["c"][i]) * xd
                at = SUB + SUB * q
                dy = None
                for k, w in enumerate(Y_WEIGHTS, start=1):
                    t = w * (pad[i, pl.ds(at + k, SUB), :] - pad[i, pl.ds(at - k, SUB), :])
                    dy = t if dy is None else dy + t
                d = us[i] * (1.0 / 12.0) + xd
                base[v, i, rows, :] = (st[i + 3] + xe) + (mxb[i, rows, :] * d + pad[NI + i, rows, :] * dy)


def block(inner, state, flux_x, flux_y, one, two, yone, ytwo, mx, my):
    vmem, hbm = pl.BlockSpec(memory_space=pltpu.VMEM), pl.BlockSpec(memory_space=pltpu.HBM)
    return pl.pallas_call(
        block_body,
        out_shape=(
            jax.ShapeDtypeStruct((NV, NI, NJ, NK), F32),
            jax.ShapeDtypeStruct((NI, NJ, NK), F32),
        ),
        in_specs=[vmem] + [hbm] * 3 + [vmem] * 6,
        out_specs=(vmem, vmem),
        scratch_shapes=[pltpu.VMEM((NV, NI, NJ, NK), F32)] * 3
        + [pltpu.VMEM((2 * NI, SUB + NJ + SUB, NK), F32), pltpu.SemaphoreType.DMA((3, NV))],
        compiler_params=pltpu.CompilerParams(vmem_limit_bytes=16 << 20),
        cost_estimate=pl.CostEstimate(flops=1 << 25, bytes_accessed=8 << 20, transcendentals=0),
        name="block",
    )(inner, *in_hbm(state, flux_x, flux_y), one, two, yone, ytwo, mx, my)


def finish_body(outer, base, mxb, z, out_hbm, out, sem):
    stores = [pltpu.make_async_copy(out.at[v], out_hbm.at[v], sem.at[v]) for v in range(NV)]
    for v in range(NV):
        for q in range(NJ // SUB):
            rows = pl.ds(SUB * q, SUB)
            lf, rf, ld, rd = (
                z[pl.ds(ROWS * SUB * q + NV * k + v, SUB, stride=ROWS), :] for k in range(4)
            )
            for i in range(NI):
                d = float(CS["left"][i]) * ld + float(CS["right"][i]) * rd
                e = outer[C_LEFT + i] * lf + outer[C_RIGHT + i] * rf
                out[v, i, rows, :] = (base[v, i, rows, :] + e) + mxb[i, rows, :] * d
        stores[v].start()
    for c in stores:
        c.wait()


def finish(outer, base, mxb, z):
    return pl.pallas_call(
        finish_body,
        out_shape=jax.ShapeDtypeStruct((NV, NI, NJ, NK), F32),
        in_specs=[pl.BlockSpec(memory_space=pltpu.VMEM)] * 4,
        out_specs=pl.BlockSpec(memory_space=pltpu.HBM),
        scratch_shapes=[pltpu.VMEM((NV, NI, NJ, NK), F32), pltpu.SemaphoreType.DMA((NV,))],
        compiler_params=pltpu.CompilerParams(vmem_limit_bytes=12 << 20),
        cost_estimate=pl.CostEstimate(flops=1 << 22, bytes_accessed=3 << 20, transcendentals=0),
        name="finish",
    )(outer, base, mxb, z)


def exchange(x):
    y = lax.all_to_all(x.reshape(PIECES, ROWS, NK), "gx", 0, 0, tiled=True)
    return y.reshape(PIECES * ROWS, NK)


def per_device(flux_x, flux_y, state, metric_x, metric_y, filter_gap):
    count_y = lax.axis_size("gy")
    pair_in = [(i, i ^ 1) for i in range(PIECES)]
    pair_out = [(i, i + 1 if i % 2 else i - 1) for i in range(1, PIECES - 1)]
    y_in = [(i, i ^ 1) for i in range(count_y)]
    y_out = [(i, (i + 1 if i % 2 else i - 1) % count_y) for i in range(count_y)]

    send_one, send_two, ysend_one, ysend_two = pack(state, flux_x, flux_y)
    one = lax.ppermute(send_one, "gx", pair_in)
    two = lax.ppermute(send_two, "gx", pair_out)
    yone = lax.ppermute(ysend_one, "gy", y_in)
    ytwo = lax.ppermute(ysend_two, "gy", y_out)
    inner, outer, edge, part = own_share(filter_gap, state, flux_x)
    ends = end_values(edge, part, one, two)
    ends, yone, ytwo = lax.optimization_barrier((ends, yone, ytwo))
    ends = exchange(ends)
    base, mxb = block(inner, state, flux_x, flux_y, one, two, yone, ytwo, metric_x, metric_y)
    ends, base, mxb = lax.optimization_barrier((ends, base, mxb))
    outside = exchange(join(ends))
    return finish(outer, base, mxb, outside)


def solution(mesh):
    return jax.shard_map(
        per_device,
        mesh=mesh,
        in_specs=(
            P(None, "gx", "gy", None),
            P(None, "gx", "gy", None),
            P(None, "gx", "gy", None),
            P("gx", "gy"),
            P("gx", "gy"),
            P("gx"),
        ),
        out_specs=P(None, "gx", "gy", None),
        check_vma=False,
    )
```

```python
import jax
import jax.numpy as jnp
import numpy as np
from jax import lax
from jax.experimental import pallas as pl
from jax.experimental.pallas import tpu as pltpu
from jax.sharding import PartitionSpec as P

NV, NI, NJ, NK = 5, 16, 32, 128
PIECES, PAIRS, HALF = 32, 16, 16
ROWS, WIDE = 24, 64
EDGE = 12 * NV * HALF
SUB = 8
F32 = jnp.float32
Y_WEIGHTS = (4.0 / 5.0, -1.0 / 5.0, 4.0 / 105.0, -1.0 / 280.0)
RHO = 25.0 / 36.0
D6 = (1.0, -6.0, 15.0, -20.0, 15.0, -6.0, 1.0)

C_C, C_MG = 0, NI
C_LEFT, C_RIGHT = 0, NI


def constant_system():
    a = 1.0 / 3.0
    t = np.eye(NI) + a * (np.eye(NI, k=1) + np.eye(NI, k=-1))
    inv = np.linalg.inv(t)
    m, c = [], []
    prev = 0.0
    for _ in range(NI):
        m.append(1.0 / (1.0 - a * prev))
        prev = a * m[-1]
        c.append(prev)
    left, right = -a * inv[:, 0], -a * inv[:, -1]
    hl, hr, tl, tr = left[0], right[0], left[-1], right[-1]
    d = 1.0 / (1.0 - tr * hl)
    w = RHO * np.array([-inv[0, 0], -inv[-1, 0], inv[0, -1], inv[-1, -1]])
    pair = dict(inv=d, inv_hl=d * hl, inv_tr=d * tr, down=[hl * tl * d, hr * d, tl * d, tr * hr * d])
    pair["low"] = [w[0] + hr * hl * d * w[1], tl * d * w[1]]
    pair["high"] = [hr * d * w[2], w[3] + tl * tr * d * w[2]]
    for k in pair:
        pair[k] = [float(t) for t in pair[k]] if isinstance(pair[k], list) else float(pair[k])
    p = dict(hl=hl + hr * hl * tl * d, hr=hr * hr * d, tl=tl * tl * d, tr=tr + tl * tr * hr * d)
    e = [p["tr"]]
    for _ in range(PAIRS - 1):
        e.append(p["tr"] + p["tl"] * p["hr"] * e[-1] / (1.0 - p["hl"] * e[-1]))
    pair.update(p, e=e)
    return dict(m=m, c=c, inv=inv, left=left, right=right, hl=hl, hr=hr, tl=tl, tr=tr, pair=pair)


CS = constant_system()


def flux_weight(row, j):
    w = CS["inv"][row]
    lo = w[j - 1] if 0 <= j - 1 < NI else 0.0
    hi = w[j + 1] if 0 <= j + 1 < NI else 0.0
    return float(RHO * (lo - hi))


def splat(x):
    return jnp.full((SUB, NK), x, F32)


def in_hbm(*arrays):
    return tuple(pltpu.with_memory_space_constraint(a, pltpu.HBM) for a in arrays)


def parity(name):
    return lax.rem(lax.axis_index(name), 2)


def pack_body(s, f, fy, one, two, yone, ytwo, lo, hi, sem):
    core, odd = parity("gx"), parity("gy")
    copies = [
        pltpu.make_async_copy(fy.at[:, :, 0:SUB, :], lo, sem.at[0]),
        pltpu.make_async_copy(fy.at[:, :, NJ - SUB : NJ, :], hi, sem.at[1]),
    ]
    for c in copies:
        c.start()

    def faces(right, left):
        moves = [
            pltpu.make_async_copy(s.at[:, NI - 3 : NI], right.at[:, 0:3], sem.at[2]),
            pltpu.make_async_copy(f.at[:, NI - 1 : NI], right.at[:, 3:4], sem.at[3]),
            pltpu.make_async_copy(s.at[:, 0:3], left.at[:, 0:3], sem.at[4]),
            pltpu.make_async_copy(f.at[:, 0:1], left.at[:, 3:4], sem.at[5]),
        ]
        for c in moves:
            c.start()
        for c in moves:
            c.wait()

    def rows(top, bottom):
        for v in range(NV):
            for i in range(NI):
                part = pl.ds(4 * (i % 2), 4)
                top[v, i // 2, part, :] = hi[v, i, 4:8, :]
                bottom[v, i // 2, part, :] = lo[v, i, 0:4, :]

    @pl.when(core == 0)
    def _():
        faces(one, two)

    @pl.when(core == 1)
    def _():
        faces(two, one)

    for c in copies:
        c.wait()

    @pl.when(odd == 0)
    def _():
        rows(yone, ytwo)

    @pl.when(odd == 1)
    def _():
        rows(ytwo, yone)


def pack(state, flux_x, flux_y):
    x_out = jax.ShapeDtypeStruct((NV, 4, NJ, NK), F32)
    y_out = jax.ShapeDtypeStruct((NV, NI // 2, SUB, NK), F32)
    return pl.pallas_call(
        pack_body,
        out_shape=(x_out, x_out, y_out, y_out),
        in_specs=[pl.BlockSpec(memory_space=pltpu.HBM)] * 3,
        out_specs=(pl.BlockSpec(memory_space=pltpu.VMEM),) * 4,
        scratch_shapes=[
            pltpu.VMEM((NV, NI, SUB, NK), F32),
            pltpu.VMEM((NV, NI, SUB, NK), F32),
            pltpu.SemaphoreType.DMA((6,)),
        ],
        compiler_params=pltpu.CompilerParams(vmem_limit_bytes=8 << 20),
        cost_estimate=pl.CostEstimate(flops=0, bytes_accessed=2 << 20, transcendentals=0),
        name="pack",
    )(*in_hbm(state, flux_x, flux_y))


def own_body(gap, s_hbm, f_hbm, inner, outer, mine, send, s, f, own, sem):
    loads = [
        (
            pltpu.make_async_copy(s_hbm.at[v], s.at[v], sem.at[0, v]),
            pltpu.make_async_copy(f_hbm.at[v], f.at[v], sem.at[1, v]),
        )
        for v in range(NV)
    ]
    for both in loads:
        for c in both:
            c.start()
    core = parity("gx")
    piece = lax.axis_index("gx")
    alpha = [0.5 - splat(gap[i]) for i in range(NI)]
    g32 = [(0.5 - a) * (1.0 / 32.0) for a in alpha]
    m, c = [None] * NI, [None] * NI
    n, b = [None] * NI, [None] * NI
    for k in range(NI):
        m[k] = 1.0 / (1.0 - alpha[k] * c[k - 1]) if k else jnp.ones((SUB, NK), F32)
        c[k] = alpha[k] * m[k]
        r = NI - 1 - k
        n[r] = 1.0 / (1.0 - alpha[r] * b[r + 1]) if k else jnp.ones((SUB, NK), F32)
        b[r] = alpha[r] * n[r]
    left, right = [None] * NI, [None] * NI
    wh, wt = [None] * NI, [None] * NI
    left[0], right[NI - 1] = -b[0], -c[NI - 1]
    qh, qt = None, None
    for k in range(NI):
        r = NI - 1 - k
        if k:
            left[k] = -b[k] * left[k - 1]
            right[r] = -c[r] * right[r + 1]
            qh = -b[k - 1] if qh is None else -b[k - 1] * qh
            qt = -c[r + 1] if qt is None else -c[r + 1] * qt
            wh[k] = qh * n[k]
            wt[r] = qt * m[r]
        else:
            wh[0], wt[NI - 1] = n[0], m[NI - 1]
    for k in range(NI):
        inner[C_C + k] = c[k]
        inner[C_MG + k] = m[k] * g32[k]
        outer[C_LEFT + k] = left[k]
        outer[C_RIGHT + k] = right[k]
    vh = [wh[k] * g32[k] for k in range(NI)]
    vt = [wt[k] * g32[k] for k in range(NI)]

    def spread(v, j):
        terms = [D6[q + 3] * v[j - q] for q in range(-3, 4) if 0 <= j - q < NI]
        total = terms[0]
        for t in terms[1:]:
            total = total + t
        return total

    edge = [-alpha[0] * wh[0], -alpha[NI - 1] * wh[NI - 1], -alpha[0] * wt[0], -alpha[NI - 1] * wt[NI - 1]]
    low = [spread(v, q - 3) for v in (vh, vt) for q in range(3)]
    high = [spread(v, NI + q) for v in (vh, vt) for q in range(3)]
    edge += [jnp.where(core == 0, h, l) for h, l in zip(high, low)]
    edge += [jnp.where(core == 0, l, h) for h, l in zip(high, low)]
    for k, t in enumerate(edge):
        mine[pl.ds(EDGE + k, 1), :] = t[0:1]
        send[pl.ds(EDGE + k, 1), :] = t[0:1]

    first = jnp.where(piece == 0, 1.0 / 36.0, 0.0).astype(F32)
    last = jnp.where(piece == PIECES - 1, -1.0 / 36.0, 0.0).astype(F32)
    inv = CS["inv"]
    fh = [flux_weight(0, j) for j in range(NI)]
    ft = [flux_weight(NI - 1, j) for j in range(NI)]
    fh[0] = fh[0] + float(inv[0, 0]) * first
    ft[0] = ft[0] + float(inv[NI - 1, 0]) * first
    fh[NI - 1] = fh[NI - 1] + float(inv[0, NI - 1]) * last
    ft[NI - 1] = ft[NI - 1] + float(inv[NI - 1, NI - 1]) * last

    for i in range(NI):
        own[i] = spread(vh, i)
        own[NI + i] = spread(vt, i)

    s_in, f_in = (NI - 3) * (1 - core), (NI - 1) * (1 - core)
    s_out, f_out = (NI - 3) * core, (NI - 1) * core
    for v in range(NV):
        for c in loads[v]:
            c.wait()
        for out, half in ((mine, core), (send, 1 - core)):
            for r in range(HALF // SUB):
                rows = pl.ds(pl.multiple_of(HALF * half + SUB * r, SUB), SUB)
                sums = [None] * 4
                for i in range(NI):
                    a, z = s[v, i, rows, :], f[v, i, rows, :]
                    terms = (own[i] * a, own[NI + i] * a, fh[i] * z, ft[i] * z)
                    sums = [t if o is None else o + t for o, t in zip(sums, terms)]
                faces = [s[v, s_in + k, rows, :] for k in range(3)] + [f[v, f_in, rows, :]]
                faces += [s[v, s_out + k, rows, :] for k in range(3)] + [f[v, f_out, rows, :]]
                for k, t in enumerate(sums + faces):
                    out[pl.ds((NV * k + v) * HALF + SUB * r, SUB), :] = t


def own_share(gap, state, flux_x):
    vmem, hbm = pl.BlockSpec(memory_space=pltpu.VMEM), pl.BlockSpec(memory_space=pltpu.HBM)
    coef = jax.ShapeDtypeStruct((2 * NI, SUB, NK), F32)
    values = jax.ShapeDtypeStruct((EDGE + 16, NK), F32)
    return pl.pallas_call(
        own_body,
        out_shape=(coef, coef, values, values),
        in_specs=[pl.BlockSpec(memory_space=pltpu.SMEM), hbm, hbm],
        out_specs=(vmem,) * 4,
        scratch_shapes=[
            pltpu.VMEM((NV, NI, NJ, NK), F32),
            pltpu.VMEM((NV, NI, NJ, NK), F32),
            pltpu.VMEM((2 * NI, SUB, NK), F32),
            pltpu.SemaphoreType.DMA((2, NV)),
        ],
        compiler_params=pltpu.CompilerParams(vmem_limit_bytes=12 << 20),
        cost_estimate=pl.CostEstimate(flops=1 << 24, bytes_accessed=4 << 20, transcendentals=0),
        name="own_share",
    )(gap, *in_hbm(state, flux_x))


def pair_body(mine, got, out, mids):
    is0 = parity("gx") == 0

    def both(rows):
        x, y = mine[rows, :], got[rows, :]
        return jnp.where(is0, x, y), jnp.where(is0, y, x)

    ca, cb = zip(*(both(pl.ds(EDGE + k, 1)) for k in range(16)))
    ca, cb = ([jnp.broadcast_to(t, (SUB, NK)) for t in c] for c in (ca, cb))
    hla, hra, tla, tra = ca[:4]
    hlb, hrb, tlb, trb = cb[:4]
    inv = 1.0 / (1.0 - tra * hlb)
    down = [hlb * tla * inv, hrb * inv, tla * inv, tra * hrb * inv]
    for k, t in enumerate(down):
        mids[pl.ds(4 * NV * HALF + k, 1), :] = t[0:1]
    cross_h, cross_t = hra * inv, tlb * inv
    edge = [hla + hra * down[0], hra * down[1], tlb * down[2], trb + tlb * down[3]]
    edge += [ca[10 + q] + (cross_h * hlb) * ca[13 + q] for q in range(3)]
    edge += [cross_t * ca[13 + q] for q in range(3)]
    edge += [cross_h * cb[10 + q] for q in range(3)]
    edge += [cb[13 + q] + (cross_t * tra) * cb[10 + q] for q in range(3)]
    lane = lax.broadcasted_iota(jnp.int32, (SUB, NK), 1)
    packed = jnp.zeros((SUB, NK), F32)
    for k, t in enumerate(edge):
        packed = jnp.where(lane == k, t, packed)

    k = CS["pair"]
    for r in range(HALF // SUB):
        at = WIDE * SUB * r
        out[pl.ds(at + 12 * NV, SUB, stride=WIDE), :] = packed
        for v in range(NV):
            a, b = zip(*(both(pl.ds((NV * e + v) * HALF + SUB * r, SUB)) for e in range(12)))
            ha, ta, hb, tb = a[0], a[1], b[0], b[1]
            for q in range(3):
                ha, ta = ha + ca[4 + q] * b[4 + q], ta + ca[7 + q] * b[4 + q]
                hb, tb = hb + cb[4 + q] * a[4 + q], tb + cb[7 + q] * a[4 + q]
            head = (hb + hlb * ta) * inv
            tail = (ta + tra * hb) * inv
            da, ea = a[2] + flux_weight(0, NI) * b[7], a[3] + flux_weight(NI - 1, NI) * b[7]
            db, eb = b[2] + flux_weight(0, -1) * a[7], b[3] + flux_weight(NI - 1, -1) * a[7]
            dhead = k["inv"] * db + k["inv_hl"] * ea
            dtail = k["inv"] * ea + k["inv_tr"] * db
            values = [ha + hra * head, tb + tlb * tail, da + float(CS["hr"]) * dhead, eb + float(CS["tl"]) * dtail]
            values += list(a[8:12]) + list(b[8:12])
            for e, t in enumerate(values):
                out[pl.ds(at + NV * e + v, SUB, stride=WIDE), :] = t
            for e, t in enumerate((head, tail, dhead, dtail)):
                mids[pl.ds((NV * e + v) * HALF + SUB * r, SUB), :] = t


def pair(mine, got):
    vmem = pl.BlockSpec(memory_space=pltpu.VMEM)
    return pl.pallas_call(
        pair_body,
        out_shape=(
            jax.ShapeDtypeStruct((PAIRS * WIDE, NK), F32),
            jax.ShapeDtypeStruct((4 * NV * HALF + SUB, NK), F32),
        ),
        in_specs=[vmem] * 2,
        out_specs=(vmem,) * 2,
        compiler_params=pltpu.CompilerParams(vmem_limit_bytes=8 << 20),
        cost_estimate=pl.CostEstimate(flops=1 << 20, bytes_accessed=1 << 20, transcendentals=0),
        name="pair",
    )(mine, got)


def join_body(x, out, coef):
    for r in range(PAIRS // SUB):
        packed = x[pl.ds(WIDE * SUB * r + 12 * NV, SUB, stride=WIDE), :]
        for k in range(16):
            coef[pl.ds(PAIRS * k + SUB * r, SUB), :] = jnp.broadcast_to(packed[:, k : k + 1], (SUB, NK))

    def row(p, k):
        return jnp.broadcast_to(coef[pl.ds(PAIRS * k + p, 1), :], (NV, NK))

    def value(p, k):
        return x[pl.ds(WIDE * p + NV * k, NV), :]

    c = CS["pair"]
    head_f, tail_f, head_d, tail_d = [], [], [], []
    for p in range(PAIRS):
        h, t, dh, dt = (value(p, k) for k in range(4))
        if p:
            for q in range(3):
                z = value(p - 1, 8 + q)
                h, t = h + row(p, 4 + q) * z, t + row(p, 7 + q) * z
            z = value(p - 1, 11)
            dh, dt = dh + c["low"][0] * z, dt + c["low"][1] * z
        if p < PAIRS - 1:
            for q in range(3):
                z = value(p + 1, 4 + q)
                h, t = h + row(p, 10 + q) * z, t + row(p, 13 + q) * z
            z = value(p + 1, 7)
            dh, dt = dh + c["high"][0] * z, dt + c["high"][1] * z
        head_f.append(h)
        tail_f.append(t)
        head_d.append(dh)
        tail_d.append(dt)

    scale = 8.0
    num, den = [None] * PAIRS, [None] * PAIRS
    hl, hr, tl, tr = ([row(p, k) for p in range(PAIRS)] for k in range(4))
    num[0], den[0] = tr[0], jnp.ones((NV, NK), F32)
    for p in range(1, PAIRS):
        cross = tl[p] * hr[p] - tr[p] * hl[p]
        num[p] = (scale * tr[p]) * den[p - 1] + (scale * cross) * num[p - 1]
        den[p] = scale * den[p - 1] - (scale * hl[p]) * num[p - 1]
    inv = [None] + [1.0 / den[p] for p in range(1, PAIRS)]
    e = [num[0]] + [num[p] * inv[p] for p in range(1, PAIRS)]
    keep = [None] + [(scale * den[p - 1]) * inv[p] for p in range(1, PAIRS)]

    fwd_f, fwd_d = [tail_f[0]], [tail_d[0]]
    chl, chr_, ctl, ce = c["hl"], c["hr"], c["tl"], c["e"]
    for p in range(1, PAIRS):
        a = tl[p] * keep[p]
        fwd_f.append((tail_f[p] + (a * e[p - 1]) * head_f[p]) + a * fwd_f[-1])
        k = ctl / (1.0 - chl * ce[p - 1])
        fwd_d.append((tail_d[p] + float(k * ce[p - 1]) * head_d[p]) + float(k) * fwd_d[-1])

    zero = jnp.zeros((NV, NK), F32)
    right_f, right_d = zero, zero
    for p in range(PAIRS - 1, -1, -1):
        if p:
            h = keep[p]
            at_f = (head_f[p] + hl[p] * fwd_f[p - 1]) * h + (hr[p] * h) * right_f
            left_f = fwd_f[p - 1] + e[p - 1] * at_f
            k = 1.0 / (1.0 - chl * ce[p - 1])
            at_d = (float(k) * head_d[p] + float(k * chl) * fwd_d[p - 1]) + float(k * chr_) * right_d
            left_d = fwd_d[p - 1] + float(ce[p - 1]) * at_d
        else:
            at_f = at_d = left_f = left_d = zero
        for k, val in enumerate((left_f, right_f, left_d, right_d)):
            out[pl.ds(ROWS * p + NV * k, NV), :] = val
        right_f, right_d = at_f, at_d


def join(x):
    vmem = pl.BlockSpec(memory_space=pltpu.VMEM)
    return pl.pallas_call(
        join_body,
        out_shape=jax.ShapeDtypeStruct((PAIRS * ROWS, NK), F32),
        in_specs=[vmem],
        out_specs=vmem,
        scratch_shapes=[pltpu.VMEM((16 * PAIRS, NK), F32)],
        compiler_params=pltpu.CompilerParams(vmem_limit_bytes=8 << 20),
        cost_estimate=pl.CostEstimate(flops=1 << 20, bytes_accessed=1 << 20, transcendentals=0),
        name="join",
    )(x)


def split_body(z, mids, own, send):
    is0 = parity("gx") == 0
    c = CS["pair"]
    down = [jnp.broadcast_to(mids[pl.ds(4 * NV * HALF + k, 1), :], (SUB, NK)) for k in range(4)]
    for r in range(HALF // SUB):
        for v in range(NV):
            lf, rf, ld, rd = (z[pl.ds(ROWS * SUB * r + NV * k + v, SUB, stride=ROWS), :] for k in range(4))
            head, tail, dhead, dtail = (mids[pl.ds((NV * k + v) * HALF + SUB * r, SUB), :] for k in range(4))
            head = head + down[0] * lf + down[1] * rf
            tail = tail + down[2] * lf + down[3] * rf
            dhead = dhead + c["down"][0] * ld + c["down"][1] * rd
            dtail = dtail + c["down"][2] * ld + c["down"][3] * rd
            a, b = (lf, head, ld, dhead), (tail, rf, dtail, rd)
            for k in range(4):
                rows = pl.ds((NV * k + v) * HALF + SUB * r, SUB)
                own[rows, :] = jnp.where(is0, a[k], b[k])
                send[rows, :] = jnp.where(is0, b[k], a[k])


def split(z, mids):
    vmem = pl.BlockSpec(memory_space=pltpu.VMEM)
    out = jax.ShapeDtypeStruct((4 * NV * HALF, NK), F32)
    return pl.pallas_call(
        split_body,
        out_shape=(out, out),
        in_specs=[vmem] * 2,
        out_specs=(vmem,) * 2,
        compiler_params=pltpu.CompilerParams(vmem_limit_bytes=8 << 20),
        cost_estimate=pl.CostEstimate(flops=1 << 20, bytes_accessed=1 << 20, transcendentals=0),
        name="split",
    )(z, mids)


def block_body(inner, s_hbm, f_hbm, fy_hbm, one, two, yone, ytwo, mx, my, base, mxb, s, f, fy, pad, sem):
    moves = ((fy_hbm, fy), (s_hbm, s), (f_hbm, f))
    for v in range(NV):
        for k, (h, t) in enumerate(moves):
            pltpu.make_async_copy(h.at[v], t.at[v], sem.at[k, v]).start()
    piece = lax.axis_index("gx")
    is0 = parity("gx") == 0
    even = parity("gy") == 0
    first = jnp.where(piece == 0, 1.0 / 36.0, 0.0).astype(F32)
    last = jnp.where(piece == PIECES - 1, -1.0 / 36.0, 0.0).astype(F32)
    mxt = jnp.transpose(mx[...] * -0.5)
    myt = jnp.transpose(my[...] * -0.5)
    for i in range(NI):
        mxb[i] = jnp.broadcast_to(mxt[:, i : i + 1], (NJ, NK))
        pad[NI + i, 0:NJ, :] = jnp.broadcast_to(myt[:, i : i + 1], (NJ, NK))

    @pl.loop(0, NV)
    def _(v):
        for k, (h, t) in enumerate(moves):
            pltpu.make_async_copy(h.at[v], t.at[v], sem.at[k, v]).wait()
        for i in range(NI):
            for q in range(NJ // SUB):
                pad[i, pl.ds(SUB + SUB * q, SUB), :] = fy[v, i, pl.ds(SUB * q, SUB), :]
            part = pl.ds(4 * (i % 2), 4)
            a, b = yone[v, i // 2, part, :], ytwo[v, i // 2, part, :]
            pad[i, SUB - 4 : SUB, :] = jnp.where(even, b, a)
            pad[i, SUB + NJ : SUB + NJ + 4, :] = jnp.where(even, a, b)

        for q in range(NJ // SUB):
            rows = pl.ds(SUB * q, SUB)
            a = [one[v, k, rows, :] for k in range(4)]
            b = [two[v, k, rows, :] for k in range(4)]
            low = [jnp.where(is0, b[k], a[k]) for k in range(4)]
            high = [jnp.where(is0, a[k], b[k]) for k in range(4)]
            st = low[:3] + [s[v, i, rows, :] for i in range(NI)] + high[:3]
            fl = [low[3]] + [f[v, i, rows, :] for i in range(NI)] + [high[3]]
            ye, yd, us = [], [], []
            for i in range(NI):
                d6 = (
                    (st[i] + st[i + 6])
                    - 6.0 * (st[i + 1] + st[i + 5])
                    + 15.0 * (st[i + 2] + st[i + 4])
                    - 20.0 * st[i + 3]
                )
                y = inner[C_MG + i] * d6
                ye.append(y - inner[C_C + i] * ye[-1] if i else y)
                u = fl[i + 2] - fl[i]
                us.append(u)
                r = float(RHO * CS["m"][i]) * u
                if i == 0:
                    r = r + (first * float(CS["m"][i])) * fl[1]
                if i == NI - 1:
                    r = r + (last * float(CS["m"][i])) * fl[NI]
                yd.append(r - float(CS["c"][i]) * yd[-1] if i else r)
            xe = xd = None
            for i in range(NI - 1, -1, -1):
                xe = ye[i] if xe is None else ye[i] - inner[C_C + i] * xe
                xd = yd[i] if xd is None else yd[i] - float(CS["c"][i]) * xd
                at = SUB + SUB * q
                dy = None
                for k, w in enumerate(Y_WEIGHTS, start=1):
                    t = w * (pad[i, pl.ds(at + k, SUB), :] - pad[i, pl.ds(at - k, SUB), :])
                    dy = t if dy is None else dy + t
                d = us[i] * (1.0 / 12.0) + xd
                base[v, i, rows, :] = (st[i + 3] + xe) + (mxb[i, rows, :] * d + pad[NI + i, rows, :] * dy)


def block(inner, state, flux_x, flux_y, one, two, yone, ytwo, mx, my):
    vmem, hbm = pl.BlockSpec(memory_space=pltpu.VMEM), pl.BlockSpec(memory_space=pltpu.HBM)
    return pl.pallas_call(
        block_body,
        out_shape=(
            jax.ShapeDtypeStruct((NV, NI, NJ, NK), F32),
            jax.ShapeDtypeStruct((NI, NJ, NK), F32),
        ),
        in_specs=[vmem] + [hbm] * 3 + [vmem] * 6,
        out_specs=(vmem, vmem),
        scratch_shapes=[pltpu.VMEM((NV, NI, NJ, NK), F32)] * 3
        + [pltpu.VMEM((2 * NI, SUB + NJ + SUB, NK), F32), pltpu.SemaphoreType.DMA((3, NV))],
        compiler_params=pltpu.CompilerParams(vmem_limit_bytes=16 << 20),
        cost_estimate=pl.CostEstimate(flops=1 << 25, bytes_accessed=8 << 20, transcendentals=0),
        name="block",
    )(inner, *in_hbm(state, flux_x, flux_y), one, two, yone, ytwo, mx, my)


def finish_body(outer, base, mxb, own, got, out_hbm, out, sem):
    core = parity("gx")
    stores = [pltpu.make_async_copy(out.at[v], out_hbm.at[v], sem.at[v]) for v in range(NV)]
    for v in range(NV):
        for z, half in ((own, core), (got, 1 - core)):
            for r in range(HALF // SUB):
                rows = pl.ds(pl.multiple_of(HALF * half + SUB * r, SUB), SUB)
                lf, rf, ld, rd = (z[pl.ds((NV * k + v) * HALF + SUB * r, SUB), :] for k in range(4))
                for i in range(NI):
                    d = float(CS["left"][i]) * ld + float(CS["right"][i]) * rd
                    e = outer[C_LEFT + i] * lf + outer[C_RIGHT + i] * rf
                    out[v, i, rows, :] = (base[v, i, rows, :] + e) + mxb[i, rows, :] * d
        stores[v].start()
    for c in stores:
        c.wait()


def finish(outer, base, mxb, own, got):
    return pl.pallas_call(
        finish_body,
        out_shape=jax.ShapeDtypeStruct((NV, NI, NJ, NK), F32),
        in_specs=[pl.BlockSpec(memory_space=pltpu.VMEM)] * 5,
        out_specs=pl.BlockSpec(memory_space=pltpu.HBM),
        scratch_shapes=[pltpu.VMEM((NV, NI, NJ, NK), F32), pltpu.SemaphoreType.DMA((NV,))],
        compiler_params=pltpu.CompilerParams(vmem_limit_bytes=12 << 20),
        cost_estimate=pl.CostEstimate(flops=1 << 22, bytes_accessed=3 << 20, transcendentals=0),
        name="finish",
    )(outer, base, mxb, own, got)


def exchange(x, rows):
    groups = [[2 * p + c for p in range(PAIRS)] for c in range(2)]
    y = lax.all_to_all(x.reshape(PAIRS, rows, NK), "gx", 0, 0, tiled=True, axis_index_groups=groups)
    return y.reshape(PAIRS * rows, NK)


def per_device(flux_x, flux_y, state, metric_x, metric_y, filter_gap):
    count_y = lax.axis_size("gy")
    pair_in = [(i, i ^ 1) for i in range(PIECES)]
    pair_out = [(i, i + 1 if i % 2 else i - 1) for i in range(1, PIECES - 1)]
    y_in = [(i, i ^ 1) for i in range(count_y)]
    y_out = [(i, (i + 1 if i % 2 else i - 1) % count_y) for i in range(count_y)]

    inner, outer, mine, send = own_share(filter_gap, state, flux_x)
    ends, mids = pair(mine, lax.ppermute(send, "gx", pair_in))
    ends, state, flux_x, flux_y = lax.optimization_barrier((ends, state, flux_x, flux_y))
    ends = exchange(ends, WIDE)
    send_one, send_two, ysend_one, ysend_two = pack(state, flux_x, flux_y)
    one = lax.ppermute(send_one, "gx", pair_in)
    two = lax.ppermute(send_two, "gx", pair_out)
    yone = lax.ppermute(ysend_one, "gy", y_in)
    ytwo = lax.ppermute(ysend_two, "gy", y_out)
    outside = join(ends)
    outside, one, two, yone, ytwo = lax.optimization_barrier((outside, one, two, yone, ytwo))
    base, mxb = block(inner, state, flux_x, flux_y, one, two, yone, ytwo, metric_x, metric_y)
    outside, base, mxb = lax.optimization_barrier((exchange(outside, ROWS), base, mxb))
    own, send = split(outside, mids)
    return finish(outer, base, mxb, own, lax.ppermute(send, "gx", pair_in))


def solution(mesh):
    return jax.shard_map(
        per_device,
        mesh=mesh,
        in_specs=(
            P(None, "gx", "gy", None),
            P(None, "gx", "gy", None),
            P(None, "gx", "gy", None),
            P("gx", "gy"),
            P("gx", "gy"),
            P("gx"),
        ),
        out_specs=P(None, "gx", "gy", None),
        check_vma=False,
    )
```

```python
import jax
import jax.numpy as jnp
import numpy as np
from jax import lax
from jax.experimental import pallas as pl
from jax.experimental.pallas import tpu as pltpu
from jax.sharding import PartitionSpec as P

NV, NI, NJ, NK = 5, 16, 32, 128
PIECES, PAIRS, HALF = 32, 16, 16
ROWS, WIDE = 24, 64
EDGE = 12 * NV * HALF
SUB = 8
F32 = jnp.float32
Y_WEIGHTS = (4.0 / 5.0, -1.0 / 5.0, 4.0 / 105.0, -1.0 / 280.0)
RHO = 25.0 / 36.0
D6 = (1.0, -6.0, 15.0, -20.0, 15.0, -6.0, 1.0)

C_C, C_MG = 0, NI
C_LEFT, C_RIGHT, C_FAR = 0, NI, 2 * NI


def constant_system():
    a = 1.0 / 3.0
    t = np.eye(NI) + a * (np.eye(NI, k=1) + np.eye(NI, k=-1))
    inv = np.linalg.inv(t)
    m, c = [], []
    prev = 0.0
    for _ in range(NI):
        m.append(1.0 / (1.0 - a * prev))
        prev = a * m[-1]
        c.append(prev)
    left, right = -a * inv[:, 0], -a * inv[:, -1]
    hl, hr, tl, tr = left[0], right[0], left[-1], right[-1]
    d = 1.0 / (1.0 - tr * hl)
    w = RHO * np.array([-inv[0, 0], -inv[-1, 0], inv[0, -1], inv[-1, -1]])
    pair = dict(inv=d, inv_hl=d * hl, inv_tr=d * tr, down=[hl * tl * d, hr * d, tl * d, tr * hr * d])
    pair["low"] = [w[0] + hr * hl * d * w[1], tl * d * w[1]]
    pair["high"] = [hr * d * w[2], w[3] + tl * tr * d * w[2]]
    for k in pair:
        pair[k] = [float(t) for t in pair[k]] if isinstance(pair[k], list) else float(pair[k])
    p = dict(hl=hl + hr * hl * tl * d, hr=hr * hr * d, tl=tl * tl * d, tr=tr + tl * tr * hr * d)
    e = [p["tr"]]
    for _ in range(PAIRS - 1):
        e.append(p["tr"] + p["tl"] * p["hr"] * e[-1] / (1.0 - p["hl"] * e[-1]))
    pair.update(p, e=e)
    return dict(m=m, c=c, inv=inv, left=left, right=right, hl=hl, hr=hr, tl=tl, tr=tr, pair=pair)


CS = constant_system()


def flux_weight(row, j):
    w = CS["inv"][row]
    lo = w[j - 1] if 0 <= j - 1 < NI else 0.0
    hi = w[j + 1] if 0 <= j + 1 < NI else 0.0
    return float(RHO * (lo - hi))


def splat(x):
    return jnp.full((SUB, NK), x, F32)


def in_hbm(*arrays):
    return tuple(pltpu.with_memory_space_constraint(a, pltpu.HBM) for a in arrays)


def parity(name):
    return lax.rem(lax.axis_index(name), 2)


def pack_body(s, f, fy, one, two, yone, ytwo, lo, hi, sem):
    core, odd = parity("gx"), parity("gy")
    copies = [
        pltpu.make_async_copy(fy.at[:, :, 0:SUB, :], lo, sem.at[0]),
        pltpu.make_async_copy(fy.at[:, :, NJ - SUB : NJ, :], hi, sem.at[1]),
    ]
    for c in copies:
        c.start()

    def faces(right, left):
        moves = [
            pltpu.make_async_copy(s.at[:, NI - 3 : NI], right.at[:, 0:3], sem.at[2]),
            pltpu.make_async_copy(f.at[:, NI - 1 : NI], right.at[:, 3:4], sem.at[3]),
            pltpu.make_async_copy(s.at[:, 0:3], left.at[:, 0:3], sem.at[4]),
            pltpu.make_async_copy(f.at[:, 0:1], left.at[:, 3:4], sem.at[5]),
        ]
        for c in moves:
            c.start()
        for c in moves:
            c.wait()

    def rows(top, bottom):
        for v in range(NV):
            for i in range(NI):
                part = pl.ds(4 * (i % 2), 4)
                top[v, i // 2, part, :] = hi[v, i, 4:8, :]
                bottom[v, i // 2, part, :] = lo[v, i, 0:4, :]

    @pl.when(core == 0)
    def _():
        faces(one, two)

    @pl.when(core == 1)
    def _():
        faces(two, one)

    for c in copies:
        c.wait()

    @pl.when(odd == 0)
    def _():
        rows(yone, ytwo)

    @pl.when(odd == 1)
    def _():
        rows(ytwo, yone)


def pack(state, flux_x, flux_y):
    x_out = jax.ShapeDtypeStruct((NV, 4, NJ, NK), F32)
    y_out = jax.ShapeDtypeStruct((NV, NI // 2, SUB, NK), F32)
    return pl.pallas_call(
        pack_body,
        out_shape=(x_out, x_out, y_out, y_out),
        in_specs=[pl.BlockSpec(memory_space=pltpu.HBM)] * 3,
        out_specs=(pl.BlockSpec(memory_space=pltpu.VMEM),) * 4,
        scratch_shapes=[
            pltpu.VMEM((NV, NI, SUB, NK), F32),
            pltpu.VMEM((NV, NI, SUB, NK), F32),
            pltpu.SemaphoreType.DMA((6,)),
        ],
        compiler_params=pltpu.CompilerParams(vmem_limit_bytes=8 << 20),
        cost_estimate=pl.CostEstimate(flops=0, bytes_accessed=2 << 20, transcendentals=0),
        name="pack",
    )(*in_hbm(state, flux_x, flux_y))


def own_body(gap_hbm, s_hbm, f_hbm, inner, outer, mine, send, gap, s, f, own, gap_sem, sem):
    gap_load = pltpu.make_async_copy(gap_hbm, gap, gap_sem)
    gap_load.start()
    loads = [
        (
            pltpu.make_async_copy(s_hbm.at[v], s.at[v], sem.at[0, v]),
            pltpu.make_async_copy(f_hbm.at[v], f.at[v], sem.at[1, v]),
        )
        for v in range(NV)
    ]
    for both in loads:
        for c in both:
            c.start()
    core = parity("gx")
    piece = lax.axis_index("gx")
    gap_load.wait()
    alpha = [0.5 - splat(gap[i]) for i in range(NI)]
    g32 = [(0.5 - a) * (1.0 / 32.0) for a in alpha]
    m, c = [None] * NI, [None] * NI
    n, b = [None] * NI, [None] * NI
    for k in range(NI):
        m[k] = 1.0 / (1.0 - alpha[k] * c[k - 1]) if k else jnp.ones((SUB, NK), F32)
        c[k] = alpha[k] * m[k]
        r = NI - 1 - k
        n[r] = 1.0 / (1.0 - alpha[r] * b[r + 1]) if k else jnp.ones((SUB, NK), F32)
        b[r] = alpha[r] * n[r]
    left, right = [None] * NI, [None] * NI
    wh, wt = [None] * NI, [None] * NI
    left[0], right[NI - 1] = -b[0], -c[NI - 1]
    qh, qt = None, None
    for k in range(NI):
        r = NI - 1 - k
        if k:
            left[k] = -b[k] * left[k - 1]
            right[r] = -c[r] * right[r + 1]
            qh = -b[k - 1] if qh is None else -b[k - 1] * qh
            qt = -c[r + 1] if qt is None else -c[r + 1] * qt
            wh[k] = qh * n[k]
            wt[r] = qt * m[r]
        else:
            wh[0], wt[NI - 1] = n[0], m[NI - 1]
    for k in range(NI):
        inner[C_C + k] = c[k]
        inner[C_MG + k] = m[k] * g32[k]
        outer[C_LEFT + k] = left[k]
        outer[C_RIGHT + k] = right[k]
    vh = [wh[k] * g32[k] for k in range(NI)]
    vt = [wt[k] * g32[k] for k in range(NI)]

    def spread(v, j):
        terms = [D6[q + 3] * v[j - q] for q in range(-3, 4) if 0 <= j - q < NI]
        total = terms[0]
        for t in terms[1:]:
            total = total + t
        return total

    edge = [-alpha[0] * wh[0], -alpha[NI - 1] * wh[NI - 1], -alpha[0] * wt[0], -alpha[NI - 1] * wt[NI - 1]]
    low = [spread(v, q - 3) for v in (vh, vt) for q in range(3)]
    high = [spread(v, NI + q) for v in (vh, vt) for q in range(3)]
    edge += [jnp.where(core == 0, h, l) for h, l in zip(high, low)]
    edge += [jnp.where(core == 0, l, h) for h, l in zip(high, low)]
    for q in range(3):
        outer[C_FAR + q] = jnp.where(core == 0, edge[13 + q], edge[10 + q])
    for k, t in enumerate(edge):
        mine[pl.ds(EDGE + k, 1), :] = t[0:1]
        send[pl.ds(EDGE + k, 1), :] = t[0:1]

    first = jnp.where(piece == 0, 1.0 / 36.0, 0.0).astype(F32)
    last = jnp.where(piece == PIECES - 1, -1.0 / 36.0, 0.0).astype(F32)
    inv = CS["inv"]
    fh = [flux_weight(0, j) for j in range(NI)]
    ft = [flux_weight(NI - 1, j) for j in range(NI)]
    fh[0] = fh[0] + float(inv[0, 0]) * first
    ft[0] = ft[0] + float(inv[NI - 1, 0]) * first
    fh[NI - 1] = fh[NI - 1] + float(inv[0, NI - 1]) * last
    ft[NI - 1] = ft[NI - 1] + float(inv[NI - 1, NI - 1]) * last

    for i in range(NI):
        own[i] = spread(vh, i)
        own[NI + i] = spread(vt, i)

    s_in, f_in = (NI - 3) * (1 - core), (NI - 1) * (1 - core)
    s_out, f_out = (NI - 3) * core, (NI - 1) * core
    for v in range(NV):
        for c in loads[v]:
            c.wait()
        for out, half in ((mine, core), (send, 1 - core)):
            for r in range(HALF // SUB):
                rows = pl.ds(pl.multiple_of(HALF * half + SUB * r, SUB), SUB)
                sums = [None] * 4
                for i in range(NI):
                    a, z = s[v, i, rows, :], f[v, i, rows, :]
                    terms = (own[i] * a, own[NI + i] * a, fh[i] * z, ft[i] * z)
                    sums = [t if o is None else o + t for o, t in zip(sums, terms)]
                faces = [s[v, s_in + k, rows, :] for k in range(3)] + [f[v, f_in, rows, :]]
                faces += [s[v, s_out + k, rows, :] for k in range(3)] + [f[v, f_out, rows, :]]
                for k, t in enumerate(sums + faces):
                    out[pl.ds((NV * k + v) * HALF + SUB * r, SUB), :] = t


def own_share(gap, state, flux_x):
    vmem, hbm = pl.BlockSpec(memory_space=pltpu.VMEM), pl.BlockSpec(memory_space=pltpu.HBM)
    coef = jax.ShapeDtypeStruct((2 * NI, SUB, NK), F32)
    coef_far = jax.ShapeDtypeStruct((2 * NI + 3, SUB, NK), F32)
    values = jax.ShapeDtypeStruct((EDGE + 16, NK), F32)
    return pl.pallas_call(
        own_body,
        out_shape=(coef, coef_far, values, values),
        in_specs=[hbm, hbm, hbm],
        out_specs=(vmem,) * 4,
        scratch_shapes=[
            pltpu.SMEM((NI,), F32),
            pltpu.VMEM((NV, NI, NJ, NK), F32),
            pltpu.VMEM((NV, NI, NJ, NK), F32),
            pltpu.VMEM((2 * NI, SUB, NK), F32),
            pltpu.SemaphoreType.DMA,
            pltpu.SemaphoreType.DMA((2, NV)),
        ],
        compiler_params=pltpu.CompilerParams(vmem_limit_bytes=12 << 20),
        cost_estimate=pl.CostEstimate(flops=1 << 24, bytes_accessed=4 << 20, transcendentals=0),
        name="own_share",
    )(*in_hbm(gap, state, flux_x))


def pair_body(mine, got, out_hbm, mids, out, sem):
    is0 = parity("gx") == 0

    def both(rows):
        x, y = mine[rows, :], got[rows, :]
        return jnp.where(is0, x, y), jnp.where(is0, y, x)

    ca, cb = zip(*(both(pl.ds(EDGE + k, 1)) for k in range(16)))
    ca, cb = ([jnp.broadcast_to(t, (SUB, NK)) for t in c] for c in (ca, cb))
    hla, hra, tla, tra = ca[:4]
    hlb, hrb, tlb, trb = cb[:4]
    inv = 1.0 / (1.0 - tra * hlb)
    down = [hlb * tla * inv, hrb * inv, tla * inv, tra * hrb * inv, hlb * inv, inv, tra * inv]
    for k, t in enumerate(down):
        mids[pl.ds(4 * NV * HALF + k, 1), :] = t[0:1]
    cross_h, cross_t = hra * inv, tlb * inv
    edge = [hla + hra * down[0], hra * down[1], tlb * down[2], trb + tlb * down[3]]
    edge += [ca[10 + q] + (cross_h * hlb) * ca[13 + q] for q in range(3)]
    edge += [cross_t * ca[13 + q] for q in range(3)]
    edge += [cross_h * cb[10 + q] for q in range(3)]
    edge += [cb[13 + q] + (cross_t * tra) * cb[10 + q] for q in range(3)]
    lane = lax.broadcasted_iota(jnp.int32, (SUB, NK), 1)
    packed = jnp.zeros((SUB, NK), F32)
    for k, t in enumerate(edge):
        packed = jnp.where(lane == k, t, packed)

    k = CS["pair"]
    blocks = [pl.ds(WIDE * SUB * r, WIDE * SUB) for r in range(HALF // SUB)]
    stores = [pltpu.make_async_copy(out.at[b], out_hbm.at[b], sem.at[r]) for r, b in enumerate(blocks)]
    for r in range(HALF // SUB):
        at = WIDE * SUB * r
        out[pl.ds(at + 12 * NV, SUB, stride=WIDE), :] = packed
        for v in range(NV):
            a, b = zip(*(both(pl.ds((NV * e + v) * HALF + SUB * r, SUB)) for e in range(12)))
            ha, ta, hb, tb = a[0], a[1], b[0], b[1]
            for q in range(3):
                ha, ta = ha + ca[4 + q] * b[4 + q], ta + ca[7 + q] * b[4 + q]
                hb, tb = hb + cb[4 + q] * a[4 + q], tb + cb[7 + q] * a[4 + q]
            head = (hb + hlb * ta) * inv
            tail = (ta + tra * hb) * inv
            da, ea = a[2] + flux_weight(0, NI) * b[7], a[3] + flux_weight(NI - 1, NI) * b[7]
            db, eb = b[2] + flux_weight(0, -1) * a[7], b[3] + flux_weight(NI - 1, -1) * a[7]
            dhead = k["inv"] * db + k["inv_hl"] * ea
            dtail = k["inv"] * ea + k["inv_tr"] * db
            values = [ha + hra * head, tb + tlb * tail, da + float(CS["hr"]) * dhead, eb + float(CS["tl"]) * dtail]
            values += list(a[8:12]) + list(b[8:12])
            for e, t in enumerate(values):
                out[pl.ds(at + NV * e + v, SUB, stride=WIDE), :] = t
            for e, t in enumerate((head, tail, dhead, dtail)):
                mids[pl.ds((NV * e + v) * HALF + SUB * r, SUB), :] = t
        stores[r].start()
    for c in stores:
        c.wait()


def pair(mine, got):
    vmem = pl.BlockSpec(memory_space=pltpu.VMEM)
    return pl.pallas_call(
        pair_body,
        out_shape=(
            jax.ShapeDtypeStruct((PAIRS * WIDE, NK), F32),
            jax.ShapeDtypeStruct((4 * NV * HALF + SUB, NK), F32),
        ),
        in_specs=[vmem] * 2,
        out_specs=(pl.BlockSpec(memory_space=pltpu.HBM), vmem),
        scratch_shapes=[pltpu.VMEM((PAIRS * WIDE, NK), F32), pltpu.SemaphoreType.DMA((HALF // SUB,))],
        compiler_params=pltpu.CompilerParams(vmem_limit_bytes=8 << 20),
        cost_estimate=pl.CostEstimate(flops=1 << 20, bytes_accessed=1 << 20, transcendentals=0),
        name="pair",
    )(mine, got)


def join_body(x, out_hbm, out, coef, sem):
    for r in range(PAIRS // SUB):
        packed = x[pl.ds(WIDE * SUB * r + 12 * NV, SUB, stride=WIDE), :]
        for k in range(16):
            coef[pl.ds(PAIRS * k + SUB * r, SUB), :] = jnp.broadcast_to(packed[:, k : k + 1], (SUB, NK))

    def row(p, k):
        return jnp.broadcast_to(coef[pl.ds(PAIRS * k + p, 1), :], (NV, NK))

    def value(p, k):
        return x[pl.ds(WIDE * p + NV * k, NV), :]

    c = CS["pair"]
    head_f, tail_f, head_d, tail_d = [], [], [], []
    for p in range(PAIRS):
        h, t, dh, dt = (value(p, k) for k in range(4))
        if p:
            for q in range(3):
                z = value(p - 1, 8 + q)
                h, t = h + row(p, 4 + q) * z, t + row(p, 7 + q) * z
            z = value(p - 1, 11)
            dh, dt = dh + c["low"][0] * z, dt + c["low"][1] * z
        if p < PAIRS - 1:
            for q in range(3):
                z = value(p + 1, 4 + q)
                h, t = h + row(p, 10 + q) * z, t + row(p, 13 + q) * z
            z = value(p + 1, 7)
            dh, dt = dh + c["high"][0] * z, dt + c["high"][1] * z
        head_f.append(h)
        tail_f.append(t)
        head_d.append(dh)
        tail_d.append(dt)

    scale = 8.0
    num, den = [None] * PAIRS, [None] * PAIRS
    hl, hr, tl, tr = ([row(p, k) for p in range(PAIRS)] for k in range(4))
    num[0], den[0] = tr[0], jnp.ones((NV, NK), F32)
    for p in range(1, PAIRS):
        cross = tl[p] * hr[p] - tr[p] * hl[p]
        num[p] = (scale * tr[p]) * den[p - 1] + (scale * cross) * num[p - 1]
        den[p] = scale * den[p - 1] - (scale * hl[p]) * num[p - 1]
    inv = [None] + [1.0 / den[p] for p in range(1, PAIRS)]
    e = [num[0]] + [num[p] * inv[p] for p in range(1, PAIRS)]
    keep = [None] + [(scale * den[p - 1]) * inv[p] for p in range(1, PAIRS)]

    fwd_f, fwd_d = [tail_f[0]], [tail_d[0]]
    chl, chr_, ctl, ce = c["hl"], c["hr"], c["tl"], c["e"]
    for p in range(1, PAIRS):
        a = tl[p] * keep[p]
        fwd_f.append((tail_f[p] + (a * e[p - 1]) * head_f[p]) + a * fwd_f[-1])
        k = ctl / (1.0 - chl * ce[p - 1])
        fwd_d.append((tail_d[p] + float(k * ce[p - 1]) * head_d[p]) + float(k) * fwd_d[-1])

    blocks = [pl.ds(ROWS * SUB * r, ROWS * SUB) for r in range(PAIRS // SUB)]
    stores = [pltpu.make_async_copy(out.at[b], out_hbm.at[b], sem.at[r]) for r, b in enumerate(blocks)]
    zero = jnp.zeros((NV, NK), F32)
    right_f, right_d = zero, zero
    for p in range(PAIRS - 1, -1, -1):
        if p:
            h = keep[p]
            at_f = (head_f[p] + hl[p] * fwd_f[p - 1]) * h + (hr[p] * h) * right_f
            left_f = fwd_f[p - 1] + e[p - 1] * at_f
            k = 1.0 / (1.0 - chl * ce[p - 1])
            at_d = (float(k) * head_d[p] + float(k * chl) * fwd_d[p - 1]) + float(k * chr_) * right_d
            left_d = fwd_d[p - 1] + float(ce[p - 1]) * at_d
        else:
            at_f = at_d = left_f = left_d = zero
        for k, val in enumerate((left_f, right_f, left_d, right_d)):
            out[pl.ds(ROWS * p + NV * k, NV), :] = val
        right_f, right_d = at_f, at_d
        if p % SUB == 0:
            stores[p // SUB].start()
    for t in stores:
        t.wait()


def join(x):
    vmem = pl.BlockSpec(memory_space=pltpu.VMEM)
    return pl.pallas_call(
        join_body,
        out_shape=jax.ShapeDtypeStruct((PAIRS * ROWS, NK), F32),
        in_specs=[vmem],
        out_specs=pl.BlockSpec(memory_space=pltpu.HBM),
        scratch_shapes=[
            pltpu.VMEM((PAIRS * ROWS, NK), F32),
            pltpu.VMEM((16 * PAIRS, NK), F32),
            pltpu.SemaphoreType.DMA((PAIRS // SUB,)),
        ],
        compiler_params=pltpu.CompilerParams(vmem_limit_bytes=8 << 20),
        cost_estimate=pl.CostEstimate(flops=1 << 20, bytes_accessed=1 << 20, transcendentals=0),
        name="join",
    )(x)


def far_body(outer, two, own, send):
    core = parity("gx")
    wd = jnp.where(core == 0, flux_weight(NI - 1, -1), flux_weight(0, NI)).astype(F32)
    for out, half in ((own, core), (send, 1 - core)):
        for v in range(NV):
            for r in range(HALF // SUB):
                rows = pl.ds(pl.multiple_of(HALF * half + SUB * r, SUB), SUB)
                a = [two[v, k, rows, :] for k in range(4)]
                f = outer[C_FAR] * a[0] + outer[C_FAR + 1] * a[1] + outer[C_FAR + 2] * a[2]
                for k, t in enumerate((f, wd * a[3])):
                    out[pl.ds((NV * k + v) * HALF + SUB * r, SUB), :] = t


def far(outer, two):
    vmem = pl.BlockSpec(memory_space=pltpu.VMEM)
    out = jax.ShapeDtypeStruct((2 * NV * HALF, NK), F32)
    return pl.pallas_call(
        far_body,
        out_shape=(out, out),
        in_specs=[vmem] * 2,
        out_specs=(vmem,) * 2,
        compiler_params=pltpu.CompilerParams(vmem_limit_bytes=8 << 20),
        cost_estimate=pl.CostEstimate(flops=1 << 18, bytes_accessed=1 << 19, transcendentals=0),
        name="far",
    )(outer, two)


def split_body(z, mids, far_own, far_got, own, send):
    is0 = parity("gx") == 0
    c = CS["pair"]
    down = [jnp.broadcast_to(mids[pl.ds(4 * NV * HALF + k, 1), :], (SUB, NK)) for k in range(7)]
    for r in range(HALF // SUB):
        for v in range(NV):
            lf, rf, ld, rd = (z[pl.ds(ROWS * SUB * r + NV * k + v, SUB, stride=ROWS), :] for k in range(4))
            head, tail, dhead, dtail = (mids[pl.ds((NV * k + v) * HALF + SUB * r, SUB), :] for k in range(4))
            fo, do = (far_own[pl.ds((NV * k + v) * HALF + SUB * r, SUB), :] for k in range(2))
            fg, dg = (far_got[pl.ds((NV * k + v) * HALF + SUB * r, SUB), :] for k in range(2))
            fa, da = jnp.where(is0, fo, fg), jnp.where(is0, do, dg)
            fb, db = jnp.where(is0, fg, fo), jnp.where(is0, dg, do)
            head = (head + down[4] * fa + down[5] * fb) + down[0] * lf + down[1] * rf
            tail = (tail + down[5] * fa + down[6] * fb) + down[2] * lf + down[3] * rf
            dhead = (dhead + c["inv_hl"] * da + c["inv"] * db) + c["down"][0] * ld + c["down"][1] * rd
            dtail = (dtail + c["inv"] * da + c["inv_tr"] * db) + c["down"][2] * ld + c["down"][3] * rd
            a, b = (lf, head, ld, dhead), (tail, rf, dtail, rd)
            for k in range(4):
                rows = pl.ds((NV * k + v) * HALF + SUB * r, SUB)
                own[rows, :] = jnp.where(is0, a[k], b[k])
                send[rows, :] = jnp.where(is0, b[k], a[k])


def split(z, mids, far_own, far_got):
    vmem = pl.BlockSpec(memory_space=pltpu.VMEM)
    out = jax.ShapeDtypeStruct((4 * NV * HALF, NK), F32)
    return pl.pallas_call(
        split_body,
        out_shape=(out, out),
        in_specs=[vmem] * 4,
        out_specs=(vmem,) * 2,
        compiler_params=pltpu.CompilerParams(vmem_limit_bytes=8 << 20),
        cost_estimate=pl.CostEstimate(flops=1 << 20, bytes_accessed=1 << 20, transcendentals=0),
        name="split",
    )(z, mids, far_own, far_got)


def block_body(inner, s_hbm, f_hbm, fy_hbm, one, two, yone, ytwo, mx, my, base, mxb, s, f, fy, pad, sem):
    moves = ((fy_hbm, fy), (s_hbm, s), (f_hbm, f))
    for v in range(NV):
        for k, (h, t) in enumerate(moves):
            pltpu.make_async_copy(h.at[v], t.at[v], sem.at[k, v]).start()
    piece = lax.axis_index("gx")
    is0 = parity("gx") == 0
    even = parity("gy") == 0
    first = jnp.where(piece == 0, 1.0 / 36.0, 0.0).astype(F32)
    last = jnp.where(piece == PIECES - 1, -1.0 / 36.0, 0.0).astype(F32)
    mxt = jnp.transpose(mx[...] * -0.5)
    myt = jnp.transpose(my[...] * -0.5)
    for i in range(NI):
        mxb[i] = jnp.broadcast_to(mxt[:, i : i + 1], (NJ, NK))
        pad[NI + i, 0:NJ, :] = jnp.broadcast_to(myt[:, i : i + 1], (NJ, NK))

    @pl.loop(0, NV)
    def _(v):
        for k, (h, t) in enumerate(moves):
            pltpu.make_async_copy(h.at[v], t.at[v], sem.at[k, v]).wait()
        for i in range(NI):
            for q in range(NJ // SUB):
                pad[i, pl.ds(SUB + SUB * q, SUB), :] = fy[v, i, pl.ds(SUB * q, SUB), :]
            part = pl.ds(4 * (i % 2), 4)
            a, b = yone[v, i // 2, part, :], ytwo[v, i // 2, part, :]
            pad[i, SUB - 4 : SUB, :] = jnp.where(even, b, a)
            pad[i, SUB + NJ : SUB + NJ + 4, :] = jnp.where(even, a, b)

        for q in range(NJ // SUB):
            rows = pl.ds(SUB * q, SUB)
            a = [one[v, k, rows, :] for k in range(4)]
            b = [two[v, k, rows, :] for k in range(4)]
            low = [jnp.where(is0, b[k], a[k]) for k in range(4)]
            high = [jnp.where(is0, a[k], b[k]) for k in range(4)]
            st = low[:3] + [s[v, i, rows, :] for i in range(NI)] + high[:3]
            fl = [low[3]] + [f[v, i, rows, :] for i in range(NI)] + [high[3]]
            ye, yd, us = [], [], []
            for i in range(NI):
                d6 = (
                    (st[i] + st[i + 6])
                    - 6.0 * (st[i + 1] + st[i + 5])
                    + 15.0 * (st[i + 2] + st[i + 4])
                    - 20.0 * st[i + 3]
                )
                y = inner[C_MG + i] * d6
                ye.append(y - inner[C_C + i] * ye[-1] if i else y)
                u = fl[i + 2] - fl[i]
                us.append(u)
                r = float(RHO * CS["m"][i]) * u
                if i == 0:
                    r = r + (first * float(CS["m"][i])) * fl[1]
                if i == NI - 1:
                    r = r + (last * float(CS["m"][i])) * fl[NI]
                yd.append(r - float(CS["c"][i]) * yd[-1] if i else r)
            xe = xd = None
            for i in range(NI - 1, -1, -1):
                xe = ye[i] if xe is None else ye[i] - inner[C_C + i] * xe
                xd = yd[i] if xd is None else yd[i] - float(CS["c"][i]) * xd
                at = SUB + SUB * q
                dy = None
                for k, w in enumerate(Y_WEIGHTS, start=1):
                    t = w * (pad[i, pl.ds(at + k, SUB), :] - pad[i, pl.ds(at - k, SUB), :])
                    dy = t if dy is None else dy + t
                d = us[i] * (1.0 / 12.0) + xd
                base[v, i, rows, :] = (st[i + 3] + xe) + (mxb[i, rows, :] * d + pad[NI + i, rows, :] * dy)


def block(inner, state, flux_x, flux_y, one, two, yone, ytwo, mx, my):
    vmem, hbm = pl.BlockSpec(memory_space=pltpu.VMEM), pl.BlockSpec(memory_space=pltpu.HBM)
    return pl.pallas_call(
        block_body,
        out_shape=(
            jax.ShapeDtypeStruct((NV, NI, NJ, NK), F32),
            jax.ShapeDtypeStruct((NI, NJ, NK), F32),
        ),
        in_specs=[vmem] + [hbm] * 3 + [vmem] * 6,
        out_specs=(vmem, vmem),
        scratch_shapes=[pltpu.VMEM((NV, NI, NJ, NK), F32)] * 3
        + [pltpu.VMEM((2 * NI, SUB + NJ + SUB, NK), F32), pltpu.SemaphoreType.DMA((3, NV))],
        compiler_params=pltpu.CompilerParams(vmem_limit_bytes=16 << 20),
        cost_estimate=pl.CostEstimate(flops=1 << 25, bytes_accessed=8 << 20, transcendentals=0),
        name="block",
    )(inner, *in_hbm(state, flux_x, flux_y), one, two, yone, ytwo, mx, my)


def finish_body(outer, base, mxb, own, got, out_hbm, out, sem):
    core = parity("gx")
    stores = [pltpu.make_async_copy(out.at[v], out_hbm.at[v], sem.at[v]) for v in range(NV)]
    for v in range(NV):
        for z, half in ((own, core), (got, 1 - core)):
            for r in range(HALF // SUB):
                rows = pl.ds(pl.multiple_of(HALF * half + SUB * r, SUB), SUB)
                lf, rf, ld, rd = (z[pl.ds((NV * k + v) * HALF + SUB * r, SUB), :] for k in range(4))
                for i in range(NI):
                    d = float(CS["left"][i]) * ld + float(CS["right"][i]) * rd
                    e = outer[C_LEFT + i] * lf + outer[C_RIGHT + i] * rf
                    out[v, i, rows, :] = (base[v, i, rows, :] + e) + mxb[i, rows, :] * d
        stores[v].start()
    for c in stores:
        c.wait()


def finish(outer, base, mxb, own, got):
    return pl.pallas_call(
        finish_body,
        out_shape=jax.ShapeDtypeStruct((NV, NI, NJ, NK), F32),
        in_specs=[pl.BlockSpec(memory_space=pltpu.VMEM)] * 5,
        out_specs=pl.BlockSpec(memory_space=pltpu.HBM),
        scratch_shapes=[pltpu.VMEM((NV, NI, NJ, NK), F32), pltpu.SemaphoreType.DMA((NV,))],
        compiler_params=pltpu.CompilerParams(vmem_limit_bytes=12 << 20),
        cost_estimate=pl.CostEstimate(flops=1 << 22, bytes_accessed=3 << 20, transcendentals=0),
        name="finish",
    )(outer, base, mxb, own, got)


def exchange(x, rows):
    groups = [[2 * p + c for p in range(PAIRS)] for c in range(2)]
    y = lax.all_to_all(x.reshape(PAIRS, rows, NK), "gx", 0, 0, tiled=True, axis_index_groups=groups)
    return y.reshape(PAIRS * rows, NK)


def per_device(flux_x, flux_y, state, metric_x, metric_y, filter_gap):
    count_y = lax.axis_size("gy")
    pair_in = [(i, i ^ 1) for i in range(PIECES)]
    pair_out = [(i, i + 1 if i % 2 else i - 1) for i in range(1, PIECES - 1)]
    y_in = [(i, i ^ 1) for i in range(count_y)]
    y_out = [(i, (i + 1 if i % 2 else i - 1) % count_y) for i in range(count_y)]

    inner, outer, mine, send = own_share(filter_gap, state, flux_x)
    send, state, flux_x, flux_y = lax.optimization_barrier((send, state, flux_x, flux_y))
    got = lax.ppermute(send, "gx", pair_in)
    got, *faces = lax.optimization_barrier((got, *pack(state, flux_x, flux_y)))
    ends, mids = pair(mine, got)
    ends, send_one, send_two, ysend_one, ysend_two = lax.optimization_barrier((ends, *faces))
    ends = exchange(ends, WIDE)
    one = lax.ppermute(send_one, "gx", pair_in)
    two = lax.ppermute(send_two, "gx", pair_out)
    yone = lax.ppermute(ysend_one, "gy", y_in)
    ytwo = lax.ppermute(ysend_two, "gy", y_out)
    outside = join(ends)
    outside, one, two, yone, ytwo = lax.optimization_barrier((outside, one, two, yone, ytwo))
    far_own, far_send = far(outer, two)
    far_got = lax.ppermute(far_send, "gx", pair_in)
    base, mxb = block(inner, state, flux_x, flux_y, one, two, yone, ytwo, metric_x, metric_y)
    outside, base, mxb, far_got = lax.optimization_barrier((exchange(outside, ROWS), base, mxb, far_got))
    own, send = split(outside, mids, far_own, far_got)
    return finish(outer, base, mxb, own, lax.ppermute(send, "gx", pair_in))


def solution(mesh):
    return jax.shard_map(
        per_device,
        mesh=mesh,
        in_specs=(
            P(None, "gx", "gy", None),
            P(None, "gx", "gy", None),
            P(None, "gx", "gy", None),
            P("gx", "gy"),
            P("gx", "gy"),
            P("gx"),
        ),
        out_specs=P(None, "gx", "gy", None),
        check_vma=False,
    )
```

```python
import jax
import jax.numpy as jnp
import numpy as np
from jax import lax
from jax.experimental import pallas as pl
from jax.experimental.pallas import tpu as pltpu
from jax.sharding import PartitionSpec as P

NV, NI, NJ, NK = 5, 16, 32, 128
PIECES, PAIRS, HALF = 32, 16, 16
ROWS, WIDE = 24, 64
EDGE = 12 * NV * HALF
SUB = 8
F32 = jnp.float32
Y_WEIGHTS = (4.0 / 5.0, -1.0 / 5.0, 4.0 / 105.0, -1.0 / 280.0)
RHO = 25.0 / 36.0
D6 = (1.0, -6.0, 15.0, -20.0, 15.0, -6.0, 1.0)

C_C, C_MG = 0, NI
C_LEFT, C_RIGHT, C_FAR = 0, NI, 2 * NI


def constant_system():
    a = 1.0 / 3.0
    t = np.eye(NI) + a * (np.eye(NI, k=1) + np.eye(NI, k=-1))
    inv = np.linalg.inv(t)
    m, c = [], []
    prev = 0.0
    for _ in range(NI):
        m.append(1.0 / (1.0 - a * prev))
        prev = a * m[-1]
        c.append(prev)
    left, right = -a * inv[:, 0], -a * inv[:, -1]
    hl, hr, tl, tr = left[0], right[0], left[-1], right[-1]
    d = 1.0 / (1.0 - tr * hl)
    w = RHO * np.array([-inv[0, 0], -inv[-1, 0], inv[0, -1], inv[-1, -1]])
    pair = dict(inv=d, inv_hl=d * hl, inv_tr=d * tr, down=[hl * tl * d, hr * d, tl * d, tr * hr * d])
    pair["low"] = [w[0] + hr * hl * d * w[1], tl * d * w[1]]
    pair["high"] = [hr * d * w[2], w[3] + tl * tr * d * w[2]]
    for k in pair:
        pair[k] = [float(t) for t in pair[k]] if isinstance(pair[k], list) else float(pair[k])
    p = dict(hl=hl + hr * hl * tl * d, hr=hr * hr * d, tl=tl * tl * d, tr=tr + tl * tr * hr * d)
    e = [p["tr"]]
    for _ in range(PAIRS - 1):
        e.append(p["tr"] + p["tl"] * p["hr"] * e[-1] / (1.0 - p["hl"] * e[-1]))
    pair.update(p, e=e)
    return dict(m=m, c=c, inv=inv, left=left, right=right, hl=hl, hr=hr, tl=tl, tr=tr, pair=pair)


CS = constant_system()


def flux_weight(row, j):
    w = CS["inv"][row]
    lo = w[j - 1] if 0 <= j - 1 < NI else 0.0
    hi = w[j + 1] if 0 <= j + 1 < NI else 0.0
    return float(RHO * (lo - hi))


def splat(x):
    return jnp.full((SUB, NK), x, F32)


def in_hbm(*arrays):
    return tuple(pltpu.with_memory_space_constraint(a, pltpu.HBM) for a in arrays)


def parity(name):
    return lax.rem(lax.axis_index(name), 2)


def pack_body(s, f, fy, one, two, yone, ytwo, lo, hi, sem):
    core, odd = parity("gx"), parity("gy")
    copies = [
        pltpu.make_async_copy(fy.at[:, :, 0:SUB, :], lo, sem.at[0]),
        pltpu.make_async_copy(fy.at[:, :, NJ - SUB : NJ, :], hi, sem.at[1]),
    ]
    for c in copies:
        c.start()

    def faces(right, left):
        moves = [
            pltpu.make_async_copy(s.at[:, NI - 3 : NI], right.at[:, 0:3], sem.at[2]),
            pltpu.make_async_copy(f.at[:, NI - 1 : NI], right.at[:, 3:4], sem.at[3]),
            pltpu.make_async_copy(s.at[:, 0:3], left.at[:, 0:3], sem.at[4]),
            pltpu.make_async_copy(f.at[:, 0:1], left.at[:, 3:4], sem.at[5]),
        ]
        for c in moves:
            c.start()
        for c in moves:
            c.wait()

    def rows(top, bottom):
        for v in range(NV):
            for i in range(NI):
                part = pl.ds(4 * (i % 2), 4)
                top[v, i // 2, part, :] = hi[v, i, 4:8, :]
                bottom[v, i // 2, part, :] = lo[v, i, 0:4, :]

    @pl.when(core == 0)
    def _():
        faces(one, two)

    @pl.when(core == 1)
    def _():
        faces(two, one)

    for c in copies:
        c.wait()

    @pl.when(odd == 0)
    def _():
        rows(yone, ytwo)

    @pl.when(odd == 1)
    def _():
        rows(ytwo, yone)


def pack(state, flux_x, flux_y):
    x_out = jax.ShapeDtypeStruct((NV, 4, NJ, NK), F32)
    y_out = jax.ShapeDtypeStruct((NV, NI // 2, SUB, NK), F32)
    return pl.pallas_call(
        pack_body,
        out_shape=(x_out, x_out, y_out, y_out),
        in_specs=[pl.BlockSpec(memory_space=pltpu.HBM)] * 3,
        out_specs=(pl.BlockSpec(memory_space=pltpu.VMEM),) * 4,
        scratch_shapes=[
            pltpu.VMEM((NV, NI, SUB, NK), F32),
            pltpu.VMEM((NV, NI, SUB, NK), F32),
            pltpu.SemaphoreType.DMA((6,)),
        ],
        compiler_params=pltpu.CompilerParams(vmem_limit_bytes=8 << 20),
        cost_estimate=pl.CostEstimate(flops=0, bytes_accessed=2 << 20, transcendentals=0),
        name="pack",
    )(*in_hbm(state, flux_x, flux_y))


def own_body(gap_hbm, s_hbm, f_hbm, inner, outer, mine, send, gap, s, f, own, gap_sem, sem):
    gap_load = pltpu.make_async_copy(gap_hbm, gap, gap_sem)
    gap_load.start()
    loads = [
        (
            pltpu.make_async_copy(s_hbm.at[v], s.at[v], sem.at[0, v]),
            pltpu.make_async_copy(f_hbm.at[v], f.at[v], sem.at[1, v]),
        )
        for v in range(NV)
    ]
    for both in loads:
        for c in both:
            c.start()
    core = parity("gx")
    piece = lax.axis_index("gx")
    gap_load.wait()
    alpha = [0.5 - splat(gap[i]) for i in range(NI)]
    g32 = [(0.5 - a) * (1.0 / 32.0) for a in alpha]
    m, c = [None] * NI, [None] * NI
    n, b = [None] * NI, [None] * NI
    for k in range(NI):
        m[k] = 1.0 / (1.0 - alpha[k] * c[k - 1]) if k else jnp.ones((SUB, NK), F32)
        c[k] = alpha[k] * m[k]
        r = NI - 1 - k
        n[r] = 1.0 / (1.0 - alpha[r] * b[r + 1]) if k else jnp.ones((SUB, NK), F32)
        b[r] = alpha[r] * n[r]
    left, right = [None] * NI, [None] * NI
    wh, wt = [None] * NI, [None] * NI
    left[0], right[NI - 1] = -b[0], -c[NI - 1]
    qh, qt = None, None
    for k in range(NI):
        r = NI - 1 - k
        if k:
            left[k] = -b[k] * left[k - 1]
            right[r] = -c[r] * right[r + 1]
            qh = -b[k - 1] if qh is None else -b[k - 1] * qh
            qt = -c[r + 1] if qt is None else -c[r + 1] * qt
            wh[k] = qh * n[k]
            wt[r] = qt * m[r]
        else:
            wh[0], wt[NI - 1] = n[0], m[NI - 1]
    for k in range(NI):
        inner[C_C + k] = c[k]
        inner[C_MG + k] = m[k] * g32[k]
        outer[C_LEFT + k] = left[k]
        outer[C_RIGHT + k] = right[k]
    vh = [wh[k] * g32[k] for k in range(NI)]
    vt = [wt[k] * g32[k] for k in range(NI)]

    def spread(v, j):
        terms = [D6[q + 3] * v[j - q] for q in range(-3, 4) if 0 <= j - q < NI]
        total = terms[0]
        for t in terms[1:]:
            total = total + t
        return total

    edge = [-alpha[0] * wh[0], -alpha[NI - 1] * wh[NI - 1], -alpha[0] * wt[0], -alpha[NI - 1] * wt[NI - 1]]
    low = [spread(v, q - 3) for v in (vh, vt) for q in range(3)]
    high = [spread(v, NI + q) for v in (vh, vt) for q in range(3)]
    edge += [jnp.where(core == 0, h, l) for h, l in zip(high, low)]
    edge += [jnp.where(core == 0, l, h) for h, l in zip(high, low)]
    for q in range(3):
        outer[C_FAR + q] = jnp.where(core == 0, edge[13 + q], edge[10 + q])
    for k, t in enumerate(edge):
        mine[pl.ds(EDGE + k, 1), :] = t[0:1]
        send[pl.ds(EDGE + k, 1), :] = t[0:1]

    first = jnp.where(piece == 0, 1.0 / 36.0, 0.0).astype(F32)
    last = jnp.where(piece == PIECES - 1, -1.0 / 36.0, 0.0).astype(F32)
    inv = CS["inv"]
    fh = [flux_weight(0, j) for j in range(NI)]
    ft = [flux_weight(NI - 1, j) for j in range(NI)]
    fh[0] = fh[0] + float(inv[0, 0]) * first
    ft[0] = ft[0] + float(inv[NI - 1, 0]) * first
    fh[NI - 1] = fh[NI - 1] + float(inv[0, NI - 1]) * last
    ft[NI - 1] = ft[NI - 1] + float(inv[NI - 1, NI - 1]) * last

    for i in range(NI):
        own[i] = spread(vh, i)
        own[NI + i] = spread(vt, i)

    s_in, f_in = (NI - 3) * (1 - core), (NI - 1) * (1 - core)
    s_out, f_out = (NI - 3) * core, (NI - 1) * core
    for v in range(NV):
        for c in loads[v]:
            c.wait()
        for out, half in ((mine, core), (send, 1 - core)):
            for r in range(HALF // SUB):
                rows = pl.ds(pl.multiple_of(HALF * half + SUB * r, SUB), SUB)
                sums = [None] * 4
                for i in range(NI):
                    a, z = s[v, i, rows, :], f[v, i, rows, :]
                    terms = (own[i] * a, own[NI + i] * a, fh[i] * z, ft[i] * z)
                    sums = [t if o is None else o + t for o, t in zip(sums, terms)]
                faces = [s[v, s_in + k, rows, :] for k in range(3)] + [f[v, f_in, rows, :]]
                faces += [s[v, s_out + k, rows, :] for k in range(3)] + [f[v, f_out, rows, :]]
                for k, t in enumerate(sums + faces):
                    out[pl.ds((NV * k + v) * HALF + SUB * r, SUB), :] = t


def own_share(gap, state, flux_x):
    vmem, hbm = pl.BlockSpec(memory_space=pltpu.VMEM), pl.BlockSpec(memory_space=pltpu.HBM)
    coef = jax.ShapeDtypeStruct((2 * NI, SUB, NK), F32)
    coef_far = jax.ShapeDtypeStruct((2 * NI + 3, SUB, NK), F32)
    values = jax.ShapeDtypeStruct((EDGE + 16, NK), F32)
    return pl.pallas_call(
        own_body,
        out_shape=(coef, coef_far, values, values),
        in_specs=[hbm, hbm, hbm],
        out_specs=(vmem,) * 4,
        scratch_shapes=[
            pltpu.SMEM((NI,), F32),
            pltpu.VMEM((NV, NI, NJ, NK), F32),
            pltpu.VMEM((NV, NI, NJ, NK), F32),
            pltpu.VMEM((2 * NI, SUB, NK), F32),
            pltpu.SemaphoreType.DMA,
            pltpu.SemaphoreType.DMA((2, NV)),
        ],
        compiler_params=pltpu.CompilerParams(vmem_limit_bytes=12 << 20),
        cost_estimate=pl.CostEstimate(flops=1 << 24, bytes_accessed=4 << 20, transcendentals=0),
        name="own_share",
    )(*in_hbm(gap, state, flux_x))


def pair_body(mine, got, out_hbm, mids, out, sem):
    is0 = parity("gx") == 0

    def both(rows):
        x, y = mine[rows, :], got[rows, :]
        return jnp.where(is0, x, y), jnp.where(is0, y, x)

    ca, cb = zip(*(both(pl.ds(EDGE + k, 1)) for k in range(16)))
    ca, cb = ([jnp.broadcast_to(t, (SUB, NK)) for t in c] for c in (ca, cb))
    hla, hra, tla, tra = ca[:4]
    hlb, hrb, tlb, trb = cb[:4]
    inv = 1.0 / (1.0 - tra * hlb)
    down = [hlb * tla * inv, hrb * inv, tla * inv, tra * hrb * inv, hlb * inv, inv, tra * inv]
    for k, t in enumerate(down):
        mids[pl.ds(4 * NV * HALF + k, 1), :] = t[0:1]
    cross_h, cross_t = hra * inv, tlb * inv
    edge = [hla + hra * down[0], hra * down[1], tlb * down[2], trb + tlb * down[3]]
    edge += [ca[10 + q] + (cross_h * hlb) * ca[13 + q] for q in range(3)]
    edge += [cross_t * ca[13 + q] for q in range(3)]
    edge += [cross_h * cb[10 + q] for q in range(3)]
    edge += [cb[13 + q] + (cross_t * tra) * cb[10 + q] for q in range(3)]
    lane = lax.broadcasted_iota(jnp.int32, (SUB, NK), 1)
    packed = jnp.zeros((SUB, NK), F32)
    for k, t in enumerate(edge):
        packed = jnp.where(lane == k, t, packed)

    k = CS["pair"]
    blocks = [pl.ds(WIDE * SUB * r, WIDE * SUB) for r in range(HALF // SUB)]
    stores = [pltpu.make_async_copy(out.at[b], out_hbm.at[b], sem.at[r]) for r, b in enumerate(blocks)]
    for r in range(HALF // SUB):
        at = WIDE * SUB * r
        out[pl.ds(at + 12 * NV, SUB, stride=WIDE), :] = packed
        for v in range(NV):
            a, b = zip(*(both(pl.ds((NV * e + v) * HALF + SUB * r, SUB)) for e in range(12)))
            ha, ta, hb, tb = a[0], a[1], b[0], b[1]
            for q in range(3):
                ha, ta = ha + ca[4 + q] * b[4 + q], ta + ca[7 + q] * b[4 + q]
                hb, tb = hb + cb[4 + q] * a[4 + q], tb + cb[7 + q] * a[4 + q]
            head = (hb + hlb * ta) * inv
            tail = (ta + tra * hb) * inv
            da, ea = a[2] + flux_weight(0, NI) * b[7], a[3] + flux_weight(NI - 1, NI) * b[7]
            db, eb = b[2] + flux_weight(0, -1) * a[7], b[3] + flux_weight(NI - 1, -1) * a[7]
            dhead = k["inv"] * db + k["inv_hl"] * ea
            dtail = k["inv"] * ea + k["inv_tr"] * db
            values = [ha + hra * head, tb + tlb * tail, da + float(CS["hr"]) * dhead, eb + float(CS["tl"]) * dtail]
            values += list(a[8:12]) + list(b[8:12])
            for e, t in enumerate(values):
                out[pl.ds(at + NV * e + v, SUB, stride=WIDE), :] = t
            for e, t in enumerate((head, tail, dhead, dtail)):
                mids[pl.ds((NV * e + v) * HALF + SUB * r, SUB), :] = t
        stores[r].start()
    for c in stores:
        c.wait()


def pair(mine, got):
    vmem = pl.BlockSpec(memory_space=pltpu.VMEM)
    return pl.pallas_call(
        pair_body,
        out_shape=(
            jax.ShapeDtypeStruct((PAIRS * WIDE, NK), F32),
            jax.ShapeDtypeStruct((4 * NV * HALF + SUB, NK), F32),
        ),
        in_specs=[vmem] * 2,
        out_specs=(pl.BlockSpec(memory_space=pltpu.HBM), vmem),
        scratch_shapes=[pltpu.VMEM((PAIRS * WIDE, NK), F32), pltpu.SemaphoreType.DMA((HALF // SUB,))],
        compiler_params=pltpu.CompilerParams(vmem_limit_bytes=8 << 20),
        cost_estimate=pl.CostEstimate(flops=1 << 20, bytes_accessed=1 << 20, transcendentals=0),
        name="pair",
    )(mine, got)


def join_body(x, out_hbm, out, coef, sem):
    for r in range(PAIRS // SUB):
        packed = x[pl.ds(WIDE * SUB * r + 12 * NV, SUB, stride=WIDE), :]
        for k in range(16):
            coef[pl.ds(PAIRS * k + SUB * r, SUB), :] = jnp.broadcast_to(packed[:, k : k + 1], (SUB, NK))

    def row(p, k):
        return jnp.broadcast_to(coef[pl.ds(PAIRS * k + p, 1), :], (NV, NK))

    def value(p, k):
        return x[pl.ds(WIDE * p + NV * k, NV), :]

    c = CS["pair"]
    head_f, tail_f, head_d, tail_d = [], [], [], []
    for p in range(PAIRS):
        h, t, dh, dt = (value(p, k) for k in range(4))
        if p:
            for q in range(3):
                z = value(p - 1, 8 + q)
                h, t = h + row(p, 4 + q) * z, t + row(p, 7 + q) * z
            z = value(p - 1, 11)
            dh, dt = dh + c["low"][0] * z, dt + c["low"][1] * z
        if p < PAIRS - 1:
            for q in range(3):
                z = value(p + 1, 4 + q)
                h, t = h + row(p, 10 + q) * z, t + row(p, 13 + q) * z
            z = value(p + 1, 7)
            dh, dt = dh + c["high"][0] * z, dt + c["high"][1] * z
        head_f.append(h)
        tail_f.append(t)
        head_d.append(dh)
        tail_d.append(dt)

    scale = 8.0
    num, den = [None] * PAIRS, [None] * PAIRS
    hl, hr, tl, tr = ([row(p, k) for p in range(PAIRS)] for k in range(4))
    num[0], den[0] = tr[0], jnp.ones((NV, NK), F32)
    for p in range(1, PAIRS):
        cross = tl[p] * hr[p] - tr[p] * hl[p]
        num[p] = (scale * tr[p]) * den[p - 1] + (scale * cross) * num[p - 1]
        den[p] = scale * den[p - 1] - (scale * hl[p]) * num[p - 1]
    inv = [None] + [1.0 / den[p] for p in range(1, PAIRS)]
    e = [num[0]] + [num[p] * inv[p] for p in range(1, PAIRS)]
    keep = [None] + [(scale * den[p - 1]) * inv[p] for p in range(1, PAIRS)]

    fwd_f, fwd_d = [tail_f[0]], [tail_d[0]]
    chl, chr_, ctl, ce = c["hl"], c["hr"], c["tl"], c["e"]
    for p in range(1, PAIRS):
        a = tl[p] * keep[p]
        fwd_f.append((tail_f[p] + (a * e[p - 1]) * head_f[p]) + a * fwd_f[-1])
        k = ctl / (1.0 - chl * ce[p - 1])
        fwd_d.append((tail_d[p] + float(k * ce[p - 1]) * head_d[p]) + float(k) * fwd_d[-1])

    blocks = [pl.ds(ROWS * SUB * r, ROWS * SUB) for r in range(PAIRS // SUB)]
    stores = [pltpu.make_async_copy(out.at[b], out_hbm.at[b], sem.at[r]) for r, b in enumerate(blocks)]
    zero = jnp.zeros((NV, NK), F32)
    right_f, right_d = zero, zero
    for p in range(PAIRS - 1, -1, -1):
        if p:
            h = keep[p]
            at_f = (head_f[p] + hl[p] * fwd_f[p - 1]) * h + (hr[p] * h) * right_f
            left_f = fwd_f[p - 1] + e[p - 1] * at_f
            k = 1.0 / (1.0 - chl * ce[p - 1])
            at_d = (float(k) * head_d[p] + float(k * chl) * fwd_d[p - 1]) + float(k * chr_) * right_d
            left_d = fwd_d[p - 1] + float(ce[p - 1]) * at_d
        else:
            at_f = at_d = left_f = left_d = zero
        for k, val in enumerate((left_f, right_f, left_d, right_d)):
            out[pl.ds(ROWS * p + NV * k, NV), :] = val
        right_f, right_d = at_f, at_d
        if p % SUB == 0:
            stores[p // SUB].start()
    for t in stores:
        t.wait()


def join(x):
    vmem = pl.BlockSpec(memory_space=pltpu.VMEM)
    return pl.pallas_call(
        join_body,
        out_shape=jax.ShapeDtypeStruct((PAIRS * ROWS, NK), F32),
        in_specs=[vmem],
        out_specs=pl.BlockSpec(memory_space=pltpu.HBM),
        scratch_shapes=[
            pltpu.VMEM((PAIRS * ROWS, NK), F32),
            pltpu.VMEM((16 * PAIRS, NK), F32),
            pltpu.SemaphoreType.DMA((PAIRS // SUB,)),
        ],
        compiler_params=pltpu.CompilerParams(vmem_limit_bytes=8 << 20),
        cost_estimate=pl.CostEstimate(flops=1 << 20, bytes_accessed=1 << 20, transcendentals=0),
        name="join",
    )(x)


def far_body(outer, two, own, send):
    core = parity("gx")
    wd = jnp.where(core == 0, flux_weight(NI - 1, -1), flux_weight(0, NI)).astype(F32)
    for out, half in ((own, core), (send, 1 - core)):
        for v in range(NV):
            for r in range(HALF // SUB):
                rows = pl.ds(pl.multiple_of(HALF * half + SUB * r, SUB), SUB)
                a = [two[v, k, rows, :] for k in range(4)]
                f = outer[C_FAR] * a[0] + outer[C_FAR + 1] * a[1] + outer[C_FAR + 2] * a[2]
                for k, t in enumerate((f, wd * a[3])):
                    out[pl.ds((NV * k + v) * HALF + SUB * r, SUB), :] = t


def far(outer, two):
    vmem = pl.BlockSpec(memory_space=pltpu.VMEM)
    out = jax.ShapeDtypeStruct((2 * NV * HALF, NK), F32)
    return pl.pallas_call(
        far_body,
        out_shape=(out, out),
        in_specs=[vmem] * 2,
        out_specs=(vmem,) * 2,
        compiler_params=pltpu.CompilerParams(vmem_limit_bytes=8 << 20),
        cost_estimate=pl.CostEstimate(flops=1 << 18, bytes_accessed=1 << 19, transcendentals=0),
        name="far",
    )(outer, two)


def split_body(z, mids, far_own, far_got, own, send):
    is0 = parity("gx") == 0
    c = CS["pair"]
    down = [jnp.broadcast_to(mids[pl.ds(4 * NV * HALF + k, 1), :], (SUB, NK)) for k in range(7)]
    for r in range(HALF // SUB):
        for v in range(NV):
            lf, rf, ld, rd = (z[pl.ds(ROWS * SUB * r + NV * k + v, SUB, stride=ROWS), :] for k in range(4))
            head, tail, dhead, dtail = (mids[pl.ds((NV * k + v) * HALF + SUB * r, SUB), :] for k in range(4))
            fo, do = (far_own[pl.ds((NV * k + v) * HALF + SUB * r, SUB), :] for k in range(2))
            fg, dg = (far_got[pl.ds((NV * k + v) * HALF + SUB * r, SUB), :] for k in range(2))
            fa, da = jnp.where(is0, fo, fg), jnp.where(is0, do, dg)
            fb, db = jnp.where(is0, fg, fo), jnp.where(is0, dg, do)
            head = (head + down[4] * fa + down[5] * fb) + down[0] * lf + down[1] * rf
            tail = (tail + down[5] * fa + down[6] * fb) + down[2] * lf + down[3] * rf
            dhead = (dhead + c["inv_hl"] * da + c["inv"] * db) + c["down"][0] * ld + c["down"][1] * rd
            dtail = (dtail + c["inv"] * da + c["inv_tr"] * db) + c["down"][2] * ld + c["down"][3] * rd
            a, b = (lf, head, ld, dhead), (tail, rf, dtail, rd)
            for k in range(4):
                rows = pl.ds((NV * k + v) * HALF + SUB * r, SUB)
                own[rows, :] = jnp.where(is0, a[k], b[k])
                send[rows, :] = jnp.where(is0, b[k], a[k])


def split(z, mids, far_own, far_got):
    vmem = pl.BlockSpec(memory_space=pltpu.VMEM)
    out = jax.ShapeDtypeStruct((4 * NV * HALF, NK), F32)
    return pl.pallas_call(
        split_body,
        out_shape=(out, out),
        in_specs=[vmem] * 4,
        out_specs=(vmem,) * 2,
        compiler_params=pltpu.CompilerParams(vmem_limit_bytes=8 << 20),
        cost_estimate=pl.CostEstimate(flops=1 << 20, bytes_accessed=1 << 20, transcendentals=0),
        name="split",
    )(z, mids, far_own, far_got)


def block_body(inner, s_hbm, f_hbm, fy_hbm, one, two, yone, ytwo, mx, my, base, mxb, s, f, fy, pad, sem):
    moves = ((fy_hbm, fy), (s_hbm, s), (f_hbm, f))
    for v in range(NV):
        for k, (h, t) in enumerate(moves):
            pltpu.make_async_copy(h.at[v], t.at[v], sem.at[k, v]).start()
    piece = lax.axis_index("gx")
    is0 = parity("gx") == 0
    even = parity("gy") == 0
    first = jnp.where(piece == 0, 1.0 / 36.0, 0.0).astype(F32)
    last = jnp.where(piece == PIECES - 1, -1.0 / 36.0, 0.0).astype(F32)
    mxt = jnp.transpose(mx[...] * -0.5)
    myt = jnp.transpose(my[...] * -0.5)
    for i in range(NI):
        mxb[i] = jnp.broadcast_to(mxt[:, i : i + 1], (NJ, NK))
        pad[NI + i, 0:NJ, :] = jnp.broadcast_to(myt[:, i : i + 1], (NJ, NK))

    @pl.loop(0, NV)
    def _(v):
        for k, (h, t) in enumerate(moves):
            pltpu.make_async_copy(h.at[v], t.at[v], sem.at[k, v]).wait()
        for i in range(NI):
            for q in range(NJ // SUB):
                pad[i, pl.ds(SUB + SUB * q, SUB), :] = fy[v, i, pl.ds(SUB * q, SUB), :]
            part = pl.ds(4 * (i % 2), 4)
            a, b = yone[v, i // 2, part, :], ytwo[v, i // 2, part, :]
            pad[i, SUB - 4 : SUB, :] = jnp.where(even, b, a)
            pad[i, SUB + NJ : SUB + NJ + 4, :] = jnp.where(even, a, b)

        for q in range(NJ // SUB):
            rows = pl.ds(SUB * q, SUB)
            a = [one[v, k, rows, :] for k in range(4)]
            b = [two[v, k, rows, :] for k in range(4)]
            low = [jnp.where(is0, b[k], a[k]) for k in range(4)]
            high = [jnp.where(is0, a[k], b[k]) for k in range(4)]
            st = low[:3] + [s[v, i, rows, :] for i in range(NI)] + high[:3]
            fl = [low[3]] + [f[v, i, rows, :] for i in range(NI)] + [high[3]]
            ye, yd, us = [], [], []
            for i in range(NI):
                d6 = (
                    (st[i] + st[i + 6])
                    - 6.0 * (st[i + 1] + st[i + 5])
                    + 15.0 * (st[i + 2] + st[i + 4])
                    - 20.0 * st[i + 3]
                )
                y = inner[C_MG + i] * d6
                ye.append(y - inner[C_C + i] * ye[-1] if i else y)
                u = fl[i + 2] - fl[i]
                us.append(u)
                r = float(RHO * CS["m"][i]) * u
                if i == 0:
                    r = r + (first * float(CS["m"][i])) * fl[1]
                if i == NI - 1:
                    r = r + (last * float(CS["m"][i])) * fl[NI]
                yd.append(r - float(CS["c"][i]) * yd[-1] if i else r)
            xe = xd = None
            for i in range(NI - 1, -1, -1):
                xe = ye[i] if xe is None else ye[i] - inner[C_C + i] * xe
                xd = yd[i] if xd is None else yd[i] - float(CS["c"][i]) * xd
                at = SUB + SUB * q
                dy = None
                for k, w in enumerate(Y_WEIGHTS, start=1):
                    t = w * (pad[i, pl.ds(at + k, SUB), :] - pad[i, pl.ds(at - k, SUB), :])
                    dy = t if dy is None else dy + t
                d = us[i] * (1.0 / 12.0) + xd
                base[v, i, rows, :] = (st[i + 3] + xe) + (mxb[i, rows, :] * d + pad[NI + i, rows, :] * dy)


def block(inner, state, flux_x, flux_y, one, two, yone, ytwo, mx, my):
    vmem, hbm = pl.BlockSpec(memory_space=pltpu.VMEM), pl.BlockSpec(memory_space=pltpu.HBM)
    return pl.pallas_call(
        block_body,
        out_shape=(
            jax.ShapeDtypeStruct((NV, NI, NJ, NK), F32),
            jax.ShapeDtypeStruct((NI, NJ, NK), F32),
        ),
        in_specs=[vmem] + [hbm] * 3 + [vmem] * 6,
        out_specs=(vmem, vmem),
        scratch_shapes=[pltpu.VMEM((NV, NI, NJ, NK), F32)] * 3
        + [pltpu.VMEM((2 * NI, SUB + NJ + SUB, NK), F32), pltpu.SemaphoreType.DMA((3, NV))],
        compiler_params=pltpu.CompilerParams(vmem_limit_bytes=16 << 20),
        cost_estimate=pl.CostEstimate(flops=1 << 25, bytes_accessed=64 << 20, transcendentals=0),
        name="block",
    )(inner, *in_hbm(state, flux_x, flux_y), one, two, yone, ytwo, mx, my)


def finish_body(outer, base, mxb, own, got, out_hbm, out, sem):
    core = parity("gx")
    stores = [pltpu.make_async_copy(out.at[v], out_hbm.at[v], sem.at[v]) for v in range(NV)]
    for v in range(NV):
        for z, half in ((own, core), (got, 1 - core)):
            for r in range(HALF // SUB):
                rows = pl.ds(pl.multiple_of(HALF * half + SUB * r, SUB), SUB)
                lf, rf, ld, rd = (z[pl.ds((NV * k + v) * HALF + SUB * r, SUB), :] for k in range(4))
                for i in range(NI):
                    d = float(CS["left"][i]) * ld + float(CS["right"][i]) * rd
                    e = outer[C_LEFT + i] * lf + outer[C_RIGHT + i] * rf
                    out[v, i, rows, :] = (base[v, i, rows, :] + e) + mxb[i, rows, :] * d
        stores[v].start()
    for c in stores:
        c.wait()


def finish(outer, base, mxb, own, got):
    return pl.pallas_call(
        finish_body,
        out_shape=jax.ShapeDtypeStruct((NV, NI, NJ, NK), F32),
        in_specs=[pl.BlockSpec(memory_space=pltpu.VMEM)] * 5,
        out_specs=pl.BlockSpec(memory_space=pltpu.HBM),
        scratch_shapes=[pltpu.VMEM((NV, NI, NJ, NK), F32), pltpu.SemaphoreType.DMA((NV,))],
        compiler_params=pltpu.CompilerParams(vmem_limit_bytes=12 << 20),
        cost_estimate=pl.CostEstimate(flops=1 << 22, bytes_accessed=3 << 20, transcendentals=0),
        name="finish",
    )(outer, base, mxb, own, got)


def exchange(x, rows):
    groups = [[2 * p + c for p in range(PAIRS)] for c in range(2)]
    y = lax.all_to_all(x.reshape(PAIRS, rows, NK), "gx", 0, 0, tiled=True, axis_index_groups=groups)
    return y.reshape(PAIRS * rows, NK)


def per_device(flux_x, flux_y, state, metric_x, metric_y, filter_gap):
    count_y = lax.axis_size("gy")
    pair_in = [(i, i ^ 1) for i in range(PIECES)]
    pair_out = [(i, i + 1 if i % 2 else i - 1) for i in range(1, PIECES - 1)]
    y_in = [(i, i ^ 1) for i in range(count_y)]
    y_out = [(i, (i + 1 if i % 2 else i - 1) % count_y) for i in range(count_y)]

    inner, outer, mine, send = own_share(filter_gap, state, flux_x)
    send, state, flux_x, flux_y = lax.optimization_barrier((send, state, flux_x, flux_y))
    got = lax.ppermute(send, "gx", pair_in)
    got, *faces = lax.optimization_barrier((got, *pack(state, flux_x, flux_y)))
    ends, mids = pair(mine, got)
    ends, send_one, send_two, ysend_one, ysend_two = lax.optimization_barrier((ends, *faces))
    ends = exchange(ends, WIDE)
    one = lax.ppermute(send_one, "gx", pair_in)
    two = lax.ppermute(send_two, "gx", pair_out)
    yone = lax.ppermute(ysend_one, "gy", y_in)
    ytwo = lax.ppermute(ysend_two, "gy", y_out)
    outside = join(ends)
    outside, one = lax.optimization_barrier((outside, one))
    two, yone, ytwo = lax.optimization_barrier((two, yone, ytwo))
    far_own, far_send = far(outer, two)
    far_got = lax.ppermute(far_send, "gx", pair_in)
    base, mxb = block(inner, state, flux_x, flux_y, one, two, yone, ytwo, metric_x, metric_y)
    outside, base, mxb, far_got = lax.optimization_barrier((exchange(outside, ROWS), base, mxb, far_got))
    own, send = split(outside, mids, far_own, far_got)
    return finish(outer, base, mxb, own, lax.ppermute(send, "gx", pair_in))


def solution(mesh):
    return jax.shard_map(
        per_device,
        mesh=mesh,
        in_specs=(
            P(None, "gx", "gy", None),
            P(None, "gx", "gy", None),
            P(None, "gx", "gy", None),
            P("gx", "gy"),
            P("gx", "gy"),
            P("gx"),
        ),
        out_specs=P(None, "gx", "gy", None),
        check_vma=False,
    )
```

```python
import jax
import jax.numpy as jnp
import numpy as np
from jax import lax
from jax.experimental import pallas as pl
from jax.experimental.pallas import tpu as pltpu
from jax.sharding import PartitionSpec as P

NV, NI, NJ, NK = 5, 16, 32, 128
PIECES, PAIRS, HALF = 32, 16, 16
VALUES = 10
ROWS, WIDE = 24, 56
EDGE = VALUES * NV * HALF
SUB = 8
F32 = jnp.float32
Y_WEIGHTS = (4.0 / 5.0, -1.0 / 5.0, 4.0 / 105.0, -1.0 / 280.0)
RHO = 25.0 / 36.0
BETA = 3.0 * RHO
D6 = (1.0, -6.0, 15.0, -20.0, 15.0, -6.0, 1.0)

C_C, C_MG = 0, NI
C_LEFT, C_RIGHT, C_FAR = 0, NI, 2 * NI


def constant_system():
    a = 1.0 / 3.0
    t = np.eye(NI) + a * (np.eye(NI, k=1) + np.eye(NI, k=-1))
    inv = np.linalg.inv(t)
    m, c = [], []
    prev = 0.0
    for _ in range(NI):
        m.append(1.0 / (1.0 - a * prev))
        prev = a * m[-1]
        c.append(prev)
    left, right = -a * inv[:, 0], -a * inv[:, -1]
    hl, hr, tl, tr = left[0], right[0], left[-1], right[-1]
    d = 1.0 / (1.0 - tr * hl)
    pair = dict(inv=d, inv_hl=d * hl, inv_tr=d * tr, down=[hl * tl * d, hr * d, tl * d, tr * hr * d])
    for k in pair:
        pair[k] = [float(t) for t in pair[k]] if isinstance(pair[k], list) else float(pair[k])
    p = dict(hl=hl + hr * hl * tl * d, hr=hr * hr * d, tl=tl * tl * d, tr=tr + tl * tr * hr * d)
    e = [p["tr"]]
    for _ in range(PAIRS - 1):
        e.append(p["tr"] + p["tl"] * p["hr"] * e[-1] / (1.0 - p["hl"] * e[-1]))
    pair.update(p, e=e)
    return dict(m=m, c=c, inv=inv, left=left, right=right, hl=hl, hr=hr, tl=tl, tr=tr, pair=pair)


CS = constant_system()


def flux_weight(row, j):
    w = CS["inv"][row]
    lo = w[j - 1] if 0 <= j - 1 < NI else 0.0
    hi = w[j + 1] if 0 <= j + 1 < NI else 0.0
    return float(RHO * (lo - hi))


def splat(x):
    return jnp.full((SUB, NK), x, F32)


def in_hbm(*arrays):
    return tuple(pltpu.with_memory_space_constraint(a, pltpu.HBM) for a in arrays)


def parity(name):
    return lax.rem(lax.axis_index(name), 2)


def pack_body(s, f, fy, one, two, yone, ytwo, sem):
    core, odd = parity("gx"), parity("gy")

    def move(right, left, top, bottom):
        pairs = (
            (s.at[:, NI - 3 : NI], right.at[:, 0:3]),
            (f.at[:, NI - 1 : NI], right.at[:, 3:4]),
            (s.at[:, 0:3], left.at[:, 0:3]),
            (f.at[:, 0:1], left.at[:, 3:4]),
            (fy.at[:, :, NJ - SUB : NJ, :], top),
            (fy.at[:, :, 0:SUB, :], bottom),
        )
        copies = [pltpu.make_async_copy(x, y, sem.at[k]) for k, (x, y) in enumerate(pairs)]
        for c in copies:
            c.start()
        for c in copies:
            c.wait()

    for c, x in enumerate(((one, two), (two, one))):
        for o, y in enumerate(((yone, ytwo), (ytwo, yone))):

            @pl.when((core == c) & (odd == o))
            def _(x=x, y=y):
                move(*x, *y)


def pack(state, flux_x, flux_y):
    x_out = jax.ShapeDtypeStruct((NV, 4, NJ, NK), F32)
    y_out = jax.ShapeDtypeStruct((NV, NI, SUB, NK), F32)
    return pl.pallas_call(
        pack_body,
        out_shape=(x_out, x_out, y_out, y_out),
        in_specs=[pl.BlockSpec(memory_space=pltpu.HBM)] * 3,
        out_specs=(pl.BlockSpec(memory_space=pltpu.VMEM),) * 4,
        scratch_shapes=[pltpu.SemaphoreType.DMA((6,))],
        compiler_params=pltpu.CompilerParams(vmem_limit_bytes=8 << 20),
        cost_estimate=pl.CostEstimate(flops=0, bytes_accessed=2 << 20, transcendentals=0),
        name="pack",
    )(*in_hbm(state, flux_x, flux_y))


def own_body(gap_hbm, s_hbm, f_hbm, inner_hbm, outer, mine, send, inner, gap, s, f, own, gap_sem, inner_sem, sem):
    gap_load = pltpu.make_async_copy(gap_hbm, gap, gap_sem)
    gap_load.start()
    loads = [
        (
            pltpu.make_async_copy(s_hbm.at[v], s.at[v], sem.at[0, v]),
            pltpu.make_async_copy(f_hbm.at[v], f.at[v], sem.at[1, v]),
        )
        for v in range(NV)
    ]
    for both in loads:
        for c in both:
            c.start()
    core = parity("gx")
    piece = lax.axis_index("gx")
    gap_load.wait()
    alpha = [0.5 - splat(gap[i]) for i in range(NI)]
    g32 = [(0.5 - a) * (1.0 / 32.0) for a in alpha]
    m, c = [None] * NI, [None] * NI
    n, b = [None] * NI, [None] * NI
    for k in range(NI):
        m[k] = 1.0 / (1.0 - alpha[k] * c[k - 1]) if k else jnp.ones((SUB, NK), F32)
        c[k] = alpha[k] * m[k]
        r = NI - 1 - k
        n[r] = 1.0 / (1.0 - alpha[r] * b[r + 1]) if k else jnp.ones((SUB, NK), F32)
        b[r] = alpha[r] * n[r]
    left, right = [None] * NI, [None] * NI
    wh, wt = [None] * NI, [None] * NI
    left[0], right[NI - 1] = -b[0], -c[NI - 1]
    qh, qt = None, None
    for k in range(NI):
        r = NI - 1 - k
        if k:
            left[k] = -b[k] * left[k - 1]
            right[r] = -c[r] * right[r + 1]
            qh = -b[k - 1] if qh is None else -b[k - 1] * qh
            qt = -c[r + 1] if qt is None else -c[r + 1] * qt
            wh[k] = qh * n[k]
            wt[r] = qt * m[r]
        else:
            wh[0], wt[NI - 1] = n[0], m[NI - 1]
    for k in range(NI):
        inner[C_C + k] = c[k]
        inner[C_MG + k] = m[k] * g32[k]
        outer[C_LEFT + k] = left[k]
        outer[C_RIGHT + k] = right[k]
    inner_store = pltpu.make_async_copy(inner, inner_hbm, inner_sem)
    inner_store.start()
    vh = [wh[k] * g32[k] for k in range(NI)]
    vt = [wt[k] * g32[k] for k in range(NI)]

    def spread(v, j):
        terms = [D6[q + 3] * v[j - q] for q in range(-3, 4) if 0 <= j - q < NI]
        total = terms[0]
        for t in terms[1:]:
            total = total + t
        return total

    edge = [-alpha[0] * wh[0], -alpha[NI - 1] * wh[NI - 1], -alpha[0] * wt[0], -alpha[NI - 1] * wt[NI - 1]]
    low = [spread(v, q - 3) for v in (vh, vt) for q in range(3)]
    high = [spread(v, NI + q) for v in (vh, vt) for q in range(3)]
    edge += [jnp.where(core == 0, h, l) for h, l in zip(high, low)]
    edge += [jnp.where(core == 0, l, h) for h, l in zip(high, low)]
    for q in range(3):
        outer[C_FAR + q] = jnp.where(core == 0, edge[13 + q], edge[10 + q])
    for k, t in enumerate(edge):
        mine[pl.ds(EDGE + k, 1), :] = t[0:1]
        send[pl.ds(EDGE + k, 1), :] = t[0:1]

    first = jnp.where(piece == 0, 1.0 / 36.0, 0.0).astype(F32)
    last = jnp.where(piece == PIECES - 1, -1.0 / 36.0, 0.0).astype(F32)
    inv = CS["inv"]
    fh = [flux_weight(0, j) for j in range(NI)]
    ft = [flux_weight(NI - 1, j) for j in range(NI)]
    fh[0] = (fh[0] - BETA) + float(inv[0, 0]) * first
    ft[0] = ft[0] + float(inv[NI - 1, 0]) * first
    fh[NI - 1] = fh[NI - 1] + float(inv[0, NI - 1]) * last
    ft[NI - 1] = (ft[NI - 1] + BETA) + float(inv[NI - 1, NI - 1]) * last

    for i in range(NI):
        own[i] = spread(vh, i)
        own[NI + i] = spread(vt, i)

    s_in, s_out = (NI - 3) * (1 - core), (NI - 3) * core
    for v in range(NV):
        for c in loads[v]:
            c.wait()
        for out, half in ((mine, core), (send, 1 - core)):
            for r in range(HALF // SUB):
                rows = pl.ds(pl.multiple_of(HALF * half + SUB * r, SUB), SUB)
                sums = [None] * 4
                for i in range(NI):
                    a, z = s[v, i, rows, :], f[v, i, rows, :]
                    terms = (own[i] * a, own[NI + i] * a, fh[i] * z, ft[i] * z)
                    sums = [t if o is None else o + t for o, t in zip(sums, terms)]
                faces = [s[v, s_in + k, rows, :] for k in range(3)] + [s[v, s_out + k, rows, :] for k in range(3)]
                for k, t in enumerate(sums + faces):
                    out[pl.ds((NV * k + v) * HALF + SUB * r, SUB), :] = t
    inner_store.wait()


def own_share(gap, state, flux_x):
    vmem, hbm = pl.BlockSpec(memory_space=pltpu.VMEM), pl.BlockSpec(memory_space=pltpu.HBM)
    coef = jax.ShapeDtypeStruct((2 * NI, SUB, NK), F32)
    coef_far = jax.ShapeDtypeStruct((2 * NI + 3, SUB, NK), F32)
    values = jax.ShapeDtypeStruct((EDGE + 16, NK), F32)
    return pl.pallas_call(
        own_body,
        out_shape=(coef, coef_far, values, values),
        in_specs=[hbm, hbm, hbm],
        out_specs=(hbm, vmem, vmem, vmem),
        scratch_shapes=[
            pltpu.VMEM((2 * NI, SUB, NK), F32),
            pltpu.SMEM((NI,), F32),
            pltpu.VMEM((NV, NI, NJ, NK), F32),
            pltpu.VMEM((NV, NI, NJ, NK), F32),
            pltpu.VMEM((2 * NI, SUB, NK), F32),
            pltpu.SemaphoreType.DMA,
            pltpu.SemaphoreType.DMA,
            pltpu.SemaphoreType.DMA((2, NV)),
        ],
        compiler_params=pltpu.CompilerParams(vmem_limit_bytes=12 << 20),
        cost_estimate=pl.CostEstimate(flops=1 << 24, bytes_accessed=4 << 20, transcendentals=0),
        name="own_share",
    )(*in_hbm(gap, state, flux_x))


def pair_body(mine, got, out_hbm, mids, out, sem):
    is0 = parity("gx") == 0

    def both(rows):
        x, y = mine[rows, :], got[rows, :]
        return jnp.where(is0, x, y), jnp.where(is0, y, x)

    ca, cb = zip(*(both(pl.ds(EDGE + k, 1)) for k in range(16)))
    ca, cb = ([jnp.broadcast_to(t, (SUB, NK)) for t in c] for c in (ca, cb))
    hla, hra, tla, tra = ca[:4]
    hlb, hrb, tlb, trb = cb[:4]
    inv = 1.0 / (1.0 - tra * hlb)
    down = [hlb * tla * inv, hrb * inv, tla * inv, tra * hrb * inv, hlb * inv, inv, tra * inv]
    for k, t in enumerate(down):
        mids[pl.ds(4 * NV * HALF + k, 1), :] = t[0:1]
    cross_h, cross_t = hra * inv, tlb * inv
    edge = [hla + hra * down[0], hra * down[1], tlb * down[2], trb + tlb * down[3]]
    edge += [ca[10 + q] + (cross_h * hlb) * ca[13 + q] for q in range(3)]
    edge += [cross_t * ca[13 + q] for q in range(3)]
    edge += [cross_h * cb[10 + q] for q in range(3)]
    edge += [cb[13 + q] + (cross_t * tra) * cb[10 + q] for q in range(3)]
    lane = lax.broadcasted_iota(jnp.int32, (SUB, NK), 1)
    packed = jnp.zeros((SUB, NK), F32)
    for k, t in enumerate(edge):
        packed = jnp.where(lane == k, t, packed)

    k = CS["pair"]
    blocks = [pl.ds(WIDE * SUB * r, WIDE * SUB) for r in range(HALF // SUB)]
    stores = [pltpu.make_async_copy(out.at[b], out_hbm.at[b], sem.at[r]) for r, b in enumerate(blocks)]
    for r in range(HALF // SUB):
        at = WIDE * SUB * r
        out[pl.ds(at + VALUES * NV, SUB, stride=WIDE), :] = packed
        for v in range(NV):
            a, b = zip(*(both(pl.ds((NV * e + v) * HALF + SUB * r, SUB)) for e in range(VALUES)))
            ha, ta, hb, tb = a[0], a[1], b[0], b[1]
            for q in range(3):
                ha, ta = ha + ca[4 + q] * b[4 + q], ta + ca[7 + q] * b[4 + q]
                hb, tb = hb + cb[4 + q] * a[4 + q], tb + cb[7 + q] * a[4 + q]
            head = (hb + hlb * ta) * inv
            tail = (ta + tra * hb) * inv
            da, ea, db, eb = a[2], a[3], b[2], b[3]
            dhead = k["inv"] * db + k["inv_hl"] * ea
            dtail = k["inv"] * ea + k["inv_tr"] * db
            values = [ha + hra * head, tb + tlb * tail, da + float(CS["hr"]) * dhead, eb + float(CS["tl"]) * dtail]
            values += list(a[7:10]) + list(b[7:10])
            for e, t in enumerate(values):
                out[pl.ds(at + NV * e + v, SUB, stride=WIDE), :] = t
            for e, t in enumerate((head, tail, dhead, dtail)):
                mids[pl.ds((NV * e + v) * HALF + SUB * r, SUB), :] = t
        stores[r].start()
    for c in stores:
        c.wait()


def pair(mine, got):
    vmem = pl.BlockSpec(memory_space=pltpu.VMEM)
    return pl.pallas_call(
        pair_body,
        out_shape=(
            jax.ShapeDtypeStruct((PAIRS * WIDE, NK), F32),
            jax.ShapeDtypeStruct((4 * NV * HALF + SUB, NK), F32),
        ),
        in_specs=[vmem] * 2,
        out_specs=(pl.BlockSpec(memory_space=pltpu.HBM), vmem),
        scratch_shapes=[pltpu.VMEM((PAIRS * WIDE, NK), F32), pltpu.SemaphoreType.DMA((HALF // SUB,))],
        compiler_params=pltpu.CompilerParams(vmem_limit_bytes=8 << 20),
        cost_estimate=pl.CostEstimate(flops=1 << 20, bytes_accessed=1 << 20, transcendentals=0),
        name="pair",
    )(mine, got)


def join_body(x, out_hbm, out, coef, sem):
    for r in range(PAIRS // SUB):
        packed = x[pl.ds(WIDE * SUB * r + VALUES * NV, SUB, stride=WIDE), :]
        for k in range(16):
            coef[pl.ds(PAIRS * k + SUB * r, SUB), :] = jnp.broadcast_to(packed[:, k : k + 1], (SUB, NK))

    def row(p, k):
        return jnp.broadcast_to(coef[pl.ds(PAIRS * k + p, 1), :], (NV, NK))

    def value(p, k):
        return x[pl.ds(WIDE * p + NV * k, NV), :]

    c = CS["pair"]
    head_f, tail_f, head_d, tail_d = [], [], [], []
    for p in range(PAIRS):
        h, t, dh, dt = (value(p, k) for k in range(4))
        if p:
            for q in range(3):
                z = value(p - 1, 7 + q)
                h, t = h + row(p, 4 + q) * z, t + row(p, 7 + q) * z
        if p < PAIRS - 1:
            for q in range(3):
                z = value(p + 1, 4 + q)
                h, t = h + row(p, 10 + q) * z, t + row(p, 13 + q) * z
        head_f.append(h)
        tail_f.append(t)
        head_d.append(dh)
        tail_d.append(dt)

    scale = 8.0
    num, den = [None] * PAIRS, [None] * PAIRS
    hl, hr, tl, tr = ([row(p, k) for p in range(PAIRS)] for k in range(4))
    num[0], den[0] = tr[0], jnp.ones((NV, NK), F32)
    for p in range(1, PAIRS):
        cross = tl[p] * hr[p] - tr[p] * hl[p]
        num[p] = (scale * tr[p]) * den[p - 1] + (scale * cross) * num[p - 1]
        den[p] = scale * den[p - 1] - (scale * hl[p]) * num[p - 1]
    inv = [None] + [1.0 / den[p] for p in range(1, PAIRS)]
    e = [num[0]] + [num[p] * inv[p] for p in range(1, PAIRS)]
    keep = [None] + [(scale * den[p - 1]) * inv[p] for p in range(1, PAIRS)]

    fwd_f, fwd_d = [tail_f[0]], [tail_d[0]]
    chl, chr_, ctl, ce = c["hl"], c["hr"], c["tl"], c["e"]
    for p in range(1, PAIRS):
        a = tl[p] * keep[p]
        fwd_f.append((tail_f[p] + (a * e[p - 1]) * head_f[p]) + a * fwd_f[-1])
        k = ctl / (1.0 - chl * ce[p - 1])
        fwd_d.append((tail_d[p] + float(k * ce[p - 1]) * head_d[p]) + float(k) * fwd_d[-1])

    blocks = [pl.ds(ROWS * SUB * r, ROWS * SUB) for r in range(PAIRS // SUB)]
    stores = [pltpu.make_async_copy(out.at[b], out_hbm.at[b], sem.at[r]) for r, b in enumerate(blocks)]
    zero = jnp.zeros((NV, NK), F32)
    right_f, right_d = zero, zero
    for p in range(PAIRS - 1, -1, -1):
        if p:
            h = keep[p]
            at_f = (head_f[p] + hl[p] * fwd_f[p - 1]) * h + (hr[p] * h) * right_f
            left_f = fwd_f[p - 1] + e[p - 1] * at_f
            k = 1.0 / (1.0 - chl * ce[p - 1])
            at_d = (float(k) * head_d[p] + float(k * chl) * fwd_d[p - 1]) + float(k * chr_) * right_d
            left_d = fwd_d[p - 1] + float(ce[p - 1]) * at_d
        else:
            at_f = at_d = left_f = left_d = zero
        for k, val in enumerate((left_f, right_f, left_d, right_d)):
            out[pl.ds(ROWS * p + NV * k, NV), :] = val
        right_f, right_d = at_f, at_d
        if p % SUB == 0:
            stores[p // SUB].start()
    for t in stores:
        t.wait()


def join(x):
    vmem = pl.BlockSpec(memory_space=pltpu.VMEM)
    return pl.pallas_call(
        join_body,
        out_shape=jax.ShapeDtypeStruct((PAIRS * ROWS, NK), F32),
        in_specs=[vmem],
        out_specs=pl.BlockSpec(memory_space=pltpu.HBM),
        scratch_shapes=[
            pltpu.VMEM((PAIRS * ROWS, NK), F32),
            pltpu.VMEM((16 * PAIRS, NK), F32),
            pltpu.SemaphoreType.DMA((PAIRS // SUB,)),
        ],
        compiler_params=pltpu.CompilerParams(vmem_limit_bytes=8 << 20),
        cost_estimate=pl.CostEstimate(flops=1 << 20, bytes_accessed=1 << 20, transcendentals=0),
        name="join",
    )(x)


def far_body(outer, two, own, other):
    core = parity("gx")
    for out, half in ((own, core), (other, 1 - core)):
        for v in range(NV):
            for r in range(HALF // SUB):
                rows = pl.ds(pl.multiple_of(HALF * half + SUB * r, SUB), SUB)
                a = [two[v, k, rows, :] for k in range(3)]
                out[pl.ds(v * HALF + SUB * r, SUB), :] = (
                    outer[C_FAR] * a[0] + outer[C_FAR + 1] * a[1] + outer[C_FAR + 2] * a[2]
                )


def far(outer, two):
    vmem = pl.BlockSpec(memory_space=pltpu.VMEM)
    out = jax.ShapeDtypeStruct((NV * HALF, NK), F32)
    return pl.pallas_call(
        far_body,
        out_shape=(out, out),
        in_specs=[vmem] * 2,
        out_specs=(vmem,) * 2,
        compiler_params=pltpu.CompilerParams(vmem_limit_bytes=8 << 20),
        cost_estimate=pl.CostEstimate(flops=1 << 18, bytes_accessed=1 << 19, transcendentals=0),
        name="far",
    )(outer, two)


def split_body(z, mids, far_own, far_other, own, send):
    is0 = parity("gx") == 0
    c = CS["pair"]
    down = [jnp.broadcast_to(mids[pl.ds(4 * NV * HALF + k, 1), :], (SUB, NK)) for k in range(7)]
    head_far, tail_far = jnp.where(is0, down[4], down[5]), jnp.where(is0, down[5], down[6])
    for r in range(HALF // SUB):
        for v in range(NV):
            lf, rf, ld, rd = (z[pl.ds(ROWS * SUB * r + NV * k + v, SUB, stride=ROWS), :] for k in range(4))
            head, tail, dhead, dtail = (mids[pl.ds((NV * k + v) * HALF + SUB * r, SUB), :] for k in range(4))
            part = pl.ds(v * HALF + SUB * r, SUB)
            w = far_own[part, :]
            head = (head + head_far * w) + down[0] * lf + down[1] * rf
            tail = (tail + tail_far * w) + down[2] * lf + down[3] * rf
            dhead = dhead + c["down"][0] * ld + c["down"][1] * rd
            dtail = dtail + c["down"][2] * ld + c["down"][3] * rd
            a, b = (lf, head, ld, dhead), (tail, rf, dtail, rd)
            for k in range(4):
                rows = pl.ds((NV * k + v) * HALF + SUB * r, SUB)
                own[rows, :] = jnp.where(is0, a[k], b[k])
                send[rows, :] = jnp.where(is0, b[k], a[k])
            send[pl.ds((4 * NV + v) * HALF + SUB * r, SUB), :] = far_other[part, :]


def split(z, mids, far_own, far_other):
    vmem = pl.BlockSpec(memory_space=pltpu.VMEM)
    own = jax.ShapeDtypeStruct((4 * NV * HALF, NK), F32)
    send = jax.ShapeDtypeStruct((5 * NV * HALF, NK), F32)
    return pl.pallas_call(
        split_body,
        out_shape=(own, send),
        in_specs=[vmem] * 4,
        out_specs=(vmem,) * 2,
        compiler_params=pltpu.CompilerParams(vmem_limit_bytes=8 << 20),
        cost_estimate=pl.CostEstimate(flops=1 << 20, bytes_accessed=1 << 20, transcendentals=0),
        name="split",
    )(z, mids, far_own, far_other)


def block_body(inner_hbm, s_hbm, f_hbm, fy_hbm, one, two, yone, ytwo, mx, my, base, mxb, inner, s, f, fy, pad, inner_sem, sem):
    inner_load = pltpu.make_async_copy(inner_hbm, inner, inner_sem)
    inner_load.start()
    moves = ((fy_hbm, fy), (s_hbm, s), (f_hbm, f))
    for v in range(NV):
        for k, (h, t) in enumerate(moves):
            pltpu.make_async_copy(h.at[v], t.at[v], sem.at[k, v]).start()
    piece = lax.axis_index("gx")
    is0 = parity("gx") == 0
    even = parity("gy") == 0
    first = jnp.where(piece == 0, 1.0 / 36.0, 0.0).astype(F32)
    last = jnp.where(piece == PIECES - 1, -1.0 / 36.0, 0.0).astype(F32)
    mxt = jnp.transpose(mx[...] * -0.5)
    myt = jnp.transpose(my[...] * -0.5)
    for i in range(NI):
        mxb[i] = jnp.broadcast_to(mxt[:, i : i + 1], (NJ, NK))
        pad[NI + i, 0:NJ, :] = jnp.broadcast_to(myt[:, i : i + 1], (NJ, NK))

    inner_load.wait()

    @pl.loop(0, NV)
    def _(v):
        for k, (h, t) in enumerate(moves):
            pltpu.make_async_copy(h.at[v], t.at[v], sem.at[k, v]).wait()
        for i in range(NI):
            for q in range(NJ // SUB):
                pad[i, pl.ds(SUB + SUB * q, SUB), :] = fy[v, i, pl.ds(SUB * q, SUB), :]
            a, b = yone[v, i], ytwo[v, i]
            pad[i, 0:SUB, :] = jnp.where(even, b, a)
            pad[i, SUB + NJ : SUB + NJ + SUB, :] = jnp.where(even, a, b)

        for q in range(NJ // SUB):
            rows = pl.ds(SUB * q, SUB)
            a = [one[v, k, rows, :] for k in range(4)]
            b = [two[v, k, rows, :] for k in range(4)]
            low = [jnp.where(is0, b[k], a[k]) for k in range(4)]
            high = [jnp.where(is0, a[k], b[k]) for k in range(4)]
            st = low[:3] + [s[v, i, rows, :] for i in range(NI)] + high[:3]
            fl = [low[3]] + [f[v, i, rows, :] for i in range(NI)] + [high[3]]
            ye, yd, us = [], [], []
            for i in range(NI):
                d6 = (
                    (st[i] + st[i + 6])
                    - 6.0 * (st[i + 1] + st[i + 5])
                    + 15.0 * (st[i + 2] + st[i + 4])
                    - 20.0 * st[i + 3]
                )
                y = inner[C_MG + i] * d6
                ye.append(y - inner[C_C + i] * ye[-1] if i else y)
                u = fl[i + 2] - fl[i]
                us.append(u)
                r = fl[2] if i == 0 else -fl[NI - 1] if i == NI - 1 else u
                r = float(RHO * CS["m"][i]) * r
                if i == 0:
                    r = r + (first * float(CS["m"][i])) * fl[1]
                if i == NI - 1:
                    r = r + (last * float(CS["m"][i])) * fl[NI]
                yd.append(r - float(CS["c"][i]) * yd[-1] if i else r)
            xe = xd = None
            for i in range(NI - 1, -1, -1):
                xe = ye[i] if xe is None else ye[i] - inner[C_C + i] * xe
                xd = yd[i] if xd is None else yd[i] - float(CS["c"][i]) * xd
                at = SUB + SUB * q
                dy = None
                for k, w in enumerate(Y_WEIGHTS, start=1):
                    t = w * (pad[i, pl.ds(at + k, SUB), :] - pad[i, pl.ds(at - k, SUB), :])
                    dy = t if dy is None else dy + t
                d = us[i] * (1.0 / 12.0) + xd
                base[v, i, rows, :] = (st[i + 3] + xe) + (mxb[i, rows, :] * d + pad[NI + i, rows, :] * dy)


def block(inner, state, flux_x, flux_y, one, two, yone, ytwo, mx, my):
    vmem, hbm = pl.BlockSpec(memory_space=pltpu.VMEM), pl.BlockSpec(memory_space=pltpu.HBM)
    return pl.pallas_call(
        block_body,
        out_shape=(
            jax.ShapeDtypeStruct((NV, NI, NJ, NK), F32),
            jax.ShapeDtypeStruct((NI, NJ, NK), F32),
        ),
        in_specs=[hbm] * 4 + [vmem] * 6,
        out_specs=(vmem, vmem),
        scratch_shapes=[pltpu.VMEM((2 * NI, SUB, NK), F32)]
        + [pltpu.VMEM((NV, NI, NJ, NK), F32)] * 3
        + [pltpu.VMEM((2 * NI, SUB + NJ + SUB, NK), F32), pltpu.SemaphoreType.DMA, pltpu.SemaphoreType.DMA((3, NV))],
        compiler_params=pltpu.CompilerParams(vmem_limit_bytes=16 << 20),
        cost_estimate=pl.CostEstimate(flops=1 << 25, bytes_accessed=64 << 20, transcendentals=0),
        name="block",
    )(*in_hbm(inner, state, flux_x, flux_y), one, two, yone, ytwo, mx, my)


def finish_body(outer, base, mxb, own, got, mids, far_other, out_hbm, out, sem):
    core = parity("gx")
    is0 = core == 0
    hl_inv, inv, tr_inv = (jnp.broadcast_to(mids[pl.ds(4 * NV * HALF + k, 1), :], (SUB, NK)) for k in (4, 5, 6))
    zero = jnp.zeros((SUB, NK), F32)
    own_far = (jnp.where(is0, zero, inv), jnp.where(is0, inv, zero))
    got_far = (jnp.where(is0, zero, tr_inv), jnp.where(is0, hl_inv, zero))
    stores = [pltpu.make_async_copy(out.at[v], out_hbm.at[v], sem.at[v]) for v in range(NV)]
    for v in range(NV):
        for z, half, far_w, far_z, far_at in (
            (own, core, own_far, got, 4 * NV),
            (got, 1 - core, got_far, far_other, 0),
        ):
            for r in range(HALF // SUB):
                rows = pl.ds(pl.multiple_of(HALF * half + SUB * r, SUB), SUB)
                lf, rf, ld, rd = (z[pl.ds((NV * k + v) * HALF + SUB * r, SUB), :] for k in range(4))
                w = far_z[pl.ds((far_at + v) * HALF + SUB * r, SUB), :]
                lf, rf = lf + far_w[0] * w, rf + far_w[1] * w
                for i in range(NI):
                    d = float(CS["left"][i]) * ld + float(CS["right"][i]) * rd
                    e = outer[C_LEFT + i] * lf + outer[C_RIGHT + i] * rf
                    out[v, i, rows, :] = (base[v, i, rows, :] + e) + mxb[i, rows, :] * d
        stores[v].start()
    for c in stores:
        c.wait()


def finish(outer, base, mxb, own, got, mids, far_other):
    return pl.pallas_call(
        finish_body,
        out_shape=jax.ShapeDtypeStruct((NV, NI, NJ, NK), F32),
        in_specs=[pl.BlockSpec(memory_space=pltpu.VMEM)] * 7,
        out_specs=pl.BlockSpec(memory_space=pltpu.HBM),
        scratch_shapes=[pltpu.VMEM((NV, NI, NJ, NK), F32), pltpu.SemaphoreType.DMA((NV,))],
        compiler_params=pltpu.CompilerParams(vmem_limit_bytes=12 << 20),
        cost_estimate=pl.CostEstimate(flops=1 << 22, bytes_accessed=3 << 20, transcendentals=0),
        name="finish",
    )(outer, base, mxb, own, got, mids, far_other)


def exchange(x, rows):
    groups = [[2 * p + c for p in range(PAIRS)] for c in range(2)]
    y = lax.all_to_all(x.reshape(PAIRS, rows, NK), "gx", 0, 0, tiled=True, axis_index_groups=groups)
    return y.reshape(PAIRS * rows, NK)


def per_device(flux_x, flux_y, state, metric_x, metric_y, filter_gap):
    count_y = lax.axis_size("gy")
    pair_in = [(i, i ^ 1) for i in range(PIECES)]
    pair_out = [(i, i + 1 if i % 2 else i - 1) for i in range(1, PIECES - 1)]
    y_in = [(i, i ^ 1) for i in range(count_y)]
    y_out = [(i, (i + 1 if i % 2 else i - 1) % count_y) for i in range(count_y)]

    inner, outer, mine, send = own_share(filter_gap, state, flux_x)
    send, state, flux_x, flux_y = lax.optimization_barrier((send, state, flux_x, flux_y))
    got = lax.ppermute(send, "gx", pair_in)
    got, *faces = lax.optimization_barrier((got, *pack(state, flux_x, flux_y)))
    ends, mids = pair(mine, got)
    ends, send_one, send_two, ysend_one, ysend_two = lax.optimization_barrier((ends, *faces))
    ends = exchange(ends, WIDE)
    one = lax.ppermute(send_one, "gx", pair_in)
    two = lax.ppermute(send_two, "gx", pair_out)
    yone = lax.ppermute(ysend_one, "gy", y_in)
    ytwo = lax.ppermute(ysend_two, "gy", y_out)
    outside = join(ends)
    outside, one = lax.optimization_barrier((outside, one))
    two, yone, ytwo = lax.optimization_barrier((two, yone, ytwo))
    far_own, far_other = far(outer, two)
    base, mxb = block(inner, state, flux_x, flux_y, one, two, yone, ytwo, metric_x, metric_y)
    outside, base, mxb, far_own = lax.optimization_barrier((exchange(outside, ROWS), base, mxb, far_own))
    own, send = split(outside, mids, far_own, far_other)
    got = lax.ppermute(send, "gx", pair_in)
    return finish(outer, base, mxb, own, got, mids, far_other)


def solution(mesh):
    return jax.shard_map(
        per_device,
        mesh=mesh,
        in_specs=(
            P(None, "gx", "gy", None),
            P(None, "gx", "gy", None),
            P(None, "gx", "gy", None),
            P("gx", "gy"),
            P("gx", "gy"),
            P("gx"),
        ),
        out_specs=P(None, "gx", "gy", None),
        check_vma=False,
    )
```

```python
import jax
import jax.numpy as jnp
import numpy as np
from jax import lax
from jax.experimental import pallas as pl
from jax.experimental.pallas import tpu as pltpu
from jax.sharding import PartitionSpec as P

NV, NI, NJ, NK = 5, 16, 32, 128
PIECES, PAIRS, HALF = 32, 16, 16
VALUES = 10
ROWS, WIDE = 24, 56
EDGE = VALUES * NV * HALF
SUB = 8
F32 = jnp.float32
Y_WEIGHTS = (4.0 / 5.0, -1.0 / 5.0, 4.0 / 105.0, -1.0 / 280.0)
RHO = 25.0 / 36.0
BETA = 3.0 * RHO
D6 = (1.0, -6.0, 15.0, -20.0, 15.0, -6.0, 1.0)

C_C, C_MG = 0, NI
C_LEFT, C_RIGHT, C_FAR = 0, NI, 2 * NI


def constant_system():
    a = 1.0 / 3.0
    t = np.eye(NI) + a * (np.eye(NI, k=1) + np.eye(NI, k=-1))
    inv = np.linalg.inv(t)
    m, c = [], []
    prev = 0.0
    for _ in range(NI):
        m.append(1.0 / (1.0 - a * prev))
        prev = a * m[-1]
        c.append(prev)
    left, right = -a * inv[:, 0], -a * inv[:, -1]
    hl, hr, tl, tr = left[0], right[0], left[-1], right[-1]
    d = 1.0 / (1.0 - tr * hl)
    pair = dict(inv=d, inv_hl=d * hl, inv_tr=d * tr, down=[hl * tl * d, hr * d, tl * d, tr * hr * d])
    for k in pair:
        pair[k] = [float(t) for t in pair[k]] if isinstance(pair[k], list) else float(pair[k])
    p = dict(hl=hl + hr * hl * tl * d, hr=hr * hr * d, tl=tl * tl * d, tr=tr + tl * tr * hr * d)
    e = [p["tr"]]
    for _ in range(PAIRS - 1):
        e.append(p["tr"] + p["tl"] * p["hr"] * e[-1] / (1.0 - p["hl"] * e[-1]))
    pair.update(p, e=e)
    return dict(m=m, c=c, inv=inv, left=left, right=right, hl=hl, hr=hr, tl=tl, tr=tr, pair=pair)


CS = constant_system()


def flux_weight(row, j):
    w = CS["inv"][row]
    lo = w[j - 1] if 0 <= j - 1 < NI else 0.0
    hi = w[j + 1] if 0 <= j + 1 < NI else 0.0
    return float(RHO * (lo - hi))


def splat(x):
    return jnp.full((SUB, NK), x, F32)


def in_hbm(*arrays):
    return tuple(pltpu.with_memory_space_constraint(a, pltpu.HBM) for a in arrays)


def parity(name):
    return lax.rem(lax.axis_index(name), 2)


def pack_body(s, f, fy, one, two, yone, ytwo, lo, hi, sem):
    core, odd = parity("gx"), parity("gy")
    copies = [
        pltpu.make_async_copy(fy.at[:, :, 0:SUB, :], lo, sem.at[0]),
        pltpu.make_async_copy(fy.at[:, :, NJ - SUB : NJ, :], hi, sem.at[1]),
    ]
    for c in copies:
        c.start()

    def faces(right, left):
        moves = [
            pltpu.make_async_copy(s.at[:, NI - 3 : NI], right.at[:, 0:3], sem.at[2]),
            pltpu.make_async_copy(f.at[:, NI - 1 : NI], right.at[:, 3:4], sem.at[3]),
            pltpu.make_async_copy(s.at[:, 0:3], left.at[:, 0:3], sem.at[4]),
            pltpu.make_async_copy(f.at[:, 0:1], left.at[:, 3:4], sem.at[5]),
        ]
        for c in moves:
            c.start()
        for c in moves:
            c.wait()

    def rows(top, bottom):
        for v in range(NV):
            for i in range(NI):
                part = pl.ds(4 * (i % 2), 4)
                top[v, i // 2, part, :] = hi[v, i, 4:8, :]
                bottom[v, i // 2, part, :] = lo[v, i, 0:4, :]

    @pl.when(core == 0)
    def _():
        faces(one, two)

    @pl.when(core == 1)
    def _():
        faces(two, one)

    for c in copies:
        c.wait()

    @pl.when(odd == 0)
    def _():
        rows(yone, ytwo)

    @pl.when(odd == 1)
    def _():
        rows(ytwo, yone)


def pack(state, flux_x, flux_y):
    x_out = jax.ShapeDtypeStruct((NV, 4, NJ, NK), F32)
    y_out = jax.ShapeDtypeStruct((NV, NI // 2, SUB, NK), F32)
    return pl.pallas_call(
        pack_body,
        out_shape=(x_out, x_out, y_out, y_out),
        in_specs=[pl.BlockSpec(memory_space=pltpu.HBM)] * 3,
        out_specs=(pl.BlockSpec(memory_space=pltpu.VMEM),) * 4,
        scratch_shapes=[
            pltpu.VMEM((NV, NI, SUB, NK), F32),
            pltpu.VMEM((NV, NI, SUB, NK), F32),
            pltpu.SemaphoreType.DMA((6,)),
        ],
        compiler_params=pltpu.CompilerParams(vmem_limit_bytes=8 << 20),
        cost_estimate=pl.CostEstimate(flops=0, bytes_accessed=2 << 20, transcendentals=0),
        name="pack",
    )(*in_hbm(state, flux_x, flux_y))


def own_body(gap_hbm, s_hbm, f_hbm, inner_hbm, outer, mine, send, inner, gap, s, f, own, gap_sem, inner_sem, sem):
    gap_load = pltpu.make_async_copy(gap_hbm, gap, gap_sem)
    gap_load.start()
    loads = [
        (
            pltpu.make_async_copy(s_hbm.at[v], s.at[v], sem.at[0, v]),
            pltpu.make_async_copy(f_hbm.at[v], f.at[v], sem.at[1, v]),
        )
        for v in range(NV)
    ]
    for both in loads:
        for c in both:
            c.start()
    core = parity("gx")
    piece = lax.axis_index("gx")
    gap_load.wait()
    alpha = [0.5 - splat(gap[i]) for i in range(NI)]
    g32 = [(0.5 - a) * (1.0 / 32.0) for a in alpha]
    m, c = [None] * NI, [None] * NI
    n, b = [None] * NI, [None] * NI
    for k in range(NI):
        m[k] = 1.0 / (1.0 - alpha[k] * c[k - 1]) if k else jnp.ones((SUB, NK), F32)
        c[k] = alpha[k] * m[k]
        r = NI - 1 - k
        n[r] = 1.0 / (1.0 - alpha[r] * b[r + 1]) if k else jnp.ones((SUB, NK), F32)
        b[r] = alpha[r] * n[r]
    left, right = [None] * NI, [None] * NI
    wh, wt = [None] * NI, [None] * NI
    left[0], right[NI - 1] = -b[0], -c[NI - 1]
    qh, qt = None, None
    for k in range(NI):
        r = NI - 1 - k
        if k:
            left[k] = -b[k] * left[k - 1]
            right[r] = -c[r] * right[r + 1]
            qh = -b[k - 1] if qh is None else -b[k - 1] * qh
            qt = -c[r + 1] if qt is None else -c[r + 1] * qt
            wh[k] = qh * n[k]
            wt[r] = qt * m[r]
        else:
            wh[0], wt[NI - 1] = n[0], m[NI - 1]
    for k in range(NI):
        inner[C_C + k] = c[k]
        inner[C_MG + k] = m[k] * g32[k]
        outer[C_LEFT + k] = left[k]
        outer[C_RIGHT + k] = right[k]
    inner_store = pltpu.make_async_copy(inner, inner_hbm, inner_sem)
    inner_store.start()
    vh = [wh[k] * g32[k] for k in range(NI)]
    vt = [wt[k] * g32[k] for k in range(NI)]

    def spread(v, j):
        terms = [D6[q + 3] * v[j - q] for q in range(-3, 4) if 0 <= j - q < NI]
        total = terms[0]
        for t in terms[1:]:
            total = total + t
        return total

    edge = [-alpha[0] * wh[0], -alpha[NI - 1] * wh[NI - 1], -alpha[0] * wt[0], -alpha[NI - 1] * wt[NI - 1]]
    low = [spread(v, q - 3) for v in (vh, vt) for q in range(3)]
    high = [spread(v, NI + q) for v in (vh, vt) for q in range(3)]
    edge += [jnp.where(core == 0, h, l) for h, l in zip(high, low)]
    edge += [jnp.where(core == 0, l, h) for h, l in zip(high, low)]
    for q in range(3):
        outer[C_FAR + q] = jnp.where(core == 0, edge[13 + q], edge[10 + q])
    for k, t in enumerate(edge):
        mine[pl.ds(EDGE + k, 1), :] = t[0:1]
        send[pl.ds(EDGE + k, 1), :] = t[0:1]

    first = jnp.where(piece == 0, 1.0 / 36.0, 0.0).astype(F32)
    last = jnp.where(piece == PIECES - 1, -1.0 / 36.0, 0.0).astype(F32)
    inv = CS["inv"]
    fh = [flux_weight(0, j) for j in range(NI)]
    ft = [flux_weight(NI - 1, j) for j in range(NI)]
    fh[0] = (fh[0] - BETA) + float(inv[0, 0]) * first
    ft[0] = ft[0] + float(inv[NI - 1, 0]) * first
    fh[NI - 1] = fh[NI - 1] + float(inv[0, NI - 1]) * last
    ft[NI - 1] = (ft[NI - 1] + BETA) + float(inv[NI - 1, NI - 1]) * last

    for i in range(NI):
        own[i] = spread(vh, i)
        own[NI + i] = spread(vt, i)

    s_in, s_out = (NI - 3) * (1 - core), (NI - 3) * core
    for v in range(NV):
        for c in loads[v]:
            c.wait()
        for out, half in ((mine, core), (send, 1 - core)):
            for r in range(HALF // SUB):
                rows = pl.ds(pl.multiple_of(HALF * half + SUB * r, SUB), SUB)
                sums = [None] * 4
                for i in range(NI):
                    a, z = s[v, i, rows, :], f[v, i, rows, :]
                    terms = (own[i] * a, own[NI + i] * a, fh[i] * z, ft[i] * z)
                    sums = [t if o is None else o + t for o, t in zip(sums, terms)]
                faces = [s[v, s_in + k, rows, :] for k in range(3)] + [s[v, s_out + k, rows, :] for k in range(3)]
                for k, t in enumerate(sums + faces):
                    out[pl.ds((NV * k + v) * HALF + SUB * r, SUB), :] = t
    inner_store.wait()


def own_share(gap, state, flux_x):
    vmem, hbm = pl.BlockSpec(memory_space=pltpu.VMEM), pl.BlockSpec(memory_space=pltpu.HBM)
    coef = jax.ShapeDtypeStruct((2 * NI, SUB, NK), F32)
    coef_far = jax.ShapeDtypeStruct((2 * NI + 3, SUB, NK), F32)
    values = jax.ShapeDtypeStruct((EDGE + 16, NK), F32)
    return pl.pallas_call(
        own_body,
        out_shape=(coef, coef_far, values, values),
        in_specs=[hbm, hbm, hbm],
        out_specs=(hbm, vmem, vmem, vmem),
        scratch_shapes=[
            pltpu.VMEM((2 * NI, SUB, NK), F32),
            pltpu.SMEM((NI,), F32),
            pltpu.VMEM((NV, NI, NJ, NK), F32),
            pltpu.VMEM((NV, NI, NJ, NK), F32),
            pltpu.VMEM((2 * NI, SUB, NK), F32),
            pltpu.SemaphoreType.DMA,
            pltpu.SemaphoreType.DMA,
            pltpu.SemaphoreType.DMA((2, NV)),
        ],
        compiler_params=pltpu.CompilerParams(vmem_limit_bytes=12 << 20),
        cost_estimate=pl.CostEstimate(flops=1 << 24, bytes_accessed=4 << 20, transcendentals=0),
        name="own_share",
    )(*in_hbm(gap, state, flux_x))


def pair_body(mine, got, out_hbm, mids, out, sem):
    is0 = parity("gx") == 0

    def both(rows):
        x, y = mine[rows, :], got[rows, :]
        return jnp.where(is0, x, y), jnp.where(is0, y, x)

    ca, cb = zip(*(both(pl.ds(EDGE + k, 1)) for k in range(16)))
    ca, cb = ([jnp.broadcast_to(t, (SUB, NK)) for t in c] for c in (ca, cb))
    hla, hra, tla, tra = ca[:4]
    hlb, hrb, tlb, trb = cb[:4]
    inv = 1.0 / (1.0 - tra * hlb)
    down = [hlb * tla * inv, hrb * inv, tla * inv, tra * hrb * inv, hlb * inv, inv, tra * inv]
    for k, t in enumerate(down):
        mids[pl.ds(4 * NV * HALF + k, 1), :] = t[0:1]
    cross_h, cross_t = hra * inv, tlb * inv
    edge = [hla + hra * down[0], hra * down[1], tlb * down[2], trb + tlb * down[3]]
    edge += [ca[10 + q] + (cross_h * hlb) * ca[13 + q] for q in range(3)]
    edge += [cross_t * ca[13 + q] for q in range(3)]
    edge += [cross_h * cb[10 + q] for q in range(3)]
    edge += [cb[13 + q] + (cross_t * tra) * cb[10 + q] for q in range(3)]
    lane = lax.broadcasted_iota(jnp.int32, (SUB, NK), 1)
    packed = jnp.zeros((SUB, NK), F32)
    for k, t in enumerate(edge):
        packed = jnp.where(lane == k, t, packed)

    k = CS["pair"]
    blocks = [pl.ds(WIDE * SUB * r, WIDE * SUB) for r in range(HALF // SUB)]
    stores = [pltpu.make_async_copy(out.at[b], out_hbm.at[b], sem.at[r]) for r, b in enumerate(blocks)]
    for r in range(HALF // SUB):
        at = WIDE * SUB * r
        out[pl.ds(at + VALUES * NV, SUB, stride=WIDE), :] = packed
        for v in range(NV):
            a, b = zip(*(both(pl.ds((NV * e + v) * HALF + SUB * r, SUB)) for e in range(VALUES)))
            ha, ta, hb, tb = a[0], a[1], b[0], b[1]
            for q in range(3):
                ha, ta = ha + ca[4 + q] * b[4 + q], ta + ca[7 + q] * b[4 + q]
                hb, tb = hb + cb[4 + q] * a[4 + q], tb + cb[7 + q] * a[4 + q]
            head = (hb + hlb * ta) * inv
            tail = (ta + tra * hb) * inv
            da, ea, db, eb = a[2], a[3], b[2], b[3]
            dhead = k["inv"] * db + k["inv_hl"] * ea
            dtail = k["inv"] * ea + k["inv_tr"] * db
            values = [ha + hra * head, tb + tlb * tail, da + float(CS["hr"]) * dhead, eb + float(CS["tl"]) * dtail]
            values += list(a[7:10]) + list(b[7:10])
            for e, t in enumerate(values):
                out[pl.ds(at + NV * e + v, SUB, stride=WIDE), :] = t
            for e, t in enumerate((head, tail, dhead, dtail)):
                mids[pl.ds((NV * e + v) * HALF + SUB * r, SUB), :] = t
        stores[r].start()
    for c in stores:
        c.wait()


def pair(mine, got):
    vmem = pl.BlockSpec(memory_space=pltpu.VMEM)
    return pl.pallas_call(
        pair_body,
        out_shape=(
            jax.ShapeDtypeStruct((PAIRS * WIDE, NK), F32),
            jax.ShapeDtypeStruct((4 * NV * HALF + SUB, NK), F32),
        ),
        in_specs=[vmem] * 2,
        out_specs=(pl.BlockSpec(memory_space=pltpu.HBM), vmem),
        scratch_shapes=[pltpu.VMEM((PAIRS * WIDE, NK), F32), pltpu.SemaphoreType.DMA((HALF // SUB,))],
        compiler_params=pltpu.CompilerParams(vmem_limit_bytes=8 << 20),
        cost_estimate=pl.CostEstimate(flops=1 << 20, bytes_accessed=1 << 20, transcendentals=0),
        name="pair",
    )(mine, got)


def join_body(x, out_hbm, out, coef, sem):
    for r in range(PAIRS // SUB):
        packed = x[pl.ds(WIDE * SUB * r + VALUES * NV, SUB, stride=WIDE), :]
        for k in range(16):
            coef[pl.ds(PAIRS * k + SUB * r, SUB), :] = jnp.broadcast_to(packed[:, k : k + 1], (SUB, NK))

    def row(p, k):
        return jnp.broadcast_to(coef[pl.ds(PAIRS * k + p, 1), :], (NV, NK))

    def value(p, k):
        return x[pl.ds(WIDE * p + NV * k, NV), :]

    c = CS["pair"]
    head_f, tail_f, head_d, tail_d = [], [], [], []
    for p in range(PAIRS):
        h, t, dh, dt = (value(p, k) for k in range(4))
        if p:
            for q in range(3):
                z = value(p - 1, 7 + q)
                h, t = h + row(p, 4 + q) * z, t + row(p, 7 + q) * z
        if p < PAIRS - 1:
            for q in range(3):
                z = value(p + 1, 4 + q)
                h, t = h + row(p, 10 + q) * z, t + row(p, 13 + q) * z
        head_f.append(h)
        tail_f.append(t)
        head_d.append(dh)
        tail_d.append(dt)

    scale = 8.0
    num, den = [None] * PAIRS, [None] * PAIRS
    hl, hr, tl, tr = ([row(p, k) for p in range(PAIRS)] for k in range(4))
    num[0], den[0] = tr[0], jnp.ones((NV, NK), F32)
    for p in range(1, PAIRS):
        cross = tl[p] * hr[p] - tr[p] * hl[p]
        num[p] = (scale * tr[p]) * den[p - 1] + (scale * cross) * num[p - 1]
        den[p] = scale * den[p - 1] - (scale * hl[p]) * num[p - 1]
    inv = [None] + [1.0 / den[p] for p in range(1, PAIRS)]
    e = [num[0]] + [num[p] * inv[p] for p in range(1, PAIRS)]
    keep = [None] + [(scale * den[p - 1]) * inv[p] for p in range(1, PAIRS)]

    fwd_f, fwd_d = [tail_f[0]], [tail_d[0]]
    chl, chr_, ctl, ce = c["hl"], c["hr"], c["tl"], c["e"]
    for p in range(1, PAIRS):
        a = tl[p] * keep[p]
        fwd_f.append((tail_f[p] + (a * e[p - 1]) * head_f[p]) + a * fwd_f[-1])
        k = ctl / (1.0 - chl * ce[p - 1])
        fwd_d.append((tail_d[p] + float(k * ce[p - 1]) * head_d[p]) + float(k) * fwd_d[-1])

    blocks = [pl.ds(ROWS * SUB * r, ROWS * SUB) for r in range(PAIRS // SUB)]
    stores = [pltpu.make_async_copy(out.at[b], out_hbm.at[b], sem.at[r]) for r, b in enumerate(blocks)]
    zero = jnp.zeros((NV, NK), F32)
    right_f, right_d = zero, zero
    for p in range(PAIRS - 1, -1, -1):
        if p:
            h = keep[p]
            at_f = (head_f[p] + hl[p] * fwd_f[p - 1]) * h + (hr[p] * h) * right_f
            left_f = fwd_f[p - 1] + e[p - 1] * at_f
            k = 1.0 / (1.0 - chl * ce[p - 1])
            at_d = (float(k) * head_d[p] + float(k * chl) * fwd_d[p - 1]) + float(k * chr_) * right_d
            left_d = fwd_d[p - 1] + float(ce[p - 1]) * at_d
        else:
            at_f = at_d = left_f = left_d = zero
        for k, val in enumerate((left_f, right_f, left_d, right_d)):
            out[pl.ds(ROWS * p + NV * k, NV), :] = val
        right_f, right_d = at_f, at_d
        if p % SUB == 0:
            stores[p // SUB].start()
    for t in stores:
        t.wait()


def join(x):
    vmem = pl.BlockSpec(memory_space=pltpu.VMEM)
    return pl.pallas_call(
        join_body,
        out_shape=jax.ShapeDtypeStruct((PAIRS * ROWS, NK), F32),
        in_specs=[vmem],
        out_specs=pl.BlockSpec(memory_space=pltpu.HBM),
        scratch_shapes=[
            pltpu.VMEM((PAIRS * ROWS, NK), F32),
            pltpu.VMEM((16 * PAIRS, NK), F32),
            pltpu.SemaphoreType.DMA((PAIRS // SUB,)),
        ],
        compiler_params=pltpu.CompilerParams(vmem_limit_bytes=8 << 20),
        cost_estimate=pl.CostEstimate(flops=1 << 20, bytes_accessed=1 << 20, transcendentals=0),
        name="join",
    )(x)


def far_body(outer, two, own, other):
    core = parity("gx")
    for out, half in ((own, core), (other, 1 - core)):
        for v in range(NV):
            for r in range(HALF // SUB):
                rows = pl.ds(pl.multiple_of(HALF * half + SUB * r, SUB), SUB)
                a = [two[v, k, rows, :] for k in range(3)]
                out[pl.ds(v * HALF + SUB * r, SUB), :] = (
                    outer[C_FAR] * a[0] + outer[C_FAR + 1] * a[1] + outer[C_FAR + 2] * a[2]
                )


def far(outer, two):
    vmem = pl.BlockSpec(memory_space=pltpu.VMEM)
    out = jax.ShapeDtypeStruct((NV * HALF, NK), F32)
    return pl.pallas_call(
        far_body,
        out_shape=(out, out),
        in_specs=[vmem] * 2,
        out_specs=(vmem,) * 2,
        compiler_params=pltpu.CompilerParams(vmem_limit_bytes=8 << 20),
        cost_estimate=pl.CostEstimate(flops=1 << 18, bytes_accessed=1 << 19, transcendentals=0),
        name="far",
    )(outer, two)


def split_body(z, mids, far_own, far_other, own, send):
    is0 = parity("gx") == 0
    c = CS["pair"]
    down = [jnp.broadcast_to(mids[pl.ds(4 * NV * HALF + k, 1), :], (SUB, NK)) for k in range(7)]
    head_far, tail_far = jnp.where(is0, down[4], down[5]), jnp.where(is0, down[5], down[6])
    for r in range(HALF // SUB):
        for v in range(NV):
            lf, rf, ld, rd = (z[pl.ds(ROWS * SUB * r + NV * k + v, SUB, stride=ROWS), :] for k in range(4))
            head, tail, dhead, dtail = (mids[pl.ds((NV * k + v) * HALF + SUB * r, SUB), :] for k in range(4))
            part = pl.ds(v * HALF + SUB * r, SUB)
            w = far_own[part, :]
            head = (head + head_far * w) + down[0] * lf + down[1] * rf
            tail = (tail + tail_far * w) + down[2] * lf + down[3] * rf
            dhead = dhead + c["down"][0] * ld + c["down"][1] * rd
            dtail = dtail + c["down"][2] * ld + c["down"][3] * rd
            a, b = (lf, head, ld, dhead), (tail, rf, dtail, rd)
            for k in range(4):
                rows = pl.ds((NV * k + v) * HALF + SUB * r, SUB)
                own[rows, :] = jnp.where(is0, a[k], b[k])
                send[rows, :] = jnp.where(is0, b[k], a[k])
            send[pl.ds((4 * NV + v) * HALF + SUB * r, SUB), :] = far_other[part, :]


def split(z, mids, far_own, far_other):
    vmem = pl.BlockSpec(memory_space=pltpu.VMEM)
    own = jax.ShapeDtypeStruct((4 * NV * HALF, NK), F32)
    send = jax.ShapeDtypeStruct((5 * NV * HALF, NK), F32)
    return pl.pallas_call(
        split_body,
        out_shape=(own, send),
        in_specs=[vmem] * 4,
        out_specs=(vmem,) * 2,
        compiler_params=pltpu.CompilerParams(vmem_limit_bytes=8 << 20),
        cost_estimate=pl.CostEstimate(flops=1 << 20, bytes_accessed=1 << 20, transcendentals=0),
        name="split",
    )(z, mids, far_own, far_other)


def block_body(inner_hbm, s_hbm, f_hbm, fy_hbm, one, two, yone, ytwo, mx, my, base, mxb, inner, s, f, fy, pad, inner_sem, sem):
    inner_load = pltpu.make_async_copy(inner_hbm, inner, inner_sem)
    inner_load.start()
    moves = ((fy_hbm, fy), (s_hbm, s), (f_hbm, f))
    for v in range(NV):
        for k, (h, t) in enumerate(moves):
            pltpu.make_async_copy(h.at[v], t.at[v], sem.at[k, v]).start()
    piece = lax.axis_index("gx")
    is0 = parity("gx") == 0
    even = parity("gy") == 0
    first = jnp.where(piece == 0, 1.0 / 36.0, 0.0).astype(F32)
    last = jnp.where(piece == PIECES - 1, -1.0 / 36.0, 0.0).astype(F32)
    mxt = jnp.transpose(mx[...] * -0.5)
    myt = jnp.transpose(my[...] * -0.5)
    for i in range(NI):
        mxb[i] = jnp.broadcast_to(mxt[:, i : i + 1], (NJ, NK))
        pad[NI + i, 0:NJ, :] = jnp.broadcast_to(myt[:, i : i + 1], (NJ, NK))

    inner_load.wait()

    @pl.loop(0, NV)
    def _(v):
        for k, (h, t) in enumerate(moves):
            pltpu.make_async_copy(h.at[v], t.at[v], sem.at[k, v]).wait()
        for i in range(NI):
            for q in range(NJ // SUB):
                pad[i, pl.ds(SUB + SUB * q, SUB), :] = fy[v, i, pl.ds(SUB * q, SUB), :]
            part = pl.ds(4 * (i % 2), 4)
            a, b = yone[v, i // 2, part, :], ytwo[v, i // 2, part, :]
            pad[i, SUB - 4 : SUB, :] = jnp.where(even, b, a)
            pad[i, SUB + NJ : SUB + NJ + 4, :] = jnp.where(even, a, b)

        for q in range(NJ // SUB):
            rows = pl.ds(SUB * q, SUB)
            a = [one[v, k, rows, :] for k in range(4)]
            b = [two[v, k, rows, :] for k in range(4)]
            low = [jnp.where(is0, b[k], a[k]) for k in range(4)]
            high = [jnp.where(is0, a[k], b[k]) for k in range(4)]
            st = low[:3] + [s[v, i, rows, :] for i in range(NI)] + high[:3]
            fl = [low[3]] + [f[v, i, rows, :] for i in range(NI)] + [high[3]]
            ye, yd, us = [], [], []
            for i in range(NI):
                d6 = (
                    (st[i] + st[i + 6])
                    - 6.0 * (st[i + 1] + st[i + 5])
                    + 15.0 * (st[i + 2] + st[i + 4])
                    - 20.0 * st[i + 3]
                )
                y = inner[C_MG + i] * d6
                ye.append(y - inner[C_C + i] * ye[-1] if i else y)
                u = fl[i + 2] - fl[i]
                us.append(u)
                r = fl[2] if i == 0 else -fl[NI - 1] if i == NI - 1 else u
                r = float(RHO * CS["m"][i]) * r
                if i == 0:
                    r = r + (first * float(CS["m"][i])) * fl[1]
                if i == NI - 1:
                    r = r + (last * float(CS["m"][i])) * fl[NI]
                yd.append(r - float(CS["c"][i]) * yd[-1] if i else r)
            xe = xd = None
            for i in range(NI - 1, -1, -1):
                xe = ye[i] if xe is None else ye[i] - inner[C_C + i] * xe
                xd = yd[i] if xd is None else yd[i] - float(CS["c"][i]) * xd
                at = SUB + SUB * q
                dy = None
                for k, w in enumerate(Y_WEIGHTS, start=1):
                    t = w * (pad[i, pl.ds(at + k, SUB), :] - pad[i, pl.ds(at - k, SUB), :])
                    dy = t if dy is None else dy + t
                d = us[i] * (1.0 / 12.0) + xd
                base[v, i, rows, :] = (st[i + 3] + xe) + (mxb[i, rows, :] * d + pad[NI + i, rows, :] * dy)


def block(inner, state, flux_x, flux_y, one, two, yone, ytwo, mx, my):
    vmem, hbm = pl.BlockSpec(memory_space=pltpu.VMEM), pl.BlockSpec(memory_space=pltpu.HBM)
    return pl.pallas_call(
        block_body,
        out_shape=(
            jax.ShapeDtypeStruct((NV, NI, NJ, NK), F32),
            jax.ShapeDtypeStruct((NI, NJ, NK), F32),
        ),
        in_specs=[hbm] * 4 + [vmem] * 6,
        out_specs=(vmem, vmem),
        scratch_shapes=[pltpu.VMEM((2 * NI, SUB, NK), F32)]
        + [pltpu.VMEM((NV, NI, NJ, NK), F32)] * 3
        + [pltpu.VMEM((2 * NI, SUB + NJ + SUB, NK), F32), pltpu.SemaphoreType.DMA, pltpu.SemaphoreType.DMA((3, NV))],
        compiler_params=pltpu.CompilerParams(vmem_limit_bytes=16 << 20),
        cost_estimate=pl.CostEstimate(flops=1 << 30, bytes_accessed=64 << 20, transcendentals=0),
        name="block",
    )(*in_hbm(inner, state, flux_x, flux_y), one, two, yone, ytwo, mx, my)


def finish_body(outer, base, mxb, own, got, mids, far_other, out_hbm, out, sem):
    core = parity("gx")
    is0 = core == 0
    hl_inv, inv, tr_inv = (jnp.broadcast_to(mids[pl.ds(4 * NV * HALF + k, 1), :], (SUB, NK)) for k in (4, 5, 6))
    zero = jnp.zeros((SUB, NK), F32)
    own_far = (jnp.where(is0, zero, inv), jnp.where(is0, inv, zero))
    got_far = (jnp.where(is0, zero, tr_inv), jnp.where(is0, hl_inv, zero))
    stores = [pltpu.make_async_copy(out.at[v], out_hbm.at[v], sem.at[v]) for v in range(NV)]
    for v in range(NV):
        for z, half, far_w, far_z, far_at in (
            (own, core, own_far, got, 4 * NV),
            (got, 1 - core, got_far, far_other, 0),
        ):
            for r in range(HALF // SUB):
                rows = pl.ds(pl.multiple_of(HALF * half + SUB * r, SUB), SUB)
                lf, rf, ld, rd = (z[pl.ds((NV * k + v) * HALF + SUB * r, SUB), :] for k in range(4))
                w = far_z[pl.ds((far_at + v) * HALF + SUB * r, SUB), :]
                lf, rf = lf + far_w[0] * w, rf + far_w[1] * w
                for i in range(NI):
                    d = float(CS["left"][i]) * ld + float(CS["right"][i]) * rd
                    e = outer[C_LEFT + i] * lf + outer[C_RIGHT + i] * rf
                    out[v, i, rows, :] = (base[v, i, rows, :] + e) + mxb[i, rows, :] * d
        stores[v].start()
    for c in stores:
        c.wait()


def finish(outer, base, mxb, own, got, mids, far_other):
    return pl.pallas_call(
        finish_body,
        out_shape=jax.ShapeDtypeStruct((NV, NI, NJ, NK), F32),
        in_specs=[pl.BlockSpec(memory_space=pltpu.VMEM)] * 7,
        out_specs=pl.BlockSpec(memory_space=pltpu.HBM),
        scratch_shapes=[pltpu.VMEM((NV, NI, NJ, NK), F32), pltpu.SemaphoreType.DMA((NV,))],
        compiler_params=pltpu.CompilerParams(vmem_limit_bytes=12 << 20),
        cost_estimate=pl.CostEstimate(flops=1 << 22, bytes_accessed=3 << 20, transcendentals=0),
        name="finish",
    )(outer, base, mxb, own, got, mids, far_other)


def exchange(x, rows):
    groups = [[2 * p + c for p in range(PAIRS)] for c in range(2)]
    y = lax.all_to_all(x.reshape(PAIRS, rows, NK), "gx", 0, 0, tiled=True, axis_index_groups=groups)
    return y.reshape(PAIRS * rows, NK)


def per_device(flux_x, flux_y, state, metric_x, metric_y, filter_gap):
    count_y = lax.axis_size("gy")
    pair_in = [(i, i ^ 1) for i in range(PIECES)]
    pair_out = [(i, i + 1 if i % 2 else i - 1) for i in range(1, PIECES - 1)]
    y_in = [(i, i ^ 1) for i in range(count_y)]
    y_out = [(i, (i + 1 if i % 2 else i - 1) % count_y) for i in range(count_y)]

    inner, outer, mine, send = own_share(filter_gap, state, flux_x)
    send, state, flux_x, flux_y = lax.optimization_barrier((send, state, flux_x, flux_y))
    got = lax.ppermute(send, "gx", pair_in)
    got, *faces = lax.optimization_barrier((got, *pack(state, flux_x, flux_y)))
    ends, mids = pair(mine, got)
    ends, send_one, send_two, ysend_one, ysend_two = lax.optimization_barrier((ends, *faces))
    ends = exchange(ends, WIDE)
    one = lax.ppermute(send_one, "gx", pair_in)
    two = lax.ppermute(send_two, "gx", pair_out)
    yone = lax.ppermute(ysend_one, "gy", y_in)
    ytwo = lax.ppermute(ysend_two, "gy", y_out)
    outside = join(ends)
    outside, one = lax.optimization_barrier((outside, one))
    two, yone, ytwo = lax.optimization_barrier((two, yone, ytwo))
    far_own, far_other = far(outer, two)
    base, mxb = block(inner, state, flux_x, flux_y, one, two, yone, ytwo, metric_x, metric_y)
    outside, base, mxb, far_own = lax.optimization_barrier((exchange(outside, ROWS), base, mxb, far_own))
    own, send = split(outside, mids, far_own, far_other)
    got = lax.ppermute(send, "gx", pair_in)
    return finish(outer, base, mxb, own, got, mids, far_other)


def solution(mesh):
    return jax.shard_map(
        per_device,
        mesh=mesh,
        in_specs=(
            P(None, "gx", "gy", None),
            P(None, "gx", "gy", None),
            P(None, "gx", "gy", None),
            P("gx", "gy"),
            P("gx", "gy"),
            P("gx"),
        ),
        out_specs=P(None, "gx", "gy", None),
        check_vma=False,
    )
```

```python
import jax
import jax.numpy as jnp
import numpy as np
from jax import lax
from jax.experimental import pallas as pl
from jax.experimental.pallas import tpu as pltpu
from jax.sharding import PartitionSpec as P

NV, NI, NJ, NK = 5, 16, 32, 128
PIECES, PAIRS, HALF = 32, 16, 16
VALUES = 10
ROWS, WIDE = 24, 56
EDGE = VALUES * NV * HALF
SUB = 8
F32 = jnp.float32
Y_WEIGHTS = (4.0 / 5.0, -1.0 / 5.0, 4.0 / 105.0, -1.0 / 280.0)
RHO = 25.0 / 36.0
BETA = 3.0 * RHO
D6 = (1.0, -6.0, 15.0, -20.0, 15.0, -6.0, 1.0)

C_C, C_MG = 0, NI
C_LEFT, C_RIGHT, C_FAR = 0, NI, 2 * NI


def constant_system():
    a = 1.0 / 3.0
    t = np.eye(NI) + a * (np.eye(NI, k=1) + np.eye(NI, k=-1))
    inv = np.linalg.inv(t)
    m, c = [], []
    prev = 0.0
    for _ in range(NI):
        m.append(1.0 / (1.0 - a * prev))
        prev = a * m[-1]
        c.append(prev)
    left, right = -a * inv[:, 0], -a * inv[:, -1]
    hl, hr, tl, tr = left[0], right[0], left[-1], right[-1]
    d = 1.0 / (1.0 - tr * hl)
    pair = dict(inv=d, inv_hl=d * hl, inv_tr=d * tr, down=[hl * tl * d, hr * d, tl * d, tr * hr * d])
    for k in pair:
        pair[k] = [float(t) for t in pair[k]] if isinstance(pair[k], list) else float(pair[k])
    p = dict(hl=hl + hr * hl * tl * d, hr=hr * hr * d, tl=tl * tl * d, tr=tr + tl * tr * hr * d)
    e = [p["tr"]]
    for _ in range(PAIRS - 1):
        e.append(p["tr"] + p["tl"] * p["hr"] * e[-1] / (1.0 - p["hl"] * e[-1]))
    pair.update(p, e=e)
    return dict(m=m, c=c, inv=inv, left=left, right=right, hl=hl, hr=hr, tl=tl, tr=tr, pair=pair)


CS = constant_system()


def flux_weight(row, j):
    w = CS["inv"][row]
    lo = w[j - 1] if 0 <= j - 1 < NI else 0.0
    hi = w[j + 1] if 0 <= j + 1 < NI else 0.0
    return float(RHO * (lo - hi))


def splat(x):
    return jnp.full((SUB, NK), x, F32)


def in_hbm(*arrays):
    return tuple(pltpu.with_memory_space_constraint(a, pltpu.HBM) for a in arrays)


def parity(name):
    return lax.rem(lax.axis_index(name), 2)


def pack_body(s, f, fy, one, two, yone, ytwo, lo, hi, sem):
    core, odd = parity("gx"), parity("gy")
    copies = [
        pltpu.make_async_copy(fy.at[:, :, 0:SUB, :], lo, sem.at[0]),
        pltpu.make_async_copy(fy.at[:, :, NJ - SUB : NJ, :], hi, sem.at[1]),
    ]
    for c in copies:
        c.start()

    def faces(right, left):
        moves = [
            pltpu.make_async_copy(s.at[:, NI - 3 : NI], right.at[:, 0:3], sem.at[2]),
            pltpu.make_async_copy(f.at[:, NI - 1 : NI], right.at[:, 3:4], sem.at[3]),
            pltpu.make_async_copy(s.at[:, 0:3], left.at[:, 0:3], sem.at[4]),
            pltpu.make_async_copy(f.at[:, 0:1], left.at[:, 3:4], sem.at[5]),
        ]
        for c in moves:
            c.start()
        for c in moves:
            c.wait()

    def rows(top, bottom):
        for v in range(NV):
            for i in range(NI):
                part = pl.ds(4 * (i % 2), 4)
                top[v, i // 2, part, :] = hi[v, i, 4:8, :]
                bottom[v, i // 2, part, :] = lo[v, i, 0:4, :]

    @pl.when(core == 0)
    def _():
        faces(one, two)

    @pl.when(core == 1)
    def _():
        faces(two, one)

    for c in copies:
        c.wait()

    @pl.when(odd == 0)
    def _():
        rows(yone, ytwo)

    @pl.when(odd == 1)
    def _():
        rows(ytwo, yone)


def pack(state, flux_x, flux_y):
    x_out = jax.ShapeDtypeStruct((NV, 4, NJ, NK), F32)
    y_out = jax.ShapeDtypeStruct((NV, NI // 2, SUB, NK), F32)
    return pl.pallas_call(
        pack_body,
        out_shape=(x_out, x_out, y_out, y_out),
        in_specs=[pl.BlockSpec(memory_space=pltpu.HBM)] * 3,
        out_specs=(pl.BlockSpec(memory_space=pltpu.VMEM),) * 4,
        scratch_shapes=[
            pltpu.VMEM((NV, NI, SUB, NK), F32),
            pltpu.VMEM((NV, NI, SUB, NK), F32),
            pltpu.SemaphoreType.DMA((6,)),
        ],
        compiler_params=pltpu.CompilerParams(vmem_limit_bytes=8 << 20),
        cost_estimate=pl.CostEstimate(flops=0, bytes_accessed=2 << 20, transcendentals=0),
        name="pack",
    )(*in_hbm(state, flux_x, flux_y))


def own_body(gap_hbm, s_hbm, f_hbm, inner, outer, mine, send, gap, s, f, own, gap_sem, sem):
    gap_load = pltpu.make_async_copy(gap_hbm, gap, gap_sem)
    gap_load.start()
    loads = [
        (
            pltpu.make_async_copy(s_hbm.at[v], s.at[v], sem.at[0, v]),
            pltpu.make_async_copy(f_hbm.at[v], f.at[v], sem.at[1, v]),
        )
        for v in range(NV)
    ]
    for both in loads:
        for c in both:
            c.start()
    core = parity("gx")
    piece = lax.axis_index("gx")
    gap_load.wait()
    alpha = [0.5 - splat(gap[i]) for i in range(NI)]
    g32 = [(0.5 - a) * (1.0 / 32.0) for a in alpha]
    m, c = [None] * NI, [None] * NI
    n, b = [None] * NI, [None] * NI
    for k in range(NI):
        m[k] = 1.0 / (1.0 - alpha[k] * c[k - 1]) if k else jnp.ones((SUB, NK), F32)
        c[k] = alpha[k] * m[k]
        r = NI - 1 - k
        n[r] = 1.0 / (1.0 - alpha[r] * b[r + 1]) if k else jnp.ones((SUB, NK), F32)
        b[r] = alpha[r] * n[r]
    left, right = [None] * NI, [None] * NI
    wh, wt = [None] * NI, [None] * NI
    left[0], right[NI - 1] = -b[0], -c[NI - 1]
    qh, qt = None, None
    for k in range(NI):
        r = NI - 1 - k
        if k:
            left[k] = -b[k] * left[k - 1]
            right[r] = -c[r] * right[r + 1]
            qh = -b[k - 1] if qh is None else -b[k - 1] * qh
            qt = -c[r + 1] if qt is None else -c[r + 1] * qt
            wh[k] = qh * n[k]
            wt[r] = qt * m[r]
        else:
            wh[0], wt[NI - 1] = n[0], m[NI - 1]
    for k in range(NI):
        inner[C_C + k] = c[k]
        inner[C_MG + k] = m[k] * g32[k]
        outer[C_LEFT + k] = left[k]
        outer[C_RIGHT + k] = right[k]
    vh = [wh[k] * g32[k] for k in range(NI)]
    vt = [wt[k] * g32[k] for k in range(NI)]

    def spread(v, j):
        terms = [D6[q + 3] * v[j - q] for q in range(-3, 4) if 0 <= j - q < NI]
        total = terms[0]
        for t in terms[1:]:
            total = total + t
        return total

    edge = [-alpha[0] * wh[0], -alpha[NI - 1] * wh[NI - 1], -alpha[0] * wt[0], -alpha[NI - 1] * wt[NI - 1]]
    low = [spread(v, q - 3) for v in (vh, vt) for q in range(3)]
    high = [spread(v, NI + q) for v in (vh, vt) for q in range(3)]
    edge += [jnp.where(core == 0, h, l) for h, l in zip(high, low)]
    edge += [jnp.where(core == 0, l, h) for h, l in zip(high, low)]
    for q in range(3):
        outer[C_FAR + q] = jnp.where(core == 0, edge[13 + q], edge[10 + q])
    for k, t in enumerate(edge):
        mine[pl.ds(EDGE + k, 1), :] = t[0:1]
        send[pl.ds(EDGE + k, 1), :] = t[0:1]

    first = jnp.where(piece == 0, 1.0 / 36.0, 0.0).astype(F32)
    last = jnp.where(piece == PIECES - 1, -1.0 / 36.0, 0.0).astype(F32)
    inv = CS["inv"]
    fh = [flux_weight(0, j) for j in range(NI)]
    ft = [flux_weight(NI - 1, j) for j in range(NI)]
    fh[0] = (fh[0] - BETA) + float(inv[0, 0]) * first
    ft[0] = ft[0] + float(inv[NI - 1, 0]) * first
    fh[NI - 1] = fh[NI - 1] + float(inv[0, NI - 1]) * last
    ft[NI - 1] = (ft[NI - 1] + BETA) + float(inv[NI - 1, NI - 1]) * last

    for i in range(NI):
        own[i] = spread(vh, i)
        own[NI + i] = spread(vt, i)

    s_in, s_out = (NI - 3) * (1 - core), (NI - 3) * core
    for v in range(NV):
        for c in loads[v]:
            c.wait()
        for out, half in ((mine, core), (send, 1 - core)):
            for r in range(HALF // SUB):
                rows = pl.ds(pl.multiple_of(HALF * half + SUB * r, SUB), SUB)
                sums = [None] * 4
                for i in range(NI):
                    a, z = s[v, i, rows, :], f[v, i, rows, :]
                    terms = (own[i] * a, own[NI + i] * a, fh[i] * z, ft[i] * z)
                    sums = [t if o is None else o + t for o, t in zip(sums, terms)]
                faces = [s[v, s_in + k, rows, :] for k in range(3)] + [s[v, s_out + k, rows, :] for k in range(3)]
                for k, t in enumerate(sums + faces):
                    out[pl.ds((NV * k + v) * HALF + SUB * r, SUB), :] = t


def own_share(gap, state, flux_x):
    vmem, hbm = pl.BlockSpec(memory_space=pltpu.VMEM), pl.BlockSpec(memory_space=pltpu.HBM)
    coef = jax.ShapeDtypeStruct((2 * NI, SUB, NK), F32)
    coef_far = jax.ShapeDtypeStruct((2 * NI + 3, SUB, NK), F32)
    values = jax.ShapeDtypeStruct((EDGE + 16, NK), F32)
    return pl.pallas_call(
        own_body,
        out_shape=(coef, coef_far, values, values),
        in_specs=[hbm, hbm, hbm],
        out_specs=(vmem,) * 4,
        scratch_shapes=[
            pltpu.SMEM((NI,), F32),
            pltpu.VMEM((NV, NI, NJ, NK), F32),
            pltpu.VMEM((NV, NI, NJ, NK), F32),
            pltpu.VMEM((2 * NI, SUB, NK), F32),
            pltpu.SemaphoreType.DMA,
            pltpu.SemaphoreType.DMA((2, NV)),
        ],
        compiler_params=pltpu.CompilerParams(vmem_limit_bytes=12 << 20),
        cost_estimate=pl.CostEstimate(flops=1 << 24, bytes_accessed=4 << 20, transcendentals=0),
        name="own_share",
    )(*in_hbm(gap, state, flux_x))


def pair_body(mine, got, out_hbm, mids, out, sem):
    is0 = parity("gx") == 0

    def both(rows):
        x, y = mine[rows, :], got[rows, :]
        return jnp.where(is0, x, y), jnp.where(is0, y, x)

    ca, cb = zip(*(both(pl.ds(EDGE + k, 1)) for k in range(16)))
    ca, cb = ([jnp.broadcast_to(t, (SUB, NK)) for t in c] for c in (ca, cb))
    hla, hra, tla, tra = ca[:4]
    hlb, hrb, tlb, trb = cb[:4]
    inv = 1.0 / (1.0 - tra * hlb)
    down = [hlb * tla * inv, hrb * inv, tla * inv, tra * hrb * inv, hlb * inv, inv, tra * inv]
    for k, t in enumerate(down):
        mids[pl.ds(4 * NV * HALF + k, 1), :] = t[0:1]
    cross_h, cross_t = hra * inv, tlb * inv
    edge = [hla + hra * down[0], hra * down[1], tlb * down[2], trb + tlb * down[3]]
    edge += [ca[10 + q] + (cross_h * hlb) * ca[13 + q] for q in range(3)]
    edge += [cross_t * ca[13 + q] for q in range(3)]
    edge += [cross_h * cb[10 + q] for q in range(3)]
    edge += [cb[13 + q] + (cross_t * tra) * cb[10 + q] for q in range(3)]
    lane = lax.broadcasted_iota(jnp.int32, (SUB, NK), 1)
    packed = jnp.zeros((SUB, NK), F32)
    for k, t in enumerate(edge):
        packed = jnp.where(lane == k, t, packed)

    k = CS["pair"]
    blocks = [pl.ds(WIDE * SUB * r, WIDE * SUB) for r in range(HALF // SUB)]
    stores = [pltpu.make_async_copy(out.at[b], out_hbm.at[b], sem.at[r]) for r, b in enumerate(blocks)]
    for r in range(HALF // SUB):
        at = WIDE * SUB * r
        out[pl.ds(at + VALUES * NV, SUB, stride=WIDE), :] = packed
        for v in range(NV):
            a, b = zip(*(both(pl.ds((NV * e + v) * HALF + SUB * r, SUB)) for e in range(VALUES)))
            ha, ta, hb, tb = a[0], a[1], b[0], b[1]
            for q in range(3):
                ha, ta = ha + ca[4 + q] * b[4 + q], ta + ca[7 + q] * b[4 + q]
                hb, tb = hb + cb[4 + q] * a[4 + q], tb + cb[7 + q] * a[4 + q]
            head = (hb + hlb * ta) * inv
            tail = (ta + tra * hb) * inv
            da, ea, db, eb = a[2], a[3], b[2], b[3]
            dhead = k["inv"] * db + k["inv_hl"] * ea
            dtail = k["inv"] * ea + k["inv_tr"] * db
            values = [ha + hra * head, tb + tlb * tail, da + float(CS["hr"]) * dhead, eb + float(CS["tl"]) * dtail]
            values += list(a[7:10]) + list(b[7:10])
            for e, t in enumerate(values):
                out[pl.ds(at + NV * e + v, SUB, stride=WIDE), :] = t
            for e, t in enumerate((head, tail, dhead, dtail)):
                mids[pl.ds((NV * e + v) * HALF + SUB * r, SUB), :] = t
        stores[r].start()
    for c in stores:
        c.wait()


def pair(mine, got):
    vmem = pl.BlockSpec(memory_space=pltpu.VMEM)
    return pl.pallas_call(
        pair_body,
        out_shape=(
            jax.ShapeDtypeStruct((PAIRS * WIDE, NK), F32),
            jax.ShapeDtypeStruct((4 * NV * HALF + SUB, NK), F32),
        ),
        in_specs=[vmem] * 2,
        out_specs=(pl.BlockSpec(memory_space=pltpu.HBM), vmem),
        scratch_shapes=[pltpu.VMEM((PAIRS * WIDE, NK), F32), pltpu.SemaphoreType.DMA((HALF // SUB,))],
        compiler_params=pltpu.CompilerParams(vmem_limit_bytes=8 << 20),
        cost_estimate=pl.CostEstimate(flops=1 << 20, bytes_accessed=1 << 20, transcendentals=0),
        name="pair",
    )(mine, got)


def join_body(x, out_hbm, out, coef, sem):
    for r in range(PAIRS // SUB):
        packed = x[pl.ds(WIDE * SUB * r + VALUES * NV, SUB, stride=WIDE), :]
        for k in range(16):
            coef[pl.ds(PAIRS * k + SUB * r, SUB), :] = jnp.broadcast_to(packed[:, k : k + 1], (SUB, NK))

    def row(p, k):
        return jnp.broadcast_to(coef[pl.ds(PAIRS * k + p, 1), :], (NV, NK))

    def value(p, k):
        return x[pl.ds(WIDE * p + NV * k, NV), :]

    c = CS["pair"]
    head_f, tail_f, head_d, tail_d = [], [], [], []
    for p in range(PAIRS):
        h, t, dh, dt = (value(p, k) for k in range(4))
        if p:
            for q in range(3):
                z = value(p - 1, 7 + q)
                h, t = h + row(p, 4 + q) * z, t + row(p, 7 + q) * z
        if p < PAIRS - 1:
            for q in range(3):
                z = value(p + 1, 4 + q)
                h, t = h + row(p, 10 + q) * z, t + row(p, 13 + q) * z
        head_f.append(h)
        tail_f.append(t)
        head_d.append(dh)
        tail_d.append(dt)

    scale = 8.0
    num, den = [None] * PAIRS, [None] * PAIRS
    hl, hr, tl, tr = ([row(p, k) for p in range(PAIRS)] for k in range(4))
    num[0], den[0] = tr[0], jnp.ones((NV, NK), F32)
    for p in range(1, PAIRS):
        cross = tl[p] * hr[p] - tr[p] * hl[p]
        num[p] = (scale * tr[p]) * den[p - 1] + (scale * cross) * num[p - 1]
        den[p] = scale * den[p - 1] - (scale * hl[p]) * num[p - 1]
    inv = [None] + [1.0 / den[p] for p in range(1, PAIRS)]
    e = [num[0]] + [num[p] * inv[p] for p in range(1, PAIRS)]
    keep = [None] + [(scale * den[p - 1]) * inv[p] for p in range(1, PAIRS)]

    fwd_f, fwd_d = [tail_f[0]], [tail_d[0]]
    chl, chr_, ctl, ce = c["hl"], c["hr"], c["tl"], c["e"]
    for p in range(1, PAIRS):
        a = tl[p] * keep[p]
        fwd_f.append((tail_f[p] + (a * e[p - 1]) * head_f[p]) + a * fwd_f[-1])
        k = ctl / (1.0 - chl * ce[p - 1])
        fwd_d.append((tail_d[p] + float(k * ce[p - 1]) * head_d[p]) + float(k) * fwd_d[-1])

    blocks = [pl.ds(ROWS * SUB * r, ROWS * SUB) for r in range(PAIRS // SUB)]
    stores = [pltpu.make_async_copy(out.at[b], out_hbm.at[b], sem.at[r]) for r, b in enumerate(blocks)]
    zero = jnp.zeros((NV, NK), F32)
    right_f, right_d = zero, zero
    for p in range(PAIRS - 1, -1, -1):
        if p:
            h = keep[p]
            at_f = (head_f[p] + hl[p] * fwd_f[p - 1]) * h + (hr[p] * h) * right_f
            left_f = fwd_f[p - 1] + e[p - 1] * at_f
            k = 1.0 / (1.0 - chl * ce[p - 1])
            at_d = (float(k) * head_d[p] + float(k * chl) * fwd_d[p - 1]) + float(k * chr_) * right_d
            left_d = fwd_d[p - 1] + float(ce[p - 1]) * at_d
        else:
            at_f = at_d = left_f = left_d = zero
        for k, val in enumerate((left_f, right_f, left_d, right_d)):
            out[pl.ds(ROWS * p + NV * k, NV), :] = val
        right_f, right_d = at_f, at_d
        if p % SUB == 0:
            stores[p // SUB].start()
    for t in stores:
        t.wait()


def join(x):
    vmem = pl.BlockSpec(memory_space=pltpu.VMEM)
    return pl.pallas_call(
        join_body,
        out_shape=jax.ShapeDtypeStruct((PAIRS * ROWS, NK), F32),
        in_specs=[vmem],
        out_specs=pl.BlockSpec(memory_space=pltpu.HBM),
        scratch_shapes=[
            pltpu.VMEM((PAIRS * ROWS, NK), F32),
            pltpu.VMEM((16 * PAIRS, NK), F32),
            pltpu.SemaphoreType.DMA((PAIRS // SUB,)),
        ],
        compiler_params=pltpu.CompilerParams(vmem_limit_bytes=8 << 20),
        cost_estimate=pl.CostEstimate(flops=1 << 20, bytes_accessed=1 << 20, transcendentals=0),
        name="join",
    )(x)


def far_body(outer, two, own, other):
    core = parity("gx")
    for out, half in ((own, core), (other, 1 - core)):
        for v in range(NV):
            for r in range(HALF // SUB):
                rows = pl.ds(pl.multiple_of(HALF * half + SUB * r, SUB), SUB)
                a = [two[v, k, rows, :] for k in range(3)]
                out[pl.ds(v * HALF + SUB * r, SUB), :] = (
                    outer[C_FAR] * a[0] + outer[C_FAR + 1] * a[1] + outer[C_FAR + 2] * a[2]
                )


def far(outer, two):
    vmem = pl.BlockSpec(memory_space=pltpu.VMEM)
    out = jax.ShapeDtypeStruct((NV * HALF, NK), F32)
    return pl.pallas_call(
        far_body,
        out_shape=(out, out),
        in_specs=[vmem] * 2,
        out_specs=(vmem,) * 2,
        compiler_params=pltpu.CompilerParams(vmem_limit_bytes=8 << 20),
        cost_estimate=pl.CostEstimate(flops=1 << 18, bytes_accessed=1 << 19, transcendentals=0),
        name="far",
    )(outer, two)


def split_body(z, mids, far_own, far_other, own, send):
    is0 = parity("gx") == 0
    c = CS["pair"]
    down = [jnp.broadcast_to(mids[pl.ds(4 * NV * HALF + k, 1), :], (SUB, NK)) for k in range(7)]
    head_far, tail_far = jnp.where(is0, down[4], down[5]), jnp.where(is0, down[5], down[6])
    for r in range(HALF // SUB):
        for v in range(NV):
            lf, rf, ld, rd = (z[pl.ds(ROWS * SUB * r + NV * k + v, SUB, stride=ROWS), :] for k in range(4))
            head, tail, dhead, dtail = (mids[pl.ds((NV * k + v) * HALF + SUB * r, SUB), :] for k in range(4))
            part = pl.ds(v * HALF + SUB * r, SUB)
            w = far_own[part, :]
            head = (head + head_far * w) + down[0] * lf + down[1] * rf
            tail = (tail + tail_far * w) + down[2] * lf + down[3] * rf
            dhead = dhead + c["down"][0] * ld + c["down"][1] * rd
            dtail = dtail + c["down"][2] * ld + c["down"][3] * rd
            a, b = (lf, head, ld, dhead), (tail, rf, dtail, rd)
            for k in range(4):
                rows = pl.ds((NV * k + v) * HALF + SUB * r, SUB)
                own[rows, :] = jnp.where(is0, a[k], b[k])
                send[rows, :] = jnp.where(is0, b[k], a[k])
            send[pl.ds((4 * NV + v) * HALF + SUB * r, SUB), :] = far_other[part, :]


def split(z, mids, far_own, far_other):
    vmem = pl.BlockSpec(memory_space=pltpu.VMEM)
    own = jax.ShapeDtypeStruct((4 * NV * HALF, NK), F32)
    send = jax.ShapeDtypeStruct((5 * NV * HALF, NK), F32)
    return pl.pallas_call(
        split_body,
        out_shape=(own, send),
        in_specs=[vmem] * 4,
        out_specs=(vmem,) * 2,
        compiler_params=pltpu.CompilerParams(vmem_limit_bytes=8 << 20),
        cost_estimate=pl.CostEstimate(flops=1 << 20, bytes_accessed=1 << 20, transcendentals=0),
        name="split",
    )(z, mids, far_own, far_other)


def block_body(inner, s_hbm, f_hbm, fy_hbm, one, two, yone, ytwo, mx, my, base, mxb, s, f, fy, pad, sem):
    moves = ((fy_hbm, fy), (s_hbm, s), (f_hbm, f))
    for v in range(NV):
        for k, (h, t) in enumerate(moves):
            pltpu.make_async_copy(h.at[v], t.at[v], sem.at[k, v]).start()
    piece = lax.axis_index("gx")
    is0 = parity("gx") == 0
    even = parity("gy") == 0
    first = jnp.where(piece == 0, 1.0 / 36.0, 0.0).astype(F32)
    last = jnp.where(piece == PIECES - 1, -1.0 / 36.0, 0.0).astype(F32)
    mxt = jnp.transpose(mx[...] * -0.5)
    myt = jnp.transpose(my[...] * -0.5)
    for i in range(NI):
        mxb[i] = jnp.broadcast_to(mxt[:, i : i + 1], (NJ, NK))
        pad[NI + i, 0:NJ, :] = jnp.broadcast_to(myt[:, i : i + 1], (NJ, NK))

    @pl.loop(0, NV)
    def _(v):
        for k, (h, t) in enumerate(moves):
            pltpu.make_async_copy(h.at[v], t.at[v], sem.at[k, v]).wait()
        for i in range(NI):
            for q in range(NJ // SUB):
                pad[i, pl.ds(SUB + SUB * q, SUB), :] = fy[v, i, pl.ds(SUB * q, SUB), :]
            part = pl.ds(4 * (i % 2), 4)
            a, b = yone[v, i // 2, part, :], ytwo[v, i // 2, part, :]
            pad[i, SUB - 4 : SUB, :] = jnp.where(even, b, a)
            pad[i, SUB + NJ : SUB + NJ + 4, :] = jnp.where(even, a, b)

        for q in range(NJ // SUB):
            rows = pl.ds(SUB * q, SUB)
            a = [one[v, k, rows, :] for k in range(4)]
            b = [two[v, k, rows, :] for k in range(4)]
            low = [jnp.where(is0, b[k], a[k]) for k in range(4)]
            high = [jnp.where(is0, a[k], b[k]) for k in range(4)]
            st = low[:3] + [s[v, i, rows, :] for i in range(NI)] + high[:3]
            fl = [low[3]] + [f[v, i, rows, :] for i in range(NI)] + [high[3]]
            ye, yd, us = [], [], []
            for i in range(NI):
                d6 = (
                    (st[i] + st[i + 6])
                    - 6.0 * (st[i + 1] + st[i + 5])
                    + 15.0 * (st[i + 2] + st[i + 4])
                    - 20.0 * st[i + 3]
                )
                y = inner[C_MG + i] * d6
                ye.append(y - inner[C_C + i] * ye[-1] if i else y)
                u = fl[i + 2] - fl[i]
                us.append(u)
                r = fl[2] if i == 0 else -fl[NI - 1] if i == NI - 1 else u
                r = float(RHO * CS["m"][i]) * r
                if i == 0:
                    r = r + (first * float(CS["m"][i])) * fl[1]
                if i == NI - 1:
                    r = r + (last * float(CS["m"][i])) * fl[NI]
                yd.append(r - float(CS["c"][i]) * yd[-1] if i else r)
            xe = xd = None
            for i in range(NI - 1, -1, -1):
                xe = ye[i] if xe is None else ye[i] - inner[C_C + i] * xe
                xd = yd[i] if xd is None else yd[i] - float(CS["c"][i]) * xd
                at = SUB + SUB * q
                dy = None
                for k, w in enumerate(Y_WEIGHTS, start=1):
                    t = w * (pad[i, pl.ds(at + k, SUB), :] - pad[i, pl.ds(at - k, SUB), :])
                    dy = t if dy is None else dy + t
                d = us[i] * (1.0 / 12.0) + xd
                base[v, i, rows, :] = (st[i + 3] + xe) + (mxb[i, rows, :] * d + pad[NI + i, rows, :] * dy)


def block(inner, state, flux_x, flux_y, one, two, yone, ytwo, mx, my):
    vmem, hbm = pl.BlockSpec(memory_space=pltpu.VMEM), pl.BlockSpec(memory_space=pltpu.HBM)
    return pl.pallas_call(
        block_body,
        out_shape=(
            jax.ShapeDtypeStruct((NV, NI, NJ, NK), F32),
            jax.ShapeDtypeStruct((NI, NJ, NK), F32),
        ),
        in_specs=[vmem] + [hbm] * 3 + [vmem] * 6,
        out_specs=(vmem, vmem),
        scratch_shapes=[pltpu.VMEM((NV, NI, NJ, NK), F32)] * 3
        + [pltpu.VMEM((2 * NI, SUB + NJ + SUB, NK), F32), pltpu.SemaphoreType.DMA((3, NV))],
        compiler_params=pltpu.CompilerParams(vmem_limit_bytes=16 << 20),
        cost_estimate=pl.CostEstimate(flops=1 << 30, bytes_accessed=64 << 20, transcendentals=0),
        name="block",
    )(inner, *in_hbm(state, flux_x, flux_y), one, two, yone, ytwo, mx, my)


def finish_body(outer, base, mxb, own, got, mids, far_other, out_hbm, out, sem):
    core = parity("gx")
    is0 = core == 0
    hl_inv, inv, tr_inv = (jnp.broadcast_to(mids[pl.ds(4 * NV * HALF + k, 1), :], (SUB, NK)) for k in (4, 5, 6))
    zero = jnp.zeros((SUB, NK), F32)
    own_far = (jnp.where(is0, zero, inv), jnp.where(is0, inv, zero))
    got_far = (jnp.where(is0, zero, tr_inv), jnp.where(is0, hl_inv, zero))
    stores = [pltpu.make_async_copy(out.at[v], out_hbm.at[v], sem.at[v]) for v in range(NV)]
    for v in range(NV):
        for z, half, far_w, far_z, far_at in (
            (own, core, own_far, got, 4 * NV),
            (got, 1 - core, got_far, far_other, 0),
        ):
            for r in range(HALF // SUB):
                rows = pl.ds(pl.multiple_of(HALF * half + SUB * r, SUB), SUB)
                lf, rf, ld, rd = (z[pl.ds((NV * k + v) * HALF + SUB * r, SUB), :] for k in range(4))
                w = far_z[pl.ds((far_at + v) * HALF + SUB * r, SUB), :]
                lf, rf = lf + far_w[0] * w, rf + far_w[1] * w
                for i in range(NI):
                    d = float(CS["left"][i]) * ld + float(CS["right"][i]) * rd
                    e = outer[C_LEFT + i] * lf + outer[C_RIGHT + i] * rf
                    out[v, i, rows, :] = (base[v, i, rows, :] + e) + mxb[i, rows, :] * d
        stores[v].start()
    for c in stores:
        c.wait()


def finish(outer, base, mxb, own, got, mids, far_other):
    return pl.pallas_call(
        finish_body,
        out_shape=jax.ShapeDtypeStruct((NV, NI, NJ, NK), F32),
        in_specs=[pl.BlockSpec(memory_space=pltpu.VMEM)] * 7,
        out_specs=pl.BlockSpec(memory_space=pltpu.HBM),
        scratch_shapes=[pltpu.VMEM((NV, NI, NJ, NK), F32), pltpu.SemaphoreType.DMA((NV,))],
        compiler_params=pltpu.CompilerParams(vmem_limit_bytes=12 << 20),
        cost_estimate=pl.CostEstimate(flops=1 << 22, bytes_accessed=3 << 20, transcendentals=0),
        name="finish",
    )(outer, base, mxb, own, got, mids, far_other)


def exchange(x, rows):
    groups = [[2 * p + c for p in range(PAIRS)] for c in range(2)]
    y = lax.all_to_all(x.reshape(PAIRS, rows, NK), "gx", 0, 0, tiled=True, axis_index_groups=groups)
    return y.reshape(PAIRS * rows, NK)


def per_device(flux_x, flux_y, state, metric_x, metric_y, filter_gap):
    count_y = lax.axis_size("gy")
    pair_in = [(i, i ^ 1) for i in range(PIECES)]
    pair_out = [(i, i + 1 if i % 2 else i - 1) for i in range(1, PIECES - 1)]
    y_in = [(i, i ^ 1) for i in range(count_y)]
    y_out = [(i, (i + 1 if i % 2 else i - 1) % count_y) for i in range(count_y)]

    inner, outer, mine, send = own_share(filter_gap, state, flux_x)
    send, state, flux_x, flux_y = lax.optimization_barrier((send, state, flux_x, flux_y))
    got = lax.ppermute(send, "gx", pair_in)
    got, *faces = lax.optimization_barrier((got, *pack(state, flux_x, flux_y)))
    ends, mids = pair(mine, got)
    ends, send_one, send_two, ysend_one, ysend_two = lax.optimization_barrier((ends, *faces))
    ends = exchange(ends, WIDE)
    one = lax.ppermute(send_one, "gx", pair_in)
    two = lax.ppermute(send_two, "gx", pair_out)
    yone = lax.ppermute(ysend_one, "gy", y_in)
    ytwo = lax.ppermute(ysend_two, "gy", y_out)
    outside = join(ends)
    outside, one = lax.optimization_barrier((outside, one))
    two, yone, ytwo = lax.optimization_barrier((two, yone, ytwo))
    far_own, far_other = far(outer, two)
    base, mxb = block(inner, state, flux_x, flux_y, one, two, yone, ytwo, metric_x, metric_y)
    outside, base, mxb, far_own = lax.optimization_barrier((exchange(outside, ROWS), base, mxb, far_own))
    own, send = split(outside, mids, far_own, far_other)
    got = lax.ppermute(send, "gx", pair_in)
    return finish(outer, base, mxb, own, got, mids, far_other)


def solution(mesh):
    return jax.shard_map(
        per_device,
        mesh=mesh,
        in_specs=(
            P(None, "gx", "gy", None),
            P(None, "gx", "gy", None),
            P(None, "gx", "gy", None),
            P("gx", "gy"),
            P("gx", "gy"),
            P("gx"),
        ),
        out_specs=P(None, "gx", "gy", None),
        check_vma=False,
    )
```

```python
import jax
import jax.numpy as jnp
import numpy as np
from jax import lax
from jax.experimental import pallas as pl
from jax.experimental.pallas import tpu as pltpu
from jax.sharding import PartitionSpec as P

NV, NI, NJ, NK = 5, 16, 32, 128
PIECES, PAIRS, HALF = 32, 16, 16
VALUES = 10
ROWS, WIDE = 24, 56
EDGE = VALUES * NV * HALF
SUB = 8
F32 = jnp.float32
Y_WEIGHTS = (4.0 / 5.0, -1.0 / 5.0, 4.0 / 105.0, -1.0 / 280.0)
RHO = 25.0 / 36.0
BETA = 3.0 * RHO
D6 = (1.0, -6.0, 15.0, -20.0, 15.0, -6.0, 1.0)

C_C, C_MG = 0, NI
C_LEFT, C_RIGHT, C_FAR = 0, NI, 2 * NI


def constant_system():
    a = 1.0 / 3.0
    t = np.eye(NI) + a * (np.eye(NI, k=1) + np.eye(NI, k=-1))
    inv = np.linalg.inv(t)
    m, c = [], []
    prev = 0.0
    for _ in range(NI):
        m.append(1.0 / (1.0 - a * prev))
        prev = a * m[-1]
        c.append(prev)
    left, right = -a * inv[:, 0], -a * inv[:, -1]
    hl, hr, tl, tr = left[0], right[0], left[-1], right[-1]
    d = 1.0 / (1.0 - tr * hl)
    pair = dict(inv=d, inv_hl=d * hl, inv_tr=d * tr, down=[hl * tl * d, hr * d, tl * d, tr * hr * d])
    for k in pair:
        pair[k] = [float(t) for t in pair[k]] if isinstance(pair[k], list) else float(pair[k])
    p = dict(hl=hl + hr * hl * tl * d, hr=hr * hr * d, tl=tl * tl * d, tr=tr + tl * tr * hr * d)
    e = [p["tr"]]
    for _ in range(PAIRS - 1):
        e.append(p["tr"] + p["tl"] * p["hr"] * e[-1] / (1.0 - p["hl"] * e[-1]))
    pair.update(p, e=e)
    return dict(m=m, c=c, inv=inv, left=left, right=right, hl=hl, hr=hr, tl=tl, tr=tr, pair=pair)


CS = constant_system()


def flux_weight(row, j):
    w = CS["inv"][row]
    lo = w[j - 1] if 0 <= j - 1 < NI else 0.0
    hi = w[j + 1] if 0 <= j + 1 < NI else 0.0
    return float(RHO * (lo - hi))


def splat(x):
    return jnp.full((SUB, NK), x, F32)


def in_hbm(*arrays):
    return tuple(pltpu.with_memory_space_constraint(a, pltpu.HBM) for a in arrays)


def parity(name):
    return lax.rem(lax.axis_index(name), 2)


def pack_body(s, f, fy, one, two, yone, ytwo, lo, hi, sem):
    core, odd = parity("gx"), parity("gy")
    copies = [
        pltpu.make_async_copy(fy.at[:, :, 0:SUB, :], lo, sem.at[0]),
        pltpu.make_async_copy(fy.at[:, :, NJ - SUB : NJ, :], hi, sem.at[1]),
    ]
    for c in copies:
        c.start()

    def faces(right, left):
        moves = [
            pltpu.make_async_copy(s.at[:, NI - 3 : NI], right.at[:, 0:3], sem.at[2]),
            pltpu.make_async_copy(f.at[:, NI - 1 : NI], right.at[:, 3:4], sem.at[3]),
            pltpu.make_async_copy(s.at[:, 0:3], left.at[:, 0:3], sem.at[4]),
            pltpu.make_async_copy(f.at[:, 0:1], left.at[:, 3:4], sem.at[5]),
        ]
        for c in moves:
            c.start()
        for c in moves:
            c.wait()

    def rows(top, bottom):
        for v in range(NV):
            for i in range(NI):
                part = pl.ds(4 * (i % 2), 4)
                top[v, i // 2, part, :] = hi[v, i, 4:8, :]
                bottom[v, i // 2, part, :] = lo[v, i, 0:4, :]

    @pl.when(core == 0)
    def _():
        faces(one, two)

    @pl.when(core == 1)
    def _():
        faces(two, one)

    for c in copies:
        c.wait()

    @pl.when(odd == 0)
    def _():
        rows(yone, ytwo)

    @pl.when(odd == 1)
    def _():
        rows(ytwo, yone)


def pack(state, flux_x, flux_y):
    x_out = jax.ShapeDtypeStruct((NV, 4, NJ, NK), F32)
    y_out = jax.ShapeDtypeStruct((NV, NI // 2, SUB, NK), F32)
    return pl.pallas_call(
        pack_body,
        out_shape=(x_out, x_out, y_out, y_out),
        in_specs=[pl.BlockSpec(memory_space=pltpu.HBM)] * 3,
        out_specs=(pl.BlockSpec(memory_space=pltpu.VMEM),) * 4,
        scratch_shapes=[
            pltpu.VMEM((NV, NI, SUB, NK), F32),
            pltpu.VMEM((NV, NI, SUB, NK), F32),
            pltpu.SemaphoreType.DMA((6,)),
        ],
        compiler_params=pltpu.CompilerParams(vmem_limit_bytes=8 << 20),
        cost_estimate=pl.CostEstimate(flops=0, bytes_accessed=2 << 20, transcendentals=0),
        name="pack",
    )(*in_hbm(state, flux_x, flux_y))


def own_body(gap_hbm, s_hbm, f_hbm, inner, outer, mine, send, gap, s, f, own, gap_sem, sem):
    gap_load = pltpu.make_async_copy(gap_hbm, gap, gap_sem)
    gap_load.start()
    loads = [
        (
            pltpu.make_async_copy(s_hbm.at[v], s.at[v], sem.at[0, v]),
            pltpu.make_async_copy(f_hbm.at[v], f.at[v], sem.at[1, v]),
        )
        for v in range(NV)
    ]
    for both in loads:
        for c in both:
            c.start()
    core = parity("gx")
    piece = lax.axis_index("gx")
    gap_load.wait()
    alpha = [0.5 - splat(gap[i]) for i in range(NI)]
    g32 = [(0.5 - a) * (1.0 / 32.0) for a in alpha]
    m, c = [None] * NI, [None] * NI
    n, b = [None] * NI, [None] * NI
    for k in range(NI):
        m[k] = 1.0 / (1.0 - alpha[k] * c[k - 1]) if k else jnp.ones((SUB, NK), F32)
        c[k] = alpha[k] * m[k]
        r = NI - 1 - k
        n[r] = 1.0 / (1.0 - alpha[r] * b[r + 1]) if k else jnp.ones((SUB, NK), F32)
        b[r] = alpha[r] * n[r]
    left, right = [None] * NI, [None] * NI
    wh, wt = [None] * NI, [None] * NI
    left[0], right[NI - 1] = -b[0], -c[NI - 1]
    qh, qt = None, None
    for k in range(NI):
        r = NI - 1 - k
        if k:
            left[k] = -b[k] * left[k - 1]
            right[r] = -c[r] * right[r + 1]
            qh = -b[k - 1] if qh is None else -b[k - 1] * qh
            qt = -c[r + 1] if qt is None else -c[r + 1] * qt
            wh[k] = qh * n[k]
            wt[r] = qt * m[r]
        else:
            wh[0], wt[NI - 1] = n[0], m[NI - 1]
    for k in range(NI):
        inner[C_C + k] = c[k]
        inner[C_MG + k] = m[k] * g32[k]
        outer[C_LEFT + k] = left[k]
        outer[C_RIGHT + k] = right[k]
    vh = [wh[k] * g32[k] for k in range(NI)]
    vt = [wt[k] * g32[k] for k in range(NI)]

    def spread(v, j):
        terms = [D6[q + 3] * v[j - q] for q in range(-3, 4) if 0 <= j - q < NI]
        total = terms[0]
        for t in terms[1:]:
            total = total + t
        return total

    edge = [-alpha[0] * wh[0], -alpha[NI - 1] * wh[NI - 1], -alpha[0] * wt[0], -alpha[NI - 1] * wt[NI - 1]]
    low = [spread(v, q - 3) for v in (vh, vt) for q in range(3)]
    high = [spread(v, NI + q) for v in (vh, vt) for q in range(3)]
    edge += [jnp.where(core == 0, h, l) for h, l in zip(high, low)]
    edge += [jnp.where(core == 0, l, h) for h, l in zip(high, low)]
    for q in range(3):
        outer[C_FAR + q] = jnp.where(core == 0, edge[13 + q], edge[10 + q])
    for k, t in enumerate(edge):
        mine[pl.ds(EDGE + k, 1), :] = t[0:1]
        send[pl.ds(EDGE + k, 1), :] = t[0:1]

    first = jnp.where(piece == 0, 1.0 / 36.0, 0.0).astype(F32)
    last = jnp.where(piece == PIECES - 1, -1.0 / 36.0, 0.0).astype(F32)
    inv = CS["inv"]
    fh = [flux_weight(0, j) for j in range(NI)]
    ft = [flux_weight(NI - 1, j) for j in range(NI)]
    fh[0] = (fh[0] - BETA) + float(inv[0, 0]) * first
    ft[0] = ft[0] + float(inv[NI - 1, 0]) * first
    fh[NI - 1] = fh[NI - 1] + float(inv[0, NI - 1]) * last
    ft[NI - 1] = (ft[NI - 1] + BETA) + float(inv[NI - 1, NI - 1]) * last

    for i in range(NI):
        own[i] = spread(vh, i)
        own[NI + i] = spread(vt, i)

    s_in, s_out = (NI - 3) * (1 - core), (NI - 3) * core
    for v in range(NV):
        for c in loads[v]:
            c.wait()
        for out, half in ((mine, core), (send, 1 - core)):
            for r in range(HALF // SUB):
                rows = pl.ds(pl.multiple_of(HALF * half + SUB * r, SUB), SUB)
                sums = [None] * 4
                for i in range(NI):
                    a, z = s[v, i, rows, :], f[v, i, rows, :]
                    terms = (own[i] * a, own[NI + i] * a, fh[i] * z, ft[i] * z)
                    sums = [t if o is None else o + t for o, t in zip(sums, terms)]
                faces = [s[v, s_in + k, rows, :] for k in range(3)] + [s[v, s_out + k, rows, :] for k in range(3)]
                for k, t in enumerate(sums + faces):
                    out[pl.ds((NV * k + v) * HALF + SUB * r, SUB), :] = t


def own_share(gap, state, flux_x):
    vmem, hbm = pl.BlockSpec(memory_space=pltpu.VMEM), pl.BlockSpec(memory_space=pltpu.HBM)
    coef = jax.ShapeDtypeStruct((2 * NI, SUB, NK), F32)
    coef_far = jax.ShapeDtypeStruct((2 * NI + 3, SUB, NK), F32)
    values = jax.ShapeDtypeStruct((EDGE + 16, NK), F32)
    return pl.pallas_call(
        own_body,
        out_shape=(coef, coef_far, values, values),
        in_specs=[hbm, hbm, hbm],
        out_specs=(vmem,) * 4,
        scratch_shapes=[
            pltpu.SMEM((NI,), F32),
            pltpu.VMEM((NV, NI, NJ, NK), F32),
            pltpu.VMEM((NV, NI, NJ, NK), F32),
            pltpu.VMEM((2 * NI, SUB, NK), F32),
            pltpu.SemaphoreType.DMA,
            pltpu.SemaphoreType.DMA((2, NV)),
        ],
        compiler_params=pltpu.CompilerParams(vmem_limit_bytes=12 << 20),
        cost_estimate=pl.CostEstimate(flops=1 << 24, bytes_accessed=4 << 20, transcendentals=0),
        name="own_share",
    )(*in_hbm(gap, state, flux_x))


def pair_body(mine, got, out_hbm, mids, out, sem):
    is0 = parity("gx") == 0

    def both(rows):
        x, y = mine[rows, :], got[rows, :]
        return jnp.where(is0, x, y), jnp.where(is0, y, x)

    ca, cb = zip(*(both(pl.ds(EDGE + k, 1)) for k in range(16)))
    ca, cb = ([jnp.broadcast_to(t, (SUB, NK)) for t in c] for c in (ca, cb))
    hla, hra, tla, tra = ca[:4]
    hlb, hrb, tlb, trb = cb[:4]
    inv = 1.0 / (1.0 - tra * hlb)
    down = [hlb * tla * inv, hrb * inv, tla * inv, tra * hrb * inv, hlb * inv, inv, tra * inv]
    for k, t in enumerate(down):
        mids[pl.ds(4 * NV * HALF + k, 1), :] = t[0:1]
    cross_h, cross_t = hra * inv, tlb * inv
    edge = [hla + hra * down[0], hra * down[1], tlb * down[2], trb + tlb * down[3]]
    edge += [ca[10 + q] + (cross_h * hlb) * ca[13 + q] for q in range(3)]
    edge += [cross_t * ca[13 + q] for q in range(3)]
    edge += [cross_h * cb[10 + q] for q in range(3)]
    edge += [cb[13 + q] + (cross_t * tra) * cb[10 + q] for q in range(3)]
    lane = lax.broadcasted_iota(jnp.int32, (SUB, NK), 1)
    packed = jnp.zeros((SUB, NK), F32)
    for k, t in enumerate(edge):
        packed = jnp.where(lane == k, t, packed)

    k = CS["pair"]
    blocks = [pl.ds(WIDE * SUB * r, WIDE * SUB) for r in range(HALF // SUB)]
    stores = [pltpu.make_async_copy(out.at[b], out_hbm.at[b], sem.at[r]) for r, b in enumerate(blocks)]
    for r in range(HALF // SUB):
        at = WIDE * SUB * r
        out[pl.ds(at + VALUES * NV, SUB, stride=WIDE), :] = packed
        for v in range(NV):
            a, b = zip(*(both(pl.ds((NV * e + v) * HALF + SUB * r, SUB)) for e in range(VALUES)))
            ha, ta, hb, tb = a[0], a[1], b[0], b[1]
            for q in range(3):
                ha, ta = ha + ca[4 + q] * b[4 + q], ta + ca[7 + q] * b[4 + q]
                hb, tb = hb + cb[4 + q] * a[4 + q], tb + cb[7 + q] * a[4 + q]
            head = (hb + hlb * ta) * inv
            tail = (ta + tra * hb) * inv
            da, ea, db, eb = a[2], a[3], b[2], b[3]
            dhead = k["inv"] * db + k["inv_hl"] * ea
            dtail = k["inv"] * ea + k["inv_tr"] * db
            values = [ha + hra * head, tb + tlb * tail, da + float(CS["hr"]) * dhead, eb + float(CS["tl"]) * dtail]
            values += list(a[7:10]) + list(b[7:10])
            for e, t in enumerate(values):
                out[pl.ds(at + NV * e + v, SUB, stride=WIDE), :] = t
            for e, t in enumerate((head, tail, dhead, dtail)):
                mids[pl.ds((NV * e + v) * HALF + SUB * r, SUB), :] = t
        stores[r].start()
    for c in stores:
        c.wait()


def pair(mine, got):
    vmem = pl.BlockSpec(memory_space=pltpu.VMEM)
    return pl.pallas_call(
        pair_body,
        out_shape=(
            jax.ShapeDtypeStruct((PAIRS * WIDE, NK), F32),
            jax.ShapeDtypeStruct((4 * NV * HALF + SUB, NK), F32),
        ),
        in_specs=[vmem] * 2,
        out_specs=(pl.BlockSpec(memory_space=pltpu.HBM), vmem),
        scratch_shapes=[pltpu.VMEM((PAIRS * WIDE, NK), F32), pltpu.SemaphoreType.DMA((HALF // SUB,))],
        compiler_params=pltpu.CompilerParams(vmem_limit_bytes=8 << 20),
        cost_estimate=pl.CostEstimate(flops=1 << 20, bytes_accessed=1 << 20, transcendentals=0),
        name="pair",
    )(mine, got)


def join_body(x, out_hbm, out, coef, sem):
    for r in range(PAIRS // SUB):
        packed = x[pl.ds(WIDE * SUB * r + VALUES * NV, SUB, stride=WIDE), :]
        for k in range(16):
            coef[pl.ds(PAIRS * k + SUB * r, SUB), :] = jnp.broadcast_to(packed[:, k : k + 1], (SUB, NK))

    def row(p, k):
        return jnp.broadcast_to(coef[pl.ds(PAIRS * k + p, 1), :], (NV, NK))

    def value(p, k):
        return x[pl.ds(WIDE * p + NV * k, NV), :]

    c = CS["pair"]
    head_f, tail_f, head_d, tail_d = [], [], [], []
    for p in range(PAIRS):
        h, t, dh, dt = (value(p, k) for k in range(4))
        if p:
            for q in range(3):
                z = value(p - 1, 7 + q)
                h, t = h + row(p, 4 + q) * z, t + row(p, 7 + q) * z
        if p < PAIRS - 1:
            for q in range(3):
                z = value(p + 1, 4 + q)
                h, t = h + row(p, 10 + q) * z, t + row(p, 13 + q) * z
        head_f.append(h)
        tail_f.append(t)
        head_d.append(dh)
        tail_d.append(dt)

    scale = 8.0
    num, den = [None] * PAIRS, [None] * PAIRS
    hl, hr, tl, tr = ([row(p, k) for p in range(PAIRS)] for k in range(4))
    num[0], den[0] = tr[0], jnp.ones((NV, NK), F32)
    for p in range(1, PAIRS):
        cross = tl[p] * hr[p] - tr[p] * hl[p]
        num[p] = (scale * tr[p]) * den[p - 1] + (scale * cross) * num[p - 1]
        den[p] = scale * den[p - 1] - (scale * hl[p]) * num[p - 1]
    inv = [None] + [1.0 / den[p] for p in range(1, PAIRS)]
    e = [num[0]] + [num[p] * inv[p] for p in range(1, PAIRS)]
    keep = [None] + [(scale * den[p - 1]) * inv[p] for p in range(1, PAIRS)]

    fwd_f, fwd_d = [tail_f[0]], [tail_d[0]]
    chl, chr_, ctl, ce = c["hl"], c["hr"], c["tl"], c["e"]
    for p in range(1, PAIRS):
        a = tl[p] * keep[p]
        fwd_f.append((tail_f[p] + (a * e[p - 1]) * head_f[p]) + a * fwd_f[-1])
        k = ctl / (1.0 - chl * ce[p - 1])
        fwd_d.append((tail_d[p] + float(k * ce[p - 1]) * head_d[p]) + float(k) * fwd_d[-1])

    blocks = [pl.ds(ROWS * SUB * r, ROWS * SUB) for r in range(PAIRS // SUB)]
    stores = [pltpu.make_async_copy(out.at[b], out_hbm.at[b], sem.at[r]) for r, b in enumerate(blocks)]
    zero = jnp.zeros((NV, NK), F32)
    right_f, right_d = zero, zero
    for p in range(PAIRS - 1, -1, -1):
        if p:
            h = keep[p]
            at_f = (head_f[p] + hl[p] * fwd_f[p - 1]) * h + (hr[p] * h) * right_f
            left_f = fwd_f[p - 1] + e[p - 1] * at_f
            k = 1.0 / (1.0 - chl * ce[p - 1])
            at_d = (float(k) * head_d[p] + float(k * chl) * fwd_d[p - 1]) + float(k * chr_) * right_d
            left_d = fwd_d[p - 1] + float(ce[p - 1]) * at_d
        else:
            at_f = at_d = left_f = left_d = zero
        for k, val in enumerate((left_f, right_f, left_d, right_d)):
            out[pl.ds(ROWS * p + NV * k, NV), :] = val
        right_f, right_d = at_f, at_d
        if p % SUB == 0:
            stores[p // SUB].start()
    for t in stores:
        t.wait()


def join(x):
    vmem = pl.BlockSpec(memory_space=pltpu.VMEM)
    return pl.pallas_call(
        join_body,
        out_shape=jax.ShapeDtypeStruct((PAIRS * ROWS, NK), F32),
        in_specs=[vmem],
        out_specs=pl.BlockSpec(memory_space=pltpu.HBM),
        scratch_shapes=[
            pltpu.VMEM((PAIRS * ROWS, NK), F32),
            pltpu.VMEM((16 * PAIRS, NK), F32),
            pltpu.SemaphoreType.DMA((PAIRS // SUB,)),
        ],
        compiler_params=pltpu.CompilerParams(vmem_limit_bytes=8 << 20),
        cost_estimate=pl.CostEstimate(flops=1 << 20, bytes_accessed=1 << 20, transcendentals=0),
        name="join",
    )(x)


def far_body(outer, two, own, other):
    core = parity("gx")
    for out, half in ((own, core), (other, 1 - core)):
        for v in range(NV):
            for r in range(HALF // SUB):
                rows = pl.ds(pl.multiple_of(HALF * half + SUB * r, SUB), SUB)
                a = [two[v, k, rows, :] for k in range(3)]
                out[pl.ds(v * HALF + SUB * r, SUB), :] = (
                    outer[C_FAR] * a[0] + outer[C_FAR + 1] * a[1] + outer[C_FAR + 2] * a[2]
                )


def far(outer, two):
    vmem = pl.BlockSpec(memory_space=pltpu.VMEM)
    out = jax.ShapeDtypeStruct((NV * HALF, NK), F32)
    return pl.pallas_call(
        far_body,
        out_shape=(out, out),
        in_specs=[vmem] * 2,
        out_specs=(vmem,) * 2,
        compiler_params=pltpu.CompilerParams(vmem_limit_bytes=8 << 20),
        cost_estimate=pl.CostEstimate(flops=1 << 18, bytes_accessed=1 << 19, transcendentals=0),
        name="far",
    )(outer, two)


def split_body(z, mids, far_own, far_other, own, send):
    is0 = parity("gx") == 0
    c = CS["pair"]
    down = [jnp.broadcast_to(mids[pl.ds(4 * NV * HALF + k, 1), :], (SUB, NK)) for k in range(7)]
    head_far, tail_far = jnp.where(is0, down[4], down[5]), jnp.where(is0, down[5], down[6])
    for r in range(HALF // SUB):
        for v in range(NV):
            lf, rf, ld, rd = (z[pl.ds(ROWS * SUB * r + NV * k + v, SUB, stride=ROWS), :] for k in range(4))
            head, tail, dhead, dtail = (mids[pl.ds((NV * k + v) * HALF + SUB * r, SUB), :] for k in range(4))
            part = pl.ds(v * HALF + SUB * r, SUB)
            w = far_own[part, :]
            head = (head + head_far * w) + down[0] * lf + down[1] * rf
            tail = (tail + tail_far * w) + down[2] * lf + down[3] * rf
            dhead = dhead + c["down"][0] * ld + c["down"][1] * rd
            dtail = dtail + c["down"][2] * ld + c["down"][3] * rd
            a, b = (lf, head, ld, dhead), (tail, rf, dtail, rd)
            for k in range(4):
                rows = pl.ds((NV * k + v) * HALF + SUB * r, SUB)
                own[rows, :] = jnp.where(is0, a[k], b[k])
                send[rows, :] = jnp.where(is0, b[k], a[k])
            send[pl.ds((4 * NV + v) * HALF + SUB * r, SUB), :] = far_other[part, :]


def split(z, mids, far_own, far_other):
    vmem = pl.BlockSpec(memory_space=pltpu.VMEM)
    own = jax.ShapeDtypeStruct((4 * NV * HALF, NK), F32)
    send = jax.ShapeDtypeStruct((5 * NV * HALF, NK), F32)
    return pl.pallas_call(
        split_body,
        out_shape=(own, send),
        in_specs=[vmem] * 4,
        out_specs=(vmem,) * 2,
        compiler_params=pltpu.CompilerParams(vmem_limit_bytes=8 << 20),
        cost_estimate=pl.CostEstimate(flops=1 << 20, bytes_accessed=1 << 20, transcendentals=0),
        name="split",
    )(z, mids, far_own, far_other)


def block_body(inner, s_hbm, f_hbm, one, two, mx, base, mxb, s, f, sem):
    moves = ((s_hbm, s), (f_hbm, f))
    for v in range(NV):
        for k, (h, t) in enumerate(moves):
            pltpu.make_async_copy(h.at[v], t.at[v], sem.at[k, v]).start()
    piece = lax.axis_index("gx")
    is0 = parity("gx") == 0
    first = jnp.where(piece == 0, 1.0 / 36.0, 0.0).astype(F32)
    last = jnp.where(piece == PIECES - 1, -1.0 / 36.0, 0.0).astype(F32)
    mxt = jnp.transpose(mx[...] * -0.5)
    for i in range(NI):
        mxb[i] = jnp.broadcast_to(mxt[:, i : i + 1], (NJ, NK))

    @pl.loop(0, NV)
    def _(v):
        for k, (h, t) in enumerate(moves):
            pltpu.make_async_copy(h.at[v], t.at[v], sem.at[k, v]).wait()
        for q in range(NJ // SUB):
            rows = pl.ds(SUB * q, SUB)
            a = [one[v, k, rows, :] for k in range(4)]
            b = [two[v, k, rows, :] for k in range(4)]
            low = [jnp.where(is0, b[k], a[k]) for k in range(4)]
            high = [jnp.where(is0, a[k], b[k]) for k in range(4)]
            st = low[:3] + [s[v, i, rows, :] for i in range(NI)] + high[:3]
            fl = [low[3]] + [f[v, i, rows, :] for i in range(NI)] + [high[3]]
            ye, yd, us = [], [], []
            for i in range(NI):
                d6 = (
                    (st[i] + st[i + 6])
                    - 6.0 * (st[i + 1] + st[i + 5])
                    + 15.0 * (st[i + 2] + st[i + 4])
                    - 20.0 * st[i + 3]
                )
                y = inner[C_MG + i] * d6
                ye.append(y - inner[C_C + i] * ye[-1] if i else y)
                u = fl[i + 2] - fl[i]
                us.append(u)
                r = fl[2] if i == 0 else -fl[NI - 1] if i == NI - 1 else u
                r = float(RHO * CS["m"][i]) * r
                if i == 0:
                    r = r + (first * float(CS["m"][i])) * fl[1]
                if i == NI - 1:
                    r = r + (last * float(CS["m"][i])) * fl[NI]
                yd.append(r - float(CS["c"][i]) * yd[-1] if i else r)
            xe = xd = None
            for i in range(NI - 1, -1, -1):
                xe = ye[i] if xe is None else ye[i] - inner[C_C + i] * xe
                xd = yd[i] if xd is None else yd[i] - float(CS["c"][i]) * xd
                d = us[i] * (1.0 / 12.0) + xd
                base[v, i, rows, :] = (st[i + 3] + xe) + mxb[i, rows, :] * d


def block(inner, state, flux_x, one, two, mx):
    vmem, hbm = pl.BlockSpec(memory_space=pltpu.VMEM), pl.BlockSpec(memory_space=pltpu.HBM)
    return pl.pallas_call(
        block_body,
        out_shape=(
            jax.ShapeDtypeStruct((NV, NI, NJ, NK), F32),
            jax.ShapeDtypeStruct((NI, NJ, NK), F32),
        ),
        in_specs=[vmem, hbm, hbm] + [vmem] * 3,
        out_specs=(vmem, vmem),
        scratch_shapes=[pltpu.VMEM((NV, NI, NJ, NK), F32)] * 2 + [pltpu.SemaphoreType.DMA((2, NV))],
        compiler_params=pltpu.CompilerParams(vmem_limit_bytes=16 << 20),
        cost_estimate=pl.CostEstimate(flops=1 << 25, bytes_accessed=8 << 20, transcendentals=0),
        name="block",
    )(inner, *in_hbm(state, flux_x), one, two, mx)


def ydiff_body(base, fy_hbm, yone, ytwo, my, out, fy, myb, pad, sem):
    for v in range(NV):
        pltpu.make_async_copy(fy_hbm.at[v], fy.at[v], sem.at[v]).start()
    even = parity("gy") == 0
    myt = jnp.transpose(my[...] * -0.5)
    for i in range(NI):
        myb[i] = jnp.broadcast_to(myt[:, i : i + 1], (NJ, NK))

    @pl.loop(0, NV)
    def _(v):
        pltpu.make_async_copy(fy_hbm.at[v], fy.at[v], sem.at[v]).wait()
        for i in range(NI):
            for q in range(NJ // SUB):
                pad[i, pl.ds(SUB + SUB * q, SUB), :] = fy[v, i, pl.ds(SUB * q, SUB), :]
            part = pl.ds(4 * (i % 2), 4)
            a, b = yone[v, i // 2, part, :], ytwo[v, i // 2, part, :]
            pad[i, SUB - 4 : SUB, :] = jnp.where(even, b, a)
            pad[i, SUB + NJ : SUB + NJ + 4, :] = jnp.where(even, a, b)
        for i in range(NI):
            for q in range(NJ // SUB):
                rows, at = pl.ds(SUB * q, SUB), SUB + SUB * q
                dy = None
                for k, w in enumerate(Y_WEIGHTS, start=1):
                    t = w * (pad[i, pl.ds(at + k, SUB), :] - pad[i, pl.ds(at - k, SUB), :])
                    dy = t if dy is None else dy + t
                out[v, i, rows, :] = base[v, i, rows, :] + myb[i, rows, :] * dy


def ydiff(base, flux_y, yone, ytwo, my):
    vmem, hbm = pl.BlockSpec(memory_space=pltpu.VMEM), pl.BlockSpec(memory_space=pltpu.HBM)
    return pl.pallas_call(
        ydiff_body,
        out_shape=jax.ShapeDtypeStruct((NV, NI, NJ, NK), F32),
        in_specs=[vmem, hbm] + [vmem] * 3,
        out_specs=vmem,
        scratch_shapes=[
            pltpu.VMEM((NV, NI, NJ, NK), F32),
            pltpu.VMEM((NI, NJ, NK), F32),
            pltpu.VMEM((NI, SUB + NJ + SUB, NK), F32),
            pltpu.SemaphoreType.DMA((NV,)),
        ],
        input_output_aliases={0: 0},
        compiler_params=pltpu.CompilerParams(vmem_limit_bytes=16 << 20),
        cost_estimate=pl.CostEstimate(flops=1 << 25, bytes_accessed=4 << 20, transcendentals=0),
        name="ydiff",
    )(base, *in_hbm(flux_y), yone, ytwo, my)


def finish_body(outer, base, mxb, own, got, mids, far_other, out_hbm, out, sem):
    core = parity("gx")
    is0 = core == 0
    hl_inv, inv, tr_inv = (jnp.broadcast_to(mids[pl.ds(4 * NV * HALF + k, 1), :], (SUB, NK)) for k in (4, 5, 6))
    zero = jnp.zeros((SUB, NK), F32)
    own_far = (jnp.where(is0, zero, inv), jnp.where(is0, inv, zero))
    got_far = (jnp.where(is0, zero, tr_inv), jnp.where(is0, hl_inv, zero))
    stores = [pltpu.make_async_copy(out.at[v], out_hbm.at[v], sem.at[v]) for v in range(NV)]
    for v in range(NV):
        for z, half, far_w, far_z, far_at in (
            (own, core, own_far, got, 4 * NV),
            (got, 1 - core, got_far, far_other, 0),
        ):
            for r in range(HALF // SUB):
                rows = pl.ds(pl.multiple_of(HALF * half + SUB * r, SUB), SUB)
                lf, rf, ld, rd = (z[pl.ds((NV * k + v) * HALF + SUB * r, SUB), :] for k in range(4))
                w = far_z[pl.ds((far_at + v) * HALF + SUB * r, SUB), :]
                lf, rf = lf + far_w[0] * w, rf + far_w[1] * w
                for i in range(NI):
                    d = float(CS["left"][i]) * ld + float(CS["right"][i]) * rd
                    e = outer[C_LEFT + i] * lf + outer[C_RIGHT + i] * rf
                    out[v, i, rows, :] = (base[v, i, rows, :] + e) + mxb[i, rows, :] * d
        stores[v].start()
    for c in stores:
        c.wait()


def finish(outer, base, mxb, own, got, mids, far_other):
    return pl.pallas_call(
        finish_body,
        out_shape=jax.ShapeDtypeStruct((NV, NI, NJ, NK), F32),
        in_specs=[pl.BlockSpec(memory_space=pltpu.VMEM)] * 7,
        out_specs=pl.BlockSpec(memory_space=pltpu.HBM),
        scratch_shapes=[pltpu.VMEM((NV, NI, NJ, NK), F32), pltpu.SemaphoreType.DMA((NV,))],
        compiler_params=pltpu.CompilerParams(vmem_limit_bytes=12 << 20),
        cost_estimate=pl.CostEstimate(flops=1 << 22, bytes_accessed=3 << 20, transcendentals=0),
        name="finish",
    )(outer, base, mxb, own, got, mids, far_other)


def exchange(x, rows):
    groups = [[2 * p + c for p in range(PAIRS)] for c in range(2)]
    y = lax.all_to_all(x.reshape(PAIRS, rows, NK), "gx", 0, 0, tiled=True, axis_index_groups=groups)
    return y.reshape(PAIRS * rows, NK)


def per_device(flux_x, flux_y, state, metric_x, metric_y, filter_gap):
    count_y = lax.axis_size("gy")
    pair_in = [(i, i ^ 1) for i in range(PIECES)]
    pair_out = [(i, i + 1 if i % 2 else i - 1) for i in range(1, PIECES - 1)]
    y_in = [(i, i ^ 1) for i in range(count_y)]
    y_out = [(i, (i + 1 if i % 2 else i - 1) % count_y) for i in range(count_y)]

    inner, outer, mine, send = own_share(filter_gap, state, flux_x)
    send, state, flux_x, flux_y = lax.optimization_barrier((send, state, flux_x, flux_y))
    got = lax.ppermute(send, "gx", pair_in)
    got, *faces = lax.optimization_barrier((got, *pack(state, flux_x, flux_y)))
    ends, mids = pair(mine, got)
    ends, send_one, send_two, ysend_one, ysend_two = lax.optimization_barrier((ends, *faces))
    ends = exchange(ends, WIDE)
    one = lax.ppermute(send_one, "gx", pair_in)
    two = lax.ppermute(send_two, "gx", pair_out)
    yone = lax.ppermute(ysend_one, "gy", y_in)
    ytwo = lax.ppermute(ysend_two, "gy", y_out)
    outside = join(ends)
    outside, one = lax.optimization_barrier((outside, one))
    far_own, far_other = far(outer, two)
    base, mxb = block(inner, state, flux_x, one, two, metric_x)
    base = ydiff(base, flux_y, yone, ytwo, metric_y)
    outside, base, mxb, far_own = lax.optimization_barrier((exchange(outside, ROWS), base, mxb, far_own))
    own, send = split(outside, mids, far_own, far_other)
    got = lax.ppermute(send, "gx", pair_in)
    return finish(outer, base, mxb, own, got, mids, far_other)


def solution(mesh):
    return jax.shard_map(
        per_device,
        mesh=mesh,
        in_specs=(
            P(None, "gx", "gy", None),
            P(None, "gx", "gy", None),
            P(None, "gx", "gy", None),
            P("gx", "gy"),
            P("gx", "gy"),
            P("gx"),
        ),
        out_specs=P(None, "gx", "gy", None),
        check_vma=False,
    )
```

```python
import jax
import jax.numpy as jnp
import numpy as np
from jax import lax
from jax.experimental import pallas as pl
from jax.experimental.pallas import tpu as pltpu
from jax.sharding import PartitionSpec as P

NV, NI, NJ, NK = 5, 16, 32, 128
PIECES, PAIRS, HALF = 32, 16, 16
VALUES = 10
ROWS, WIDE = 24, 56
EDGE = VALUES * NV * HALF
SUB = 8
F32 = jnp.float32
Y_WEIGHTS = (4.0 / 5.0, -1.0 / 5.0, 4.0 / 105.0, -1.0 / 280.0)
RHO = 25.0 / 36.0
BETA = 3.0 * RHO
D6 = (1.0, -6.0, 15.0, -20.0, 15.0, -6.0, 1.0)

C_C, C_MG = 0, NI
C_LEFT, C_RIGHT, C_FAR = 0, NI, 2 * NI


def constant_system():
    a = 1.0 / 3.0
    t = np.eye(NI) + a * (np.eye(NI, k=1) + np.eye(NI, k=-1))
    inv = np.linalg.inv(t)
    m, c = [], []
    prev = 0.0
    for _ in range(NI):
        m.append(1.0 / (1.0 - a * prev))
        prev = a * m[-1]
        c.append(prev)
    left, right = -a * inv[:, 0], -a * inv[:, -1]
    hl, hr, tl, tr = left[0], right[0], left[-1], right[-1]
    d = 1.0 / (1.0 - tr * hl)
    pair = dict(inv=d, inv_hl=d * hl, inv_tr=d * tr, down=[hl * tl * d, hr * d, tl * d, tr * hr * d])
    for k in pair:
        pair[k] = [float(t) for t in pair[k]] if isinstance(pair[k], list) else float(pair[k])
    p = dict(hl=hl + hr * hl * tl * d, hr=hr * hr * d, tl=tl * tl * d, tr=tr + tl * tr * hr * d)
    e = [p["tr"]]
    for _ in range(PAIRS - 1):
        e.append(p["tr"] + p["tl"] * p["hr"] * e[-1] / (1.0 - p["hl"] * e[-1]))
    pair.update(p, e=e)
    return dict(m=m, c=c, inv=inv, left=left, right=right, hl=hl, hr=hr, tl=tl, tr=tr, pair=pair)


CS = constant_system()


def flux_weight(row, j):
    w = CS["inv"][row]
    lo = w[j - 1] if 0 <= j - 1 < NI else 0.0
    hi = w[j + 1] if 0 <= j + 1 < NI else 0.0
    return float(RHO * (lo - hi))


def splat(x):
    return jnp.full((SUB, NK), x, F32)


def in_hbm(*arrays):
    return tuple(pltpu.with_memory_space_constraint(a, pltpu.HBM) for a in arrays)


def parity(name):
    return lax.rem(lax.axis_index(name), 2)


def pack_x_body(s, f, one, two, sem):
    core = parity("gx")

    def faces(right, left):
        moves = [
            pltpu.make_async_copy(s.at[:, NI - 3 : NI], right.at[:, 0:3], sem.at[0]),
            pltpu.make_async_copy(f.at[:, NI - 1 : NI], right.at[:, 3:4], sem.at[1]),
            pltpu.make_async_copy(s.at[:, 0:3], left.at[:, 0:3], sem.at[2]),
            pltpu.make_async_copy(f.at[:, 0:1], left.at[:, 3:4], sem.at[3]),
        ]
        for c in moves:
            c.start()
        for c in moves:
            c.wait()

    @pl.when(core == 0)
    def _():
        faces(one, two)

    @pl.when(core == 1)
    def _():
        faces(two, one)


def pack_x(state, flux_x):
    out = jax.ShapeDtypeStruct((NV, 4, NJ, NK), F32)
    return pl.pallas_call(
        pack_x_body,
        out_shape=(out, out),
        in_specs=[pl.BlockSpec(memory_space=pltpu.HBM)] * 2,
        out_specs=(pl.BlockSpec(memory_space=pltpu.VMEM),) * 2,
        scratch_shapes=[pltpu.SemaphoreType.DMA((4,))],
        compiler_params=pltpu.CompilerParams(vmem_limit_bytes=8 << 20),
        cost_estimate=pl.CostEstimate(flops=0, bytes_accessed=1 << 20, transcendentals=0),
        name="pack_x",
    )(*in_hbm(state, flux_x))


def pack_y_body(fy, yone, ytwo, lo, hi, sem):
    odd = parity("gy")
    copies = [
        (
            pltpu.make_async_copy(fy.at[v, :, 0:SUB, :], lo.at[v], sem.at[0, v]),
            pltpu.make_async_copy(fy.at[v, :, NJ - SUB : NJ, :], hi.at[v], sem.at[1, v]),
        )
        for v in range(NV)
    ]
    for both in copies:
        for c in both:
            c.start()

    def rows(top, bottom):
        for v in range(NV):
            for c in copies[v]:
                c.wait()
            for i in range(NI):
                part = pl.ds(4 * (i % 2), 4)
                top[v, i // 2, part, :] = hi[v, i, 4:8, :]
                bottom[v, i // 2, part, :] = lo[v, i, 0:4, :]

    @pl.when(odd == 0)
    def _():
        rows(yone, ytwo)

    @pl.when(odd == 1)
    def _():
        rows(ytwo, yone)


def pack_y(flux_y):
    out = jax.ShapeDtypeStruct((NV, NI // 2, SUB, NK), F32)
    return pl.pallas_call(
        pack_y_body,
        out_shape=(out, out),
        in_specs=[pl.BlockSpec(memory_space=pltpu.HBM)],
        out_specs=(pl.BlockSpec(memory_space=pltpu.VMEM),) * 2,
        scratch_shapes=[
            pltpu.VMEM((NV, NI, SUB, NK), F32),
            pltpu.VMEM((NV, NI, SUB, NK), F32),
            pltpu.SemaphoreType.DMA((2, NV)),
        ],
        compiler_params=pltpu.CompilerParams(vmem_limit_bytes=8 << 20),
        cost_estimate=pl.CostEstimate(flops=0, bytes_accessed=1 << 20, transcendentals=0),
        name="pack_y",
    )(*in_hbm(flux_y))


def own_body(gap_hbm, s_hbm, f_hbm, inner, outer, mine, send, gap, s, f, own, gap_sem, sem):
    gap_load = pltpu.make_async_copy(gap_hbm, gap, gap_sem)
    gap_load.start()
    loads = [
        (
            pltpu.make_async_copy(s_hbm.at[v], s.at[v], sem.at[0, v]),
            pltpu.make_async_copy(f_hbm.at[v], f.at[v], sem.at[1, v]),
        )
        for v in range(NV)
    ]
    for both in loads:
        for c in both:
            c.start()
    core = parity("gx")
    piece = lax.axis_index("gx")
    gap_load.wait()
    alpha = [0.5 - splat(gap[i]) for i in range(NI)]
    g32 = [(0.5 - a) * (1.0 / 32.0) for a in alpha]
    m, c = [None] * NI, [None] * NI
    n, b = [None] * NI, [None] * NI
    for k in range(NI):
        m[k] = 1.0 / (1.0 - alpha[k] * c[k - 1]) if k else jnp.ones((SUB, NK), F32)
        c[k] = alpha[k] * m[k]
        r = NI - 1 - k
        n[r] = 1.0 / (1.0 - alpha[r] * b[r + 1]) if k else jnp.ones((SUB, NK), F32)
        b[r] = alpha[r] * n[r]
    left, right = [None] * NI, [None] * NI
    wh, wt = [None] * NI, [None] * NI
    left[0], right[NI - 1] = -b[0], -c[NI - 1]
    qh, qt = None, None
    for k in range(NI):
        r = NI - 1 - k
        if k:
            left[k] = -b[k] * left[k - 1]
            right[r] = -c[r] * right[r + 1]
            qh = -b[k - 1] if qh is None else -b[k - 1] * qh
            qt = -c[r + 1] if qt is None else -c[r + 1] * qt
            wh[k] = qh * n[k]
            wt[r] = qt * m[r]
        else:
            wh[0], wt[NI - 1] = n[0], m[NI - 1]
    for k in range(NI):
        inner[C_C + k] = c[k]
        inner[C_MG + k] = m[k] * g32[k]
        outer[C_LEFT + k] = left[k]
        outer[C_RIGHT + k] = right[k]
    vh = [wh[k] * g32[k] for k in range(NI)]
    vt = [wt[k] * g32[k] for k in range(NI)]

    def spread(v, j):
        terms = [D6[q + 3] * v[j - q] for q in range(-3, 4) if 0 <= j - q < NI]
        total = terms[0]
        for t in terms[1:]:
            total = total + t
        return total

    edge = [-alpha[0] * wh[0], -alpha[NI - 1] * wh[NI - 1], -alpha[0] * wt[0], -alpha[NI - 1] * wt[NI - 1]]
    low = [spread(v, q - 3) for v in (vh, vt) for q in range(3)]
    high = [spread(v, NI + q) for v in (vh, vt) for q in range(3)]
    edge += [jnp.where(core == 0, h, l) for h, l in zip(high, low)]
    edge += [jnp.where(core == 0, l, h) for h, l in zip(high, low)]
    for q in range(3):
        outer[C_FAR + q] = jnp.where(core == 0, edge[13 + q], edge[10 + q])
    for k, t in enumerate(edge):
        mine[pl.ds(EDGE + k, 1), :] = t[0:1]
        send[pl.ds(EDGE + k, 1), :] = t[0:1]

    first = jnp.where(piece == 0, 1.0 / 36.0, 0.0).astype(F32)
    last = jnp.where(piece == PIECES - 1, -1.0 / 36.0, 0.0).astype(F32)
    inv = CS["inv"]
    fh = [flux_weight(0, j) for j in range(NI)]
    ft = [flux_weight(NI - 1, j) for j in range(NI)]
    fh[0] = (fh[0] - BETA) + float(inv[0, 0]) * first
    ft[0] = ft[0] + float(inv[NI - 1, 0]) * first
    fh[NI - 1] = fh[NI - 1] + float(inv[0, NI - 1]) * last
    ft[NI - 1] = (ft[NI - 1] + BETA) + float(inv[NI - 1, NI - 1]) * last

    for i in range(NI):
        own[i] = spread(vh, i)
        own[NI + i] = spread(vt, i)

    s_in, s_out = (NI - 3) * (1 - core), (NI - 3) * core
    for v in range(NV):
        for c in loads[v]:
            c.wait()
        for out, half in ((mine, core), (send, 1 - core)):
            for r in range(HALF // SUB):
                rows = pl.ds(pl.multiple_of(HALF * half + SUB * r, SUB), SUB)
                sums = [None] * 4
                for i in range(NI):
                    a, z = s[v, i, rows, :], f[v, i, rows, :]
                    terms = (own[i] * a, own[NI + i] * a, fh[i] * z, ft[i] * z)
                    sums = [t if o is None else o + t for o, t in zip(sums, terms)]
                faces = [s[v, s_in + k, rows, :] for k in range(3)] + [s[v, s_out + k, rows, :] for k in range(3)]
                for k, t in enumerate(sums + faces):
                    out[pl.ds((NV * k + v) * HALF + SUB * r, SUB), :] = t


def own_share(gap, state, flux_x):
    vmem, hbm = pl.BlockSpec(memory_space=pltpu.VMEM), pl.BlockSpec(memory_space=pltpu.HBM)
    coef = jax.ShapeDtypeStruct((2 * NI, SUB, NK), F32)
    coef_far = jax.ShapeDtypeStruct((2 * NI + 3, SUB, NK), F32)
    values = jax.ShapeDtypeStruct((EDGE + 16, NK), F32)
    return pl.pallas_call(
        own_body,
        out_shape=(coef, coef_far, values, values),
        in_specs=[hbm, hbm, hbm],
        out_specs=(vmem,) * 4,
        scratch_shapes=[
            pltpu.SMEM((NI,), F32),
            pltpu.VMEM((NV, NI, NJ, NK), F32),
            pltpu.VMEM((NV, NI, NJ, NK), F32),
            pltpu.VMEM((2 * NI, SUB, NK), F32),
            pltpu.SemaphoreType.DMA,
            pltpu.SemaphoreType.DMA((2, NV)),
        ],
        compiler_params=pltpu.CompilerParams(vmem_limit_bytes=12 << 20),
        cost_estimate=pl.CostEstimate(flops=1 << 24, bytes_accessed=4 << 20, transcendentals=0),
        name="own_share",
    )(*in_hbm(gap, state, flux_x))


def pair_body(mine, got, out_hbm, mids, out, sem):
    is0 = parity("gx") == 0

    def both(rows):
        x, y = mine[rows, :], got[rows, :]
        return jnp.where(is0, x, y), jnp.where(is0, y, x)

    ca, cb = zip(*(both(pl.ds(EDGE + k, 1)) for k in range(16)))
    ca, cb = ([jnp.broadcast_to(t, (SUB, NK)) for t in c] for c in (ca, cb))
    hla, hra, tla, tra = ca[:4]
    hlb, hrb, tlb, trb = cb[:4]
    inv = 1.0 / (1.0 - tra * hlb)
    down = [hlb * tla * inv, hrb * inv, tla * inv, tra * hrb * inv, hlb * inv, inv, tra * inv]
    for k, t in enumerate(down):
        mids[pl.ds(4 * NV * HALF + k, 1), :] = t[0:1]
    cross_h, cross_t = hra * inv, tlb * inv
    edge = [hla + hra * down[0], hra * down[1], tlb * down[2], trb + tlb * down[3]]
    edge += [ca[10 + q] + (cross_h * hlb) * ca[13 + q] for q in range(3)]
    edge += [cross_t * ca[13 + q] for q in range(3)]
    edge += [cross_h * cb[10 + q] for q in range(3)]
    edge += [cb[13 + q] + (cross_t * tra) * cb[10 + q] for q in range(3)]
    lane = lax.broadcasted_iota(jnp.int32, (SUB, NK), 1)
    packed = jnp.zeros((SUB, NK), F32)
    for k, t in enumerate(edge):
        packed = jnp.where(lane == k, t, packed)

    k = CS["pair"]
    blocks = [pl.ds(WIDE * SUB * r, WIDE * SUB) for r in range(HALF // SUB)]
    stores = [pltpu.make_async_copy(out.at[b], out_hbm.at[b], sem.at[r]) for r, b in enumerate(blocks)]
    for r in range(HALF // SUB):
        at = WIDE * SUB * r
        out[pl.ds(at + VALUES * NV, SUB, stride=WIDE), :] = packed
        for v in range(NV):
            a, b = zip(*(both(pl.ds((NV * e + v) * HALF + SUB * r, SUB)) for e in range(VALUES)))
            ha, ta, hb, tb = a[0], a[1], b[0], b[1]
            for q in range(3):
                ha, ta = ha + ca[4 + q] * b[4 + q], ta + ca[7 + q] * b[4 + q]
                hb, tb = hb + cb[4 + q] * a[4 + q], tb + cb[7 + q] * a[4 + q]
            head = (hb + hlb * ta) * inv
            tail = (ta + tra * hb) * inv
            da, ea, db, eb = a[2], a[3], b[2], b[3]
            dhead = k["inv"] * db + k["inv_hl"] * ea
            dtail = k["inv"] * ea + k["inv_tr"] * db
            values = [ha + hra * head, tb + tlb * tail, da + float(CS["hr"]) * dhead, eb + float(CS["tl"]) * dtail]
            values += list(a[7:10]) + list(b[7:10])
            for e, t in enumerate(values):
                out[pl.ds(at + NV * e + v, SUB, stride=WIDE), :] = t
            for e, t in enumerate((head, tail, dhead, dtail)):
                mids[pl.ds((NV * e + v) * HALF + SUB * r, SUB), :] = t
        stores[r].start()
    for c in stores:
        c.wait()


def pair(mine, got):
    vmem = pl.BlockSpec(memory_space=pltpu.VMEM)
    return pl.pallas_call(
        pair_body,
        out_shape=(
            jax.ShapeDtypeStruct((PAIRS * WIDE, NK), F32),
            jax.ShapeDtypeStruct((4 * NV * HALF + SUB, NK), F32),
        ),
        in_specs=[vmem] * 2,
        out_specs=(pl.BlockSpec(memory_space=pltpu.HBM), vmem),
        scratch_shapes=[pltpu.VMEM((PAIRS * WIDE, NK), F32), pltpu.SemaphoreType.DMA((HALF // SUB,))],
        compiler_params=pltpu.CompilerParams(vmem_limit_bytes=8 << 20),
        cost_estimate=pl.CostEstimate(flops=1 << 20, bytes_accessed=1 << 20, transcendentals=0),
        name="pair",
    )(mine, got)


def join_body(x, out_hbm, out, coef, sem):
    for r in range(PAIRS // SUB):
        packed = x[pl.ds(WIDE * SUB * r + VALUES * NV, SUB, stride=WIDE), :]
        for k in range(16):
            coef[pl.ds(PAIRS * k + SUB * r, SUB), :] = jnp.broadcast_to(packed[:, k : k + 1], (SUB, NK))

    def row(p, k):
        return jnp.broadcast_to(coef[pl.ds(PAIRS * k + p, 1), :], (NV, NK))

    def value(p, k):
        return x[pl.ds(WIDE * p + NV * k, NV), :]

    c = CS["pair"]
    head_f, tail_f, head_d, tail_d = [], [], [], []
    for p in range(PAIRS):
        h, t, dh, dt = (value(p, k) for k in range(4))
        if p:
            for q in range(3):
                z = value(p - 1, 7 + q)
                h, t = h + row(p, 4 + q) * z, t + row(p, 7 + q) * z
        if p < PAIRS - 1:
            for q in range(3):
                z = value(p + 1, 4 + q)
                h, t = h + row(p, 10 + q) * z, t + row(p, 13 + q) * z
        head_f.append(h)
        tail_f.append(t)
        head_d.append(dh)
        tail_d.append(dt)

    scale = 8.0
    num, den = [None] * PAIRS, [None] * PAIRS
    hl, hr, tl, tr = ([row(p, k) for p in range(PAIRS)] for k in range(4))
    num[0], den[0] = tr[0], jnp.ones((NV, NK), F32)
    for p in range(1, PAIRS):
        cross = tl[p] * hr[p] - tr[p] * hl[p]
        num[p] = (scale * tr[p]) * den[p - 1] + (scale * cross) * num[p - 1]
        den[p] = scale * den[p - 1] - (scale * hl[p]) * num[p - 1]
    inv = [None] + [1.0 / den[p] for p in range(1, PAIRS)]
    e = [num[0]] + [num[p] * inv[p] for p in range(1, PAIRS)]
    keep = [None] + [(scale * den[p - 1]) * inv[p] for p in range(1, PAIRS)]

    fwd_f, fwd_d = [tail_f[0]], [tail_d[0]]
    chl, chr_, ctl, ce = c["hl"], c["hr"], c["tl"], c["e"]
    for p in range(1, PAIRS):
        a = tl[p] * keep[p]
        fwd_f.append((tail_f[p] + (a * e[p - 1]) * head_f[p]) + a * fwd_f[-1])
        k = ctl / (1.0 - chl * ce[p - 1])
        fwd_d.append((tail_d[p] + float(k * ce[p - 1]) * head_d[p]) + float(k) * fwd_d[-1])

    blocks = [pl.ds(ROWS * SUB * r, ROWS * SUB) for r in range(PAIRS // SUB)]
    stores = [pltpu.make_async_copy(out.at[b], out_hbm.at[b], sem.at[r]) for r, b in enumerate(blocks)]
    zero = jnp.zeros((NV, NK), F32)
    right_f, right_d = zero, zero
    for p in range(PAIRS - 1, -1, -1):
        if p:
            h = keep[p]
            at_f = (head_f[p] + hl[p] * fwd_f[p - 1]) * h + (hr[p] * h) * right_f
            left_f = fwd_f[p - 1] + e[p - 1] * at_f
            k = 1.0 / (1.0 - chl * ce[p - 1])
            at_d = (float(k) * head_d[p] + float(k * chl) * fwd_d[p - 1]) + float(k * chr_) * right_d
            left_d = fwd_d[p - 1] + float(ce[p - 1]) * at_d
        else:
            at_f = at_d = left_f = left_d = zero
        for k, val in enumerate((left_f, right_f, left_d, right_d)):
            out[pl.ds(ROWS * p + NV * k, NV), :] = val
        right_f, right_d = at_f, at_d
        if p % SUB == 0:
            stores[p // SUB].start()
    for t in stores:
        t.wait()


def join(x):
    vmem = pl.BlockSpec(memory_space=pltpu.VMEM)
    return pl.pallas_call(
        join_body,
        out_shape=jax.ShapeDtypeStruct((PAIRS * ROWS, NK), F32),
        in_specs=[vmem],
        out_specs=pl.BlockSpec(memory_space=pltpu.HBM),
        scratch_shapes=[
            pltpu.VMEM((PAIRS * ROWS, NK), F32),
            pltpu.VMEM((16 * PAIRS, NK), F32),
            pltpu.SemaphoreType.DMA((PAIRS // SUB,)),
        ],
        compiler_params=pltpu.CompilerParams(vmem_limit_bytes=8 << 20),
        cost_estimate=pl.CostEstimate(flops=1 << 20, bytes_accessed=1 << 20, transcendentals=0),
        name="join",
    )(x)


def far_body(outer, two, own, other):
    core = parity("gx")
    for out, half in ((own, core), (other, 1 - core)):
        for v in range(NV):
            for r in range(HALF // SUB):
                rows = pl.ds(pl.multiple_of(HALF * half + SUB * r, SUB), SUB)
                a = [two[v, k, rows, :] for k in range(3)]
                out[pl.ds(v * HALF + SUB * r, SUB), :] = (
                    outer[C_FAR] * a[0] + outer[C_FAR + 1] * a[1] + outer[C_FAR + 2] * a[2]
                )


def far(outer, two):
    vmem = pl.BlockSpec(memory_space=pltpu.VMEM)
    out = jax.ShapeDtypeStruct((NV * HALF, NK), F32)
    return pl.pallas_call(
        far_body,
        out_shape=(out, out),
        in_specs=[vmem] * 2,
        out_specs=(vmem,) * 2,
        compiler_params=pltpu.CompilerParams(vmem_limit_bytes=8 << 20),
        cost_estimate=pl.CostEstimate(flops=1 << 18, bytes_accessed=1 << 19, transcendentals=0),
        name="far",
    )(outer, two)


def split_body(z, mids, far_own, far_other, own, send):
    is0 = parity("gx") == 0
    c = CS["pair"]
    down = [jnp.broadcast_to(mids[pl.ds(4 * NV * HALF + k, 1), :], (SUB, NK)) for k in range(7)]
    head_far, tail_far = jnp.where(is0, down[4], down[5]), jnp.where(is0, down[5], down[6])
    for r in range(HALF // SUB):
        for v in range(NV):
            lf, rf, ld, rd = (z[pl.ds(ROWS * SUB * r + NV * k + v, SUB, stride=ROWS), :] for k in range(4))
            head, tail, dhead, dtail = (mids[pl.ds((NV * k + v) * HALF + SUB * r, SUB), :] for k in range(4))
            part = pl.ds(v * HALF + SUB * r, SUB)
            w = far_own[part, :]
            head = (head + head_far * w) + down[0] * lf + down[1] * rf
            tail = (tail + tail_far * w) + down[2] * lf + down[3] * rf
            dhead = dhead + c["down"][0] * ld + c["down"][1] * rd
            dtail = dtail + c["down"][2] * ld + c["down"][3] * rd
            a, b = (lf, head, ld, dhead), (tail, rf, dtail, rd)
            for k in range(4):
                rows = pl.ds((NV * k + v) * HALF + SUB * r, SUB)
                own[rows, :] = jnp.where(is0, a[k], b[k])
                send[rows, :] = jnp.where(is0, b[k], a[k])
            send[pl.ds((4 * NV + v) * HALF + SUB * r, SUB), :] = far_other[part, :]


def split(z, mids, far_own, far_other):
    vmem = pl.BlockSpec(memory_space=pltpu.VMEM)
    own = jax.ShapeDtypeStruct((4 * NV * HALF, NK), F32)
    send = jax.ShapeDtypeStruct((5 * NV * HALF, NK), F32)
    return pl.pallas_call(
        split_body,
        out_shape=(own, send),
        in_specs=[vmem] * 4,
        out_specs=(vmem,) * 2,
        compiler_params=pltpu.CompilerParams(vmem_limit_bytes=8 << 20),
        cost_estimate=pl.CostEstimate(flops=1 << 20, bytes_accessed=1 << 20, transcendentals=0),
        name="split",
    )(z, mids, far_own, far_other)


def block_body(inner, s_hbm, f_hbm, fy_hbm, one, two, yone, ytwo, mx, my, base, mxb, s, f, fy, pad, sem):
    moves = ((fy_hbm, fy), (s_hbm, s), (f_hbm, f))
    for v in range(NV):
        for k, (h, t) in enumerate(moves):
            pltpu.make_async_copy(h.at[v], t.at[v], sem.at[k, v]).start()
    piece = lax.axis_index("gx")
    is0 = parity("gx") == 0
    even = parity("gy") == 0
    first = jnp.where(piece == 0, 1.0 / 36.0, 0.0).astype(F32)
    last = jnp.where(piece == PIECES - 1, -1.0 / 36.0, 0.0).astype(F32)
    mxt = jnp.transpose(mx[...] * -0.5)
    myt = jnp.transpose(my[...] * -0.5)
    for i in range(NI):
        mxb[i] = jnp.broadcast_to(mxt[:, i : i + 1], (NJ, NK))
        pad[NI + i, 0:NJ, :] = jnp.broadcast_to(myt[:, i : i + 1], (NJ, NK))

    @pl.loop(0, NV)
    def _(v):
        for k, (h, t) in enumerate(moves):
            pltpu.make_async_copy(h.at[v], t.at[v], sem.at[k, v]).wait()
        for i in range(NI):
            for q in range(NJ // SUB):
                pad[i, pl.ds(SUB + SUB * q, SUB), :] = fy[v, i, pl.ds(SUB * q, SUB), :]
            part = pl.ds(4 * (i % 2), 4)
            a, b = yone[v, i // 2, part, :], ytwo[v, i // 2, part, :]
            pad[i, SUB - 4 : SUB, :] = jnp.where(even, b, a)
            pad[i, SUB + NJ : SUB + NJ + 4, :] = jnp.where(even, a, b)

        for q in range(NJ // SUB):
            rows = pl.ds(SUB * q, SUB)
            a = [one[v, k, rows, :] for k in range(4)]
            b = [two[v, k, rows, :] for k in range(4)]
            low = [jnp.where(is0, b[k], a[k]) for k in range(4)]
            high = [jnp.where(is0, a[k], b[k]) for k in range(4)]
            st = low[:3] + [s[v, i, rows, :] for i in range(NI)] + high[:3]
            fl = [low[3]] + [f[v, i, rows, :] for i in range(NI)] + [high[3]]
            ye, yd, us = [], [], []
            for i in range(NI):
                d6 = (
                    (st[i] + st[i + 6])
                    - 6.0 * (st[i + 1] + st[i + 5])
                    + 15.0 * (st[i + 2] + st[i + 4])
                    - 20.0 * st[i + 3]
                )
                y = inner[C_MG + i] * d6
                ye.append(y - inner[C_C + i] * ye[-1] if i else y)
                u = fl[i + 2] - fl[i]
                us.append(u)
                r = fl[2] if i == 0 else -fl[NI - 1] if i == NI - 1 else u
                r = float(RHO * CS["m"][i]) * r
                if i == 0:
                    r = r + (first * float(CS["m"][i])) * fl[1]
                if i == NI - 1:
                    r = r + (last * float(CS["m"][i])) * fl[NI]
                yd.append(r - float(CS["c"][i]) * yd[-1] if i else r)
            xe = xd = None
            for i in range(NI - 1, -1, -1):
                xe = ye[i] if xe is None else ye[i] - inner[C_C + i] * xe
                xd = yd[i] if xd is None else yd[i] - float(CS["c"][i]) * xd
                at = SUB + SUB * q
                dy = None
                for k, w in enumerate(Y_WEIGHTS, start=1):
                    t = w * (pad[i, pl.ds(at + k, SUB), :] - pad[i, pl.ds(at - k, SUB), :])
                    dy = t if dy is None else dy + t
                d = us[i] * (1.0 / 12.0) + xd
                base[v, i, rows, :] = (st[i + 3] + xe) + (mxb[i, rows, :] * d + pad[NI + i, rows, :] * dy)


def block(inner, state, flux_x, flux_y, one, two, yone, ytwo, mx, my):
    vmem, hbm = pl.BlockSpec(memory_space=pltpu.VMEM), pl.BlockSpec(memory_space=pltpu.HBM)
    return pl.pallas_call(
        block_body,
        out_shape=(
            jax.ShapeDtypeStruct((NV, NI, NJ, NK), F32),
            jax.ShapeDtypeStruct((NI, NJ, NK), F32),
        ),
        in_specs=[vmem] + [hbm] * 3 + [vmem] * 6,
        out_specs=(vmem, vmem),
        scratch_shapes=[pltpu.VMEM((NV, NI, NJ, NK), F32)] * 3
        + [pltpu.VMEM((2 * NI, SUB + NJ + SUB, NK), F32), pltpu.SemaphoreType.DMA((3, NV))],
        compiler_params=pltpu.CompilerParams(vmem_limit_bytes=16 << 20),
        cost_estimate=pl.CostEstimate(flops=1 << 30, bytes_accessed=64 << 20, transcendentals=0),
        name="block",
    )(inner, *in_hbm(state, flux_x, flux_y), one, two, yone, ytwo, mx, my)


def finish_body(outer, base, mxb, own, got, mids, far_other, out_hbm, out, sem):
    core = parity("gx")
    is0 = core == 0
    hl_inv, inv, tr_inv = (jnp.broadcast_to(mids[pl.ds(4 * NV * HALF + k, 1), :], (SUB, NK)) for k in (4, 5, 6))
    zero = jnp.zeros((SUB, NK), F32)
    own_far = (jnp.where(is0, zero, inv), jnp.where(is0, inv, zero))
    got_far = (jnp.where(is0, zero, tr_inv), jnp.where(is0, hl_inv, zero))
    stores = [pltpu.make_async_copy(out.at[v], out_hbm.at[v], sem.at[v]) for v in range(NV)]
    for v in range(NV):
        for z, half, far_w, far_z, far_at in (
            (own, core, own_far, got, 4 * NV),
            (got, 1 - core, got_far, far_other, 0),
        ):
            for r in range(HALF // SUB):
                rows = pl.ds(pl.multiple_of(HALF * half + SUB * r, SUB), SUB)
                lf, rf, ld, rd = (z[pl.ds((NV * k + v) * HALF + SUB * r, SUB), :] for k in range(4))
                w = far_z[pl.ds((far_at + v) * HALF + SUB * r, SUB), :]
                lf, rf = lf + far_w[0] * w, rf + far_w[1] * w
                for i in range(NI):
                    d = float(CS["left"][i]) * ld + float(CS["right"][i]) * rd
                    e = outer[C_LEFT + i] * lf + outer[C_RIGHT + i] * rf
                    out[v, i, rows, :] = (base[v, i, rows, :] + e) + mxb[i, rows, :] * d
        stores[v].start()
    for c in stores:
        c.wait()


def finish(outer, base, mxb, own, got, mids, far_other):
    return pl.pallas_call(
        finish_body,
        out_shape=jax.ShapeDtypeStruct((NV, NI, NJ, NK), F32),
        in_specs=[pl.BlockSpec(memory_space=pltpu.VMEM)] * 7,
        out_specs=pl.BlockSpec(memory_space=pltpu.HBM),
        scratch_shapes=[pltpu.VMEM((NV, NI, NJ, NK), F32), pltpu.SemaphoreType.DMA((NV,))],
        compiler_params=pltpu.CompilerParams(vmem_limit_bytes=12 << 20),
        cost_estimate=pl.CostEstimate(flops=1 << 22, bytes_accessed=3 << 20, transcendentals=0),
        name="finish",
    )(outer, base, mxb, own, got, mids, far_other)


def exchange(x, rows):
    groups = [[2 * p + c for p in range(PAIRS)] for c in range(2)]
    y = lax.all_to_all(x.reshape(PAIRS, rows, NK), "gx", 0, 0, tiled=True, axis_index_groups=groups)
    return y.reshape(PAIRS * rows, NK)


def per_device(flux_x, flux_y, state, metric_x, metric_y, filter_gap):
    count_y = lax.axis_size("gy")
    pair_in = [(i, i ^ 1) for i in range(PIECES)]
    pair_out = [(i, i + 1 if i % 2 else i - 1) for i in range(1, PIECES - 1)]
    y_in = [(i, i ^ 1) for i in range(count_y)]
    y_out = [(i, (i + 1 if i % 2 else i - 1) % count_y) for i in range(count_y)]

    inner, outer, mine, send = own_share(filter_gap, state, flux_x)
    send, state, flux_x, flux_y = lax.optimization_barrier((send, state, flux_x, flux_y))
    got = lax.ppermute(send, "gx", pair_in)
    got, *faces = lax.optimization_barrier((got, *pack_y(flux_y)))
    ends, mids = pair(mine, got)
    ends, ysend_one, ysend_two, state, flux_x = lax.optimization_barrier((ends, *faces, state, flux_x))
    ends = exchange(ends, WIDE)
    send_one, send_two = pack_x(state, flux_x)
    one = lax.ppermute(send_one, "gx", pair_in)
    two = lax.ppermute(send_two, "gx", pair_out)
    yone = lax.ppermute(ysend_one, "gy", y_in)
    ytwo = lax.ppermute(ysend_two, "gy", y_out)
    outside = join(ends)
    outside, one = lax.optimization_barrier((outside, one))
    two, yone, ytwo = lax.optimization_barrier((two, yone, ytwo))
    far_own, far_other = far(outer, two)
    base, mxb = block(inner, state, flux_x, flux_y, one, two, yone, ytwo, metric_x, metric_y)
    outside, base, mxb, far_own = lax.optimization_barrier((exchange(outside, ROWS), base, mxb, far_own))
    own, send = split(outside, mids, far_own, far_other)
    got = lax.ppermute(send, "gx", pair_in)
    return finish(outer, base, mxb, own, got, mids, far_other)


def solution(mesh):
    return jax.shard_map(
        per_device,
        mesh=mesh,
        in_specs=(
            P(None, "gx", "gy", None),
            P(None, "gx", "gy", None),
            P(None, "gx", "gy", None),
            P("gx", "gy"),
            P("gx", "gy"),
            P("gx"),
        ),
        out_specs=P(None, "gx", "gy", None),
        check_vma=False,
    )
```

```python
import jax
import jax.numpy as jnp
import numpy as np
from jax import lax
from jax.experimental import pallas as pl
from jax.experimental.pallas import tpu as pltpu
from jax.sharding import PartitionSpec as P

NV, NI, NJ, NK = 5, 16, 32, 128
PIECES, PAIRS, HALF = 32, 16, 16
VALUES = 10
ROWS, WIDE = 24, 56
EDGE = VALUES * NV * HALF
SUB = 8
F32 = jnp.float32
Y_WEIGHTS = (4.0 / 5.0, -1.0 / 5.0, 4.0 / 105.0, -1.0 / 280.0)
RHO = 25.0 / 36.0
BETA = 3.0 * RHO
D6 = (1.0, -6.0, 15.0, -20.0, 15.0, -6.0, 1.0)

C_C, C_MG = 0, NI
C_LEFT, C_RIGHT, C_FAR = 0, NI, 2 * NI


def constant_system():
    a = 1.0 / 3.0
    t = np.eye(NI) + a * (np.eye(NI, k=1) + np.eye(NI, k=-1))
    inv = np.linalg.inv(t)
    m, c = [], []
    prev = 0.0
    for _ in range(NI):
        m.append(1.0 / (1.0 - a * prev))
        prev = a * m[-1]
        c.append(prev)
    left, right = -a * inv[:, 0], -a * inv[:, -1]
    hl, hr, tl, tr = left[0], right[0], left[-1], right[-1]
    d = 1.0 / (1.0 - tr * hl)
    pair = dict(inv=d, inv_hl=d * hl, inv_tr=d * tr, down=[hl * tl * d, hr * d, tl * d, tr * hr * d])
    for k in pair:
        pair[k] = [float(t) for t in pair[k]] if isinstance(pair[k], list) else float(pair[k])
    p = dict(hl=hl + hr * hl * tl * d, hr=hr * hr * d, tl=tl * tl * d, tr=tr + tl * tr * hr * d)
    e = [p["tr"]]
    for _ in range(PAIRS - 1):
        e.append(p["tr"] + p["tl"] * p["hr"] * e[-1] / (1.0 - p["hl"] * e[-1]))
    pair.update(p, e=e)
    return dict(m=m, c=c, inv=inv, left=left, right=right, hl=hl, hr=hr, tl=tl, tr=tr, pair=pair)


CS = constant_system()


def flux_weight(row, j):
    w = CS["inv"][row]
    lo = w[j - 1] if 0 <= j - 1 < NI else 0.0
    hi = w[j + 1] if 0 <= j + 1 < NI else 0.0
    return float(RHO * (lo - hi))


def splat(x):
    return jnp.full((SUB, NK), x, F32)


def in_hbm(*arrays):
    return tuple(pltpu.with_memory_space_constraint(a, pltpu.HBM) for a in arrays)


def parity(name):
    return lax.rem(lax.axis_index(name), 2)


def pack_body(s, f, fy, one, two, yone, ytwo, lo, hi, sem):
    core, odd = parity("gx"), parity("gy")
    copies = [
        pltpu.make_async_copy(fy.at[:, :, 0:SUB, :], lo, sem.at[0]),
        pltpu.make_async_copy(fy.at[:, :, NJ - SUB : NJ, :], hi, sem.at[1]),
    ]
    for c in copies:
        c.start()

    def faces(right, left):
        moves = [
            pltpu.make_async_copy(s.at[:, NI - 3 : NI], right.at[:, 0:3], sem.at[2]),
            pltpu.make_async_copy(f.at[:, NI - 1 : NI], right.at[:, 3:4], sem.at[3]),
            pltpu.make_async_copy(s.at[:, 0:3], left.at[:, 0:3], sem.at[4]),
            pltpu.make_async_copy(f.at[:, 0:1], left.at[:, 3:4], sem.at[5]),
        ]
        for c in moves:
            c.start()
        for c in moves:
            c.wait()

    def rows(top, bottom):
        for v in range(NV):
            for i in range(NI):
                part = pl.ds(4 * (i % 2), 4)
                top[v, i // 2, part, :] = hi[v, i, 4:8, :]
                bottom[v, i // 2, part, :] = lo[v, i, 0:4, :]

    @pl.when(core == 0)
    def _():
        faces(one, two)

    @pl.when(core == 1)
    def _():
        faces(two, one)

    for c in copies:
        c.wait()

    @pl.when(odd == 0)
    def _():
        rows(yone, ytwo)

    @pl.when(odd == 1)
    def _():
        rows(ytwo, yone)


def pack(state, flux_x, flux_y):
    x_out = jax.ShapeDtypeStruct((NV, 4, NJ, NK), F32)
    y_out = jax.ShapeDtypeStruct((NV, NI // 2, SUB, NK), F32)
    return pl.pallas_call(
        pack_body,
        out_shape=(x_out, x_out, y_out, y_out),
        in_specs=[pl.BlockSpec(memory_space=pltpu.HBM)] * 3,
        out_specs=(pl.BlockSpec(memory_space=pltpu.VMEM),) * 4,
        scratch_shapes=[
            pltpu.VMEM((NV, NI, SUB, NK), F32),
            pltpu.VMEM((NV, NI, SUB, NK), F32),
            pltpu.SemaphoreType.DMA((6,)),
        ],
        compiler_params=pltpu.CompilerParams(vmem_limit_bytes=8 << 20),
        cost_estimate=pl.CostEstimate(flops=0, bytes_accessed=2 << 20, transcendentals=0),
        name="pack",
    )(*in_hbm(state, flux_x, flux_y))


def own_body(gap_hbm, s_hbm, f_hbm, inner, outer, mine, send, gap, s, f, own, gap_sem, sem):
    gap_load = pltpu.make_async_copy(gap_hbm, gap, gap_sem)
    gap_load.start()
    loads = [
        (
            pltpu.make_async_copy(s_hbm.at[v], s.at[v], sem.at[0, v]),
            pltpu.make_async_copy(f_hbm.at[v], f.at[v], sem.at[1, v]),
        )
        for v in range(NV)
    ]
    for both in loads:
        for c in both:
            c.start()
    core = parity("gx")
    piece = lax.axis_index("gx")
    gap_load.wait()
    alpha = [0.5 - splat(gap[i]) for i in range(NI)]
    g32 = [(0.5 - a) * (1.0 / 32.0) for a in alpha]
    m, c = [None] * NI, [None] * NI
    n, b = [None] * NI, [None] * NI
    for k in range(NI):
        m[k] = 1.0 / (1.0 - alpha[k] * c[k - 1]) if k else jnp.ones((SUB, NK), F32)
        c[k] = alpha[k] * m[k]
        r = NI - 1 - k
        n[r] = 1.0 / (1.0 - alpha[r] * b[r + 1]) if k else jnp.ones((SUB, NK), F32)
        b[r] = alpha[r] * n[r]
    left, right = [None] * NI, [None] * NI
    wh, wt = [None] * NI, [None] * NI
    left[0], right[NI - 1] = -b[0], -c[NI - 1]
    qh, qt = None, None
    for k in range(NI):
        r = NI - 1 - k
        if k:
            left[k] = -b[k] * left[k - 1]
            right[r] = -c[r] * right[r + 1]
            qh = -b[k - 1] if qh is None else -b[k - 1] * qh
            qt = -c[r + 1] if qt is None else -c[r + 1] * qt
            wh[k] = qh * n[k]
            wt[r] = qt * m[r]
        else:
            wh[0], wt[NI - 1] = n[0], m[NI - 1]
    for k in range(NI):
        inner[C_C + k] = c[k]
        inner[C_MG + k] = m[k] * g32[k]
        outer[C_LEFT + k] = left[k]
        outer[C_RIGHT + k] = right[k]
    vh = [wh[k] * g32[k] for k in range(NI)]
    vt = [wt[k] * g32[k] for k in range(NI)]

    def spread(v, j):
        terms = [D6[q + 3] * v[j - q] for q in range(-3, 4) if 0 <= j - q < NI]
        total = terms[0]
        for t in terms[1:]:
            total = total + t
        return total

    edge = [-alpha[0] * wh[0], -alpha[NI - 1] * wh[NI - 1], -alpha[0] * wt[0], -alpha[NI - 1] * wt[NI - 1]]
    low = [spread(v, q - 3) for v in (vh, vt) for q in range(3)]
    high = [spread(v, NI + q) for v in (vh, vt) for q in range(3)]
    edge += [jnp.where(core == 0, h, l) for h, l in zip(high, low)]
    edge += [jnp.where(core == 0, l, h) for h, l in zip(high, low)]
    for q in range(3):
        outer[C_FAR + q] = jnp.where(core == 0, edge[13 + q], edge[10 + q])
    for k, t in enumerate(edge):
        mine[pl.ds(EDGE + k, 1), :] = t[0:1]
        send[pl.ds(EDGE + k, 1), :] = t[0:1]

    first = jnp.where(piece == 0, 1.0 / 36.0, 0.0).astype(F32)
    last = jnp.where(piece == PIECES - 1, -1.0 / 36.0, 0.0).astype(F32)
    inv = CS["inv"]
    fh = [flux_weight(0, j) for j in range(NI)]
    ft = [flux_weight(NI - 1, j) for j in range(NI)]
    fh[0] = (fh[0] - BETA) + float(inv[0, 0]) * first
    ft[0] = ft[0] + float(inv[NI - 1, 0]) * first
    fh[NI - 1] = fh[NI - 1] + float(inv[0, NI - 1]) * last
    ft[NI - 1] = (ft[NI - 1] + BETA) + float(inv[NI - 1, NI - 1]) * last

    for i in range(NI):
        own[i] = spread(vh, i)
        own[NI + i] = spread(vt, i)

    s_in, s_out = (NI - 3) * (1 - core), (NI - 3) * core
    for v in range(NV):
        for c in loads[v]:
            c.wait()
        for out, half in ((mine, core), (send, 1 - core)):
            for r in range(HALF // SUB):
                rows = pl.ds(pl.multiple_of(HALF * half + SUB * r, SUB), SUB)
                sums = [None] * 4
                for i in range(NI):
                    a, z = s[v, i, rows, :], f[v, i, rows, :]
                    terms = (own[i] * a, own[NI + i] * a, fh[i] * z, ft[i] * z)
                    sums = [t if o is None else o + t for o, t in zip(sums, terms)]
                faces = [s[v, s_in + k, rows, :] for k in range(3)] + [s[v, s_out + k, rows, :] for k in range(3)]
                for k, t in enumerate(sums + faces):
                    out[pl.ds((NV * k + v) * HALF + SUB * r, SUB), :] = t


def own_share(gap, state, flux_x):
    vmem, hbm = pl.BlockSpec(memory_space=pltpu.VMEM), pl.BlockSpec(memory_space=pltpu.HBM)
    coef = jax.ShapeDtypeStruct((2 * NI, SUB, NK), F32)
    coef_far = jax.ShapeDtypeStruct((2 * NI + 3, SUB, NK), F32)
    values = jax.ShapeDtypeStruct((EDGE + 16, NK), F32)
    return pl.pallas_call(
        own_body,
        out_shape=(coef, coef_far, values, values),
        in_specs=[hbm, hbm, hbm],
        out_specs=(vmem,) * 4,
        scratch_shapes=[
            pltpu.SMEM((NI,), F32),
            pltpu.VMEM((NV, NI, NJ, NK), F32),
            pltpu.VMEM((NV, NI, NJ, NK), F32),
            pltpu.VMEM((2 * NI, SUB, NK), F32),
            pltpu.SemaphoreType.DMA,
            pltpu.SemaphoreType.DMA((2, NV)),
        ],
        compiler_params=pltpu.CompilerParams(vmem_limit_bytes=12 << 20),
        cost_estimate=pl.CostEstimate(flops=1 << 24, bytes_accessed=4 << 20, transcendentals=0),
        name="own_share",
    )(*in_hbm(gap, state, flux_x))


def pair_body(mine, got, out_hbm, mids, out, sem):
    is0 = parity("gx") == 0

    def both(rows):
        x, y = mine[rows, :], got[rows, :]
        return jnp.where(is0, x, y), jnp.where(is0, y, x)

    ca, cb = zip(*(both(pl.ds(EDGE + k, 1)) for k in range(16)))
    ca, cb = ([jnp.broadcast_to(t, (SUB, NK)) for t in c] for c in (ca, cb))
    hla, hra, tla, tra = ca[:4]
    hlb, hrb, tlb, trb = cb[:4]
    inv = 1.0 / (1.0 - tra * hlb)
    down = [hlb * tla * inv, hrb * inv, tla * inv, tra * hrb * inv, hlb * inv, inv, tra * inv]
    for k, t in enumerate(down):
        mids[pl.ds(4 * NV * HALF + k, 1), :] = t[0:1]
    cross_h, cross_t = hra * inv, tlb * inv
    edge = [hla + hra * down[0], hra * down[1], tlb * down[2], trb + tlb * down[3]]
    edge += [ca[10 + q] + (cross_h * hlb) * ca[13 + q] for q in range(3)]
    edge += [cross_t * ca[13 + q] for q in range(3)]
    edge += [cross_h * cb[10 + q] for q in range(3)]
    edge += [cb[13 + q] + (cross_t * tra) * cb[10 + q] for q in range(3)]
    lane = lax.broadcasted_iota(jnp.int32, (SUB, NK), 1)
    packed = jnp.zeros((SUB, NK), F32)
    for k, t in enumerate(edge):
        packed = jnp.where(lane == k, t, packed)

    k = CS["pair"]
    blocks = [pl.ds(WIDE * SUB * r, WIDE * SUB) for r in range(HALF // SUB)]
    stores = [pltpu.make_async_copy(out.at[b], out_hbm.at[b], sem.at[r]) for r, b in enumerate(blocks)]
    for r in range(HALF // SUB):
        at = WIDE * SUB * r
        out[pl.ds(at + VALUES * NV, SUB, stride=WIDE), :] = packed
        for v in range(NV):
            a, b = zip(*(both(pl.ds((NV * e + v) * HALF + SUB * r, SUB)) for e in range(VALUES)))
            ha, ta, hb, tb = a[0], a[1], b[0], b[1]
            for q in range(3):
                ha, ta = ha + ca[4 + q] * b[4 + q], ta + ca[7 + q] * b[4 + q]
                hb, tb = hb + cb[4 + q] * a[4 + q], tb + cb[7 + q] * a[4 + q]
            head = (hb + hlb * ta) * inv
            tail = (ta + tra * hb) * inv
            da, ea, db, eb = a[2], a[3], b[2], b[3]
            dhead = k["inv"] * db + k["inv_hl"] * ea
            dtail = k["inv"] * ea + k["inv_tr"] * db
            values = [ha + hra * head, tb + tlb * tail, da + float(CS["hr"]) * dhead, eb + float(CS["tl"]) * dtail]
            values += list(a[7:10]) + list(b[7:10])
            for e, t in enumerate(values):
                out[pl.ds(at + NV * e + v, SUB, stride=WIDE), :] = t
            for e, t in enumerate((head, tail, dhead, dtail)):
                mids[pl.ds((NV * e + v) * HALF + SUB * r, SUB), :] = t
        stores[r].start()
    for c in stores:
        c.wait()


def pair(mine, got):
    vmem = pl.BlockSpec(memory_space=pltpu.VMEM)
    return pl.pallas_call(
        pair_body,
        out_shape=(
            jax.ShapeDtypeStruct((PAIRS * WIDE, NK), F32),
            jax.ShapeDtypeStruct((4 * NV * HALF + SUB, NK), F32),
        ),
        in_specs=[vmem] * 2,
        out_specs=(pl.BlockSpec(memory_space=pltpu.HBM), vmem),
        scratch_shapes=[pltpu.VMEM((PAIRS * WIDE, NK), F32), pltpu.SemaphoreType.DMA((HALF // SUB,))],
        compiler_params=pltpu.CompilerParams(vmem_limit_bytes=8 << 20),
        cost_estimate=pl.CostEstimate(flops=1 << 20, bytes_accessed=1 << 20, transcendentals=0),
        name="pair",
    )(mine, got)


def join_body(x, out_hbm, out, coef, sem):
    for r in range(PAIRS // SUB):
        packed = x[pl.ds(WIDE * SUB * r + VALUES * NV, SUB, stride=WIDE), :]
        for k in range(16):
            coef[pl.ds(PAIRS * k + SUB * r, SUB), :] = jnp.broadcast_to(packed[:, k : k + 1], (SUB, NK))

    def row(p, k):
        return jnp.broadcast_to(coef[pl.ds(PAIRS * k + p, 1), :], (NV, NK))

    def value(p, k):
        return x[pl.ds(WIDE * p + NV * k, NV), :]

    c = CS["pair"]
    head_f, tail_f, head_d, tail_d = [], [], [], []
    for p in range(PAIRS):
        h, t, dh, dt = (value(p, k) for k in range(4))
        if p:
            for q in range(3):
                z = value(p - 1, 7 + q)
                h, t = h + row(p, 4 + q) * z, t + row(p, 7 + q) * z
        if p < PAIRS - 1:
            for q in range(3):
                z = value(p + 1, 4 + q)
                h, t = h + row(p, 10 + q) * z, t + row(p, 13 + q) * z
        head_f.append(h)
        tail_f.append(t)
        head_d.append(dh)
        tail_d.append(dt)

    scale = 8.0
    num, den = [None] * PAIRS, [None] * PAIRS
    hl, hr, tl, tr = ([row(p, k) for p in range(PAIRS)] for k in range(4))
    num[0], den[0] = tr[0], jnp.ones((NV, NK), F32)
    for p in range(1, PAIRS):
        cross = tl[p] * hr[p] - tr[p] * hl[p]
        num[p] = (scale * tr[p]) * den[p - 1] + (scale * cross) * num[p - 1]
        den[p] = scale * den[p - 1] - (scale * hl[p]) * num[p - 1]
    inv = [None] + [1.0 / den[p] for p in range(1, PAIRS)]
    e = [num[0]] + [num[p] * inv[p] for p in range(1, PAIRS)]
    keep = [None] + [(scale * den[p - 1]) * inv[p] for p in range(1, PAIRS)]

    fwd_f, fwd_d = [tail_f[0]], [tail_d[0]]
    chl, chr_, ctl, ce = c["hl"], c["hr"], c["tl"], c["e"]
    for p in range(1, PAIRS):
        a = tl[p] * keep[p]
        fwd_f.append((tail_f[p] + (a * e[p - 1]) * head_f[p]) + a * fwd_f[-1])
        k = ctl / (1.0 - chl * ce[p - 1])
        fwd_d.append((tail_d[p] + float(k * ce[p - 1]) * head_d[p]) + float(k) * fwd_d[-1])

    blocks = [pl.ds(ROWS * SUB * r, ROWS * SUB) for r in range(PAIRS // SUB)]
    stores = [pltpu.make_async_copy(out.at[b], out_hbm.at[b], sem.at[r]) for r, b in enumerate(blocks)]
    zero = jnp.zeros((NV, NK), F32)
    right_f, right_d = zero, zero
    for p in range(PAIRS - 1, -1, -1):
        if p:
            h = keep[p]
            at_f = (head_f[p] + hl[p] * fwd_f[p - 1]) * h + (hr[p] * h) * right_f
            left_f = fwd_f[p - 1] + e[p - 1] * at_f
            k = 1.0 / (1.0 - chl * ce[p - 1])
            at_d = (float(k) * head_d[p] + float(k * chl) * fwd_d[p - 1]) + float(k * chr_) * right_d
            left_d = fwd_d[p - 1] + float(ce[p - 1]) * at_d
        else:
            at_f = at_d = left_f = left_d = zero
        for k, val in enumerate((left_f, right_f, left_d, right_d)):
            out[pl.ds(ROWS * p + NV * k, NV), :] = val
        right_f, right_d = at_f, at_d
        if p % SUB == 0:
            stores[p // SUB].start()
    for t in stores:
        t.wait()


def join(x):
    vmem = pl.BlockSpec(memory_space=pltpu.VMEM)
    return pl.pallas_call(
        join_body,
        out_shape=jax.ShapeDtypeStruct((PAIRS * ROWS, NK), F32),
        in_specs=[vmem],
        out_specs=pl.BlockSpec(memory_space=pltpu.HBM),
        scratch_shapes=[
            pltpu.VMEM((PAIRS * ROWS, NK), F32),
            pltpu.VMEM((16 * PAIRS, NK), F32),
            pltpu.SemaphoreType.DMA((PAIRS // SUB,)),
        ],
        compiler_params=pltpu.CompilerParams(vmem_limit_bytes=8 << 20),
        cost_estimate=pl.CostEstimate(flops=1 << 20, bytes_accessed=1 << 20, transcendentals=0),
        name="join",
    )(x)


def far_body(outer, two, own, other):
    core = parity("gx")
    for out, half in ((own, core), (other, 1 - core)):
        for v in range(NV):
            for r in range(HALF // SUB):
                rows = pl.ds(pl.multiple_of(HALF * half + SUB * r, SUB), SUB)
                a = [two[v, k, rows, :] for k in range(3)]
                out[pl.ds(v * HALF + SUB * r, SUB), :] = (
                    outer[C_FAR] * a[0] + outer[C_FAR + 1] * a[1] + outer[C_FAR + 2] * a[2]
                )


def far(outer, two):
    vmem = pl.BlockSpec(memory_space=pltpu.VMEM)
    out = jax.ShapeDtypeStruct((NV * HALF, NK), F32)
    return pl.pallas_call(
        far_body,
        out_shape=(out, out),
        in_specs=[vmem] * 2,
        out_specs=(vmem,) * 2,
        compiler_params=pltpu.CompilerParams(vmem_limit_bytes=8 << 20),
        cost_estimate=pl.CostEstimate(flops=1 << 18, bytes_accessed=1 << 19, transcendentals=0),
        name="far",
    )(outer, two)


def split_body(z, mids, far_own, far_other, own, send):
    is0 = parity("gx") == 0
    c = CS["pair"]
    down = [jnp.broadcast_to(mids[pl.ds(4 * NV * HALF + k, 1), :], (SUB, NK)) for k in range(7)]
    head_far, tail_far = jnp.where(is0, down[4], down[5]), jnp.where(is0, down[5], down[6])
    for r in range(HALF // SUB):
        for v in range(NV):
            lf, rf, ld, rd = (z[pl.ds(ROWS * SUB * r + NV * k + v, SUB, stride=ROWS), :] for k in range(4))
            head, tail, dhead, dtail = (mids[pl.ds((NV * k + v) * HALF + SUB * r, SUB), :] for k in range(4))
            part = pl.ds(v * HALF + SUB * r, SUB)
            w = far_own[part, :]
            head = (head + head_far * w) + down[0] * lf + down[1] * rf
            tail = (tail + tail_far * w) + down[2] * lf + down[3] * rf
            dhead = dhead + c["down"][0] * ld + c["down"][1] * rd
            dtail = dtail + c["down"][2] * ld + c["down"][3] * rd
            a, b = (lf, head, ld, dhead), (tail, rf, dtail, rd)
            for k in range(4):
                rows = pl.ds((NV * k + v) * HALF + SUB * r, SUB)
                own[rows, :] = jnp.where(is0, a[k], b[k])
                send[rows, :] = jnp.where(is0, b[k], a[k])
            send[pl.ds((4 * NV + v) * HALF + SUB * r, SUB), :] = far_other[part, :]


def split(z, mids, far_own, far_other):
    vmem = pl.BlockSpec(memory_space=pltpu.VMEM)
    own = jax.ShapeDtypeStruct((4 * NV * HALF, NK), F32)
    send = jax.ShapeDtypeStruct((5 * NV * HALF, NK), F32)
    return pl.pallas_call(
        split_body,
        out_shape=(own, send),
        in_specs=[vmem] * 4,
        out_specs=(vmem,) * 2,
        compiler_params=pltpu.CompilerParams(vmem_limit_bytes=8 << 20),
        cost_estimate=pl.CostEstimate(flops=1 << 20, bytes_accessed=1 << 20, transcendentals=0),
        name="split",
    )(z, mids, far_own, far_other)


def block_body(inner, s_hbm, f_hbm, fy_hbm, one, two, yone, ytwo, mx, my, base, mxb, s, f, fy, pad, sem):
    moves = ((fy_hbm, fy), (s_hbm, s), (f_hbm, f))
    for v in range(NV):
        for k, (h, t) in enumerate(moves):
            pltpu.make_async_copy(h.at[v], t.at[v], sem.at[k, v]).start()
    piece = lax.axis_index("gx")
    is0 = parity("gx") == 0
    even = parity("gy") == 0
    first = jnp.where(piece == 0, 1.0 / 36.0, 0.0).astype(F32)
    last = jnp.where(piece == PIECES - 1, -1.0 / 36.0, 0.0).astype(F32)
    mxt = jnp.transpose(mx[...] * -0.5)
    myt = jnp.transpose(my[...] * -0.5)
    for i in range(NI):
        mxb[i] = jnp.broadcast_to(mxt[:, i : i + 1], (NJ, NK))
        pad[NI + i, 0:NJ, :] = jnp.broadcast_to(myt[:, i : i + 1], (NJ, NK))

    @pl.loop(0, NV)
    def _(v):
        for k, (h, t) in enumerate(moves):
            pltpu.make_async_copy(h.at[v], t.at[v], sem.at[k, v]).wait()
        for i in range(NI):
            for q in range(NJ // SUB):
                pad[i, pl.ds(SUB + SUB * q, SUB), :] = fy[v, i, pl.ds(SUB * q, SUB), :]
            part = pl.ds(4 * (i % 2), 4)
            a, b = yone[v, i // 2, part, :], ytwo[v, i // 2, part, :]
            pad[i, SUB - 4 : SUB, :] = jnp.where(even, b, a)
            pad[i, SUB + NJ : SUB + NJ + 4, :] = jnp.where(even, a, b)

        for q in range(NJ // SUB):
            rows = pl.ds(SUB * q, SUB)
            a = [one[v, k, rows, :] for k in range(4)]
            b = [two[v, k, rows, :] for k in range(4)]
            low = [jnp.where(is0, b[k], a[k]) for k in range(4)]
            high = [jnp.where(is0, a[k], b[k]) for k in range(4)]
            st = low[:3] + [s[v, i, rows, :] for i in range(NI)] + high[:3]
            fl = [low[3]] + [f[v, i, rows, :] for i in range(NI)] + [high[3]]
            ye, yd, us = [], [], []
            for i in range(NI):
                d6 = (
                    (st[i] + st[i + 6])
                    - 6.0 * (st[i + 1] + st[i + 5])
                    + 15.0 * (st[i + 2] + st[i + 4])
                    - 20.0 * st[i + 3]
                )
                y = inner[C_MG + i] * d6
                ye.append(y - inner[C_C + i] * ye[-1] if i else y)
                u = fl[i + 2] - fl[i]
                us.append(u)
                r = fl[2] if i == 0 else -fl[NI - 1] if i == NI - 1 else u
                r = float(RHO * CS["m"][i]) * r
                if i == 0:
                    r = r + (first * float(CS["m"][i])) * fl[1]
                if i == NI - 1:
                    r = r + (last * float(CS["m"][i])) * fl[NI]
                yd.append(r - float(CS["c"][i]) * yd[-1] if i else r)
            xe = xd = None
            for i in range(NI - 1, -1, -1):
                xe = ye[i] if xe is None else ye[i] - inner[C_C + i] * xe
                xd = yd[i] if xd is None else yd[i] - float(CS["c"][i]) * xd
                at = SUB + SUB * q
                dy = None
                for k, w in enumerate(Y_WEIGHTS, start=1):
                    t = w * (pad[i, pl.ds(at + k, SUB), :] - pad[i, pl.ds(at - k, SUB), :])
                    dy = t if dy is None else dy + t
                d = us[i] * (1.0 / 12.0) + xd
                base[v, i, rows, :] = (st[i + 3] + xe) + (mxb[i, rows, :] * d + pad[NI + i, rows, :] * dy)


def block(inner, state, flux_x, flux_y, one, two, yone, ytwo, mx, my):
    vmem, hbm = pl.BlockSpec(memory_space=pltpu.VMEM), pl.BlockSpec(memory_space=pltpu.HBM)
    return pl.pallas_call(
        block_body,
        out_shape=(
            jax.ShapeDtypeStruct((NV, NI, NJ, NK), F32),
            jax.ShapeDtypeStruct((NI, NJ, NK), F32),
        ),
        in_specs=[vmem] + [hbm] * 3 + [vmem] * 6,
        out_specs=(vmem, vmem),
        scratch_shapes=[pltpu.VMEM((NV, NI, NJ, NK), F32)] * 3
        + [pltpu.VMEM((2 * NI, SUB + NJ + SUB, NK), F32), pltpu.SemaphoreType.DMA((3, NV))],
        compiler_params=pltpu.CompilerParams(vmem_limit_bytes=16 << 20),
        cost_estimate=pl.CostEstimate(flops=1 << 30, bytes_accessed=64 << 20, transcendentals=0),
        name="block",
    )(inner, *in_hbm(state, flux_x, flux_y), one, two, yone, ytwo, mx, my)


def add_outside(v, half, r, outer, base, mxb, values, out):
    rows = pl.ds(pl.multiple_of(HALF * half + SUB * r, SUB), SUB)
    lf, rf, ld, rd = values
    for i in range(NI):
        d = float(CS["left"][i]) * ld + float(CS["right"][i]) * rd
        e = outer[C_LEFT + i] * lf + outer[C_RIGHT + i] * rf
        out[v, i, rows, :] = (base[v, i, rows, :] + e) + mxb[i, rows, :] * d


def finish_own_body(outer, base, mxb, own, out):
    core = parity("gx")
    for v in range(NV):
        for r in range(HALF // SUB):
            values = [own[pl.ds((NV * k + v) * HALF + SUB * r, SUB), :] for k in range(4)]
            add_outside(v, core, r, outer, base, mxb, values, out)


def finish_own(outer, base, mxb, own):
    vmem = pl.BlockSpec(memory_space=pltpu.VMEM)
    return pl.pallas_call(
        finish_own_body,
        out_shape=jax.ShapeDtypeStruct((NV, NI, NJ, NK), F32),
        in_specs=[vmem] * 4,
        out_specs=vmem,
        input_output_aliases={1: 0},
        compiler_params=pltpu.CompilerParams(vmem_limit_bytes=12 << 20),
        cost_estimate=pl.CostEstimate(flops=1 << 22, bytes_accessed=2 << 20, transcendentals=0),
        name="finish_own",
    )(outer, base, mxb, own)


def finish_body(outer, base, mxb, got, mids, far_other, out_hbm, out, sem):
    core = parity("gx")
    is0 = core == 0
    hl_inv, inv, tr_inv = (jnp.broadcast_to(mids[pl.ds(4 * NV * HALF + k, 1), :], (SUB, NK)) for k in (4, 5, 6))
    zero = jnp.zeros((SUB, NK), F32)
    got_far = (jnp.where(is0, zero, tr_inv), jnp.where(is0, hl_inv, zero))
    side = jnp.where(is0, C_RIGHT, C_LEFT)
    stores = [pltpu.make_async_copy(out.at[v], out_hbm.at[v], sem.at[v]) for v in range(NV)]
    for v in range(NV):
        for r in range(HALF // SUB):
            rows = pl.ds(pl.multiple_of(HALF * core + SUB * r, SUB), SUB)
            w = inv * got[pl.ds((4 * NV + v) * HALF + SUB * r, SUB), :]
            for i in range(NI):
                out[v, i, rows, :] = base[v, i, rows, :] + outer[side + i] * w
            lf, rf, ld, rd = (got[pl.ds((NV * k + v) * HALF + SUB * r, SUB), :] for k in range(4))
            w = far_other[pl.ds(v * HALF + SUB * r, SUB), :]
            values = (lf + got_far[0] * w, rf + got_far[1] * w, ld, rd)
            add_outside(v, 1 - core, r, outer, base, mxb, values, out)
        stores[v].start()
    for c in stores:
        c.wait()


def finish(outer, base, mxb, got, mids, far_other):
    return pl.pallas_call(
        finish_body,
        out_shape=jax.ShapeDtypeStruct((NV, NI, NJ, NK), F32),
        in_specs=[pl.BlockSpec(memory_space=pltpu.VMEM)] * 6,
        out_specs=pl.BlockSpec(memory_space=pltpu.HBM),
        scratch_shapes=[pltpu.VMEM((NV, NI, NJ, NK), F32), pltpu.SemaphoreType.DMA((NV,))],
        compiler_params=pltpu.CompilerParams(vmem_limit_bytes=12 << 20),
        cost_estimate=pl.CostEstimate(flops=1 << 22, bytes_accessed=3 << 20, transcendentals=0),
        name="finish",
    )(outer, base, mxb, got, mids, far_other)


def exchange(x, rows):
    groups = [[2 * p + c for p in range(PAIRS)] for c in range(2)]
    y = lax.all_to_all(x.reshape(PAIRS, rows, NK), "gx", 0, 0, tiled=True, axis_index_groups=groups)
    return y.reshape(PAIRS * rows, NK)


def per_device(flux_x, flux_y, state, metric_x, metric_y, filter_gap):
    count_y = lax.axis_size("gy")
    pair_in = [(i, i ^ 1) for i in range(PIECES)]
    pair_out = [(i, i + 1 if i % 2 else i - 1) for i in range(1, PIECES - 1)]
    y_in = [(i, i ^ 1) for i in range(count_y)]
    y_out = [(i, (i + 1 if i % 2 else i - 1) % count_y) for i in range(count_y)]

    inner, outer, mine, send = own_share(filter_gap, state, flux_x)
    send, state, flux_x, flux_y = lax.optimization_barrier((send, state, flux_x, flux_y))
    got = lax.ppermute(send, "gx", pair_in)
    got, *faces = lax.optimization_barrier((got, *pack(state, flux_x, flux_y)))
    ends, mids = pair(mine, got)
    ends, send_one, send_two, ysend_one, ysend_two = lax.optimization_barrier((ends, *faces))
    ends = exchange(ends, WIDE)
    one = lax.ppermute(send_one, "gx", pair_in)
    two = lax.ppermute(send_two, "gx", pair_out)
    yone = lax.ppermute(ysend_one, "gy", y_in)
    ytwo = lax.ppermute(ysend_two, "gy", y_out)
    outside = join(ends)
    outside, one = lax.optimization_barrier((outside, one))
    two, yone, ytwo = lax.optimization_barrier((two, yone, ytwo))
    far_own, far_other = far(outer, two)
    base, mxb = block(inner, state, flux_x, flux_y, one, two, yone, ytwo, metric_x, metric_y)
    outside, base, mxb, far_own = lax.optimization_barrier((exchange(outside, ROWS), base, mxb, far_own))
    own, send = split(outside, mids, far_own, far_other)
    got = lax.ppermute(send, "gx", pair_in)
    got, base = lax.optimization_barrier((got, finish_own(outer, base, mxb, own)))
    return finish(outer, base, mxb, got, mids, far_other)


def solution(mesh):
    return jax.shard_map(
        per_device,
        mesh=mesh,
        in_specs=(
            P(None, "gx", "gy", None),
            P(None, "gx", "gy", None),
            P(None, "gx", "gy", None),
            P("gx", "gy"),
            P("gx", "gy"),
            P("gx"),
        ),
        out_specs=P(None, "gx", "gy", None),
        check_vma=False,
    )
```

```python
import jax
import jax.numpy as jnp
import numpy as np
from jax import lax
from jax.experimental import pallas as pl
from jax.experimental.pallas import tpu as pltpu
from jax.sharding import PartitionSpec as P

NV, NI, NJ, NK = 5, 16, 32, 128
PIECES, PAIRS, HALF = 32, 16, 16
VALUES = 10
ROWS, WIDE = 24, 56
EDGE = VALUES * NV * HALF
SUB = 8
F32 = jnp.float32
Y_WEIGHTS = (4.0 / 5.0, -1.0 / 5.0, 4.0 / 105.0, -1.0 / 280.0)
RHO = 25.0 / 36.0
BETA = 3.0 * RHO
D6 = (1.0, -6.0, 15.0, -20.0, 15.0, -6.0, 1.0)

C_C, C_MG = 0, NI
C_LEFT, C_RIGHT, C_FAR = 0, NI, 2 * NI


def constant_system():
    a = 1.0 / 3.0
    t = np.eye(NI) + a * (np.eye(NI, k=1) + np.eye(NI, k=-1))
    inv = np.linalg.inv(t)
    m, c = [], []
    prev = 0.0
    for _ in range(NI):
        m.append(1.0 / (1.0 - a * prev))
        prev = a * m[-1]
        c.append(prev)
    left, right = -a * inv[:, 0], -a * inv[:, -1]
    hl, hr, tl, tr = left[0], right[0], left[-1], right[-1]
    d = 1.0 / (1.0 - tr * hl)
    pair = dict(inv=d, inv_hl=d * hl, inv_tr=d * tr, down=[hl * tl * d, hr * d, tl * d, tr * hr * d])
    for k in pair:
        pair[k] = [float(t) for t in pair[k]] if isinstance(pair[k], list) else float(pair[k])
    p = dict(hl=hl + hr * hl * tl * d, hr=hr * hr * d, tl=tl * tl * d, tr=tr + tl * tr * hr * d)
    e = [p["tr"]]
    for _ in range(PAIRS - 1):
        e.append(p["tr"] + p["tl"] * p["hr"] * e[-1] / (1.0 - p["hl"] * e[-1]))
    pair.update(p, e=e)
    return dict(m=m, c=c, inv=inv, left=left, right=right, hl=hl, hr=hr, tl=tl, tr=tr, pair=pair)


CS = constant_system()


def flux_weight(row, j):
    w = CS["inv"][row]
    lo = w[j - 1] if 0 <= j - 1 < NI else 0.0
    hi = w[j + 1] if 0 <= j + 1 < NI else 0.0
    return float(RHO * (lo - hi))


def splat(x):
    return jnp.full((SUB, NK), x, F32)


def in_hbm(*arrays):
    return tuple(pltpu.with_memory_space_constraint(a, pltpu.HBM) for a in arrays)


def parity(name):
    return lax.rem(lax.axis_index(name), 2)


def pack_body(s, f, fy, one, two, yone, ytwo, lo, hi, sem):
    core, odd = parity("gx"), parity("gy")
    copies = [
        pltpu.make_async_copy(fy.at[:, :, 0:SUB, :], lo, sem.at[0]),
        pltpu.make_async_copy(fy.at[:, :, NJ - SUB : NJ, :], hi, sem.at[1]),
    ]
    for c in copies:
        c.start()

    def faces(right, left):
        moves = [
            pltpu.make_async_copy(s.at[:, NI - 3 : NI], right.at[:, 0:3], sem.at[2]),
            pltpu.make_async_copy(f.at[:, NI - 1 : NI], right.at[:, 3:4], sem.at[3]),
            pltpu.make_async_copy(s.at[:, 0:3], left.at[:, 0:3], sem.at[4]),
            pltpu.make_async_copy(f.at[:, 0:1], left.at[:, 3:4], sem.at[5]),
        ]
        for c in moves:
            c.start()
        for c in moves:
            c.wait()

    def rows(top, bottom):
        for v in range(NV):
            for i in range(NI):
                part = pl.ds(4 * (i % 2), 4)
                top[v, i // 2, part, :] = hi[v, i, 4:8, :]
                bottom[v, i // 2, part, :] = lo[v, i, 0:4, :]

    @pl.when(core == 0)
    def _():
        faces(one, two)

    @pl.when(core == 1)
    def _():
        faces(two, one)

    for c in copies:
        c.wait()

    @pl.when(odd == 0)
    def _():
        rows(yone, ytwo)

    @pl.when(odd == 1)
    def _():
        rows(ytwo, yone)


def pack(state, flux_x, flux_y):
    x_out = jax.ShapeDtypeStruct((NV, 4, NJ, NK), F32)
    y_out = jax.ShapeDtypeStruct((NV, NI // 2, SUB, NK), F32)
    return pl.pallas_call(
        pack_body,
        out_shape=(x_out, x_out, y_out, y_out),
        in_specs=[pl.BlockSpec(memory_space=pltpu.HBM)] * 3,
        out_specs=(pl.BlockSpec(memory_space=pltpu.VMEM),) * 4,
        scratch_shapes=[
            pltpu.VMEM((NV, NI, SUB, NK), F32),
            pltpu.VMEM((NV, NI, SUB, NK), F32),
            pltpu.SemaphoreType.DMA((6,)),
        ],
        compiler_params=pltpu.CompilerParams(vmem_limit_bytes=8 << 20),
        cost_estimate=pl.CostEstimate(flops=0, bytes_accessed=2 << 20, transcendentals=0),
        name="pack",
    )(*in_hbm(state, flux_x, flux_y))


def own_body(gap_hbm, s_hbm, f_hbm, inner, outer, mine, send, gap, s, f, own, gap_sem, sem):
    gap_load = pltpu.make_async_copy(gap_hbm, gap, gap_sem)
    gap_load.start()
    loads = [
        (
            pltpu.make_async_copy(s_hbm.at[v], s.at[v], sem.at[0, v]),
            pltpu.make_async_copy(f_hbm.at[v], f.at[v], sem.at[1, v]),
        )
        for v in range(NV)
    ]
    for both in loads:
        for c in both:
            c.start()
    core = parity("gx")
    piece = lax.axis_index("gx")
    gap_load.wait()
    alpha = [0.5 - splat(gap[i]) for i in range(NI)]
    g32 = [(0.5 - a) * (1.0 / 32.0) for a in alpha]
    m, c = [None] * NI, [None] * NI
    n, b = [None] * NI, [None] * NI
    for k in range(NI):
        m[k] = 1.0 / (1.0 - alpha[k] * c[k - 1]) if k else jnp.ones((SUB, NK), F32)
        c[k] = alpha[k] * m[k]
        r = NI - 1 - k
        n[r] = 1.0 / (1.0 - alpha[r] * b[r + 1]) if k else jnp.ones((SUB, NK), F32)
        b[r] = alpha[r] * n[r]
    left, right = [None] * NI, [None] * NI
    wh, wt = [None] * NI, [None] * NI
    left[0], right[NI - 1] = -b[0], -c[NI - 1]
    qh, qt = None, None
    for k in range(NI):
        r = NI - 1 - k
        if k:
            left[k] = -b[k] * left[k - 1]
            right[r] = -c[r] * right[r + 1]
            qh = -b[k - 1] if qh is None else -b[k - 1] * qh
            qt = -c[r + 1] if qt is None else -c[r + 1] * qt
            wh[k] = qh * n[k]
            wt[r] = qt * m[r]
        else:
            wh[0], wt[NI - 1] = n[0], m[NI - 1]
    for k in range(NI):
        inner[C_C + k] = c[k]
        inner[C_MG + k] = m[k] * g32[k]
        outer[C_LEFT + k] = left[k]
        outer[C_RIGHT + k] = right[k]
    vh = [wh[k] * g32[k] for k in range(NI)]
    vt = [wt[k] * g32[k] for k in range(NI)]

    def spread(v, j):
        terms = [D6[q + 3] * v[j - q] for q in range(-3, 4) if 0 <= j - q < NI]
        total = terms[0]
        for t in terms[1:]:
            total = total + t
        return total

    edge = [-alpha[0] * wh[0], -alpha[NI - 1] * wh[NI - 1], -alpha[0] * wt[0], -alpha[NI - 1] * wt[NI - 1]]
    low = [spread(v, q - 3) for v in (vh, vt) for q in range(3)]
    high = [spread(v, NI + q) for v in (vh, vt) for q in range(3)]
    edge += [jnp.where(core == 0, h, l) for h, l in zip(high, low)]
    edge += [jnp.where(core == 0, l, h) for h, l in zip(high, low)]
    for q in range(3):
        outer[C_FAR + q] = jnp.where(core == 0, edge[13 + q], edge[10 + q])
    for k, t in enumerate(edge):
        mine[pl.ds(EDGE + k, 1), :] = t[0:1]
        send[pl.ds(EDGE + k, 1), :] = t[0:1]

    first = jnp.where(piece == 0, 1.0 / 36.0, 0.0).astype(F32)
    last = jnp.where(piece == PIECES - 1, -1.0 / 36.0, 0.0).astype(F32)
    inv = CS["inv"]
    fh = [flux_weight(0, j) for j in range(NI)]
    ft = [flux_weight(NI - 1, j) for j in range(NI)]
    fh[0] = (fh[0] - BETA) + float(inv[0, 0]) * first
    ft[0] = ft[0] + float(inv[NI - 1, 0]) * first
    fh[NI - 1] = fh[NI - 1] + float(inv[0, NI - 1]) * last
    ft[NI - 1] = (ft[NI - 1] + BETA) + float(inv[NI - 1, NI - 1]) * last

    for i in range(NI):
        own[i] = spread(vh, i)
        own[NI + i] = spread(vt, i)

    s_in, s_out = (NI - 3) * (1 - core), (NI - 3) * core
    for v in range(NV):
        for c in loads[v]:
            c.wait()
        for out, half in ((mine, core), (send, 1 - core)):
            for r in range(HALF // SUB):
                rows = pl.ds(pl.multiple_of(HALF * half + SUB * r, SUB), SUB)
                sums = [None] * 4
                for i in range(NI):
                    a, z = s[v, i, rows, :], f[v, i, rows, :]
                    terms = (own[i] * a, own[NI + i] * a, fh[i] * z, ft[i] * z)
                    sums = [t if o is None else o + t for o, t in zip(sums, terms)]
                faces = [s[v, s_in + k, rows, :] for k in range(3)] + [s[v, s_out + k, rows, :] for k in range(3)]
                for k, t in enumerate(sums + faces):
                    out[pl.ds((NV * k + v) * HALF + SUB * r, SUB), :] = t


def own_share(gap, state, flux_x):
    vmem, hbm = pl.BlockSpec(memory_space=pltpu.VMEM), pl.BlockSpec(memory_space=pltpu.HBM)
    coef = jax.ShapeDtypeStruct((2 * NI, SUB, NK), F32)
    coef_far = jax.ShapeDtypeStruct((2 * NI + 3, SUB, NK), F32)
    values = jax.ShapeDtypeStruct((EDGE + 16, NK), F32)
    return pl.pallas_call(
        own_body,
        out_shape=(coef, coef_far, values, values),
        in_specs=[hbm, hbm, hbm],
        out_specs=(vmem,) * 4,
        scratch_shapes=[
            pltpu.SMEM((NI,), F32),
            pltpu.VMEM((NV, NI, NJ, NK), F32),
            pltpu.VMEM((NV, NI, NJ, NK), F32),
            pltpu.VMEM((2 * NI, SUB, NK), F32),
            pltpu.SemaphoreType.DMA,
            pltpu.SemaphoreType.DMA((2, NV)),
        ],
        compiler_params=pltpu.CompilerParams(vmem_limit_bytes=12 << 20),
        cost_estimate=pl.CostEstimate(flops=1 << 24, bytes_accessed=4 << 20, transcendentals=0),
        name="own_share",
    )(*in_hbm(gap, state, flux_x))


def pair_body(mine, got, out_hbm, mids, out, sem):
    is0 = parity("gx") == 0

    def both(rows):
        x, y = mine[rows, :], got[rows, :]
        return jnp.where(is0, x, y), jnp.where(is0, y, x)

    ca, cb = zip(*(both(pl.ds(EDGE + k, 1)) for k in range(16)))
    ca, cb = ([jnp.broadcast_to(t, (SUB, NK)) for t in c] for c in (ca, cb))
    hla, hra, tla, tra = ca[:4]
    hlb, hrb, tlb, trb = cb[:4]
    inv = 1.0 / (1.0 - tra * hlb)
    down = [hlb * tla * inv, hrb * inv, tla * inv, tra * hrb * inv, hlb * inv, inv, tra * inv]
    for k, t in enumerate(down):
        mids[pl.ds(4 * NV * HALF + k, 1), :] = t[0:1]
    cross_h, cross_t = hra * inv, tlb * inv
    edge = [hla + hra * down[0], hra * down[1], tlb * down[2], trb + tlb * down[3]]
    edge += [ca[10 + q] + (cross_h * hlb) * ca[13 + q] for q in range(3)]
    edge += [cross_t * ca[13 + q] for q in range(3)]
    edge += [cross_h * cb[10 + q] for q in range(3)]
    edge += [cb[13 + q] + (cross_t * tra) * cb[10 + q] for q in range(3)]
    lane = lax.broadcasted_iota(jnp.int32, (SUB, NK), 1)
    packed = jnp.zeros((SUB, NK), F32)
    for k, t in enumerate(edge):
        packed = jnp.where(lane == k, t, packed)

    k = CS["pair"]
    blocks = [pl.ds(WIDE * SUB * r, WIDE * SUB) for r in range(HALF // SUB)]
    stores = [pltpu.make_async_copy(out.at[b], out_hbm.at[b], sem.at[r]) for r, b in enumerate(blocks)]
    for r in range(HALF // SUB):
        at = WIDE * SUB * r
        out[pl.ds(at + VALUES * NV, SUB, stride=WIDE), :] = packed
        for v in range(NV):
            a, b = zip(*(both(pl.ds((NV * e + v) * HALF + SUB * r, SUB)) for e in range(VALUES)))
            ha, ta, hb, tb = a[0], a[1], b[0], b[1]
            for q in range(3):
                ha, ta = ha + ca[4 + q] * b[4 + q], ta + ca[7 + q] * b[4 + q]
                hb, tb = hb + cb[4 + q] * a[4 + q], tb + cb[7 + q] * a[4 + q]
            head = (hb + hlb * ta) * inv
            tail = (ta + tra * hb) * inv
            da, ea, db, eb = a[2], a[3], b[2], b[3]
            dhead = k["inv"] * db + k["inv_hl"] * ea
            dtail = k["inv"] * ea + k["inv_tr"] * db
            values = [ha + hra * head, tb + tlb * tail, da + float(CS["hr"]) * dhead, eb + float(CS["tl"]) * dtail]
            values += list(a[7:10]) + list(b[7:10])
            for e, t in enumerate(values):
                out[pl.ds(at + NV * e + v, SUB, stride=WIDE), :] = t
            for e, t in enumerate((head, tail, dhead, dtail)):
                mids[pl.ds((NV * e + v) * HALF + SUB * r, SUB), :] = t
        stores[r].start()
    for c in stores:
        c.wait()


def pair(mine, got):
    vmem = pl.BlockSpec(memory_space=pltpu.VMEM)
    return pl.pallas_call(
        pair_body,
        out_shape=(
            jax.ShapeDtypeStruct((PAIRS * WIDE, NK), F32),
            jax.ShapeDtypeStruct((4 * NV * HALF + SUB, NK), F32),
        ),
        in_specs=[vmem] * 2,
        out_specs=(pl.BlockSpec(memory_space=pltpu.HBM), vmem),
        scratch_shapes=[pltpu.VMEM((PAIRS * WIDE, NK), F32), pltpu.SemaphoreType.DMA((HALF // SUB,))],
        compiler_params=pltpu.CompilerParams(vmem_limit_bytes=8 << 20),
        cost_estimate=pl.CostEstimate(flops=1 << 20, bytes_accessed=1 << 20, transcendentals=0),
        name="pair",
    )(mine, got)


def join_body(x, out_hbm, out, coef, sem):
    for r in range(PAIRS // SUB):
        packed = x[pl.ds(WIDE * SUB * r + VALUES * NV, SUB, stride=WIDE), :]
        for k in range(16):
            coef[pl.ds(PAIRS * k + SUB * r, SUB), :] = jnp.broadcast_to(packed[:, k : k + 1], (SUB, NK))

    def row(p, k):
        return jnp.broadcast_to(coef[pl.ds(PAIRS * k + p, 1), :], (NV, NK))

    def value(p, k):
        return x[pl.ds(WIDE * p + NV * k, NV), :]

    c = CS["pair"]
    head_f, tail_f, head_d, tail_d = [], [], [], []
    for p in range(PAIRS):
        h, t, dh, dt = (value(p, k) for k in range(4))
        if p:
            for q in range(3):
                z = value(p - 1, 7 + q)
                h, t = h + row(p, 4 + q) * z, t + row(p, 7 + q) * z
        if p < PAIRS - 1:
            for q in range(3):
                z = value(p + 1, 4 + q)
                h, t = h + row(p, 10 + q) * z, t + row(p, 13 + q) * z
        head_f.append(h)
        tail_f.append(t)
        head_d.append(dh)
        tail_d.append(dt)

    scale = 8.0
    num, den = [None] * PAIRS, [None] * PAIRS
    hl, hr, tl, tr = ([row(p, k) for p in range(PAIRS)] for k in range(4))
    num[0], den[0] = tr[0], jnp.ones((NV, NK), F32)
    for p in range(1, PAIRS):
        cross = tl[p] * hr[p] - tr[p] * hl[p]
        num[p] = (scale * tr[p]) * den[p - 1] + (scale * cross) * num[p - 1]
        den[p] = scale * den[p - 1] - (scale * hl[p]) * num[p - 1]
    inv = [None] + [1.0 / den[p] for p in range(1, PAIRS)]
    e = [num[0]] + [num[p] * inv[p] for p in range(1, PAIRS)]
    keep = [None] + [(scale * den[p - 1]) * inv[p] for p in range(1, PAIRS)]

    fwd_f, fwd_d = [tail_f[0]], [tail_d[0]]
    chl, chr_, ctl, ce = c["hl"], c["hr"], c["tl"], c["e"]
    for p in range(1, PAIRS):
        a = tl[p] * keep[p]
        fwd_f.append((tail_f[p] + (a * e[p - 1]) * head_f[p]) + a * fwd_f[-1])
        k = ctl / (1.0 - chl * ce[p - 1])
        fwd_d.append((tail_d[p] + float(k * ce[p - 1]) * head_d[p]) + float(k) * fwd_d[-1])

    blocks = [pl.ds(ROWS * SUB * r, ROWS * SUB) for r in range(PAIRS // SUB)]
    stores = [pltpu.make_async_copy(out.at[b], out_hbm.at[b], sem.at[r]) for r, b in enumerate(blocks)]
    zero = jnp.zeros((NV, NK), F32)
    right_f, right_d = zero, zero
    for p in range(PAIRS - 1, -1, -1):
        if p:
            h = keep[p]
            at_f = (head_f[p] + hl[p] * fwd_f[p - 1]) * h + (hr[p] * h) * right_f
            left_f = fwd_f[p - 1] + e[p - 1] * at_f
            k = 1.0 / (1.0 - chl * ce[p - 1])
            at_d = (float(k) * head_d[p] + float(k * chl) * fwd_d[p - 1]) + float(k * chr_) * right_d
            left_d = fwd_d[p - 1] + float(ce[p - 1]) * at_d
        else:
            at_f = at_d = left_f = left_d = zero
        for k, val in enumerate((left_f, right_f, left_d, right_d)):
            out[pl.ds(ROWS * p + NV * k, NV), :] = val
        right_f, right_d = at_f, at_d
        if p % SUB == 0:
            stores[p // SUB].start()
    for t in stores:
        t.wait()


def join(x):
    vmem = pl.BlockSpec(memory_space=pltpu.VMEM)
    return pl.pallas_call(
        join_body,
        out_shape=jax.ShapeDtypeStruct((PAIRS * ROWS, NK), F32),
        in_specs=[vmem],
        out_specs=pl.BlockSpec(memory_space=pltpu.HBM),
        scratch_shapes=[
            pltpu.VMEM((PAIRS * ROWS, NK), F32),
            pltpu.VMEM((16 * PAIRS, NK), F32),
            pltpu.SemaphoreType.DMA((PAIRS // SUB,)),
        ],
        compiler_params=pltpu.CompilerParams(vmem_limit_bytes=8 << 20),
        cost_estimate=pl.CostEstimate(flops=1 << 20, bytes_accessed=1 << 20, transcendentals=0),
        name="join",
    )(x)


def far_body(outer, two, own, other):
    core = parity("gx")
    for out, half in ((own, core), (other, 1 - core)):
        for v in range(NV):
            for r in range(HALF // SUB):
                rows = pl.ds(pl.multiple_of(HALF * half + SUB * r, SUB), SUB)
                a = [two[v, k, rows, :] for k in range(3)]
                out[pl.ds(v * HALF + SUB * r, SUB), :] = (
                    outer[C_FAR] * a[0] + outer[C_FAR + 1] * a[1] + outer[C_FAR + 2] * a[2]
                )


def far(outer, two):
    vmem = pl.BlockSpec(memory_space=pltpu.VMEM)
    out = jax.ShapeDtypeStruct((NV * HALF, NK), F32)
    return pl.pallas_call(
        far_body,
        out_shape=(out, out),
        in_specs=[vmem] * 2,
        out_specs=(vmem,) * 2,
        compiler_params=pltpu.CompilerParams(vmem_limit_bytes=8 << 20),
        cost_estimate=pl.CostEstimate(flops=1 << 18, bytes_accessed=1 << 19, transcendentals=0),
        name="far",
    )(outer, two)


def split_body(z, mids, far_own, far_got, own, send):
    is0 = parity("gx") == 0
    c = CS["pair"]
    down = [jnp.broadcast_to(mids[pl.ds(4 * NV * HALF + k, 1), :], (SUB, NK)) for k in range(7)]
    for r in range(HALF // SUB):
        for v in range(NV):
            lf, rf, ld, rd = (z[pl.ds(ROWS * SUB * r + NV * k + v, SUB, stride=ROWS), :] for k in range(4))
            head, tail, dhead, dtail = (mids[pl.ds((NV * k + v) * HALF + SUB * r, SUB), :] for k in range(4))
            part = pl.ds(v * HALF + SUB * r, SUB)
            x, y = far_own[part, :], far_got[part, :]
            fa, fb = jnp.where(is0, x, y), jnp.where(is0, y, x)
            head = (head + down[4] * fa + down[5] * fb) + down[0] * lf + down[1] * rf
            tail = (tail + down[5] * fa + down[6] * fb) + down[2] * lf + down[3] * rf
            dhead = dhead + c["down"][0] * ld + c["down"][1] * rd
            dtail = dtail + c["down"][2] * ld + c["down"][3] * rd
            a, b = (lf, head, ld, dhead), (tail, rf, dtail, rd)
            for k in range(4):
                rows = pl.ds((NV * k + v) * HALF + SUB * r, SUB)
                own[rows, :] = jnp.where(is0, a[k], b[k])
                send[rows, :] = jnp.where(is0, b[k], a[k])


def split(z, mids, far_own, far_got):
    vmem = pl.BlockSpec(memory_space=pltpu.VMEM)
    own = jax.ShapeDtypeStruct((4 * NV * HALF, NK), F32)
    send = jax.ShapeDtypeStruct((4 * NV * HALF, NK), F32)
    return pl.pallas_call(
        split_body,
        out_shape=(own, send),
        in_specs=[vmem] * 4,
        out_specs=(vmem,) * 2,
        compiler_params=pltpu.CompilerParams(vmem_limit_bytes=8 << 20),
        cost_estimate=pl.CostEstimate(flops=1 << 20, bytes_accessed=1 << 20, transcendentals=0),
        name="split",
    )(z, mids, far_own, far_got)


def block_body(inner, s_hbm, f_hbm, fy_hbm, one, two, yone, ytwo, mx, my, base, mxb, s, f, fy, pad, sem):
    moves = ((fy_hbm, fy), (s_hbm, s), (f_hbm, f))
    for v in range(NV):
        for k, (h, t) in enumerate(moves):
            pltpu.make_async_copy(h.at[v], t.at[v], sem.at[k, v]).start()
    piece = lax.axis_index("gx")
    is0 = parity("gx") == 0
    even = parity("gy") == 0
    first = jnp.where(piece == 0, 1.0 / 36.0, 0.0).astype(F32)
    last = jnp.where(piece == PIECES - 1, -1.0 / 36.0, 0.0).astype(F32)
    mxt = jnp.transpose(mx[...] * -0.5)
    myt = jnp.transpose(my[...] * -0.5)
    for i in range(NI):
        mxb[i] = jnp.broadcast_to(mxt[:, i : i + 1], (NJ, NK))
        pad[NI + i, 0:NJ, :] = jnp.broadcast_to(myt[:, i : i + 1], (NJ, NK))

    @pl.loop(0, NV)
    def _(v):
        for k, (h, t) in enumerate(moves):
            pltpu.make_async_copy(h.at[v], t.at[v], sem.at[k, v]).wait()
        for i in range(NI):
            for q in range(NJ // SUB):
                pad[i, pl.ds(SUB + SUB * q, SUB), :] = fy[v, i, pl.ds(SUB * q, SUB), :]
            part = pl.ds(4 * (i % 2), 4)
            a, b = yone[v, i // 2, part, :], ytwo[v, i // 2, part, :]
            pad[i, SUB - 4 : SUB, :] = jnp.where(even, b, a)
            pad[i, SUB + NJ : SUB + NJ + 4, :] = jnp.where(even, a, b)

        for q in range(NJ // SUB):
            rows = pl.ds(SUB * q, SUB)
            a = [one[v, k, rows, :] for k in range(4)]
            b = [two[v, k, rows, :] for k in range(4)]
            low = [jnp.where(is0, b[k], a[k]) for k in range(4)]
            high = [jnp.where(is0, a[k], b[k]) for k in range(4)]
            st = low[:3] + [s[v, i, rows, :] for i in range(NI)] + high[:3]
            fl = [low[3]] + [f[v, i, rows, :] for i in range(NI)] + [high[3]]
            ye, yd, us = [], [], []
            for i in range(NI):
                d6 = (
                    (st[i] + st[i + 6])
                    - 6.0 * (st[i + 1] + st[i + 5])
                    + 15.0 * (st[i + 2] + st[i + 4])
                    - 20.0 * st[i + 3]
                )
                y = inner[C_MG + i] * d6
                ye.append(y - inner[C_C + i] * ye[-1] if i else y)
                u = fl[i + 2] - fl[i]
                us.append(u)
                r = fl[2] if i == 0 else -fl[NI - 1] if i == NI - 1 else u
                r = float(RHO * CS["m"][i]) * r
                if i == 0:
                    r = r + (first * float(CS["m"][i])) * fl[1]
                if i == NI - 1:
                    r = r + (last * float(CS["m"][i])) * fl[NI]
                yd.append(r - float(CS["c"][i]) * yd[-1] if i else r)
            xe = xd = None
            for i in range(NI - 1, -1, -1):
                xe = ye[i] if xe is None else ye[i] - inner[C_C + i] * xe
                xd = yd[i] if xd is None else yd[i] - float(CS["c"][i]) * xd
                at = SUB + SUB * q
                dy = None
                for k, w in enumerate(Y_WEIGHTS, start=1):
                    t = w * (pad[i, pl.ds(at + k, SUB), :] - pad[i, pl.ds(at - k, SUB), :])
                    dy = t if dy is None else dy + t
                d = us[i] * (1.0 / 12.0) + xd
                base[v, i, rows, :] = (st[i + 3] + xe) + (mxb[i, rows, :] * d + pad[NI + i, rows, :] * dy)


def block(inner, state, flux_x, flux_y, one, two, yone, ytwo, mx, my):
    vmem, hbm = pl.BlockSpec(memory_space=pltpu.VMEM), pl.BlockSpec(memory_space=pltpu.HBM)
    return pl.pallas_call(
        block_body,
        out_shape=(
            jax.ShapeDtypeStruct((NV, NI, NJ, NK), F32),
            jax.ShapeDtypeStruct((NI, NJ, NK), F32),
        ),
        in_specs=[vmem] + [hbm] * 3 + [vmem] * 6,
        out_specs=(vmem, vmem),
        scratch_shapes=[pltpu.VMEM((NV, NI, NJ, NK), F32)] * 3
        + [pltpu.VMEM((2 * NI, SUB + NJ + SUB, NK), F32), pltpu.SemaphoreType.DMA((3, NV))],
        compiler_params=pltpu.CompilerParams(vmem_limit_bytes=16 << 20),
        cost_estimate=pl.CostEstimate(flops=1 << 30, bytes_accessed=64 << 20, transcendentals=0),
        name="block",
    )(inner, *in_hbm(state, flux_x, flux_y), one, two, yone, ytwo, mx, my)


def add_outside(half, outer, base, mxb, z, out_hbm, out, sem):
    target = pl.ds(pl.multiple_of(HALF * half, HALF), HALF)
    stores = [pltpu.make_async_copy(out.at[v], out_hbm.at[v, :, target, :], sem.at[v]) for v in range(NV)]
    for v in range(NV):
        for r in range(HALF // SUB):
            rows, part = pl.ds(pl.multiple_of(HALF * half + SUB * r, SUB), SUB), pl.ds(SUB * r, SUB)
            lf, rf, ld, rd = (z[pl.ds((NV * k + v) * HALF + SUB * r, SUB), :] for k in range(4))
            for i in range(NI):
                d = float(CS["left"][i]) * ld + float(CS["right"][i]) * rd
                e = outer[C_LEFT + i] * lf + outer[C_RIGHT + i] * rf
                out[v, i, part, :] = (base[v, i, rows, :] + e) + mxb[i, rows, :] * d
        stores[v].start()
    for c in stores:
        c.wait()


def finish_own_body(outer, base, mxb, z, out_hbm, out, sem):
    add_outside(parity("gx"), outer, base, mxb, z, out_hbm, out, sem)


def finish_body(outer, base, mxb, z, written, out_hbm, out, sem):
    add_outside(1 - parity("gx"), outer, base, mxb, z, out_hbm, out, sem)


def finish(outer, base, mxb, z, *written):
    vmem, hbm = pl.BlockSpec(memory_space=pltpu.VMEM), pl.BlockSpec(memory_space=pltpu.HBM)
    return pl.pallas_call(
        finish_body if written else finish_own_body,
        out_shape=jax.ShapeDtypeStruct((NV, NI, NJ, NK), F32),
        in_specs=[vmem] * 4 + [hbm] * len(written),
        out_specs=hbm,
        scratch_shapes=[pltpu.VMEM((NV, NI, HALF, NK), F32), pltpu.SemaphoreType.DMA((NV,))],
        input_output_aliases={4: 0} if written else {},
        compiler_params=pltpu.CompilerParams(vmem_limit_bytes=12 << 20),
        cost_estimate=pl.CostEstimate(flops=1 << 22, bytes_accessed=2 << 20, transcendentals=0),
        name="finish" if written else "finish_own",
    )(outer, base, mxb, z, *written)


def exchange(x, rows):
    groups = [[2 * p + c for p in range(PAIRS)] for c in range(2)]
    y = lax.all_to_all(x.reshape(PAIRS, rows, NK), "gx", 0, 0, tiled=True, axis_index_groups=groups)
    return y.reshape(PAIRS * rows, NK)


def per_device(flux_x, flux_y, state, metric_x, metric_y, filter_gap):
    count_y = lax.axis_size("gy")
    pair_in = [(i, i ^ 1) for i in range(PIECES)]
    pair_out = [(i, i + 1 if i % 2 else i - 1) for i in range(1, PIECES - 1)]
    y_in = [(i, i ^ 1) for i in range(count_y)]
    y_out = [(i, (i + 1 if i % 2 else i - 1) % count_y) for i in range(count_y)]

    inner, outer, mine, send = own_share(filter_gap, state, flux_x)
    send, state, flux_x, flux_y = lax.optimization_barrier((send, state, flux_x, flux_y))
    got = lax.ppermute(send, "gx", pair_in)
    got, *faces = lax.optimization_barrier((got, *pack(state, flux_x, flux_y)))
    ends, mids = pair(mine, got)
    ends, send_one, send_two, ysend_one, ysend_two = lax.optimization_barrier((ends, *faces))
    ends = exchange(ends, WIDE)
    one = lax.ppermute(send_one, "gx", pair_in)
    two = lax.ppermute(send_two, "gx", pair_out)
    yone = lax.ppermute(ysend_one, "gy", y_in)
    ytwo = lax.ppermute(ysend_two, "gy", y_out)
    outside = join(ends)
    outside, one = lax.optimization_barrier((outside, one))
    two, yone, ytwo = lax.optimization_barrier((two, yone, ytwo))
    base, mxb = block(inner, state, flux_x, flux_y, one, two, yone, ytwo, metric_x, metric_y)
    two, base = lax.optimization_barrier((two, base))
    far_own, far_send = far(outer, two)
    far_got = lax.ppermute(far_send, "gx", pair_in)
    outside, base, mxb, far_got = lax.optimization_barrier((exchange(outside, ROWS), base, mxb, far_got))
    own, send = split(outside, mids, far_own, far_got)
    got = lax.ppermute(send, "gx", pair_in)
    got, out = lax.optimization_barrier((got, finish(outer, base, mxb, own)))
    return finish(outer, base, mxb, got, out)


def solution(mesh):
    return jax.shard_map(
        per_device,
        mesh=mesh,
        in_specs=(
            P(None, "gx", "gy", None),
            P(None, "gx", "gy", None),
            P(None, "gx", "gy", None),
            P("gx", "gy"),
            P("gx", "gy"),
            P("gx"),
        ),
        out_specs=P(None, "gx", "gy", None),
        check_vma=False,
    )
```

```python
import jax
import jax.numpy as jnp
import numpy as np
from jax import lax
from jax.experimental import pallas as pl
from jax.experimental.pallas import tpu as pltpu
from jax.sharding import PartitionSpec as P

NV, NI, NJ, NK = 5, 16, 32, 128
PIECES, PAIRS, HALF = 32, 16, 16
VALUES = 10
ROWS, WIDE = 24, 56
EDGE = VALUES * NV * HALF
SUB = 8
F32 = jnp.float32
Y_WEIGHTS = (4.0 / 5.0, -1.0 / 5.0, 4.0 / 105.0, -1.0 / 280.0)
RHO = 25.0 / 36.0
BETA = 3.0 * RHO
D6 = (1.0, -6.0, 15.0, -20.0, 15.0, -6.0, 1.0)

C_C, C_MG = 0, NI
C_LEFT, C_RIGHT, C_FAR = 0, NI, 2 * NI


def constant_system():
    a = 1.0 / 3.0
    t = np.eye(NI) + a * (np.eye(NI, k=1) + np.eye(NI, k=-1))
    inv = np.linalg.inv(t)
    m, c = [], []
    prev = 0.0
    for _ in range(NI):
        m.append(1.0 / (1.0 - a * prev))
        prev = a * m[-1]
        c.append(prev)
    left, right = -a * inv[:, 0], -a * inv[:, -1]
    hl, hr, tl, tr = left[0], right[0], left[-1], right[-1]
    d = 1.0 / (1.0 - tr * hl)
    pair = dict(inv=d, inv_hl=d * hl, inv_tr=d * tr, down=[hl * tl * d, hr * d, tl * d, tr * hr * d])
    for k in pair:
        pair[k] = [float(t) for t in pair[k]] if isinstance(pair[k], list) else float(pair[k])
    p = dict(hl=hl + hr * hl * tl * d, hr=hr * hr * d, tl=tl * tl * d, tr=tr + tl * tr * hr * d)
    e = [p["tr"]]
    for _ in range(PAIRS - 1):
        e.append(p["tr"] + p["tl"] * p["hr"] * e[-1] / (1.0 - p["hl"] * e[-1]))
    pair.update(p, e=e)
    return dict(m=m, c=c, inv=inv, left=left, right=right, hl=hl, hr=hr, tl=tl, tr=tr, pair=pair)


CS = constant_system()


def flux_weight(row, j):
    w = CS["inv"][row]
    lo = w[j - 1] if 0 <= j - 1 < NI else 0.0
    hi = w[j + 1] if 0 <= j + 1 < NI else 0.0
    return float(RHO * (lo - hi))


def splat(x):
    return jnp.full((SUB, NK), x, F32)


def in_hbm(*arrays):
    return tuple(pltpu.with_memory_space_constraint(a, pltpu.HBM) for a in arrays)


def parity(name):
    return lax.rem(lax.axis_index(name), 2)


def pack_body(s, f, fy, one, two, yone, ytwo, lo, hi, sem, y_sem):
    core, odd = parity("gx"), parity("gy")
    copies = [
        (
            pltpu.make_async_copy(fy.at[v, :, 0:SUB, :], lo.at[v], y_sem.at[0, v]),
            pltpu.make_async_copy(fy.at[v, :, NJ - SUB : NJ, :], hi.at[v], y_sem.at[1, v]),
        )
        for v in range(NV)
    ]
    for both in copies:
        for c in both:
            c.start()

    def faces(right, left):
        moves = [
            pltpu.make_async_copy(s.at[:, NI - 3 : NI], right.at[:, 0:3], sem.at[2]),
            pltpu.make_async_copy(f.at[:, NI - 1 : NI], right.at[:, 3:4], sem.at[3]),
            pltpu.make_async_copy(s.at[:, 0:3], left.at[:, 0:3], sem.at[4]),
            pltpu.make_async_copy(f.at[:, 0:1], left.at[:, 3:4], sem.at[5]),
        ]
        for c in moves:
            c.start()
        for c in moves:
            c.wait()

    def rows(top, bottom):
        for v in range(NV):
            for c in copies[v]:
                c.wait()
            for i in range(NI):
                part = pl.ds(4 * (i % 2), 4)
                top[v, i // 2, part, :] = hi[v, i, 4:8, :]
                bottom[v, i // 2, part, :] = lo[v, i, 0:4, :]

    @pl.when(core == 0)
    def _():
        faces(one, two)

    @pl.when(core == 1)
    def _():
        faces(two, one)

    @pl.when(odd == 0)
    def _():
        rows(yone, ytwo)

    @pl.when(odd == 1)
    def _():
        rows(ytwo, yone)


def pack(state, flux_x, flux_y):
    x_out = jax.ShapeDtypeStruct((NV, 4, NJ, NK), F32)
    y_out = jax.ShapeDtypeStruct((NV, NI // 2, SUB, NK), F32)
    return pl.pallas_call(
        pack_body,
        out_shape=(x_out, x_out, y_out, y_out),
        in_specs=[pl.BlockSpec(memory_space=pltpu.HBM)] * 3,
        out_specs=(pl.BlockSpec(memory_space=pltpu.VMEM),) * 4,
        scratch_shapes=[
            pltpu.VMEM((NV, NI, SUB, NK), F32),
            pltpu.VMEM((NV, NI, SUB, NK), F32),
            pltpu.SemaphoreType.DMA((6,)),
            pltpu.SemaphoreType.DMA((2, NV)),
        ],
        compiler_params=pltpu.CompilerParams(vmem_limit_bytes=8 << 20),
        cost_estimate=pl.CostEstimate(flops=0, bytes_accessed=2 << 20, transcendentals=0),
        name="pack",
    )(*in_hbm(state, flux_x, flux_y))


def own_body(gap_hbm, s_hbm, f_hbm, inner, outer, mine, send, gap, s, f, own, gap_sem, sem):
    gap_load = pltpu.make_async_copy(gap_hbm, gap, gap_sem)
    gap_load.start()
    loads = [
        (
            pltpu.make_async_copy(s_hbm.at[v], s.at[v], sem.at[0, v]),
            pltpu.make_async_copy(f_hbm.at[v], f.at[v], sem.at[1, v]),
        )
        for v in range(NV)
    ]
    for both in loads:
        for c in both:
            c.start()
    core = parity("gx")
    piece = lax.axis_index("gx")
    gap_load.wait()
    alpha = [0.5 - splat(gap[i]) for i in range(NI)]
    g32 = [(0.5 - a) * (1.0 / 32.0) for a in alpha]
    m, c = [None] * NI, [None] * NI
    n, b = [None] * NI, [None] * NI
    for k in range(NI):
        m[k] = 1.0 / (1.0 - alpha[k] * c[k - 1]) if k else jnp.ones((SUB, NK), F32)
        c[k] = alpha[k] * m[k]
        r = NI - 1 - k
        n[r] = 1.0 / (1.0 - alpha[r] * b[r + 1]) if k else jnp.ones((SUB, NK), F32)
        b[r] = alpha[r] * n[r]
    left, right = [None] * NI, [None] * NI
    wh, wt = [None] * NI, [None] * NI
    left[0], right[NI - 1] = -b[0], -c[NI - 1]
    qh, qt = None, None
    for k in range(NI):
        r = NI - 1 - k
        if k:
            left[k] = -b[k] * left[k - 1]
            right[r] = -c[r] * right[r + 1]
            qh = -b[k - 1] if qh is None else -b[k - 1] * qh
            qt = -c[r + 1] if qt is None else -c[r + 1] * qt
            wh[k] = qh * n[k]
            wt[r] = qt * m[r]
        else:
            wh[0], wt[NI - 1] = n[0], m[NI - 1]
    for k in range(NI):
        inner[C_C + k] = c[k]
        inner[C_MG + k] = m[k] * g32[k]
        outer[C_LEFT + k] = left[k]
        outer[C_RIGHT + k] = right[k]
    vh = [wh[k] * g32[k] for k in range(NI)]
    vt = [wt[k] * g32[k] for k in range(NI)]

    def spread(v, j):
        terms = [D6[q + 3] * v[j - q] for q in range(-3, 4) if 0 <= j - q < NI]
        total = terms[0]
        for t in terms[1:]:
            total = total + t
        return total

    edge = [-alpha[0] * wh[0], -alpha[NI - 1] * wh[NI - 1], -alpha[0] * wt[0], -alpha[NI - 1] * wt[NI - 1]]
    low = [spread(v, q - 3) for v in (vh, vt) for q in range(3)]
    high = [spread(v, NI + q) for v in (vh, vt) for q in range(3)]
    edge += [jnp.where(core == 0, h, l) for h, l in zip(high, low)]
    edge += [jnp.where(core == 0, l, h) for h, l in zip(high, low)]
    for q in range(3):
        outer[C_FAR + q] = jnp.where(core == 0, edge[13 + q], edge[10 + q])
    for k, t in enumerate(edge):
        mine[pl.ds(EDGE + k, 1), :] = t[0:1]
        send[pl.ds(EDGE + k, 1), :] = t[0:1]

    first = jnp.where(piece == 0, 1.0 / 36.0, 0.0).astype(F32)
    last = jnp.where(piece == PIECES - 1, -1.0 / 36.0, 0.0).astype(F32)
    inv = CS["inv"]
    fh = [flux_weight(0, j) for j in range(NI)]
    ft = [flux_weight(NI - 1, j) for j in range(NI)]
    fh[0] = (fh[0] - BETA) + float(inv[0, 0]) * first
    ft[0] = ft[0] + float(inv[NI - 1, 0]) * first
    fh[NI - 1] = fh[NI - 1] + float(inv[0, NI - 1]) * last
    ft[NI - 1] = (ft[NI - 1] + BETA) + float(inv[NI - 1, NI - 1]) * last

    for i in range(NI):
        own[i] = spread(vh, i)
        own[NI + i] = spread(vt, i)

    s_in, s_out = (NI - 3) * (1 - core), (NI - 3) * core
    for v in range(NV):
        for c in loads[v]:
            c.wait()
        for out, half in ((mine, core), (send, 1 - core)):
            for r in range(HALF // SUB):
                rows = pl.ds(pl.multiple_of(HALF * half + SUB * r, SUB), SUB)
                sums = [None] * 4
                for i in range(NI):
                    a, z = s[v, i, rows, :], f[v, i, rows, :]
                    terms = (own[i] * a, own[NI + i] * a, fh[i] * z, ft[i] * z)
                    sums = [t if o is None else o + t for o, t in zip(sums, terms)]
                faces = [s[v, s_in + k, rows, :] for k in range(3)] + [s[v, s_out + k, rows, :] for k in range(3)]
                for k, t in enumerate(sums + faces):
                    out[pl.ds((NV * k + v) * HALF + SUB * r, SUB), :] = t


def own_share(gap, state, flux_x):
    vmem, hbm = pl.BlockSpec(memory_space=pltpu.VMEM), pl.BlockSpec(memory_space=pltpu.HBM)
    coef = jax.ShapeDtypeStruct((2 * NI, SUB, NK), F32)
    coef_far = jax.ShapeDtypeStruct((2 * NI + 3, SUB, NK), F32)
    values = jax.ShapeDtypeStruct((EDGE + 16, NK), F32)
    return pl.pallas_call(
        own_body,
        out_shape=(coef, coef_far, values, values),
        in_specs=[hbm, hbm, hbm],
        out_specs=(vmem,) * 4,
        scratch_shapes=[
            pltpu.SMEM((NI,), F32),
            pltpu.VMEM((NV, NI, NJ, NK), F32),
            pltpu.VMEM((NV, NI, NJ, NK), F32),
            pltpu.VMEM((2 * NI, SUB, NK), F32),
            pltpu.SemaphoreType.DMA,
            pltpu.SemaphoreType.DMA((2, NV)),
        ],
        compiler_params=pltpu.CompilerParams(vmem_limit_bytes=12 << 20),
        cost_estimate=pl.CostEstimate(flops=1 << 24, bytes_accessed=4 << 20, transcendentals=0),
        name="own_share",
    )(*in_hbm(gap, state, flux_x))


def pair_body(mine, got, out_hbm, mids, out, sem):
    is0 = parity("gx") == 0

    def both(rows):
        x, y = mine[rows, :], got[rows, :]
        return jnp.where(is0, x, y), jnp.where(is0, y, x)

    ca, cb = zip(*(both(pl.ds(EDGE + k, 1)) for k in range(16)))
    ca, cb = ([jnp.broadcast_to(t, (SUB, NK)) for t in c] for c in (ca, cb))
    hla, hra, tla, tra = ca[:4]
    hlb, hrb, tlb, trb = cb[:4]
    inv = 1.0 / (1.0 - tra * hlb)
    down = [hlb * tla * inv, hrb * inv, tla * inv, tra * hrb * inv, hlb * inv, inv, tra * inv]
    for k, t in enumerate(down):
        mids[pl.ds(4 * NV * HALF + k, 1), :] = t[0:1]
    cross_h, cross_t = hra * inv, tlb * inv
    edge = [hla + hra * down[0], hra * down[1], tlb * down[2], trb + tlb * down[3]]
    edge += [ca[10 + q] + (cross_h * hlb) * ca[13 + q] for q in range(3)]
    edge += [cross_t * ca[13 + q] for q in range(3)]
    edge += [cross_h * cb[10 + q] for q in range(3)]
    edge += [cb[13 + q] + (cross_t * tra) * cb[10 + q] for q in range(3)]
    lane = lax.broadcasted_iota(jnp.int32, (SUB, NK), 1)
    packed = jnp.zeros((SUB, NK), F32)
    for k, t in enumerate(edge):
        packed = jnp.where(lane == k, t, packed)

    k = CS["pair"]
    blocks = [pl.ds(WIDE * SUB * r, WIDE * SUB) for r in range(HALF // SUB)]
    stores = [pltpu.make_async_copy(out.at[b], out_hbm.at[b], sem.at[r]) for r, b in enumerate(blocks)]
    for r in range(HALF // SUB):
        at = WIDE * SUB * r
        out[pl.ds(at + VALUES * NV, SUB, stride=WIDE), :] = packed
        for v in range(NV):
            a, b = zip(*(both(pl.ds((NV * e + v) * HALF + SUB * r, SUB)) for e in range(VALUES)))
            ha, ta, hb, tb = a[0], a[1], b[0], b[1]
            for q in range(3):
                ha, ta = ha + ca[4 + q] * b[4 + q], ta + ca[7 + q] * b[4 + q]
                hb, tb = hb + cb[4 + q] * a[4 + q], tb + cb[7 + q] * a[4 + q]
            head = (hb + hlb * ta) * inv
            tail = (ta + tra * hb) * inv
            da, ea, db, eb = a[2], a[3], b[2], b[3]
            dhead = k["inv"] * db + k["inv_hl"] * ea
            dtail = k["inv"] * ea + k["inv_tr"] * db
            values = [ha + hra * head, tb + tlb * tail, da + float(CS["hr"]) * dhead, eb + float(CS["tl"]) * dtail]
            values += list(a[7:10]) + list(b[7:10])
            for e, t in enumerate(values):
                out[pl.ds(at + NV * e + v, SUB, stride=WIDE), :] = t
            for e, t in enumerate((head, tail, dhead, dtail)):
                mids[pl.ds((NV * e + v) * HALF + SUB * r, SUB), :] = t
        stores[r].start()
    for c in stores:
        c.wait()


def pair(mine, got):
    vmem = pl.BlockSpec(memory_space=pltpu.VMEM)
    return pl.pallas_call(
        pair_body,
        out_shape=(
            jax.ShapeDtypeStruct((PAIRS * WIDE, NK), F32),
            jax.ShapeDtypeStruct((4 * NV * HALF + SUB, NK), F32),
        ),
        in_specs=[vmem] * 2,
        out_specs=(pl.BlockSpec(memory_space=pltpu.HBM), vmem),
        scratch_shapes=[pltpu.VMEM((PAIRS * WIDE, NK), F32), pltpu.SemaphoreType.DMA((HALF // SUB,))],
        compiler_params=pltpu.CompilerParams(vmem_limit_bytes=8 << 20),
        cost_estimate=pl.CostEstimate(flops=1 << 20, bytes_accessed=1 << 20, transcendentals=0),
        name="pair",
    )(mine, got)


def join_body(x, out_hbm, out, coef, sem):
    for r in range(PAIRS // SUB):
        packed = x[pl.ds(WIDE * SUB * r + VALUES * NV, SUB, stride=WIDE), :]
        for k in range(16):
            coef[pl.ds(PAIRS * k + SUB * r, SUB), :] = jnp.broadcast_to(packed[:, k : k + 1], (SUB, NK))

    def row(p, k):
        return jnp.broadcast_to(coef[pl.ds(PAIRS * k + p, 1), :], (NV, NK))

    def value(p, k):
        return x[pl.ds(WIDE * p + NV * k, NV), :]

    c = CS["pair"]
    head_f, tail_f, head_d, tail_d = [], [], [], []
    for p in range(PAIRS):
        h, t, dh, dt = (value(p, k) for k in range(4))
        if p:
            for q in range(3):
                z = value(p - 1, 7 + q)
                h, t = h + row(p, 4 + q) * z, t + row(p, 7 + q) * z
        if p < PAIRS - 1:
            for q in range(3):
                z = value(p + 1, 4 + q)
                h, t = h + row(p, 10 + q) * z, t + row(p, 13 + q) * z
        head_f.append(h)
        tail_f.append(t)
        head_d.append(dh)
        tail_d.append(dt)

    scale = 8.0
    num, den = [None] * PAIRS, [None] * PAIRS
    hl, hr, tl, tr = ([row(p, k) for p in range(PAIRS)] for k in range(4))
    num[0], den[0] = tr[0], jnp.ones((NV, NK), F32)
    for p in range(1, PAIRS):
        cross = tl[p] * hr[p] - tr[p] * hl[p]
        num[p] = (scale * tr[p]) * den[p - 1] + (scale * cross) * num[p - 1]
        den[p] = scale * den[p - 1] - (scale * hl[p]) * num[p - 1]
    inv = [None] + [1.0 / den[p] for p in range(1, PAIRS)]
    e = [num[0]] + [num[p] * inv[p] for p in range(1, PAIRS)]
    keep = [None] + [(scale * den[p - 1]) * inv[p] for p in range(1, PAIRS)]

    fwd_f, fwd_d = [tail_f[0]], [tail_d[0]]
    chl, chr_, ctl, ce = c["hl"], c["hr"], c["tl"], c["e"]
    for p in range(1, PAIRS):
        a = tl[p] * keep[p]
        fwd_f.append((tail_f[p] + (a * e[p - 1]) * head_f[p]) + a * fwd_f[-1])
        k = ctl / (1.0 - chl * ce[p - 1])
        fwd_d.append((tail_d[p] + float(k * ce[p - 1]) * head_d[p]) + float(k) * fwd_d[-1])

    blocks = [pl.ds(ROWS * SUB * r, ROWS * SUB) for r in range(PAIRS // SUB)]
    stores = [pltpu.make_async_copy(out.at[b], out_hbm.at[b], sem.at[r]) for r, b in enumerate(blocks)]
    zero = jnp.zeros((NV, NK), F32)
    right_f, right_d = zero, zero
    for p in range(PAIRS - 1, -1, -1):
        if p:
            h = keep[p]
            at_f = (head_f[p] + hl[p] * fwd_f[p - 1]) * h + (hr[p] * h) * right_f
            left_f = fwd_f[p - 1] + e[p - 1] * at_f
            k = 1.0 / (1.0 - chl * ce[p - 1])
            at_d = (float(k) * head_d[p] + float(k * chl) * fwd_d[p - 1]) + float(k * chr_) * right_d
            left_d = fwd_d[p - 1] + float(ce[p - 1]) * at_d
        else:
            at_f = at_d = left_f = left_d = zero
        for k, val in enumerate((left_f, right_f, left_d, right_d)):
            out[pl.ds(ROWS * p + NV * k, NV), :] = val
        right_f, right_d = at_f, at_d
        if p % SUB == 0:
            stores[p // SUB].start()
    for t in stores:
        t.wait()


def join(x):
    vmem = pl.BlockSpec(memory_space=pltpu.VMEM)
    return pl.pallas_call(
        join_body,
        out_shape=jax.ShapeDtypeStruct((PAIRS * ROWS, NK), F32),
        in_specs=[vmem],
        out_specs=pl.BlockSpec(memory_space=pltpu.HBM),
        scratch_shapes=[
            pltpu.VMEM((PAIRS * ROWS, NK), F32),
            pltpu.VMEM((16 * PAIRS, NK), F32),
            pltpu.SemaphoreType.DMA((PAIRS // SUB,)),
        ],
        compiler_params=pltpu.CompilerParams(vmem_limit_bytes=8 << 20),
        cost_estimate=pl.CostEstimate(flops=1 << 20, bytes_accessed=1 << 20, transcendentals=0),
        name="join",
    )(x)


def far_body(outer, two, own, other):
    core = parity("gx")
    for out, half in ((own, core), (other, 1 - core)):
        for v in range(NV):
            for r in range(HALF // SUB):
                rows = pl.ds(pl.multiple_of(HALF * half + SUB * r, SUB), SUB)
                a = [two[v, k, rows, :] for k in range(3)]
                out[pl.ds(v * HALF + SUB * r, SUB), :] = (
                    outer[C_FAR] * a[0] + outer[C_FAR + 1] * a[1] + outer[C_FAR + 2] * a[2]
                )


def far(outer, two):
    vmem = pl.BlockSpec(memory_space=pltpu.VMEM)
    out = jax.ShapeDtypeStruct((NV * HALF, NK), F32)
    return pl.pallas_call(
        far_body,
        out_shape=(out, out),
        in_specs=[vmem] * 2,
        out_specs=(vmem,) * 2,
        compiler_params=pltpu.CompilerParams(vmem_limit_bytes=8 << 20),
        cost_estimate=pl.CostEstimate(flops=1 << 18, bytes_accessed=1 << 19, transcendentals=0),
        name="far",
    )(outer, two)


def split_body(z, mids, far_own, far_got, own, send):
    is0 = parity("gx") == 0
    c = CS["pair"]
    down = [jnp.broadcast_to(mids[pl.ds(4 * NV * HALF + k, 1), :], (SUB, NK)) for k in range(7)]
    for r in range(HALF // SUB):
        for v in range(NV):
            lf, rf, ld, rd = (z[pl.ds(ROWS * SUB * r + NV * k + v, SUB, stride=ROWS), :] for k in range(4))
            head, tail, dhead, dtail = (mids[pl.ds((NV * k + v) * HALF + SUB * r, SUB), :] for k in range(4))
            part = pl.ds(v * HALF + SUB * r, SUB)
            x, y = far_own[part, :], far_got[part, :]
            fa, fb = jnp.where(is0, x, y), jnp.where(is0, y, x)
            head = (head + down[4] * fa + down[5] * fb) + down[0] * lf + down[1] * rf
            tail = (tail + down[5] * fa + down[6] * fb) + down[2] * lf + down[3] * rf
            dhead = dhead + c["down"][0] * ld + c["down"][1] * rd
            dtail = dtail + c["down"][2] * ld + c["down"][3] * rd
            a, b = (lf, head, ld, dhead), (tail, rf, dtail, rd)
            for k in range(4):
                rows = pl.ds((NV * k + v) * HALF + SUB * r, SUB)
                own[rows, :] = jnp.where(is0, a[k], b[k])
                send[rows, :] = jnp.where(is0, b[k], a[k])


def split(z, mids, far_own, far_got):
    vmem = pl.BlockSpec(memory_space=pltpu.VMEM)
    own = jax.ShapeDtypeStruct((4 * NV * HALF, NK), F32)
    send = jax.ShapeDtypeStruct((4 * NV * HALF, NK), F32)
    return pl.pallas_call(
        split_body,
        out_shape=(own, send),
        in_specs=[vmem] * 4,
        out_specs=(vmem,) * 2,
        compiler_params=pltpu.CompilerParams(vmem_limit_bytes=8 << 20),
        cost_estimate=pl.CostEstimate(flops=1 << 20, bytes_accessed=1 << 20, transcendentals=0),
        name="split",
    )(z, mids, far_own, far_got)


def block_body(inner, s_hbm, f_hbm, fy_hbm, one, two, yone, ytwo, mx, my, base, mxb, s, f, fy, pad, sem):
    moves = ((fy_hbm, fy), (s_hbm, s), (f_hbm, f))
    for v in range(NV):
        for k, (h, t) in enumerate(moves):
            pltpu.make_async_copy(h.at[v], t.at[v], sem.at[k, v]).start()
    piece = lax.axis_index("gx")
    is0 = parity("gx") == 0
    even = parity("gy") == 0
    first = jnp.where(piece == 0, 1.0 / 36.0, 0.0).astype(F32)
    last = jnp.where(piece == PIECES - 1, -1.0 / 36.0, 0.0).astype(F32)
    mxt = jnp.transpose(mx[...] * -0.5)
    myt = jnp.transpose(my[...] * -0.5)
    for i in range(NI):
        mxb[i] = jnp.broadcast_to(mxt[:, i : i + 1], (NJ, NK))
        pad[NI + i, 0:NJ, :] = jnp.broadcast_to(myt[:, i : i + 1], (NJ, NK))

    @pl.loop(0, NV)
    def _(v):
        for k, (h, t) in enumerate(moves):
            pltpu.make_async_copy(h.at[v], t.at[v], sem.at[k, v]).wait()
        for i in range(NI):
            for q in range(NJ // SUB):
                pad[i, pl.ds(SUB + SUB * q, SUB), :] = fy[v, i, pl.ds(SUB * q, SUB), :]
            part = pl.ds(4 * (i % 2), 4)
            a, b = yone[v, i // 2, part, :], ytwo[v, i // 2, part, :]
            pad[i, SUB - 4 : SUB, :] = jnp.where(even, b, a)
            pad[i, SUB + NJ : SUB + NJ + 4, :] = jnp.where(even, a, b)

        for q in range(NJ // SUB):
            rows = pl.ds(SUB * q, SUB)
            a = [one[v, k, rows, :] for k in range(4)]
            b = [two[v, k, rows, :] for k in range(4)]
            low = [jnp.where(is0, b[k], a[k]) for k in range(4)]
            high = [jnp.where(is0, a[k], b[k]) for k in range(4)]
            st = low[:3] + [s[v, i, rows, :] for i in range(NI)] + high[:3]
            fl = [low[3]] + [f[v, i, rows, :] for i in range(NI)] + [high[3]]
            ye, yd, us = [], [], []
            for i in range(NI):
                d6 = (
                    (st[i] + st[i + 6])
                    - 6.0 * (st[i + 1] + st[i + 5])
                    + 15.0 * (st[i + 2] + st[i + 4])
                    - 20.0 * st[i + 3]
                )
                y = inner[C_MG + i] * d6
                ye.append(y - inner[C_C + i] * ye[-1] if i else y)
                u = fl[i + 2] - fl[i]
                us.append(u)
                r = fl[2] if i == 0 else -fl[NI - 1] if i == NI - 1 else u
                r = float(RHO * CS["m"][i]) * r
                if i == 0:
                    r = r + (first * float(CS["m"][i])) * fl[1]
                if i == NI - 1:
                    r = r + (last * float(CS["m"][i])) * fl[NI]
                yd.append(r - float(CS["c"][i]) * yd[-1] if i else r)
            xe = xd = None
            for i in range(NI - 1, -1, -1):
                xe = ye[i] if xe is None else ye[i] - inner[C_C + i] * xe
                xd = yd[i] if xd is None else yd[i] - float(CS["c"][i]) * xd
                at = SUB + SUB * q
                dy = None
                for k, w in enumerate(Y_WEIGHTS, start=1):
                    t = w * (pad[i, pl.ds(at + k, SUB), :] - pad[i, pl.ds(at - k, SUB), :])
                    dy = t if dy is None else dy + t
                d = us[i] * (1.0 / 12.0) + xd
                base[v, i, rows, :] = (st[i + 3] + xe) + (mxb[i, rows, :] * d + pad[NI + i, rows, :] * dy)


def block(inner, state, flux_x, flux_y, one, two, yone, ytwo, mx, my):
    vmem, hbm = pl.BlockSpec(memory_space=pltpu.VMEM), pl.BlockSpec(memory_space=pltpu.HBM)
    return pl.pallas_call(
        block_body,
        out_shape=(
            jax.ShapeDtypeStruct((NV, NI, NJ, NK), F32),
            jax.ShapeDtypeStruct((NI, NJ, NK), F32),
        ),
        in_specs=[vmem] + [hbm] * 3 + [vmem] * 6,
        out_specs=(vmem, vmem),
        scratch_shapes=[pltpu.VMEM((NV, NI, NJ, NK), F32)] * 3
        + [pltpu.VMEM((2 * NI, SUB + NJ + SUB, NK), F32), pltpu.SemaphoreType.DMA((3, NV))],
        compiler_params=pltpu.CompilerParams(vmem_limit_bytes=16 << 20),
        cost_estimate=pl.CostEstimate(flops=1 << 30, bytes_accessed=64 << 20, transcendentals=0),
        name="block",
    )(inner, *in_hbm(state, flux_x, flux_y), one, two, yone, ytwo, mx, my)


def add_outside(half, outer, base, mxb, z, out_hbm, out, sem):
    target = pl.ds(pl.multiple_of(HALF * half, HALF), HALF)
    stores = [pltpu.make_async_copy(out.at[v], out_hbm.at[v, :, target, :], sem.at[v]) for v in range(NV)]
    for v in range(NV):
        for r in range(HALF // SUB):
            rows, part = pl.ds(pl.multiple_of(HALF * half + SUB * r, SUB), SUB), pl.ds(SUB * r, SUB)
            lf, rf, ld, rd = (z[pl.ds((NV * k + v) * HALF + SUB * r, SUB), :] for k in range(4))
            for i in range(NI):
                d = float(CS["left"][i]) * ld + float(CS["right"][i]) * rd
                e = outer[C_LEFT + i] * lf + outer[C_RIGHT + i] * rf
                out[v, i, part, :] = (base[v, i, rows, :] + e) + mxb[i, rows, :] * d
        stores[v].start()
    for c in stores:
        c.wait()


def finish_own_body(outer, base, mxb, z, out_hbm, out, sem):
    add_outside(parity("gx"), outer, base, mxb, z, out_hbm, out, sem)


def finish_body(outer, base, mxb, z, written, out_hbm, out, sem):
    add_outside(1 - parity("gx"), outer, base, mxb, z, out_hbm, out, sem)


def finish(outer, base, mxb, z, *written):
    vmem, hbm = pl.BlockSpec(memory_space=pltpu.VMEM), pl.BlockSpec(memory_space=pltpu.HBM)
    return pl.pallas_call(
        finish_body if written else finish_own_body,
        out_shape=jax.ShapeDtypeStruct((NV, NI, NJ, NK), F32),
        in_specs=[vmem] * 4 + [hbm] * len(written),
        out_specs=hbm,
        scratch_shapes=[pltpu.VMEM((NV, NI, HALF, NK), F32), pltpu.SemaphoreType.DMA((NV,))],
        input_output_aliases={4: 0} if written else {},
        compiler_params=pltpu.CompilerParams(vmem_limit_bytes=12 << 20),
        cost_estimate=pl.CostEstimate(flops=1 << 22, bytes_accessed=2 << 20, transcendentals=0),
        name="finish" if written else "finish_own",
    )(outer, base, mxb, z, *written)


def exchange(x, rows):
    groups = [[2 * p + c for p in range(PAIRS)] for c in range(2)]
    y = lax.all_to_all(x.reshape(PAIRS, rows, NK), "gx", 0, 0, tiled=True, axis_index_groups=groups)
    return y.reshape(PAIRS * rows, NK)


def per_device(flux_x, flux_y, state, metric_x, metric_y, filter_gap):
    count_y = lax.axis_size("gy")
    pair_in = [(i, i ^ 1) for i in range(PIECES)]
    pair_out = [(i, i + 1 if i % 2 else i - 1) for i in range(1, PIECES - 1)]
    y_in = [(i, i ^ 1) for i in range(count_y)]
    y_out = [(i, (i + 1 if i % 2 else i - 1) % count_y) for i in range(count_y)]

    inner, outer, mine, send = own_share(filter_gap, state, flux_x)
    send, state, flux_x, flux_y = lax.optimization_barrier((send, state, flux_x, flux_y))
    got = lax.ppermute(send, "gx", pair_in)
    got, *faces = lax.optimization_barrier((got, *pack(state, flux_x, flux_y)))
    ends, mids = pair(mine, got)
    ends, send_one, send_two, ysend_one, ysend_two = lax.optimization_barrier((ends, *faces))
    ends = exchange(ends, WIDE)
    one = lax.ppermute(send_one, "gx", pair_in)
    two = lax.ppermute(send_two, "gx", pair_out)
    yone = lax.ppermute(ysend_one, "gy", y_in)
    ytwo = lax.ppermute(ysend_two, "gy", y_out)
    outside = join(ends)
    outside, one = lax.optimization_barrier((outside, one))
    two, yone, ytwo = lax.optimization_barrier((two, yone, ytwo))
    base, mxb = block(inner, state, flux_x, flux_y, one, two, yone, ytwo, metric_x, metric_y)
    two, base = lax.optimization_barrier((two, base))
    far_own, far_send = far(outer, two)
    far_got = lax.ppermute(far_send, "gx", pair_in)
    outside, base, mxb, far_got = lax.optimization_barrier((exchange(outside, ROWS), base, mxb, far_got))
    own, send = split(outside, mids, far_own, far_got)
    got = lax.ppermute(send, "gx", pair_in)
    got, out = lax.optimization_barrier((got, finish(outer, base, mxb, own)))
    return finish(outer, base, mxb, got, out)


def solution(mesh):
    return jax.shard_map(
        per_device,
        mesh=mesh,
        in_specs=(
            P(None, "gx", "gy", None),
            P(None, "gx", "gy", None),
            P(None, "gx", "gy", None),
            P("gx", "gy"),
            P("gx", "gy"),
            P("gx"),
        ),
        out_specs=P(None, "gx", "gy", None),
        check_vma=False,
    )
```
